32 devices in a mesh: dp: 4 (over y, x), heads: 2 (over core), tensor: 4 (over z).
Axes of the slice: x: 2, y: 2, z: 4, core: 2. Of those that a mesh axis runs over, the one named last changes fastest.
Arguments:
- inputs: bfloat16 [6304, 512], P(('dp', 'heads', 'tensor')), may hold values from -6 to 6
- cotangent: bfloat16 [6304, 512], P(('dp', 'heads', 'tensor')), may hold values from -6 to 6
- routes: int32 [6304, 2], P(('dp', 'heads')), may hold values from 0 to 31, all different within a row; in each aligned block of 788 rows (0 to 787, 788 to 1575, ...) at most 64 rows name the same one
- gain_attn: float32 [512], replicated, may hold values from 0.25 to 1.75
- gain_expert: float32 [512], replicated, may hold values from 0.25 to 1.75
- tau: float32 [8], replicated, may hold values from 2 to 12
- w_qkv: bfloat16 [3, 512, 512], P(None, ('dp', 'tensor'), 'heads'), may hold values from -0.25 to 0.25
- w_out_attn: bfloat16 [512, 512], P('heads', ('dp', 'tensor')), may hold values from -2 to 2
- w_router: bfloat16 [512, 32], P(('dp', 'heads')), may hold values from -0.21875 to 0.21875
- w_in: bfloat16 [32, 512, 2048], P(('dp', 'heads'), None, 'tensor'), may hold values from -0.25 to 0.25
- w_out: bfloat16 [32, 2048, 512], P(('dp', 'heads'), 'tensor'), may hold values from -0.125 to 0.125
Outputs:
- output: bfloat16 [6304, 512], P(('dp', 'heads', 'tensor'))
- grad_input: bfloat16 [6304, 512], P(('dp', 'heads', 'tensor'))
- grad_gain_attn: float32 [512], replicated
- grad_gain_expert: float32 [512], replicated
- grad_qkv: float32 [3, 512, 512], P(None, ('dp', 'tensor'), 'heads')
- grad_out_attn: float32 [512, 512], P('heads', ('dp', 'tensor'))
- grad_router: float32 [512, 32], P(('dp', 'heads'))
- grad_in: float32 [32, 512, 2048], P(('dp', 'heads'), None, 'tensor')
- grad_out: float32 [32, 2048, 512], P(('dp', 'heads'), 'tensor')
- clipped_qk: bfloat16 [2, 512, 512], P(None, ('dp', 'tensor'), 'heads')
The draws below stay inside these ranges and needn't reach their ends.
Inputs may be any that keep to these rules, and one draw needn't show every extreme that they name: `routes`: each row names two different experts. In each aligned block of 788 rows, no expert is named by more than 64 rows, a bound that some block reaches.
All inputs are finite; a program needn't handle non-finite values.
Results may differ from the reference program's by a relative error of at most 0.017.
Values may be sent and summed in bfloat16 or wider, within the bound.
A program may use at most 192 MiB of HBM per device.

```python
import math
import jax
import jax.numpy as jnp
import numpy as np
from jax import lax

D = 512
HEADS = 8
HEAD_DIM = 64
FF = 2048
EXPERTS = 32
SEQ = 197
ROWS = 197
IMAGES = 32
TOKENS = 6304
CAP = 64
N_DP = 4
N_HEADS = 2
N_TENSOR = 4


def block_levels(key, shape, shards, low, high):
    level, own = 1.0, jax.random.fold_in(key, 6)
    for axis_at, blocks in shards:
        steps = jnp.exp(jax.random.uniform(jax.random.fold_in(own, axis_at), (blocks,), jnp.float32, low / len(shards), high / len(shards)))
        level = level * jnp.repeat(steps, shape[axis_at] // blocks).reshape([-1 if axis == axis_at else 1 for axis in range(len(shape))])
    return level


def shared_out(stream_key, own, number, rows, number_of, top, reach, slope):
    sequence = jax.random.permutation(stream_key, number_of)
    heavy_load, common = load_shares(number_of, rows * top, reach, slope, True), load_shares(number_of, rows * top, reach, slope, False)
    places = jnp.arange(number_of)

    def named(lengths, turn):
        used = int((lengths > 0).sum())
        fixed = max(1, used // 4)
        moved = fixed + (places - fixed + turn * (used - fixed)) % max(1, number_of - fixed)
        return jnp.zeros((number_of,), jnp.int32).at[sequence[jnp.where(places < fixed, places, moved)]].set(jnp.asarray(lengths, jnp.int32))

    lengths = jnp.where(number % 4 == 0, named(heavy_load, number // 4), named(common, number - number // 4 - 1))
    mixed = jax.random.permutation(jax.random.fold_in(own, 3), number_of)
    source_of, sink = mixed[0:number_of // 2 * 2:2], mixed[1:number_of // 2 * 2:2]
    slack = jnp.minimum(lengths[source_of] - 1, reach - lengths[sink]) // 2
    slack = jnp.where((source_of == sequence[0]) | (sink == sequence[0]) | (lengths[sink] == 0), 0, jnp.maximum(slack, 0))
    moved = jax.random.randint(jax.random.fold_in(own, 4), (number_of // 2,), 0, 1 << 20) % (slack + 1)
    lengths = lengths.at[source_of].add(-moved).at[sink].add(moved)
    items = jnp.searchsorted(jnp.cumsum(lengths), jnp.arange(rows * top), side="right").astype(jnp.int32)
    grid = items.reshape(top, rows).T
    grid = grid[jax.random.permutation(jax.random.fold_in(own, 1), rows)]
    turn = jax.random.randint(jax.random.fold_in(own, 2), (rows, 1), 0, top)
    return jnp.take_along_axis(grid, (jnp.arange(top)[None, :] + turn) % top, axis=1)


def load_shares(count, total, most, lean, full):
    portions = [(1 << 20) // math.isqrt(standing ** lean) + 1 for standing in range(1, count + 1)]
    largest = most if full else min(most, max(-(-total // count), total * portions[0] // sum(portions)))
    least = 1 if total - largest >= count - 1 else 0
    counts, rest = [largest] + [least] * (count - 1), total - largest - least * (count - 1)
    while rest > 0:
        free = [i for i in range(1, count) if counts[i] < largest] or [i for i in range(1, count) if counts[i] < most]
        whole, budget = sum([portions[i] for i in free]), rest
        for i in free:
            more = min(most - counts[i], max(1, budget * portions[i] // whole), rest)
            counts[i] = counts[i] + more
            rest = rest - more
    return np.array(counts)


def centred(stream_key, extent, scale, limit, cuts=(), kind=jnp.bfloat16):
    drawn = scale * jax.random.normal(stream_key, extent, jnp.float32)
    if cuts:
        drawn = drawn * block_levels(stream_key, extent, cuts, -0.22, 0.18)
    return jnp.clip(drawn, -limit, limit).astype(kind)


def setup_inputs(seed: int = 0) -> dict:
    key_list = jax.random.split(jax.random.key(seed), 12)
    inputs = centred(key_list[0], (TOKENS, D), 1.0, 6.0, ((0, 32),))
    cotangent = centred(key_list[1], (TOKENS, D), 1.0, 6.0, ((0, 32),))
    routes_keys = jax.random.split(jax.random.fold_in(key_list[2], 1), TOKENS // (N_TENSOR * ROWS))
    routes_turns = jax.random.permutation(jax.random.fold_in(key_list[2], 3), TOKENS // (N_TENSOR * ROWS))
    routes = jax.vmap(lambda own, number: shared_out(jax.random.fold_in(key_list[2], 2), own, number, N_TENSOR * ROWS, EXPERTS, 2, CAP, 1))(routes_keys, routes_turns).reshape((TOKENS, 2))
    gain_attn = jnp.clip(1.0 + 0.15 * jax.random.normal(key_list[3], (D,), jnp.float32), 0.25, 1.75)
    gain_expert = jnp.clip(1.0 + 0.15 * jax.random.normal(key_list[4], (D,), jnp.float32), 0.25, 1.75)
    tau = jnp.clip(jnp.exp(jax.random.uniform(key_list[5], (HEADS,), jnp.float32, math.log(2.0), math.log(12.0))), 2.0, 12.0)
    w_qkv = centred(key_list[6], (3, D, D), D ** -0.5, 0.25, ((1, 16), (2, 2)))
    w_out_attn = centred(key_list[7], (D, D), (max(1, D * 4 // SEQ)) ** -0.5, 2.0, ((0, 2), (1, 16)))
    w_router = centred(key_list[8], (D, EXPERTS), (0.8 * D ** -0.5), 0.21875, ((0, 8),))
    w_in = centred(key_list[9], (EXPERTS, D, FF), D ** -0.5, 0.25, ((0, 8), (2, 4)))
    w_out = centred(key_list[10], (EXPERTS, FF, D), FF ** -0.5, 0.125, ((0, 8), (1, 4)))
    return {"inputs": inputs, "cotangent": cotangent, "routes": routes, "gain_attn": gain_attn, "gain_expert": gain_expert, "tau": tau, "w_qkv": w_qkv, "w_out_attn": w_out_attn, "w_router": w_router, "w_in": w_in, "w_out": w_out}


@jax.custom_vjp
def low(v):
    return lax.optimization_barrier(v.astype(jnp.bfloat16)).astype(jnp.float32)

@jax.custom_vjp
def low_back(v):
    return v

def low_keep(v):
    return (low(v), None)

def low_pass(kept, grad):
    return (grad,)

def back_keep(v):
    return (v, None)

def back_low(kept, grad):
    return (low(grad),)
low.defvjp(low_keep, low_pass)
low_back.defvjp(back_keep, back_low)

def matmul(left, right):
    return jnp.dot(left, right, precision=lax.Precision.HIGHEST, preferred_element_type=jnp.float32)

def gelu_tanh(inputs):
    return 0.5 * inputs * (1.0 + jnp.tanh(0.7978845608028654 * (inputs + 0.044715 * inputs * inputs * inputs)))

def normalize(inputs, gain):
    centered = inputs - lax.optimization_barrier(jnp.mean(inputs, -1, keepdims=True))
    return centered * lax.rsqrt(lax.optimization_barrier(jnp.mean(centered * centered, -1, keepdims=True)) + 1e-06) * gain

def softmax_last(scores):
    shifted = jnp.exp(scores - lax.optimization_barrier(jnp.max(scores, -1, keepdims=True)))
    return shifted / lax.optimization_barrier(jnp.sum(shifted, -1, keepdims=True))

def attend(normed_rows, weights):
    split = (-1, SEQ, HEADS, HEAD_DIM)
    queries = low(low_back(matmul(normed_rows, weights[0]))).reshape(split)
    key_rows = low(low_back(matmul(normed_rows, weights[1]))).reshape(split)
    value_rows = low(low_back(matmul(normed_rows, weights[2]))).reshape(split)
    scores = low_back(jnp.einsum('bqhd,bkhd->bhqk', queries, key_rows, precision=lax.Precision.HIGHEST) * HEAD_DIM ** (-0.5))
    soft_weights = low(softmax_last(scores))
    mixed_heads = low(low_back(jnp.einsum('bhqk,bkhd->bqhd', soft_weights, value_rows, precision=lax.Precision.HIGHEST)))
    return (mixed_heads.reshape(-1, D), lax.optimization_barrier(jnp.max(scores, axis=(0, 2, 3))))

def expert_tables(routes):

    def one_expert(expert):
        hit = routes == expert
        taken = jnp.any(hit, 1)
        ordering = jnp.argsort(jnp.where(taken, 0, 1).astype(jnp.int32), stable=True)[:CAP * N_DP * N_HEADS].astype(jnp.int32)
        return (ordering, hit[ordering, 1].astype(jnp.int32), taken[ordering])
    return lax.map(one_expert, jnp.arange(EXPERTS, dtype=jnp.int32))

def reference(inputs, cotangent, routes, gain_attn, gain_expert, tau, w_qkv, w_out_attn, w_router, w_in, w_out):
    slot_rows, slot_column, slot_valid = expert_tables(routes)

    def forward(x_rows, gain_one, gain_two, proj_w, attn_w, router_w, first_w, second_w):
        normed = low(normalize(x_rows, gain_one))
        blocks = normed.reshape(IMAGES // 8, 8 * SEQ, D)

        def attend_block(block):
            return attend(block, proj_w)
        mixed, peaks = lax.map(jax.checkpoint(attend_block), blocks)
        attn_out = low_back(matmul(mixed.reshape(TOKENS, D), attn_w))
        hidden = x_rows + attn_out
        normed_two = low(normalize(hidden, gain_two))
        logits = low_back(matmul(normed_two, router_w))
        gate_values = softmax_last(jnp.take_along_axis(logits, routes, 1))

        def expert_block(parts):
            w_first, w_second, rows_taken, column, valid = parts
            gate = jnp.where(valid, gate_values[rows_taken, column], 0.0)
            pre_gelu = low_back(matmul(normed_two[rows_taken], w_first))
            result = low_back(matmul(low(gelu_tanh(pre_gelu)), w_second))
            return gate[:, None] * result
        contrib = lax.map(jax.checkpoint(expert_block), (first_w, second_w, slot_rows, slot_column, slot_valid))
        expert_mix = jnp.zeros_like(hidden).at[slot_rows.reshape(-1)].add(contrib.reshape(-1, D))
        return (hidden + expert_mix, lax.optimization_barrier(jnp.max(peaks, 0)))
    qkv_float = w_qkv.astype(jnp.float32)
    result, pullback, peak_logit = jax.vjp(forward, inputs.astype(jnp.float32), gain_attn, gain_expert, qkv_float, w_out_attn.astype(jnp.float32), w_router.astype(jnp.float32), w_in.astype(jnp.float32), w_out.astype(jnp.float32), has_aux=True)
    grads = pullback(cotangent.astype(jnp.float32))
    factor = jnp.sqrt(tau / jnp.maximum(peak_logit, tau))
    clipped = (qkv_float[:2] * jnp.repeat(factor, HEAD_DIM)).astype(jnp.bfloat16)
    return (result.astype(jnp.bfloat16), grads[0].astype(jnp.bfloat16), grads[1], grads[2], grads[3], grads[4], grads[5], grads[6], grads[7], clipped)
```

```python
import functools
import jax
import jax.numpy as jnp
from jax import lax
from jax.experimental import pallas as pl
from jax.experimental.pallas import tpu as pltpu
from jax.sharding import PartitionSpec as P

HEADS = 8
HEAD_DIM = 64
SEQ = 197
F32 = jnp.float32
BF16 = jnp.bfloat16
MESH = pl.DeviceIdType.MESH
NEG = -1e30


class Sizes:
    def __init__(self, n_dp, n_heads, n_tensor, inputs, routes, w_qkv, w_router, w_in):
        self.nd, self.nh, self.nt = n_dp, n_heads, n_tensor
        self.groups = n_dp * n_heads
        self.rows, self.width = inputs.shape
        self.pad = -(-self.rows // 16) * 16
        self.block = self.pad * n_tensor
        self.block_rows = routes.shape[0]
        self.own = w_in.shape[0]
        self.hidden = w_in.shape[2]
        self.experts = self.own * self.groups
        self.cap = (self.block_rows * 5 // (16 * self.experts) + 1) * 8
        self.group_slots = self.own * self.cap
        self.slots = self.experts * self.cap
        self.row_piece, self.col_piece = w_qkv.shape[1], w_qkv.shape[2]
        self.band = self.row_piece * n_tensor
        self.router_rows = w_router.shape[0]

    def fits(self):
        return (
            self.rows == SEQ
            and self.block_rows == self.rows * self.nt
            and self.cap == 64
            and self.experts == 32
            and self.group_slots % 128 == 0
            and self.col_piece % 128 == 0
            and self.row_piece % 16 == 0
            and self.router_rows % 16 == 0
            and self.own * self.groups * 4 == 128
            and self.width == HEADS * HEAD_DIM
            and self.block * self.width * 2 <= 2**20
        )


def nn(a, b):
    return jnp.dot(a, b, preferred_element_type=F32)


def nt(a, b):
    return lax.dot_general(a, b, (((1,), (1,)), ((), ())), preferred_element_type=F32)


def tn(a, b):
    return lax.dot_general(a, b, (((0,), (0,)), ((), ())), preferred_element_type=F32)


def iota(shape, axis):
    return lax.broadcasted_iota(jnp.int32, shape, axis)


def normalize(rows):
    centered = rows - jnp.mean(rows, -1, keepdims=True)
    factor = lax.rsqrt(jnp.mean(centered * centered, -1, keepdims=True) + 1e-06)
    return centered * factor, factor


def norm_back(grad_norm, unit_rows, factor, gain):
    grad_hat = grad_norm * gain
    inner = (
        grad_hat
        - jnp.mean(grad_hat, -1, keepdims=True)
        - unit_rows * jnp.mean(grad_hat * unit_rows, -1, keepdims=True)
    )
    return factor * inner, jnp.sum(grad_norm * unit_rows, 0, keepdims=True)


def split_high_low(values):
    high = values.astype(BF16)
    low = (values - high.astype(F32)).astype(BF16)
    return jnp.concatenate([high, low], 0)


class Place:
    def __init__(self, sz):
        self.sz = sz
        self.d = lax.axis_index("dp")
        self.h = lax.axis_index("heads")
        self.z = lax.axis_index("tensor")
        self.group = self.d * sz.nh + self.h

    def plane(self, group):
        return (group // self.sz.nh, group % self.sz.nh, self.z)

    def line(self, z):
        return (self.d, self.h, z)

    def next_group(self, k):
        return (self.group + k) % self.sz.groups

    def next_z(self, j):
        return (self.z + j) % self.sz.nt

    def enter(self):
        sz = self.sz
        barrier = pltpu.get_barrier_semaphore()
        for k in range(1, sz.groups):
            pl.semaphore_signal(barrier, inc=1, device_id=self.plane(self.next_group(k)), device_id_type=MESH)
        for j in range(1, sz.nt):
            pl.semaphore_signal(barrier, inc=1, device_id=self.line(self.next_z(j)), device_id_type=MESH)
        pl.semaphore_wait(barrier, sz.groups + sz.nt - 2)


def remote(src, dst, send, recv, device):
    return pltpu.make_async_remote_copy(
        src_ref=src, dst_ref=dst, send_sem=send, recv_sem=recv, device_id=device, device_id_type=MESH
    )


def route_table(sz, routes_ref, table):
    table[...] = jnp.full_like(table, -1.0)
    for z in range(sz.nt):
        table[z * sz.pad : z * sz.pad + sz.rows, 0:2] = routes_ref[
            z * sz.rows : (z + 1) * sz.rows, :
        ].astype(F32)


def front_kernel(
    sz, x_ref, cot_ref, routes_ref, gain_one_ref, gain_two_ref, w_qkv_ref, w_out_ref, w_router_ref,
    slots_out, cot_slots_out, gate_out, w_full, router_t, qkv_out, probs_out, mixed_out, hidden_out,
    block_out, gates_out, peak_out,
    w_own, router_own, router_full, table, select, cot_block, slots_send, cot_send, gate_send,
    z_send, z_recv, x_send, x_recv, c_send, c_recv, r_send, r_recv, q_send, q_recv, n_send, n_recv,
    s_send, s_recv, t_send, t_recv, g_send, g_recv, local_sem,
):
    at = Place(sz)
    d, h, z, me = at.d, at.h, at.z, at.group
    band, rp, cp, pad = sz.band, sz.row_piece, sz.col_piece, sz.pad

    w_own[0:3] = w_qkv_ref[...]
    w_own[3] = w_out_ref[...].astype(F32).T.astype(BF16)
    router_own[...] = jnp.zeros_like(router_own)
    router_own[:, 0 : sz.experts] = w_router_ref[...]

    own_columns = pl.ds(pl.multiple_of(h * cp, cp), cp)

    def rows_of(dp, tensor):
        return pl.ds(pl.multiple_of((dp * sz.nt + tensor) * rp, rp), rp)

    def band_of(dp):
        return pl.ds(pl.multiple_of(dp * band, band), band)

    at.enter()

    w_z = [
        remote(w_own, w_full.at[:, rows_of(d, z), own_columns], z_send.at[j - 1], z_recv.at[j - 1], at.line(at.next_z(j)))
        for j in range(1, sz.nt)
    ]
    for copy in w_z:
        copy.start()
    router_rows = pl.ds(pl.multiple_of(me * sz.router_rows, sz.router_rows), sz.router_rows)
    routers = [
        remote(router_own, router_full.at[router_rows], r_send.at[k - 1], r_recv.at[k - 1], at.plane(at.next_group(k)))
        for k in range(1, sz.groups)
    ]
    for copy in routers:
        copy.start()

    w_full[:, rows_of(d, z), own_columns] = w_own[...]
    router_full[router_rows] = router_own[...]
    cot_block[pl.ds(pl.multiple_of(z * pad, pad), pad)] = jnp.zeros((pad, sz.width), BF16)
    cot_block[pl.ds(pl.multiple_of(z * pad, pad), sz.rows)] = cot_ref[...]
    own_block = pl.ds(pl.multiple_of(z * pad, pad), pad)

    x_rows = jnp.concatenate([x_ref[...].astype(F32), jnp.zeros((pad - sz.rows, sz.width), F32)], 0)
    unit_one, _ = normalize(x_rows)
    normed_one = (unit_one * gain_one_ref[...]).astype(BF16)

    for copy in w_z:
        copy.wait()

    def peer_dp(k):
        return (d + k) % sz.nd

    w_x = [
        remote(
            w_full.at[:, band_of(d), own_columns], w_full.at[:, band_of(d), own_columns],
            x_send.at[k - 1], x_recv.at[k - 1], (peer_dp(k), h, z),
        )
        for k in range(1, sz.nd)
    ]
    for copy in w_x:
        copy.start()

    def to_core(i, dp, other):
        place = w_full.at[:, band_of(dp), own_columns]
        return remote(place, place, c_send.at[i], c_recv.at[i], (d, (h + other) % sz.nh, z))

    w_c = [to_core((other - 1) * sz.nd, d, other) for other in range(1, sz.nh)]
    for copy in w_c:
        copy.start()
    cot_z = [
        remote(cot_block.at[own_block], cot_block.at[own_block], q_send.at[j - 1], q_recv.at[j - 1], at.line(at.next_z(j)))
        for j in range(1, sz.nt)
    ]
    for copy in cot_z:
        copy.start()

    route_table(sz, routes_ref, table)
    turned = table[...].T
    route_a, route_b = turned[0:1, :], turned[1:2, :]
    expert = iota((sz.experts, sz.block), 0).astype(F32)
    named_a, named_b = route_a == expert, route_b == expert
    named = jnp.logical_or(named_a, named_b)
    before = (iota((sz.block, sz.block), 0) < iota((sz.block, sz.block), 1)).astype(BF16)
    rank = nn(named.astype(BF16), before) + expert * float(sz.cap)
    slot_a = jnp.sum(jnp.where(named_a, rank, 0.0), 0, keepdims=True)
    slot_b = jnp.sum(jnp.where(named_b, rank, 0.0), 0, keepdims=True)
    slot_a = jnp.where(route_a < 0.0, -1.0, slot_a)
    slot_b = jnp.where(route_b < 0.0, -1.0, slot_b)

    def fill(g, carry):
        slot = iota((sz.group_slots, sz.block), 0).astype(F32) + (g * sz.group_slots).astype(F32)
        hit = jnp.logical_or(slot == slot_a, slot == slot_b)
        select[pl.ds(pl.multiple_of(g * sz.group_slots, sz.group_slots), sz.group_slots), :] = jnp.where(
            hit, 1.0, 0.0
        ).astype(BF16)
        return carry

    lax.fori_loop(0, sz.groups, fill, 0)

    for k in range(1, sz.nd):
        w_x[k - 1].wait_recv()
        source = (d - k + sz.nd) % sz.nd
        for other in range(1, sz.nh):
            copy = to_core((other - 1) * sz.nd + k, source, other)
            copy.start()
            w_c.append(copy)
    for copy in w_c:
        copy.wait()
    for copy in w_x:
        copy.wait_send()
    for copy in routers:
        copy.wait()
    router_t[...] = router_full[...].astype(F32).T[0 : sz.experts].astype(BF16)

    for i in range(3):
        qkv_out[i] = nn(normed_one, w_full[i]).astype(BF16)
    lane = iota((1, 2 * HEAD_DIM), 1)
    halves = (lane < HEAD_DIM, lane >= HEAD_DIM)
    key_valid = iota((1, pad), 1) < sz.rows
    row_valid = iota((pad, 1), 0) < sz.rows
    peak_lane = iota((1, 128), 1)
    peak_out[...] = jnp.full_like(peak_out, NEG)

    def attend(pair, carry):
        columns = pl.ds(pl.multiple_of(pair * 2 * HEAD_DIM, 2 * HEAD_DIM), 2 * HEAD_DIM)
        q_pair, k_pair, v_pair = (qkv_out[i, :, columns] for i in range(3))
        mixed = []
        for side in range(2):
            q_own = jnp.where(halves[side], q_pair, jnp.zeros_like(q_pair))
            scores = nt(q_own, k_pair) * HEAD_DIM ** (-0.5)
            scores = jnp.where(key_valid, scores, NEG)
            row_peak = jnp.max(scores, -1, keepdims=True)
            exponent = jnp.exp(scores - row_peak)
            probs = (exponent / jnp.sum(exponent, -1, keepdims=True)).astype(BF16)
            head = pair * 2 + side
            probs_out[head] = probs
            mixed.append(nn(probs, v_pair))
            peak = jnp.max(jnp.where(row_valid, row_peak, NEG), 0, keepdims=True)
            peak_out[0:1, :] = jnp.where(peak_lane == head, peak, peak_out[0:1, :])
        mixed_out[:, columns] = jnp.where(halves[0], mixed[0], mixed[1]).astype(BF16)
        return carry

    def dispatch(block, send, out, send_sems, recv_sems):
        def step(i, carry):
            k = sz.groups - 1 - i
            g = (me + k) % sz.groups
            rows = pl.ds(pl.multiple_of(g * sz.group_slots, sz.group_slots), sz.group_slots)
            send[g] = nn(select[rows, :], block[...]).astype(BF16)

            @pl.when(k > 0)
            def _():
                remote(send.at[g], out.at[me], send_sems.at[k], recv_sems.at[k], at.plane(g)).start()

            return carry

        lax.fori_loop(0, sz.groups, step, 0)

    def collect(send, out, send_sems, recv_sems):
        def step(i, carry):
            k = i + 1
            g = (me + k) % sz.groups
            remote(send.at[g], out.at[me], send_sems.at[k], recv_sems.at[k], at.plane(g)).wait()
            return carry

        lax.fori_loop(0, sz.groups - 1, step, 0)

    pairs = HEADS // 2
    lax.fori_loop(0, pairs // 2, attend, 0)
    for copy in cot_z:
        copy.wait()
    dispatch(cot_block, cot_send, cot_slots_out, t_send, t_recv)
    cot_own = pltpu.make_async_copy(cot_send.at[me], cot_slots_out.at[me], local_sem.at[0])
    cot_own.start()
    lax.fori_loop(pairs // 2, pairs, attend, 0)

    hidden = x_rows + nt(mixed_out[...], w_full[3])
    hidden_out[...] = hidden
    unit_two, _ = normalize(hidden)
    normed_two = jnp.where(row_valid, unit_two * gain_two_ref[...], 0.0).astype(BF16)
    block_out[own_block] = normed_two
    rows_z = [
        remote(block_out.at[own_block], block_out.at[own_block], n_send.at[j - 1], n_recv.at[j - 1], at.line(at.next_z(j)))
        for j in range(1, sz.nt)
    ]
    for copy in rows_z:
        copy.start()
    for copy in rows_z:
        copy.wait()
    dispatch(block_out, slots_send, slots_out, s_send, s_recv)
    rows_own = pltpu.make_async_copy(slots_send.at[me], slots_out.at[me], local_sem.at[1])
    rows_own.start()

    logits = jnp.where(named, nt(router_t[...], block_out[...]), NEG)
    exponent = jnp.where(named, jnp.exp(logits - jnp.max(logits, 0, keepdims=True)), 0.0)
    total = jnp.sum(exponent, 0, keepdims=True)
    gates = exponent / jnp.where(total > 0.0, total, 1.0)
    gates_out[...] = gates
    by_slot = nt(split_high_low(gates), select[...])
    by_slot = by_slot[0 : sz.experts] + by_slot[sz.experts :]
    own_slot = iota((sz.experts, sz.slots), 1) // sz.cap == iota((sz.experts, sz.slots), 0)
    by_slot = jnp.where(own_slot, by_slot, 0.0)
    folded = by_slot[:, 0:128]
    for i in range(1, sz.slots // 128):
        folded = folded + by_slot[:, i * 128 : (i + 1) * 128]
    gate_send[...] = folded
    gate_copies = [
        remote(gate_send, gate_out.at[me], g_send.at[k - 1], g_recv.at[k - 1], at.plane(at.next_group(k)))
        for k in range(1, sz.groups)
    ]
    for copy in gate_copies:
        copy.start()
    gate_out[me] = folded

    collect(cot_send, cot_slots_out, t_send, t_recv)
    for copy in gate_copies:
        copy.wait()
    collect(slots_send, slots_out, s_send, s_recv)
    cot_own.wait()
    rows_own.wait()


def expert_kernel(sz, slots_ref, cot_ref, gate_ref, first_ref, second_ref,
                  grad_slots_ref, value_ref, dgate_ref, grad_first_ref, grad_second_ref):
    e = pl.program_id(0)
    me = lax.axis_index("dp") * sz.nh + lax.axis_index("heads")
    many = sz.groups * sz.cap
    gate_rows = gate_ref[:, pl.ds(me * sz.own + e, 1), :].reshape(sz.groups, 128)
    turned = gate_rows.T
    odd = (e % 2) == 1
    gate_columns = jnp.where(odd, turned[sz.cap : 2 * sz.cap], turned[0 : sz.cap])
    gate = jnp.concatenate([gate_columns[:, s : s + 1] for s in range(sz.groups)], 0)
    rows = slots_ref[...].reshape(many, sz.width)
    cot = cot_ref[...].reshape(many, sz.width).astype(F32)
    first, second = first_ref[0], second_ref[0]
    grad_value = (cot * gate).astype(BF16)
    pre = nn(rows, first)
    grad_act = nt(grad_value, second)
    scale, cubic = 0.7978845608028654, 0.044715
    square = pre * pre
    bent = jnp.tanh(scale * pre * (1.0 + cubic * square))
    half = 0.5 * (1.0 + bent)
    act = (pre * half).astype(BF16)
    slope = half + 0.5 * pre * (1.0 - bent * bent) * scale * (1.0 + 3.0 * cubic * square)
    grad_pre = (grad_act * slope).astype(BF16)
    value = nn(act, second)
    value_ref[...] = (value * gate).astype(BF16).reshape(sz.groups, sz.cap, sz.width)
    dgate = nt(jnp.ones((8, sz.width), BF16), (value * cot).astype(BF16))

    @pl.when(e == 0)
    def _():
        dgate_ref[...] = jnp.zeros_like(dgate_ref)

    dgate_ref[...] = jnp.where(iota((8, many), 0) == e, dgate, dgate_ref[...])
    grad_slots_ref[...] = nt(grad_pre, first).astype(BF16).reshape(sz.groups, sz.cap, sz.width)
    grad_first_ref[0] = tn(rows, grad_pre)
    grad_second_ref[0] = tn(act, grad_value)


def back_kernel(
    sz, grad_slots, values, dgate_ref, x_ref, cot_ref, routes_ref, gain_one_ref, gain_two_ref, tau_ref, w_qkv_ref,
    w_full, router_t, qkv, probs, mixed_ref, hidden_ref, block_ref, gates_ref, peak_ref,
    output_out, grad_input_out, gains_out, weight_out, router_out, clipped_out,
    table, select, slots_recv, values_recv, dgate_recv, dgate_rows, part, part_own, part_send, part_recv,
    mix_own, mix_send, mix_recv, grad_mixed, grad_qkv, grad_w, w_half, core_recv, band_send, band_recv, line_send,
    line_recv, small, small_send, small_core, small_x, small_z, rt, rt_core, rt_x, rt_z,
    s_send, s_recv, v_send, v_recv, a_send, a_recv, p_send, p_recv, m_send, m_recv, c_send, c_recv, x_send, x_recv,
    l_send, l_recv, local_sem,
):
    at = Place(sz)
    d, h, z, me = at.d, at.h, at.z, at.group
    pad, cp, rp, band = sz.pad, sz.col_piece, sz.row_piece, sz.band
    at.enter()

    def exchange(source, landing, send_sems, recv_sems, k):
        g = at.next_group(k)
        return remote(source.at[g], landing.at[me], send_sems.at[k], recv_sems.at[k], at.plane(g))

    def start_all(source, landing, send_sems, recv_sems):
        def step(i, carry):
            exchange(source, landing, send_sems, recv_sems, sz.groups - 1 - i).start()
            return carry

        lax.fori_loop(0, sz.groups - 1, step, 0)

    def wait_all(source, landing, send_sems, recv_sems):
        def step(i, carry):
            exchange(source, landing, send_sems, recv_sems, i + 1).wait()
            return carry

        lax.fori_loop(0, sz.groups - 1, step, 0)

    start_all(grad_slots, slots_recv, s_send, s_recv)
    dgates = [
        remote(dgate_ref, dgate_recv.at[me], a_send.at[k - 1], a_recv.at[k - 1], at.plane(at.next_group(k)))
        for k in range(1, sz.groups)
    ]
    for copy in dgates:
        copy.start()
    own_grad = pltpu.make_async_copy(grad_slots.at[me], slots_recv.at[me], local_sem.at[0])
    own_grad.start()
    own_value = pltpu.make_async_copy(values.at[me], values_recv.at[me], local_sem.at[1])
    own_value.start()
    dgate_recv[me] = dgate_ref[...]

    route_table(sz, routes_ref, table)
    route_a, route_b = table[:, 0:1], table[:, 1:2]
    expert = iota((sz.block, 128), 1).astype(F32)
    named_a, named_b = route_a == expert, route_b == expert
    before = (iota((sz.block, sz.block), 1) < iota((sz.block, sz.block), 0)).astype(BF16)
    rank = nn(before, jnp.logical_or(named_a, named_b).astype(BF16)) + expert * float(sz.cap)
    slot_a = jnp.sum(jnp.where(named_a, rank, 0.0), 1, keepdims=True)
    slot_b = jnp.sum(jnp.where(named_b, rank, 0.0), 1, keepdims=True)
    table[:, 0:1] = jnp.where(route_a < 0.0, -1.0, slot_a)
    table[:, 1:2] = jnp.where(route_b < 0.0, -1.0, slot_b)

    def fill(i, carry):
        rows = pl.ds(pl.multiple_of(i * pad, pad), pad)
        slot = iota((pad, sz.slots), 1).astype(F32)
        hit = jnp.logical_or(slot == table[rows, 0:1], slot == table[rows, 1:2])
        select[rows, :] = jnp.where(hit, 1.0, 0.0).astype(BF16)
        return carry

    lax.fori_loop(0, sz.nt, fill, 0)

    for copy in dgates:
        copy.wait()
    many = sz.groups * sz.cap
    mine = iota((8, many), 1) // sz.cap == me
    for g in range(sz.groups):
        masked = jnp.where(mine, dgate_recv[g], 0.0)
        folded = masked[:, 0:128]
        for i in range(1, many // 128):
            folded = folded + masked[:, i * 128 : (i + 1) * 128]
        folded = folded + pltpu.roll(folded, 64, 1)
        dgate_rows[g * sz.own : (g + 1) * sz.own, :] = folded[0 : sz.own]
    spread = jnp.concatenate([dgate_rows[...]] * (sz.slots // 128), 1)
    own_slot = iota((sz.experts, sz.slots), 1) // sz.cap == iota((sz.experts, sz.slots), 0)
    dgate = nt(split_high_low(jnp.where(own_slot, spread, 0.0)), select[...])
    dgate = dgate[0 : sz.experts] + dgate[sz.experts :]
    gates = gates_ref[...]
    dlogits = (gates * (dgate - jnp.sum(gates * dgate, 0, keepdims=True))).astype(BF16)
    rt[...] = nn(dlogits, block_ref[...])
    part[...] = tn(dlogits, router_t[...])

    def block_rows(zz):
        return pl.ds(pl.multiple_of(zz * pad, pad), pad)

    def scatter(slots_recv, base, own, send, recv, send_sems, recv_sems):
        copies = []
        for j in [*range(1, sz.nt), 0]:
            zz = at.next_z(j)
            flat = slots_recv[...].reshape(sz.slots, sz.width)
            sums = nn(select[block_rows(zz), :], flat)
            if base is not None:
                sums = sums + base[block_rows(zz), :]
            if j == 0:
                own[...] = sums
            else:
                send[j - 1] = sums.astype(BF16)
                copy = remote(send.at[j - 1], recv.at[j - 1], send_sems.at[j - 1], recv_sems.at[j - 1], at.line(zz))
                copy.start()
                copies.append(copy)
        return copies

    def gathered(copies, own, recv):
        for copy in copies:
            copy.wait()
        sums = own[...]
        for j in range(1, sz.nt):
            sums = sums + recv[j - 1].astype(F32)
        return sums

    own_grad.wait()
    wait_all(grad_slots, slots_recv, s_send, s_recv)
    start_all(values, values_recv, v_send, v_recv)
    copies = scatter(slots_recv, part, part_own, part_send, part_recv, p_send, p_recv)

    row_valid = iota((pad, 1), 0) < sz.rows
    zeros = jnp.zeros((pad - sz.rows, sz.width), F32)
    unit_two, factor_two = normalize(hidden_ref[...])
    grad_normed = jnp.where(row_valid, gathered(copies, part_own, part_recv), 0.0)
    grad_hidden, gain_two = norm_back(grad_normed, unit_two, factor_two, gain_two_ref[...])
    grad_hidden = jnp.concatenate([cot_ref[...].astype(F32), zeros], 0) + jnp.where(row_valid, grad_hidden, 0.0)
    grad_attn = grad_hidden.astype(BF16)
    part_own[...] = grad_hidden
    grad_mixed[...] = nn(grad_attn, w_full[3]).astype(BF16)
    grad_w[3] = tn(grad_attn, mixed_ref[...]).astype(BF16)

    lane = iota((1, 2 * HEAD_DIM), 1)
    halves = (lane < HEAD_DIM, lane >= HEAD_DIM)
    scale = HEAD_DIM ** (-0.5)

    def attend_back(pair, carry):
        columns = pl.ds(pl.multiple_of(pair * 2 * HEAD_DIM, 2 * HEAD_DIM), 2 * HEAD_DIM)
        q_pair, k_pair, v_pair = (qkv[i, :, columns] for i in range(3))
        g_pair = grad_mixed[:, columns]
        dq, dk, dv = [], [], []
        for side in range(2):
            weights = probs[pair * 2 + side]
            soft = weights.astype(F32)
            g_own = jnp.where(halves[side], g_pair, jnp.zeros_like(g_pair))
            grad_soft = nt(g_own, v_pair)
            inner = jnp.sum(soft * grad_soft, -1, keepdims=True)
            grad_scores = (soft * (grad_soft - inner)).astype(BF16)
            dq.append(nn(grad_scores, k_pair))
            dk.append(tn(grad_scores, q_pair))
            dv.append(tn(weights, g_pair))
        grad_qkv[0, :, columns] = (jnp.where(halves[0], dq[0], dq[1]) * scale).astype(BF16)
        grad_qkv[1, :, columns] = (jnp.where(halves[0], dk[0], dk[1]) * scale).astype(BF16)
        grad_qkv[2, :, columns] = jnp.where(halves[0], dv[0], dv[1]).astype(BF16)
        return carry

    lax.fori_loop(0, HEADS // 2, attend_back, 0)

    own_value.wait()
    wait_all(values, values_recv, v_send, v_recv)
    mix_copies = scatter(values_recv, None, mix_own, mix_send, mix_recv, m_send, m_recv)

    x_rows = jnp.concatenate([x_ref[...].astype(F32), zeros], 0)
    unit_one, factor_one = normalize(x_rows)
    normed_one = (unit_one * gain_one_ref[...]).astype(BF16)
    grad_one = jnp.zeros((pad, sz.width), F32)
    for i in range(3):
        grad_w[i] = tn(normed_one, grad_qkv[i]).astype(BF16)
        grad_one = grad_one + nt(grad_qkv[i], w_full[i])
    grad_one = jnp.where(row_valid, grad_one, 0.0)
    grad_input, gain_one = norm_back(grad_one, unit_one, factor_one, gain_one_ref[...])
    grad_input_out[...] = (part_own[...] + grad_input)[0 : sz.rows].astype(BF16)

    small[...] = jnp.zeros_like(small)
    small[0:1, :] = gain_one
    small[1:2, :] = gain_two
    small[2:3, 0:128] = peak_ref[0:1, :]
    peak_row = iota(small.shape, 0) == 2

    def join(a, b):
        return jnp.where(peak_row, jnp.maximum(a, b), a + b)

    def columns_of(core):
        return pl.ds(pl.multiple_of(core * cp, cp), cp)

    core_copies = []
    for other in range(1, sz.nh):
        core = (h + other) % sz.nh
        n, device = 3 * (other - 1), (d, core, z)
        core_copies += [
            remote(grad_w.at[:, :, columns_of(core)], core_recv.at[other - 1], c_send.at[n], c_recv.at[n], device),
            remote(small, small_core.at[other - 1], c_send.at[n + 1], c_recv.at[n + 1], device),
            remote(rt, rt_core.at[other - 1], c_send.at[n + 2], c_recv.at[n + 2], device),
        ]
    for copy in core_copies:
        copy.start()
    for copy in core_copies:
        copy.wait()
    for i in range(4):
        sums = grad_w[i, :, columns_of(h)].astype(F32)
        for other in range(1, sz.nh):
            sums = sums + core_recv[other - 1, i].astype(F32)
        w_half[i] = sums
        band_send[i] = sums.astype(BF16)
    for other in range(1, sz.nh):
        small[...] = join(small[...], small_core[other - 1])
        rt[...] = rt[...] + rt_core[other - 1]
    small_send[0] = small[...]

    def band_of(dp):
        return pl.ds(pl.multiple_of(dp * band, band), band)

    x_copies = []
    for k in range(1, sz.nd):
        to, n = (d + k) % sz.nd, 3 * (k - 1)
        device = (to, h, z)
        x_copies += [
            remote(band_send.at[:, band_of(to), :], band_recv.at[k - 1], x_send.at[n], x_recv.at[n], device),
            remote(small_send.at[0], small_x.at[k - 1], x_send.at[n + 1], x_recv.at[n + 1], device),
            remote(rt.at[:, band_of(to)], rt_x.at[k - 1], x_send.at[n + 2], x_recv.at[n + 2], device),
        ]
    for copy in x_copies:
        copy.start()

    mix = gathered(mix_copies, mix_own, mix_recv)
    output_out[...] = (hidden_ref[...] + mix)[0 : sz.rows].astype(BF16)

    for copy in x_copies:
        copy.wait()
    router_sum = rt[:, band_of(d)]
    for k in range(1, sz.nd):
        small[...] = join(small[...], small_x[k - 1])
        router_sum = router_sum + rt_x[k - 1]
    rt_z[sz.nt - 1] = router_sum
    small_send[1] = small[...]
    for i in range(4):
        sums = w_half[i, band_of(d), :]
        for k in range(1, sz.nd):
            sums = sums + band_recv[k - 1, i].astype(F32)
        w_half[i, 0:band, :] = sums
        line_send[i] = sums.astype(BF16)

    def rows_of(zz):
        return pl.ds(pl.multiple_of(zz * rp, rp), rp)

    z_copies = []
    for j in range(1, sz.nt):
        to, n = at.next_z(j), 3 * (j - 1)
        device = at.line(to)
        z_copies += [
            remote(line_send.at[:, rows_of(to), :], line_recv.at[j - 1], l_send.at[n], l_recv.at[n], device),
            remote(small_send.at[1], small_z.at[j - 1], l_send.at[n + 1], l_recv.at[n + 1], device),
            remote(rt_z.at[sz.nt - 1], rt_z.at[j - 1], l_send.at[n + 2], l_recv.at[n + 2], device),
        ]
    for copy in z_copies:
        copy.start()
    for copy in z_copies:
        copy.wait()
    totals = small[...]
    router_sum = rt_z[sz.nt - 1]
    for j in range(1, sz.nt):
        totals = join(totals, small_z[j - 1])
        router_sum = router_sum + rt_z[j - 1]
    gains_out[...] = totals
    router_out[...] = router_sum
    for i in range(4):
        sums = w_half[i, rows_of(z), :]
        for j in range(1, sz.nt):
            sums = sums + line_recv[j - 1, i].astype(F32)
        weight_out[i] = sums

    tau = tau_ref[...]
    factor = jnp.sqrt(tau / jnp.maximum(totals[2:3, 0:128], tau))
    column = iota((1, cp), 1) // HEAD_DIM + h * (cp // HEAD_DIM)
    scale_row = jnp.zeros((1, cp), F32)
    for head in range(HEADS):
        scale_row = jnp.where(column == head, factor[:, head : head + 1], scale_row)
    for i in range(2):
        clipped_out[i] = (w_qkv_ref[i].astype(F32) * scale_row).astype(BF16)


def fast_body(
    sz, inputs, cotangent, routes, gain_attn, gain_expert, tau, w_qkv, w_out_attn, w_router, w_in, w_out
):
    ng, nz, nd, nh, pad, width = sz.groups, sz.nt, sz.nd, sz.nh, sz.pad, sz.width
    vmem, hbm = pl.BlockSpec(memory_space=pltpu.VMEM), pl.BlockSpec(memory_space=pl.ANY)
    dma = pltpu.SemaphoreType.DMA
    gain_one, gain_two = gain_attn[None, :], gain_expert[None, :]

    def shape(dims, dtype):
        return jax.ShapeDtypeStruct(dims, dtype)

    slot_shape = (ng, sz.group_slots, width)
    (slots, cot_slots, gate_slots, w_full, router_t, qkv, probs, mixed, hidden, block, gates, peak) = pl.pallas_call(
        functools.partial(front_kernel, sz),
        out_shape=(
            shape(slot_shape, BF16), shape(slot_shape, BF16), shape((ng, sz.experts, 128), F32),
            shape((4, width, width), BF16), shape((sz.experts, width), BF16), shape((3, pad, width), BF16),
            shape((HEADS, pad, pad), BF16), shape((pad, width), BF16), shape((pad, width), F32),
            shape((sz.block, width), BF16), shape((sz.experts, sz.block), F32), shape((8, 128), F32),
        ),
        in_specs=[vmem] * 8,
        out_specs=(hbm, hbm) + (vmem,) * 10,
        scratch_shapes=[
            pltpu.VMEM((4, sz.row_piece, sz.col_piece), BF16),
            pltpu.VMEM((sz.router_rows, 128), BF16), pltpu.VMEM((width, 128), BF16),
            pltpu.VMEM((sz.block, 128), F32), pltpu.VMEM((sz.slots, sz.block), BF16),
            pltpu.VMEM((sz.block, width), BF16),
            pltpu.VMEM(slot_shape, BF16), pltpu.VMEM(slot_shape, BF16), pltpu.VMEM((sz.experts, 128), F32),
            dma((nz - 1,)), dma((nz - 1,)), dma((nd - 1,)), dma((nd - 1,)),
            dma((nd * (nh - 1),)), dma((nd * (nh - 1),)), dma((ng - 1,)), dma((ng - 1,)),
            dma((nz - 1,)), dma((nz - 1,)), dma((nz - 1,)), dma((nz - 1,)),
            dma((ng,)), dma((ng,)), dma((ng,)), dma((ng,)), dma((ng - 1,)), dma((ng - 1,)), dma((2,)),
        ],
        compiler_params=pltpu.CompilerParams(collective_id=0, has_side_effects=True, vmem_limit_bytes=56 * 2**20),
        name="front",
    )(inputs, cotangent, routes, gain_one, gain_two, w_qkv, w_out_attn, w_router)

    slot_spec = pl.BlockSpec((ng, sz.cap, width), lambda e: (0, e, 0))
    first_spec = pl.BlockSpec((1, width, sz.hidden), lambda e: (e, 0, 0))
    second_spec = pl.BlockSpec((1, sz.hidden, width), lambda e: (e, 0, 0))
    many = ng * sz.cap
    grad_slots, values, dgate, grad_first, grad_second = pl.pallas_call(
        functools.partial(expert_kernel, sz),
        grid=(sz.own,),
        out_shape=(
            shape(slot_shape, BF16), shape(slot_shape, BF16), shape((8, many), F32),
            shape(w_in.shape, F32), shape(w_out.shape, F32),
        ),
        in_specs=[slot_spec, slot_spec, pl.BlockSpec((ng, sz.experts, 128), lambda e: (0, 0, 0)), first_spec, second_spec],
        out_specs=(slot_spec, slot_spec, pl.BlockSpec((8, many), lambda e: (0, 0)), first_spec, second_spec),
        compiler_params=pltpu.CompilerParams(vmem_limit_bytes=48 * 2**20),
        name="experts",
    )(slots, cot_slots, gate_slots, w_in, w_out)

    tau_row = jnp.pad(tau, (0, 128 - tau.shape[0]), constant_values=1.0)[None, :]
    rp, cp, band = sz.row_piece, sz.col_piece, sz.band
    output, grad_input, gains, weight, router, clipped = pl.pallas_call(
        functools.partial(back_kernel, sz),
        out_shape=(
            shape(inputs.shape, BF16), shape(inputs.shape, BF16), shape((8, width), F32),
            shape((4, rp, cp), F32), shape((sz.experts, band), F32), shape((2, rp, cp), BF16),
        ),
        in_specs=[hbm, hbm] + [vmem] * 17,
        out_specs=(vmem,) * 6,
        scratch_shapes=[
            pltpu.VMEM((sz.block, 128), F32), pltpu.VMEM((sz.block, sz.slots), BF16),
            pltpu.VMEM(slot_shape, BF16), pltpu.VMEM(slot_shape, BF16),
            pltpu.VMEM((ng, 8, many), F32), pltpu.VMEM((sz.experts, 128), F32),
            pltpu.VMEM((sz.block, width), F32), pltpu.VMEM((pad, width), F32),
            pltpu.VMEM((nz - 1, pad, width), BF16), pltpu.VMEM((nz - 1, pad, width), BF16),
            pltpu.VMEM((pad, width), F32),
            pltpu.VMEM((nz - 1, pad, width), BF16), pltpu.VMEM((nz - 1, pad, width), BF16),
            pltpu.VMEM((pad, width), BF16), pltpu.VMEM((3, pad, width), BF16),
            pltpu.VMEM((4, width, width), BF16), pltpu.VMEM((4, width, cp), F32),
            pltpu.VMEM((nh - 1, 4, width, cp), BF16), pltpu.VMEM((4, width, cp), BF16),
            pltpu.VMEM((nd - 1, 4, band, cp), BF16), pltpu.VMEM((4, band, cp), BF16),
            pltpu.VMEM((nz - 1, 4, rp, cp), BF16),
            pltpu.VMEM((8, width), F32), pltpu.VMEM((2, 8, width), F32), pltpu.VMEM((nh - 1, 8, width), F32),
            pltpu.VMEM((nd - 1, 8, width), F32), pltpu.VMEM((nz - 1, 8, width), F32),
            pltpu.VMEM((sz.experts, width), F32), pltpu.VMEM((nh - 1, sz.experts, width), F32),
            pltpu.VMEM((nd - 1, sz.experts, band), F32), pltpu.VMEM((nz, sz.experts, band), F32),
            dma((ng,)), dma((ng,)), dma((ng,)), dma((ng,)), dma((ng - 1,)), dma((ng - 1,)),
            dma((nz - 1,)), dma((nz - 1,)), dma((nz - 1,)), dma((nz - 1,)),
            dma((3 * (nh - 1),)), dma((3 * (nh - 1),)), dma((3 * (nd - 1),)), dma((3 * (nd - 1),)),
            dma((3 * (nz - 1),)), dma((3 * (nz - 1),)), dma((2,)),
        ],
        compiler_params=pltpu.CompilerParams(collective_id=1, has_side_effects=True, vmem_limit_bytes=58 * 2**20),
        name="back",
    )(
        grad_slots, values, dgate, inputs, cotangent, routes, gain_one, gain_two, tau_row, w_qkv,
        w_full, router_t, qkv, probs, mixed, hidden, block, gates, peak,
    )
    heads_at = lax.axis_index("heads")
    router_grad = lax.dynamic_slice_in_dim(router, heads_at * sz.router_rows, sz.router_rows, 1).T
    return (
        output, grad_input, gains[0], gains[1], weight[0:3], weight[3].T, router_grad,
        grad_first, grad_second, clipped,
    )


def gelu_tanh(inputs):
    return (
        0.5
        * inputs
        * (1.0 + jnp.tanh(0.7978845608028654 * (inputs + 0.044715 * inputs * inputs * inputs)))
    )


def unit_and_factor(inputs):
    centered = inputs - jnp.mean(inputs, -1, keepdims=True)
    factor = lax.rsqrt(jnp.mean(centered * centered, -1, keepdims=True) + 1e-06)
    return (centered * factor, factor)


def general_norm_back(grad_norm, unit_rows, factor, gain):
    grad, gain_row = norm_back(grad_norm, unit_rows, factor, gain)
    return grad, gain_row[0]


def attn_forward(block_parts):
    queries, key_rows, value_rows = block_parts
    scores = jnp.einsum(
        "bhqd,bhkd->bhqk", queries, key_rows, preferred_element_type=jnp.float32
    ) * HEAD_DIM ** (-0.5)
    row_peak = jnp.max(scores, -1, keepdims=True)
    exponent = jnp.exp(scores - row_peak)
    summed = jnp.sum(exponent, -1, keepdims=True)
    soft_weights = (exponent / summed).astype(jnp.bfloat16)
    mixed = jnp.einsum(
        "bhqk,bhkd->bhqd", soft_weights, value_rows, preferred_element_type=jnp.float32
    ).astype(jnp.bfloat16)
    return (mixed, (row_peak + jnp.log(summed))[..., 0], jnp.max(row_peak, axis=(0, 2, 3)))


def attn_backward(block_parts):
    queries, key_rows, value_rows, grad_mixed, log_total = block_parts
    score_scale = HEAD_DIM ** (-0.5)
    scores = (
        jnp.einsum("bhqd,bhkd->bhqk", queries, key_rows, preferred_element_type=jnp.float32)
        * score_scale
    )
    soft_weights = jnp.exp(scores - log_total[..., None])
    grad_soft = jnp.einsum(
        "bhqd,bhkd->bhqk", grad_mixed, value_rows, preferred_element_type=jnp.float32
    )
    inner_sum = jnp.sum(soft_weights * grad_soft, -1, keepdims=True)
    grad_scores = (soft_weights * (grad_soft - inner_sum)).astype(jnp.bfloat16)
    grad_query = (
        jnp.einsum("bhqk,bhkd->bhqd", grad_scores, key_rows, preferred_element_type=jnp.float32)
        * score_scale
    ).astype(jnp.bfloat16)
    grad_key = (
        jnp.einsum("bhqk,bhqd->bhkd", grad_scores, queries, preferred_element_type=jnp.float32)
        * score_scale
    ).astype(jnp.bfloat16)
    grad_value = jnp.einsum(
        "bhqk,bhqd->bhkd",
        soft_weights.astype(jnp.bfloat16),
        grad_mixed,
        preferred_element_type=jnp.float32,
    ).astype(jnp.bfloat16)
    return (grad_query, grad_key, grad_value)


def general_body(
    inputs, cotangent, routes, gain_attn, gain_expert, tau, w_qkv, w_out_attn, w_router, w_in, w_out
):
    row_count, width = inputs.shape
    n_dp = lax.axis_size("dp")
    n_heads = lax.axis_size("heads")
    n_tensor = lax.axis_size("tensor")
    row_piece = w_qkv.shape[1]
    col_piece = w_qkv.shape[2]
    own_heads = col_piece // HEAD_DIM
    head_start = lax.axis_index("heads") * col_piece
    x_float = inputs.astype(jnp.float32)
    unit_one, factor_one = unit_and_factor(x_float)
    normed_one = (unit_one * gain_attn).astype(jnp.bfloat16)
    stack_qkv, stack_out = (
        lax.all_gather(w_qkv[None], ("dp", "heads", "tensor"), axis=0, tiled=True),
        lax.all_gather(w_out_attn[None], ("dp", "heads", "tensor"), axis=0, tiled=True),
    )
    full_qkv = (
        stack_qkv.reshape(n_dp, n_heads, n_tensor, 3, row_piece, col_piece)
        .transpose(3, 0, 2, 4, 1, 5)
        .reshape(3, width, width)
    )
    full_out = (
        stack_out.reshape(n_dp, n_heads, n_tensor, col_piece, row_piece)
        .transpose(1, 3, 0, 2, 4)
        .reshape(width, width)
    )
    proj_w = lax.dynamic_slice_in_dim(full_qkv, head_start, col_piece, 2)
    attn_w = lax.dynamic_slice_in_dim(full_out, head_start, col_piece, 0)
    normed_all = lax.all_gather(normed_one, "heads", axis=0, tiled=True)
    head_cols = attn_w.shape[0]
    local_heads = head_cols // HEAD_DIM
    joined_w = jnp.concatenate([proj_w[0], proj_w[1], proj_w[2]], 1)
    projected = jnp.dot(normed_all, joined_w, preferred_element_type=jnp.float32).astype(
        jnp.bfloat16
    )
    images = normed_all.shape[0] // SEQ
    per_block = 4 if images % 4 == 0 else 3 if images % 3 == 0 else 2 if images % 2 == 0 else 1
    block_shape = (images // per_block, per_block, SEQ, local_heads, HEAD_DIM)

    def to_blocks(row_matrix):
        return row_matrix.reshape(block_shape).transpose(0, 1, 3, 2, 4)

    def from_blocks(block_array):
        return block_array.transpose(0, 1, 3, 2, 4).reshape(-1, head_cols)

    queries = to_blocks(projected[:, :head_cols])
    key_rows = to_blocks(projected[:, head_cols : 2 * head_cols])
    value_rows = to_blocks(projected[:, 2 * head_cols :])
    mixed, log_total, head_peaks = lax.map(attn_forward, (queries, key_rows, value_rows))
    mixed_rows = from_blocks(mixed)
    block_peak = jnp.max(head_peaks, 0)
    attn_out = lax.psum_scatter(
        jnp.dot(mixed_rows, attn_w, preferred_element_type=jnp.float32),
        "heads",
        scatter_dimension=0,
        tiled=True,
    )
    peak_full = lax.dynamic_update_slice_in_dim(
        jnp.full((HEADS,), -1e30, jnp.float32), block_peak, lax.axis_index("heads") * local_heads, 0
    )
    hidden = x_float + attn_out
    peak_all = lax.pmax(peak_full, ("dp", "heads", "tensor"))
    peak_logit = lax.dynamic_slice_in_dim(
        peak_all, lax.axis_index("heads") * own_heads, own_heads, 0
    )
    unit_two, factor_two = unit_and_factor(hidden)
    normed_two = (unit_two * gain_expert).astype(jnp.bfloat16)
    group_rows, group_cot = (
        lax.all_gather(normed_two, "tensor", axis=0, tiled=True),
        lax.all_gather(cotangent, "tensor", axis=0, tiled=True),
    )
    first_w, second_w, router_w = (
        lax.all_gather(w_in, ("dp", "heads"), axis=0, tiled=True),
        lax.all_gather(w_out, ("dp", "heads"), axis=0, tiled=True),
        lax.all_gather(w_router, ("dp", "heads"), axis=0, tiled=True),
    )
    logits = jnp.dot(group_rows, router_w, preferred_element_type=jnp.float32)
    chosen = jnp.take_along_axis(logits, routes, 1)
    exponent = jnp.exp(chosen - jnp.max(chosen, -1, keepdims=True))
    gate_values = exponent / jnp.sum(exponent, -1, keepdims=True)
    group_count = routes.shape[0]
    experts = router_w.shape[1]
    capacity = (group_count * 5 // (16 * experts) + 1) * 8
    flat_ids = routes.reshape(-1)
    ordering = jnp.argsort(flat_ids, stable=True)
    sorted_ids = flat_ids[ordering]
    counts = jnp.sum(
        (flat_ids[:, None] == jnp.arange(experts, dtype=jnp.int32)[None, :]).astype(jnp.int32), 0
    )
    expert_ids = jnp.arange(experts, dtype=jnp.int32)
    starts = jnp.sum(jnp.where(expert_ids[None, :] < expert_ids[:, None], counts[None, :], 0), 1)
    slot_rank = jnp.arange(2 * group_count, dtype=jnp.int32) - starts[sorted_ids]
    slot_table = (
        jnp.full((experts * capacity,), 2 * group_count, jnp.int32)
        .at[sorted_ids * capacity + slot_rank]
        .set(ordering)
    )
    slot_token = slot_table // 2
    padded_rows = jnp.concatenate([group_rows, jnp.zeros((1, width), jnp.bfloat16)], 0)
    slot_in = padded_rows[slot_token].reshape(experts, capacity, width)
    slot_gate = jnp.concatenate([gate_values.reshape(-1), jnp.zeros((1,), jnp.float32)], 0)[
        slot_table
    ]
    pre_gelu = jnp.einsum("ecd,edf->ecf", slot_in, first_w, preferred_element_type=jnp.float32)
    activated = gelu_tanh(pre_gelu).astype(jnp.bfloat16)
    slot_out = jnp.einsum(
        "ecf,efd->ecd", activated, second_w, preferred_element_type=jnp.float32
    ).reshape(-1, width)
    partial_value = (
        jnp.zeros((group_count + 1, width), jnp.float32)
        .at[slot_token]
        .add(slot_gate[:, None] * slot_out)[:group_count]
    )
    expert_mix = lax.psum_scatter(
        partial_value.astype(jnp.bfloat16), "tensor", scatter_dimension=0, tiled=True
    ).astype(jnp.float32)
    output = (hidden + expert_mix).astype(jnp.bfloat16)
    padded_cot = jnp.concatenate([group_cot, jnp.zeros((1, width), jnp.bfloat16)], 0)
    slot_cot = padded_cot[slot_token].astype(jnp.float32)
    grad_slot_out = (
        (slot_gate[:, None] * slot_cot).astype(jnp.bfloat16).reshape(experts, capacity, width)
    )
    gate_part = (
        jnp.zeros((2 * group_count + 1,), jnp.float32)
        .at[slot_table]
        .add(jnp.sum(slot_cot * slot_out, -1))[: 2 * group_count]
        .reshape(group_count, 2)
    )
    grad_act = jnp.einsum(
        "ecd,efd->ecf", grad_slot_out, second_w, preferred_element_type=jnp.float32
    )
    grad_pre = jax.vjp(gelu_tanh, pre_gelu)[1](grad_act)[0].astype(jnp.bfloat16)
    grad_first = jnp.einsum("ecd,ecf->edf", slot_in, grad_pre, preferred_element_type=jnp.float32)
    grad_second = jnp.einsum(
        "ecf,ecd->efd", activated, grad_slot_out, preferred_element_type=jnp.float32
    )
    grad_slots = jnp.einsum(
        "ecf,edf->ecd", grad_pre, first_w, preferred_element_type=jnp.float32
    ).reshape(-1, width)
    grad_part = (
        jnp.zeros((group_count + 1, width), jnp.float32)
        .at[slot_token]
        .add(grad_slots)[:group_count]
    )
    grad_normed_two, grad_gates = (
        lax.psum_scatter(
            grad_part.astype(jnp.bfloat16), "tensor", scatter_dimension=0, tiled=True
        ).astype(jnp.float32),
        lax.psum_scatter(
            gate_part.astype(jnp.bfloat16), "tensor", scatter_dimension=0, tiled=True
        ).astype(jnp.float32),
    )
    shard_first, shard_second = (
        lax.psum_scatter(
            grad_first.astype(jnp.bfloat16), ("dp", "heads"), scatter_dimension=0, tiled=True
        ).astype(jnp.float32),
        lax.psum_scatter(
            grad_second.astype(jnp.bfloat16), ("dp", "heads"), scatter_dimension=0, tiled=True
        ).astype(jnp.float32),
    )
    offset = lax.axis_index("tensor") * row_count
    local_gates = lax.dynamic_slice_in_dim(gate_values, offset, row_count, 0)
    local_routes = lax.dynamic_slice_in_dim(routes, offset, row_count, 0)
    grad_chosen = local_gates * (grad_gates - jnp.sum(local_gates * grad_gates, -1, keepdims=True))
    columns = jnp.arange(experts, dtype=jnp.int32)[None, :]
    grad_logits = (
        jnp.where(local_routes[:, 0:1] == columns, grad_chosen[:, 0:1], 0.0)
        + jnp.where(local_routes[:, 1:2] == columns, grad_chosen[:, 1:2], 0.0)
    ).astype(jnp.bfloat16)
    grad_normed_two = grad_normed_two + jnp.einsum(
        "re,de->rd", grad_logits, router_w, preferred_element_type=jnp.float32
    )
    router_term = jnp.einsum(
        "rd,re->de", normed_two, grad_logits, preferred_element_type=jnp.float32
    )
    grad_hidden_norm, gain_two_term = general_norm_back(grad_normed_two, unit_two, factor_two, gain_expert)
    grad_hidden = cotangent.astype(jnp.float32) + grad_hidden_norm
    grad_attn = lax.all_gather(grad_hidden.astype(jnp.bfloat16), "heads", axis=0, tiled=True)
    grad_mixed = jnp.einsum(
        "rd,cd->rc", grad_attn, attn_w, preferred_element_type=jnp.float32
    ).astype(jnp.bfloat16)
    out_term = jnp.einsum("rc,rd->cd", mixed_rows, grad_attn, preferred_element_type=jnp.float32)
    grad_query, grad_key, grad_value = lax.map(
        attn_backward, (queries, key_rows, value_rows, to_blocks(grad_mixed), log_total)
    )
    grad_proj = jnp.concatenate(
        [from_blocks(grad_query), from_blocks(grad_key), from_blocks(grad_value)], 1
    )
    grad_normed_one = lax.psum_scatter(
        jnp.einsum("rc,dc->rd", grad_proj, joined_w, preferred_element_type=jnp.float32).astype(
            jnp.bfloat16
        ),
        "heads",
        scatter_dimension=0,
        tiled=True,
    ).astype(jnp.float32)
    proj_term = jnp.einsum("rd,rc->dc", normed_all, grad_proj, preferred_element_type=jnp.float32)
    proj_stack = jnp.stack(
        [
            proj_term[:, :head_cols],
            proj_term[:, head_cols : 2 * head_cols],
            proj_term[:, 2 * head_cols :],
        ],
        0,
    )
    whole_proj = lax.dynamic_update_slice_in_dim(
        jnp.zeros((3, width, width), jnp.float32), proj_stack, head_start, 2
    )
    whole_out = lax.dynamic_update_slice_in_dim(
        jnp.zeros((width, width), jnp.float32), out_term, head_start, 0
    )
    send_qkv = (
        whole_proj.reshape(3, n_dp, n_tensor, row_piece, n_heads, col_piece)
        .transpose(1, 4, 2, 0, 3, 5)
        .reshape(-1, 3, row_piece, col_piece)
    )
    send_out = (
        whole_out.reshape(n_heads, col_piece, n_dp, n_tensor, row_piece)
        .transpose(2, 0, 3, 1, 4)
        .reshape(-1, col_piece, row_piece)
    )
    shard_proj, shard_attn = (
        lax.psum_scatter(send_qkv, ("dp", "heads", "tensor"), scatter_dimension=0, tiled=True),
        lax.psum_scatter(send_out, ("dp", "heads", "tensor"), scatter_dimension=0, tiled=True),
    )
    grad_input_norm, gain_one_term = general_norm_back(grad_normed_one, unit_one, factor_one, gain_attn)
    grad_input = (grad_hidden + grad_input_norm).astype(jnp.bfloat16)
    gain_one_grad, gain_two_grad, router_all = lax.psum(
        (gain_one_term, gain_two_term, router_term), ("dp", "heads", "tensor")
    )
    router_grad = lax.dynamic_slice_in_dim(
        router_all, lax.axis_index(("dp", "heads")) * w_router.shape[0], w_router.shape[0], 0
    )
    local_tau = lax.dynamic_slice_in_dim(tau, lax.axis_index("heads") * own_heads, own_heads, 0)
    clip_factor = jnp.sqrt(local_tau / jnp.maximum(peak_logit, local_tau))
    clipped = (w_qkv[:2].astype(jnp.float32) * jnp.repeat(clip_factor, HEAD_DIM)).astype(
        jnp.bfloat16
    )
    return (
        output,
        grad_input,
        gain_one_grad,
        gain_two_grad,
        shard_proj[0],
        shard_attn[0],
        router_grad,
        shard_first,
        shard_second,
        clipped,
    )


def body(*args):
    inputs, _, routes, _, _, _, w_qkv, _, w_router, w_in, _ = args
    sz = Sizes(
        lax.axis_size("dp"), lax.axis_size("heads"), lax.axis_size("tensor"), inputs, routes, w_qkv, w_router, w_in
    )
    if sz.fits():
        return fast_body(sz, *args)
    return general_body(*args)


def solution(mesh):
    return jax.shard_map(
        body,
        mesh=mesh,
        in_specs=(
            P(("dp", "heads", "tensor"), None),
            P(("dp", "heads", "tensor"), None),
            P(("dp", "heads"), None),
            P(),
            P(),
            P(),
            P(None, ("dp", "tensor"), "heads"),
            P("heads", ("dp", "tensor")),
            P(("dp", "heads"), None),
            P(("dp", "heads"), None, "tensor"),
            P(("dp", "heads"), "tensor", None),
        ),
        out_specs=(
            P(("dp", "heads", "tensor"), None),
            P(("dp", "heads", "tensor"), None),
            P(),
            P(),
            P(None, ("dp", "tensor"), "heads"),
            P("heads", ("dp", "tensor")),
            P(("dp", "heads"), None),
            P(("dp", "heads"), None, "tensor"),
            P(("dp", "heads"), "tensor", None),
            P(None, ("dp", "tensor"), "heads"),
        ),
        check_vma=False,
    )
```

```python
import functools
import jax
import jax.numpy as jnp
from jax import lax
from jax.experimental import pallas as pl
from jax.experimental.pallas import tpu as pltpu
from jax.sharding import PartitionSpec as P

HEADS = 8
HEAD_DIM = 64
SEQ = 197
F32 = jnp.float32
BF16 = jnp.bfloat16
MESH = pl.DeviceIdType.MESH
NEG = -1e30


class Sizes:
    def __init__(self, n_dp, n_heads, n_tensor, inputs, routes, w_qkv, w_router, w_in):
        self.nd, self.nh, self.nt = n_dp, n_heads, n_tensor
        self.groups = n_dp * n_heads
        self.rows, self.width = inputs.shape
        self.pad = -(-self.rows // 16) * 16
        self.block = self.pad * n_tensor
        self.block_rows = routes.shape[0]
        self.own = w_in.shape[0]
        self.hidden = w_in.shape[2]
        self.experts = self.own * self.groups
        self.cap = (self.block_rows * 5 // (16 * self.experts) + 1) * 8
        self.group_slots = self.own * self.cap
        self.slots = self.experts * self.cap
        self.row_piece, self.col_piece = w_qkv.shape[1], w_qkv.shape[2]
        self.band = self.row_piece * n_tensor
        self.router_rows = w_router.shape[0]
        self.parts = 4

    def fits(self):
        return (
            self.rows == SEQ
            and self.block_rows == self.rows * self.nt
            and self.cap == 64
            and self.experts == 32
            and self.group_slots % 128 == 0
            and self.col_piece % 128 == 0
            and self.row_piece % 16 == 0
            and self.router_rows % 16 == 0
            and self.own * self.groups * 4 == 128
            and self.width == HEADS * HEAD_DIM
            and self.block * self.width * 2 <= 2**20
        )


def nn(a, b):
    return jnp.dot(a, b, preferred_element_type=F32)


def nt(a, b):
    return lax.dot_general(a, b, (((1,), (1,)), ((), ())), preferred_element_type=F32)


def tn(a, b):
    return lax.dot_general(a, b, (((0,), (0,)), ((), ())), preferred_element_type=F32)


def iota(shape, axis):
    return lax.broadcasted_iota(jnp.int32, shape, axis)


def normalize(rows):
    centered = rows - jnp.mean(rows, -1, keepdims=True)
    factor = lax.rsqrt(jnp.mean(centered * centered, -1, keepdims=True) + 1e-06)
    return centered * factor, factor


def norm_back(grad_norm, unit_rows, factor, gain):
    grad_hat = grad_norm * gain
    inner = (
        grad_hat
        - jnp.mean(grad_hat, -1, keepdims=True)
        - unit_rows * jnp.mean(grad_hat * unit_rows, -1, keepdims=True)
    )
    return factor * inner, jnp.sum(grad_norm * unit_rows, 0, keepdims=True)


def split_high_low(values):
    high = values.astype(BF16)
    low = (values - high.astype(F32)).astype(BF16)
    return jnp.concatenate([high, low], 0)


class Place:
    def __init__(self, sz):
        self.sz = sz
        self.d = lax.axis_index("dp")
        self.h = lax.axis_index("heads")
        self.z = lax.axis_index("tensor")
        self.group = self.d * sz.nh + self.h

    def plane(self, group):
        return (group // self.sz.nh, group % self.sz.nh, self.z)

    def line(self, z):
        return (self.d, self.h, z)

    def next_group(self, k):
        return (self.group + k) % self.sz.groups

    def next_z(self, j):
        return (self.z + j) % self.sz.nt

    def enter(self):
        sz = self.sz
        barrier = pltpu.get_barrier_semaphore()
        for k in range(1, sz.groups):
            pl.semaphore_signal(barrier, inc=1, device_id=self.plane(self.next_group(k)), device_id_type=MESH)
        for j in range(1, sz.nt):
            pl.semaphore_signal(barrier, inc=1, device_id=self.line(self.next_z(j)), device_id_type=MESH)
        pl.semaphore_wait(barrier, sz.groups + sz.nt - 2)


def remote(src, dst, send, recv, device):
    return pltpu.make_async_remote_copy(
        src_ref=src, dst_ref=dst, send_sem=send, recv_sem=recv, device_id=device, device_id_type=MESH
    )


def route_table(sz, routes_ref, table):
    table[...] = jnp.full_like(table, -1.0)
    for z in range(sz.nt):
        table[0:2, z * sz.pad : z * sz.pad + sz.rows] = routes_ref[:, z * sz.rows : (z + 1) * sz.rows].astype(F32)


def block_kernel(
    sz, x_ref, cot_ref, routes_ref, gain_one_ref, gain_two_ref, w_qkv_ref, w_out_ref, w_router_ref, first_hbm, second_hbm,
    output_out, grad_input_out, small_out, weight_out, router_out, grad_first_out, grad_second_out,
    w_own, w_full, router_own, router_full, router_t, route_rows, route_columns, select, select_t,
    cot_block, rows_block, send_a, send_b, cot_slots, slots, grad_slots, values,
    first, second, act, grad_pre, grad_act, grad_first, grad_second,
    gate_send, gate_recv, gates_at, dgate_send, dgate_recv, dgate_rows,
    qkv, probs, mixed, hidden_at, peak_at, part, part_own, part_send, part_recv, mix_own, mix_send, mix_recv,
    grad_mixed, grad_qkv, core_send, core_recv, w_half, band_send, band_recv, line_send, line_recv,
    small, small_send, small_core, small_x, small_z, rt, rt_core, rt_x, rt_z,
    wz_s, wz_r, wx_s, wx_r, wc_s, wc_r, r_s, r_r, qz_s, qz_r, nz_s, nz_r, qa_s, qa_r, na_s, na_r, ga_s, ga_r,
    d0_s, d0_r, da_s, da_r, va_s, va_r, dg_s, dg_r, pz_s, pz_r, mz_s, mz_r, gc_s, gc_r, gx_s, gx_r, gl_s, gl_r,
    sc_s, sc_r, sx_s, sx_r, sz_s, sz_r, local_sem,
):
    at = Place(sz)
    d, h, z, me = at.d, at.h, at.z, at.group
    nd, nh, nz, ng = sz.nd, sz.nh, sz.nt, sz.groups
    band, rp, cp, pad, width = sz.band, sz.row_piece, sz.col_piece, sz.pad, sz.width
    many = ng * sz.cap
    parts, part_width = sz.parts, width // sz.parts

    def lanes(c):
        return pl.ds(c * part_width, part_width)

    def rows_at(n, size):
        return pl.ds(pl.multiple_of(n * size, size), size)

    own_block, own_columns = rows_at(z, pad), rows_at(h, cp)

    w_own[0:3] = w_qkv_ref[...]
    w_own[3] = w_out_ref[...]
    router_own[...] = jnp.zeros_like(router_own)
    router_own[:, 0 : sz.router_rows] = w_router_ref[...]
    cot_block[own_block] = jnp.concatenate(
        [cot_ref[...].astype(F32), jnp.zeros((pad - sz.rows, width), F32)], 0
    ).astype(BF16)

    at.enter()

    w_rows = rows_at(d * nz + z, rp)
    w_z = [
        remote(w_own, w_full.at[:, w_rows, own_columns], wz_s.at[j - 1], wz_r.at[j - 1], at.line(at.next_z(j)))
        for j in range(1, nz)
    ]
    for copy in w_z:
        copy.start()
    loads = [
        pltpu.make_async_copy(first_hbm, first, local_sem.at[0]),
        pltpu.make_async_copy(second_hbm, second, local_sem.at[1]),
    ]
    for copy in loads:
        copy.start()
    routers = [
        remote(router_own, router_full.at[me], r_s.at[k - 1], r_r.at[k - 1], at.plane(at.next_group(k)))
        for k in range(1, ng)
    ]
    for copy in routers:
        copy.start()
    w_full[:, w_rows, own_columns] = w_own[...]
    router_full[me] = router_own[...]

    zeros = jnp.zeros((pad - sz.rows, width), F32)
    x_rows = jnp.concatenate([x_ref[...].astype(F32), zeros], 0)
    unit_one, _ = normalize(x_rows)
    normed_one = (unit_one * gain_one_ref[...]).astype(BF16)

    for copy in w_z:
        copy.wait()

    def to_core(i, dp, other):
        place = w_full.at[:, rows_at(dp, band), own_columns]
        return remote(place, place, wc_s.at[i], wc_r.at[i], (d, (h + other) % nh, z))

    w_band = w_full.at[:, rows_at(d, band), own_columns]
    w_x = [
        remote(w_band, w_band, wx_s.at[k - 1], wx_r.at[k - 1], ((d + k) % nd, h, z)) for k in range(1, nd)
    ]
    for copy in w_x:
        copy.start()
    w_c = [to_core((other - 1) * nd, d, other) for other in range(1, nh)]
    for copy in w_c:
        copy.start()

    def along(block, send_sems, recv_sems, c):
        place = block.at[own_block, lanes(c)]
        return [
            remote(place, place, send_sems.at[c, j - 1], recv_sems.at[c, j - 1], at.line(at.next_z(j)))
            for j in range(1, nz)
        ]

    for c in range(parts):
        for copy in along(cot_block, qz_s, qz_r, c):
            copy.start()

    route_table(sz, routes_ref, route_rows)
    route_a, route_b = route_rows[0:1, :], route_rows[1:2, :]
    expert = iota((sz.experts, sz.block), 0).astype(F32)
    named_a, named_b = route_a == expert, route_b == expert
    named = jnp.logical_or(named_a, named_b)
    before = (iota((sz.block, sz.block), 0) < iota((sz.block, sz.block), 1)).astype(BF16)
    rank = nn(named.astype(BF16), before) + expert * float(sz.cap)
    slot_a = jnp.sum(jnp.where(named_a, rank, 0.0), 0, keepdims=True)
    slot_b = jnp.sum(jnp.where(named_b, rank, 0.0), 0, keepdims=True)
    slot_a = jnp.where(route_a < 0.0, -1.0, slot_a)
    slot_b = jnp.where(route_b < 0.0, -1.0, slot_b)
    slot_pair = jnp.concatenate([slot_a, slot_b] * 64, 0)
    route_columns[...] = slot_pair.T

    def fill(g, carry):
        slot = iota((sz.group_slots, sz.block), 0).astype(F32) + (g * sz.group_slots).astype(F32)
        hit = jnp.logical_or(slot == slot_a, slot == slot_b)
        select[rows_at(g, sz.group_slots), :] = jnp.where(hit, 1.0, 0.0).astype(BF16)
        return carry

    lax.fori_loop(0, ng, fill, 0)

    def dispatch(c, block, send, out):
        def step(g, carry):
            send[g, :, lanes(c)] = nn(select[rows_at(g, sz.group_slots), :], block[:, lanes(c)]).astype(BF16)
            return carry

        lax.fori_loop(0, ng, step, 0)
        out[me, :, lanes(c)] = send[me, :, lanes(c)]

    def exchange(c, k, send, out, send_sems, recv_sems):
        g = (me + k) % ng
        return remote(
            send.at[g, :, lanes(c)], out.at[me, :, lanes(c)], send_sems.at[c, k], recv_sems.at[c, k], at.plane(g)
        )

    def start_part(c, *flow):
        def step(i, carry):
            exchange(c, ng - 1 - i, *flow).start()
            return carry

        lax.fori_loop(0, ng - 1, step, 0)

    def wait_part(c, *flow):
        def step(i, carry):
            exchange(c, i + 1, *flow).wait()
            return carry

        lax.fori_loop(0, ng - 1, step, 0)

    cot_flow = (send_a, cot_slots, qa_s, qa_r)
    row_flow = (send_b, slots, na_s, na_r)

    def send_cot(c):
        for copy in along(cot_block, qz_s, qz_r, c):
            copy.wait()
        dispatch(c, cot_block, send_a, cot_slots)

    send_cot(0)
    for k in range(1, nd):
        w_x[k - 1].wait_recv()
        for other in range(1, nh):
            copy = to_core((other - 1) * nd + k, (d - k + nd) % nd, other)
            copy.start()
            w_c.append(copy)
    start_part(0, *cot_flow)
    for copy in w_c:
        copy.wait()
    for copy in w_x:
        copy.wait_send()

    for i in range(3):
        qkv[i] = nn(normed_one, w_full[i]).astype(BF16)
    lane = iota((1, 2 * HEAD_DIM), 1)
    halves = (lane < HEAD_DIM, lane >= HEAD_DIM)
    key_valid = iota((1, pad), 1) < sz.rows
    row_valid = iota((pad, 1), 0) < sz.rows
    peak_lane = iota((1, 128), 1)
    peak_at[...] = jnp.full_like(peak_at, NEG)
    scale = HEAD_DIM ** (-0.5)

    def attend(pair, carry):
        columns = rows_at(pair, 2 * HEAD_DIM)
        q_pair, k_pair, v_pair = (qkv[i, :, columns] for i in range(3))
        sides = []
        for side in range(2):
            q_own = jnp.where(halves[side], q_pair, jnp.zeros_like(q_pair))
            scores = jnp.where(key_valid, nt(q_own, k_pair) * scale, NEG)
            row_peak = jnp.max(scores, -1, keepdims=True)
            exponent = jnp.exp(scores - row_peak)
            weights = (exponent / jnp.sum(exponent, -1, keepdims=True)).astype(BF16)
            head = pair * 2 + side
            probs[head] = weights
            sides.append(nn(weights, v_pair))
            peak = jnp.max(jnp.where(row_valid, row_peak, NEG), 0, keepdims=True)
            peak_at[0:1, :] = jnp.where(peak_lane == head, peak, peak_at[0:1, :])
        mixed[:, columns] = jnp.where(halves[0], sides[0], sides[1]).astype(BF16)
        return carry

    pairs = HEADS // 2
    sent = 1
    for turn in range(2):
        until = 1 + ((parts - 1) * (turn + 1)) // 2
        for c in range(sent, until):
            send_cot(c)
            start_part(c, *cot_flow)
        sent = until
        lax.fori_loop(turn * pairs // 2, (turn + 1) * pairs // 2, attend, 0)

    hidden = x_rows + nt(mixed[...], w_full[3])
    hidden_at[...] = hidden
    unit_two, _ = normalize(hidden)
    rows_block[own_block] = jnp.where(row_valid, unit_two * gain_two_ref[...], 0.0).astype(BF16)
    for c in range(parts):
        for copy in along(rows_block, nz_s, nz_r, c):
            copy.start()

    def fill_t(i, carry):
        rows = rows_at(i, pad)
        slot = iota((pad, sz.slots), 1).astype(F32)
        hit = jnp.logical_or(slot == route_columns[rows, 0:1], slot == route_columns[rows, 1:2])
        select_t[rows, :] = jnp.where(hit, 1.0, 0.0).astype(BF16)
        return carry

    lax.fori_loop(0, nz, fill_t, 0)
    for copy in routers:
        copy.wait()
    for g in range(ng):
        router_t[:, g * sz.router_rows : (g + 1) * sz.router_rows] = router_full[g, :, 0 : sz.router_rows]

    def expert_rows(ref, e):
        return ref[:, rows_at(e, sz.cap), :].reshape(many, width)

    def cot_grad(e, carry):
        grad_act[e] = nt(expert_rows(cot_slots, e), second[e])
        return carry

    for c in range(parts):
        for copy in along(rows_block, nz_s, nz_r, c):
            copy.wait()
        dispatch(c, rows_block, send_b, slots)
        start_part(c, *row_flow)
        if c == parts // 2 - 1:
            for i in range(parts):
                wait_part(i, *cot_flow)
            for copy in loads:
                copy.wait()
            lax.fori_loop(0, sz.own, cot_grad, 0)

    logits = jnp.where(named, nt(router_t[...], rows_block[...]), NEG)
    exponent = jnp.where(named, jnp.exp(logits - jnp.max(logits, 0, keepdims=True)), 0.0)
    total = jnp.sum(exponent, 0, keepdims=True)
    gates = exponent / jnp.where(total > 0.0, total, 1.0)
    gates_at[...] = gates
    by_slot = nt(split_high_low(gates), select[...])
    by_slot = by_slot[0 : sz.experts] + by_slot[sz.experts :]
    own_slot = iota((sz.experts, sz.slots), 1) // sz.cap == iota((sz.experts, sz.slots), 0)
    by_slot = jnp.where(own_slot, by_slot, 0.0)
    folded = by_slot[:, 0:128]
    for i in range(1, sz.slots // 128):
        folded = folded + by_slot[:, i * 128 : (i + 1) * 128]
    gate_send[...] = folded
    gate_copies = [
        remote(gate_send, gate_recv.at[me], ga_s.at[k - 1], ga_r.at[k - 1], at.plane(at.next_group(k)))
        for k in range(1, ng)
    ]
    for copy in gate_copies:
        copy.start()
    gate_recv[me] = folded
    for copy in gate_copies:
        copy.wait()
    for c in range(parts):
        wait_part(c, *row_flow)

    def gate_of(e):
        turned = gate_recv[:, pl.ds(me * sz.own + e, 1), :].reshape(ng, 128).T
        columns = jnp.where((e % 2) == 1, turned[sz.cap : 2 * sz.cap], turned[0 : sz.cap])
        return jnp.concatenate([columns[:, s : s + 1] for s in range(ng)], 0)

    def first_piece(e, k):
        g = (me + k) % ng
        piece = (rows_at(e, sz.cap), lanes(0))
        return remote(
            send_a.at[(g, *piece)], grad_slots.at[(me, *piece)], d0_s.at[e, k], d0_r.at[e, k], at.plane(g)
        )

    def expert_back(e, carry):
        gate = gate_of(e)
        half_rows = many // 2
        for part_at in range(2):
            some = slice(part_at * half_rows, (part_at + 1) * half_rows)
            groups = slice(part_at * ng // 2, (part_at + 1) * ng // 2)
            pre = nn(slots[groups, rows_at(e, sz.cap), :].reshape(half_rows, width), first[e])
            const, cubic = 0.7978845608028654, 0.044715
            square = pre * pre
            bent = jnp.tanh(const * pre * (1.0 + cubic * square))
            half = 0.5 * (1.0 + bent)
            act[e, some] = (pre * half).astype(BF16)
            slope = half + 0.5 * pre * (1.0 - bent * bent) * const * (1.0 + 3.0 * cubic * square)
            grads = (grad_act[e, some] * gate[some] * slope).astype(BF16)
            grad_pre[e, some] = grads
            send_a[groups, rows_at(e, sz.cap), :] = (
                nt(grads, first[e]).astype(BF16).reshape(ng // 2, sz.cap, width)
            )

        def step(i, carry):
            first_piece(e, ng - 1 - i).start()
            return carry

        lax.fori_loop(0, ng - 1, step, 0)
        return carry

    lax.fori_loop(0, sz.own, expert_back, 0)
    grad_flow = (send_a, grad_slots, da_s, da_r)
    value_flow = (send_b, values, va_s, va_r)
    for c in range(1, parts):
        start_part(c, *grad_flow)
    grad_slots[me] = send_a[me]

    dgate_send[...] = jnp.zeros_like(dgate_send)

    def expert_value(e, carry):
        value = nn(act[e], second[e])
        send_b[:, rows_at(e, sz.cap), :] = (value * gate_of(e)).astype(BF16).reshape(ng, sz.cap, width)
        product = (value * expert_rows(cot_slots, e).astype(F32)).astype(BF16)
        dgate = nt(jnp.ones((8, width), BF16), product)
        dgate_send[...] = jnp.where(iota((8, many), 0) == e, dgate, dgate_send[...])
        return carry

    lax.fori_loop(0, sz.own, expert_value, 0)
    values[me] = send_b[me]
    dgates = [
        remote(dgate_send, dgate_recv.at[me], dg_s.at[k - 1], dg_r.at[k - 1], at.plane(at.next_group(k)))
        for k in range(1, ng)
    ]
    for copy in dgates:
        copy.start()
    dgate_recv[me] = dgate_send[...]

    def weight_grads(e, carry):
        grad_value = (expert_rows(cot_slots, e).astype(F32) * gate_of(e)).astype(BF16)
        grad_second[e] = tn(act[e], grad_value).astype(BF16)
        grad_first[e] = tn(expert_rows(slots, e), grad_pre[e]).astype(BF16)
        return carry

    for copy in dgates:
        copy.wait()
    mine = iota((8, many), 1) // sz.cap == me
    for g in range(ng):
        masked = jnp.where(mine, dgate_recv[g], 0.0)
        folded = masked[:, 0:128]
        for i in range(1, many // 128):
            folded = folded + masked[:, i * 128 : (i + 1) * 128]
        folded = folded + pltpu.roll(folded, 64, 1)
        dgate_rows[g * sz.own : (g + 1) * sz.own, :] = folded[0 : sz.own]
    spread = jnp.concatenate([dgate_rows[...]] * (sz.slots // 128), 1)
    own_slot = iota((sz.experts, sz.slots), 1) // sz.cap == iota((sz.experts, sz.slots), 0)
    dgate = nt(split_high_low(jnp.where(own_slot, spread, 0.0)), select_t[...])
    dgate = dgate[0 : sz.experts] + dgate[sz.experts :]
    gates = gates_at[...]
    dlogits = (gates * (dgate - jnp.sum(gates * dgate, 0, keepdims=True))).astype(BF16)
    rt[...] = nn(dlogits, rows_block[...])
    part[...] = tn(dlogits, router_t[...])

    def line_copy(c, j, send, recv, send_sems, recv_sems):
        return remote(
            send.at[j - 1, :, lanes(c)], recv.at[j - 1, :, lanes(c)], send_sems.at[c, j - 1], recv_sems.at[c, j - 1],
            at.line(at.next_z(j)),
        )

    def scatter(c, source, base, own, *flow):
        flat = source[:, :, lanes(c)].reshape(sz.slots, part_width)
        for j in [*range(1, nz), 0]:
            tokens = rows_at(at.next_z(j), pad)
            sums = nn(select_t[tokens, :], flat)
            if base is not None:
                sums = sums + base[tokens, lanes(c)]
            if j == 0:
                own[:, lanes(c)] = sums
            else:
                flow[0][j - 1, :, lanes(c)] = sums.astype(BF16)
                line_copy(c, j, *flow).start()

    def gathered(own, *flow):
        for c in range(parts):
            for j in range(1, nz):
                line_copy(c, j, *flow).wait()
        sums = own[...]
        for j in range(1, nz):
            sums = sums + flow[1][j - 1].astype(F32)
        return sums

    part_flow = (part_send, part_recv, pz_s, pz_r)
    mix_flow = (mix_send, mix_recv, mz_s, mz_r)

    def wait_first(e, carry):
        def step(i, carry):
            first_piece(e, i + 1).wait()
            return carry

        return lax.fori_loop(0, ng - 1, step, carry)

    done = 0
    for c in range(parts):
        if c == 0:
            lax.fori_loop(0, sz.own, wait_first, 0)
        else:
            wait_part(c, *grad_flow)
        if c == parts - 1:
            for i in range(parts):
                start_part(i, *value_flow)
        scatter(c, grad_slots, part, part_own, *part_flow)
        until = sz.own * (c + 1) // parts
        lax.fori_loop(done, until, weight_grads, 0)
        done = until
    stores = [
        pltpu.make_async_copy(grad_first, grad_first_out, local_sem.at[2]),
        pltpu.make_async_copy(grad_second, grad_second_out, local_sem.at[3]),
    ]
    for copy in stores:
        copy.start()

    unit_two, factor_two = normalize(hidden_at[...])
    grad_normed = jnp.where(row_valid, gathered(part_own, *part_flow), 0.0)
    grad_hidden, gain_two = norm_back(grad_normed, unit_two, factor_two, gain_two_ref[...])
    grad_hidden = jnp.concatenate([cot_ref[...].astype(F32), zeros], 0) + jnp.where(row_valid, grad_hidden, 0.0)
    part_own[...] = grad_hidden
    grad_attn = grad_hidden.astype(BF16)

    def core_copy(i, other):
        n = 4 * (other - 1) + i
        return remote(
            core_send.at[other - 1, i], core_recv.at[other - 1, i], gc_s.at[n], gc_r.at[n], (d, (h + other) % nh, z)
        )

    def half_sum(i, sums):
        for other in range(1, nh):
            core_copy(i, other).wait()
            sums = sums + core_recv[other - 1, i].astype(F32)
        w_half[i] = sums
        band_send[i] = sums.astype(BF16)

    def band_copy(k, matrices, n):
        to = (d + k) % nd
        n = 2 * (k - 1) + n
        return remote(
            band_send.at[matrices, rows_at(to, band), :], band_recv.at[k - 1, matrices], gx_s.at[n], gx_r.at[n], (to, h, z)
        )

    for other in [*range(1, nh), 0]:
        sums = tn(grad_attn, mixed[:, rows_at((h + other) % nh, cp)])
        if other:
            core_send[other - 1, 3] = sums.astype(BF16)
            core_copy(3, other).start()
        else:
            w_half[3] = sums
    grad_mixed[...] = nn(grad_attn, w_full[3]).astype(BF16)
    half_sum(3, w_half[3])
    out_band = [band_copy(k, pl.ds(3, 1), 0) for k in range(1, nd)]
    for copy in out_band:
        copy.start()

    def attend_back(pair):
        columns = rows_at(pair, 2 * HEAD_DIM)
        q_pair, k_pair, v_pair = (qkv[i, :, columns] for i in range(3))
        g_pair = grad_mixed[:, columns]
        dq, dk, dv = [], [], []
        for side in range(2):
            weights = probs[pair * 2 + side]
            soft = weights.astype(F32)
            g_own = jnp.where(halves[side], g_pair, jnp.zeros_like(g_pair))
            grad_soft = nt(g_own, v_pair)
            inner = jnp.sum(soft * grad_soft, -1, keepdims=True)
            grad_scores = (soft * (grad_soft - inner)).astype(BF16)
            dq.append(nn(grad_scores, k_pair))
            dk.append(tn(grad_scores, q_pair))
            dv.append(tn(weights, g_pair))
        grad_qkv[0, :, columns] = (jnp.where(halves[0], dq[0], dq[1]) * scale).astype(BF16)
        grad_qkv[1, :, columns] = (jnp.where(halves[0], dk[0], dk[1]) * scale).astype(BF16)
        grad_qkv[2, :, columns] = jnp.where(halves[0], dv[0], dv[1]).astype(BF16)

    unit_one, factor_one = normalize(jnp.concatenate([x_ref[...].astype(F32), zeros], 0))
    normed_one = (unit_one * gain_one_ref[...]).astype(BF16)
    core_pairs = cp // (2 * HEAD_DIM)
    turns, mixed_parts = nh * core_pairs, 0
    turn = 0
    for other in [*range(1, nh), 0]:
        core = (h + other) % nh
        for q in range(core_pairs):
            attend_back(core * core_pairs + q)
            turn += 1
            if turn < turns:
                until = parts * turn // turns
                for c in range(mixed_parts, until):
                    wait_part(c, *value_flow)
                    scatter(c, values, None, mix_own, *mix_flow)
                mixed_parts = until
        for i in range(3):
            sums = tn(normed_one, grad_qkv[i, :, rows_at(core, cp)])
            if other:
                core_send[other - 1, i] = sums.astype(BF16)
                core_copy(i, other).start()
            else:
                half_sum(i, sums)
    qkv_band = [band_copy(k, pl.ds(0, 3), 1) for k in range(1, nd)]
    for copy in qkv_band:
        copy.start()

    grad_one = jnp.zeros((pad, width), F32)
    for i in range(3):
        grad_one = grad_one + nt(grad_qkv[i], w_full[i])
    grad_one = jnp.where(row_valid, grad_one, 0.0)
    grad_input, gain_one = norm_back(grad_one, unit_one, factor_one, gain_one_ref[...])
    grad_input_out[...] = (part_own[...] + grad_input)[0 : sz.rows].astype(BF16)

    small[...] = jnp.zeros_like(small)
    small[0:1, :] = gain_one
    small[1:2, :] = gain_two
    small[2:3, 0:128] = peak_at[0:1, :]
    peak_row = iota(small.shape, 0) == 2

    def join(a, b):
        return jnp.where(peak_row, jnp.maximum(a, b), a + b)

    small_copies = []
    for other in range(1, nh):
        device, n = (d, (h + other) % nh, z), 2 * (other - 1)
        small_copies += [
            remote(small, small_core.at[other - 1], sc_s.at[n], sc_r.at[n], device),
            remote(rt, rt_core.at[other - 1], sc_s.at[n + 1], sc_r.at[n + 1], device),
        ]
    for copy in small_copies:
        copy.start()
    for copy in small_copies:
        copy.wait()
    for other in range(1, nh):
        small[...] = join(small[...], small_core[other - 1])
        rt[...] = rt[...] + rt_core[other - 1]
    small_send[0] = small[...]
    small_copies = []
    for k in range(1, nd):
        to, n = (d + k) % nd, 2 * (k - 1)
        small_copies += [
            remote(small_send.at[0], small_x.at[k - 1], sx_s.at[n], sx_r.at[n], (to, h, z)),
            remote(rt.at[:, rows_at(to, band)], rt_x.at[k - 1], sx_s.at[n + 1], sx_r.at[n + 1], (to, h, z)),
        ]
    for copy in small_copies:
        copy.start()

    for c in range(mixed_parts, parts):
        wait_part(c, *value_flow)
        scatter(c, values, None, mix_own, *mix_flow)

    for copy in small_copies:
        copy.wait()
    router_sum = rt[:, rows_at(d, band)]
    for k in range(1, nd):
        small[...] = join(small[...], small_x[k - 1])
        router_sum = router_sum + rt_x[k - 1]
    rt_z[nz - 1] = router_sum
    small_send[1] = small[...]
    for copy in out_band:
        copy.wait()
    for copy in qkv_band:
        copy.wait()
    for i in range(4):
        sums = w_half[i, rows_at(d, band), :]
        for k in range(1, nd):
            sums = sums + band_recv[k - 1, i].astype(F32)
        w_half[i, 0:band, :] = sums
        line_send[i] = sums.astype(BF16)
    z_copies = []
    for j in range(1, nz):
        to, n = at.next_z(j), 3 * (j - 1)
        device = at.line(to)
        z_copies += [
            remote(line_send.at[:, rows_at(to, rp), :], line_recv.at[j - 1], gl_s.at[n], gl_r.at[n], device),
            remote(small_send.at[1], small_z.at[j - 1], gl_s.at[n + 1], gl_r.at[n + 1], device),
            remote(rt_z.at[nz - 1], rt_z.at[j - 1], gl_s.at[n + 2], gl_r.at[n + 2], device),
        ]
    for copy in z_copies:
        copy.start()

    mix = gathered(mix_own, *mix_flow)
    output_out[...] = (hidden_at[...] + mix)[0 : sz.rows].astype(BF16)

    for copy in z_copies:
        copy.wait()
    totals = small[...]
    router_sum = rt_z[nz - 1]
    for j in range(1, nz):
        totals = join(totals, small_z[j - 1])
        router_sum = router_sum + rt_z[j - 1]
    small_out[...] = totals
    router_out[...] = router_sum
    for i in range(4):
        sums = w_half[i, rows_at(z, rp), :]
        for j in range(1, nz):
            sums = sums + line_recv[j - 1, i].astype(F32)
        weight_out[i] = sums
    for copy in stores:
        copy.wait()


def finish_kernel(
    sz, output_ref, grad_input_ref, small_ref, weight_ref, router_ref, grad_first_ref, grad_second_ref, tau_ref, w_qkv_ref,
    output, grad_input, gain_one, gain_two, grad_qkv, grad_out, grad_router, grad_first, grad_second, clipped,
):
    grad_first[...] = grad_first_ref[...].astype(F32)
    grad_second[...] = grad_second_ref[...].astype(F32)

    @pl.when(pl.program_id(0) == 0)
    def _():
        h = lax.axis_index("heads")
        cp, rr = sz.col_piece, sz.router_rows
        output[...] = output_ref[...]
        grad_input[...] = grad_input_ref[...]
        gain_one[...] = small_ref[0:1, :]
        gain_two[...] = small_ref[1:2, :]
        grad_qkv[...] = weight_ref[0:3]
        grad_out[...] = weight_ref[3]
        piece = router_ref[:, 0:rr]
        for i in range(1, sz.nh):
            piece = jnp.where(h == i, router_ref[:, i * rr : (i + 1) * rr], piece)
        grad_router[...] = piece
        tau = tau_ref[...]
        factor = jnp.sqrt(tau / jnp.maximum(small_ref[2:3, 0:HEADS], tau))
        column = iota((1, cp), 1) // HEAD_DIM + h * (cp // HEAD_DIM)
        scale_row = jnp.zeros((1, cp), F32)
        for head in range(HEADS):
            scale_row = jnp.where(column == head, factor[:, head : head + 1], scale_row)
        for i in range(2):
            clipped[i] = (w_qkv_ref[i].astype(F32) * scale_row).astype(BF16)


def fast_body(
    sz, inputs, cotangent, routes, gain_attn, gain_expert, tau, w_qkv, w_out_attn, w_router, w_in, w_out
):
    ng, nz, nd, nh, pad, width, own = sz.groups, sz.nt, sz.nd, sz.nh, sz.pad, sz.width, sz.own
    rp, cp, band, parts, block = sz.row_piece, sz.col_piece, sz.band, sz.parts, sz.block
    many, hidden = ng * sz.cap, sz.hidden
    on_chip, anywhere = pl.BlockSpec(memory_space=pltpu.VMEM), pl.BlockSpec(memory_space=pl.ANY)

    def shape(dims, dtype):
        return jax.ShapeDtypeStruct(dims, dtype)

    def half(*dims):
        return pltpu.VMEM(dims, BF16)

    def full(*dims):
        return pltpu.VMEM(dims, F32)

    def pair(*dims):
        return [pltpu.SemaphoreType.DMA(dims)] * 2

    slot_buffer = half(ng, sz.group_slots, width)
    line_buffer = half(nz - 1, pad, width)
    packed = pl.pallas_call(
        functools.partial(block_kernel, sz),
        out_shape=(
            shape(inputs.shape, BF16), shape(inputs.shape, BF16), shape((8, width), F32), shape((4, rp, cp), F32),
            shape((sz.experts, band), F32), shape(w_in.shape, BF16), shape(w_out.shape, BF16),
        ),
        in_specs=[on_chip] * 8 + [anywhere] * 2,
        out_specs=(on_chip,) * 5 + (anywhere,) * 2,
        scratch_shapes=[
            half(4, rp, cp), half(4, width, width), half(sz.experts, 128), half(ng, sz.experts, 128),
            half(sz.experts, width), full(8, block), full(block, 128), half(sz.slots, block), half(block, sz.slots),
            half(block, width), half(block, width), *[slot_buffer] * 6,
            half(own, width, hidden), half(own, hidden, width), half(own, many, hidden), half(own, many, hidden),
            full(own, many, hidden), half(own, width, hidden), half(own, hidden, width),
            full(sz.experts, 128), full(ng, sz.experts, 128), full(sz.experts, block), full(8, many),
            full(ng, 8, many), full(sz.experts, 128),
            half(3, pad, width), half(HEADS, pad, pad), half(pad, width), full(pad, width), full(8, 128),
            full(block, width), full(pad, width), line_buffer, line_buffer, full(pad, width), line_buffer, line_buffer,
            half(pad, width), half(3, pad, width), half(nh - 1, 4, width, cp), half(nh - 1, 4, width, cp),
            full(4, width, cp), half(4, width, cp), half(nd - 1, 4, band, cp), half(4, band, cp),
            half(nz - 1, 4, rp, cp),
            full(8, width), full(2, 8, width), full(nh - 1, 8, width), full(nd - 1, 8, width), full(nz - 1, 8, width),
            full(sz.experts, width), full(nh - 1, sz.experts, width), full(nd - 1, sz.experts, band),
            full(nz, sz.experts, band),
            *pair(nz - 1), *pair(nd - 1), *pair(nd * (nh - 1)), *pair(ng - 1), *pair(parts, nz - 1),
            *pair(parts, nz - 1), *pair(parts, ng), *pair(parts, ng), *pair(ng - 1), *pair(own, ng), *pair(parts, ng),
            *pair(parts, ng), *pair(ng - 1), *pair(parts, nz - 1), *pair(parts, nz - 1), *pair(4 * (nh - 1)),
            *pair(2 * (nd - 1)), *pair(3 * (nz - 1)), *pair(2 * (nh - 1)), *pair(2 * (nd - 1)),
            *pair(1), pltpu.SemaphoreType.DMA((4,)),
        ],
        compiler_params=pltpu.CompilerParams(collective_id=0, has_side_effects=True, vmem_limit_bytes=62 * 2**20),
        name="block",
    )(
        inputs, cotangent, routes.T, gain_attn[None, :], gain_expert[None, :], w_qkv, w_out_attn.T, w_router.T,
        w_in, w_out,
    )

    rr = sz.router_rows

    def same(*dims):
        return pl.BlockSpec(dims, lambda e: (0,) * len(dims))

    first_spec = pl.BlockSpec((1, width, hidden), lambda e: (e, 0, 0))
    second_spec = pl.BlockSpec((1, hidden, width), lambda e: (e, 0, 0))
    results = (
        shape(inputs.shape, BF16), shape(inputs.shape, BF16), shape((1, width), F32), shape((1, width), F32),
        shape((3, rp, cp), F32), shape((rp, cp), F32), shape((sz.experts, rr), F32), shape(w_in.shape, F32),
        shape(w_out.shape, F32), shape((2, rp, cp), BF16),
    )
    output, grad_input, gain_one, gain_two, grad_qkv, grad_out, grad_router, grad_first, grad_second, clipped = (
        pl.pallas_call(
            functools.partial(finish_kernel, sz),
            grid=(own,),
            out_shape=results,
            in_specs=[same(*p.shape) for p in packed[:5]]
            + [first_spec, second_spec, same(1, HEADS), same(*w_qkv.shape)],
            out_specs=[
                {7: first_spec, 8: second_spec}.get(i, same(*r.shape)) for i, r in enumerate(results)
            ],
            name="finish",
        )(*packed, tau[None, :], w_qkv)
    )
    return (
        output, grad_input, gain_one[0], gain_two[0], grad_qkv, grad_out.T, grad_router.T, grad_first, grad_second,
        clipped,
    )


def gelu_tanh(inputs):
    return (
        0.5
        * inputs
        * (1.0 + jnp.tanh(0.7978845608028654 * (inputs + 0.044715 * inputs * inputs * inputs)))
    )


def unit_and_factor(inputs):
    centered = inputs - jnp.mean(inputs, -1, keepdims=True)
    factor = lax.rsqrt(jnp.mean(centered * centered, -1, keepdims=True) + 1e-06)
    return (centered * factor, factor)


def general_norm_back(grad_norm, unit_rows, factor, gain):
    grad, gain_row = norm_back(grad_norm, unit_rows, factor, gain)
    return grad, gain_row[0]


def attn_forward(block_parts):
    queries, key_rows, value_rows = block_parts
    scores = jnp.einsum(
        "bhqd,bhkd->bhqk", queries, key_rows, preferred_element_type=jnp.float32
    ) * HEAD_DIM ** (-0.5)
    row_peak = jnp.max(scores, -1, keepdims=True)
    exponent = jnp.exp(scores - row_peak)
    summed = jnp.sum(exponent, -1, keepdims=True)
    soft_weights = (exponent / summed).astype(jnp.bfloat16)
    mixed = jnp.einsum(
        "bhqk,bhkd->bhqd", soft_weights, value_rows, preferred_element_type=jnp.float32
    ).astype(jnp.bfloat16)
    return (mixed, (row_peak + jnp.log(summed))[..., 0], jnp.max(row_peak, axis=(0, 2, 3)))


def attn_backward(block_parts):
    queries, key_rows, value_rows, grad_mixed, log_total = block_parts
    score_scale = HEAD_DIM ** (-0.5)
    scores = (
        jnp.einsum("bhqd,bhkd->bhqk", queries, key_rows, preferred_element_type=jnp.float32)
        * score_scale
    )
    soft_weights = jnp.exp(scores - log_total[..., None])
    grad_soft = jnp.einsum(
        "bhqd,bhkd->bhqk", grad_mixed, value_rows, preferred_element_type=jnp.float32
    )
    inner_sum = jnp.sum(soft_weights * grad_soft, -1, keepdims=True)
    grad_scores = (soft_weights * (grad_soft - inner_sum)).astype(jnp.bfloat16)
    grad_query = (
        jnp.einsum("bhqk,bhkd->bhqd", grad_scores, key_rows, preferred_element_type=jnp.float32)
        * score_scale
    ).astype(jnp.bfloat16)
    grad_key = (
        jnp.einsum("bhqk,bhqd->bhkd", grad_scores, queries, preferred_element_type=jnp.float32)
        * score_scale
    ).astype(jnp.bfloat16)
    grad_value = jnp.einsum(
        "bhqk,bhqd->bhkd",
        soft_weights.astype(jnp.bfloat16),
        grad_mixed,
        preferred_element_type=jnp.float32,
    ).astype(jnp.bfloat16)
    return (grad_query, grad_key, grad_value)


def general_body(
    inputs, cotangent, routes, gain_attn, gain_expert, tau, w_qkv, w_out_attn, w_router, w_in, w_out
):
    row_count, width = inputs.shape
    n_dp = lax.axis_size("dp")
    n_heads = lax.axis_size("heads")
    n_tensor = lax.axis_size("tensor")
    row_piece = w_qkv.shape[1]
    col_piece = w_qkv.shape[2]
    own_heads = col_piece // HEAD_DIM
    head_start = lax.axis_index("heads") * col_piece
    x_float = inputs.astype(jnp.float32)
    unit_one, factor_one = unit_and_factor(x_float)
    normed_one = (unit_one * gain_attn).astype(jnp.bfloat16)
    stack_qkv, stack_out = (
        lax.all_gather(w_qkv[None], ("dp", "heads", "tensor"), axis=0, tiled=True),
        lax.all_gather(w_out_attn[None], ("dp", "heads", "tensor"), axis=0, tiled=True),
    )
    full_qkv = (
        stack_qkv.reshape(n_dp, n_heads, n_tensor, 3, row_piece, col_piece)
        .transpose(3, 0, 2, 4, 1, 5)
        .reshape(3, width, width)
    )
    full_out = (
        stack_out.reshape(n_dp, n_heads, n_tensor, col_piece, row_piece)
        .transpose(1, 3, 0, 2, 4)
        .reshape(width, width)
    )
    proj_w = lax.dynamic_slice_in_dim(full_qkv, head_start, col_piece, 2)
    attn_w = lax.dynamic_slice_in_dim(full_out, head_start, col_piece, 0)
    normed_all = lax.all_gather(normed_one, "heads", axis=0, tiled=True)
    head_cols = attn_w.shape[0]
    local_heads = head_cols // HEAD_DIM
    joined_w = jnp.concatenate([proj_w[0], proj_w[1], proj_w[2]], 1)
    projected = jnp.dot(normed_all, joined_w, preferred_element_type=jnp.float32).astype(
        jnp.bfloat16
    )
    images = normed_all.shape[0] // SEQ
    per_block = 4 if images % 4 == 0 else 3 if images % 3 == 0 else 2 if images % 2 == 0 else 1
    block_shape = (images // per_block, per_block, SEQ, local_heads, HEAD_DIM)

    def to_blocks(row_matrix):
        return row_matrix.reshape(block_shape).transpose(0, 1, 3, 2, 4)

    def from_blocks(block_array):
        return block_array.transpose(0, 1, 3, 2, 4).reshape(-1, head_cols)

    queries = to_blocks(projected[:, :head_cols])
    key_rows = to_blocks(projected[:, head_cols : 2 * head_cols])
    value_rows = to_blocks(projected[:, 2 * head_cols :])
    mixed, log_total, head_peaks = lax.map(attn_forward, (queries, key_rows, value_rows))
    mixed_rows = from_blocks(mixed)
    block_peak = jnp.max(head_peaks, 0)
    attn_out = lax.psum_scatter(
        jnp.dot(mixed_rows, attn_w, preferred_element_type=jnp.float32),
        "heads",
        scatter_dimension=0,
        tiled=True,
    )
    peak_full = lax.dynamic_update_slice_in_dim(
        jnp.full((HEADS,), -1e30, jnp.float32), block_peak, lax.axis_index("heads") * local_heads, 0
    )
    hidden = x_float + attn_out
    peak_all = lax.pmax(peak_full, ("dp", "heads", "tensor"))
    peak_logit = lax.dynamic_slice_in_dim(
        peak_all, lax.axis_index("heads") * own_heads, own_heads, 0
    )
    unit_two, factor_two = unit_and_factor(hidden)
    normed_two = (unit_two * gain_expert).astype(jnp.bfloat16)
    group_rows, group_cot = (
        lax.all_gather(normed_two, "tensor", axis=0, tiled=True),
        lax.all_gather(cotangent, "tensor", axis=0, tiled=True),
    )
    first_w, second_w, router_w = (
        lax.all_gather(w_in, ("dp", "heads"), axis=0, tiled=True),
        lax.all_gather(w_out, ("dp", "heads"), axis=0, tiled=True),
        lax.all_gather(w_router, ("dp", "heads"), axis=0, tiled=True),
    )
    logits = jnp.dot(group_rows, router_w, preferred_element_type=jnp.float32)
    chosen = jnp.take_along_axis(logits, routes, 1)
    exponent = jnp.exp(chosen - jnp.max(chosen, -1, keepdims=True))
    gate_values = exponent / jnp.sum(exponent, -1, keepdims=True)
    group_count = routes.shape[0]
    experts = router_w.shape[1]
    capacity = (group_count * 5 // (16 * experts) + 1) * 8
    flat_ids = routes.reshape(-1)
    ordering = jnp.argsort(flat_ids, stable=True)
    sorted_ids = flat_ids[ordering]
    counts = jnp.sum(
        (flat_ids[:, None] == jnp.arange(experts, dtype=jnp.int32)[None, :]).astype(jnp.int32), 0
    )
    expert_ids = jnp.arange(experts, dtype=jnp.int32)
    starts = jnp.sum(jnp.where(expert_ids[None, :] < expert_ids[:, None], counts[None, :], 0), 1)
    slot_rank = jnp.arange(2 * group_count, dtype=jnp.int32) - starts[sorted_ids]
    slot_table = (
        jnp.full((experts * capacity,), 2 * group_count, jnp.int32)
        .at[sorted_ids * capacity + slot_rank]
        .set(ordering)
    )
    slot_token = slot_table // 2
    padded_rows = jnp.concatenate([group_rows, jnp.zeros((1, width), jnp.bfloat16)], 0)
    slot_in = padded_rows[slot_token].reshape(experts, capacity, width)
    slot_gate = jnp.concatenate([gate_values.reshape(-1), jnp.zeros((1,), jnp.float32)], 0)[
        slot_table
    ]
    pre_gelu = jnp.einsum("ecd,edf->ecf", slot_in, first_w, preferred_element_type=jnp.float32)
    activated = gelu_tanh(pre_gelu).astype(jnp.bfloat16)
    slot_out = jnp.einsum(
        "ecf,efd->ecd", activated, second_w, preferred_element_type=jnp.float32
    ).reshape(-1, width)
    partial_value = (
        jnp.zeros((group_count + 1, width), jnp.float32)
        .at[slot_token]
        .add(slot_gate[:, None] * slot_out)[:group_count]
    )
    expert_mix = lax.psum_scatter(
        partial_value.astype(jnp.bfloat16), "tensor", scatter_dimension=0, tiled=True
    ).astype(jnp.float32)
    output = (hidden + expert_mix).astype(jnp.bfloat16)
    padded_cot = jnp.concatenate([group_cot, jnp.zeros((1, width), jnp.bfloat16)], 0)
    slot_cot = padded_cot[slot_token].astype(jnp.float32)
    grad_slot_out = (
        (slot_gate[:, None] * slot_cot).astype(jnp.bfloat16).reshape(experts, capacity, width)
    )
    gate_part = (
        jnp.zeros((2 * group_count + 1,), jnp.float32)
        .at[slot_table]
        .add(jnp.sum(slot_cot * slot_out, -1))[: 2 * group_count]
        .reshape(group_count, 2)
    )
    grad_act = jnp.einsum(
        "ecd,efd->ecf", grad_slot_out, second_w, preferred_element_type=jnp.float32
    )
    grad_pre = jax.vjp(gelu_tanh, pre_gelu)[1](grad_act)[0].astype(jnp.bfloat16)
    grad_first = jnp.einsum("ecd,ecf->edf", slot_in, grad_pre, preferred_element_type=jnp.float32)
    grad_second = jnp.einsum(
        "ecf,ecd->efd", activated, grad_slot_out, preferred_element_type=jnp.float32
    )
    grad_slots = jnp.einsum(
        "ecf,edf->ecd", grad_pre, first_w, preferred_element_type=jnp.float32
    ).reshape(-1, width)
    grad_part = (
        jnp.zeros((group_count + 1, width), jnp.float32)
        .at[slot_token]
        .add(grad_slots)[:group_count]
    )
    grad_normed_two, grad_gates = (
        lax.psum_scatter(
            grad_part.astype(jnp.bfloat16), "tensor", scatter_dimension=0, tiled=True
        ).astype(jnp.float32),
        lax.psum_scatter(
            gate_part.astype(jnp.bfloat16), "tensor", scatter_dimension=0, tiled=True
        ).astype(jnp.float32),
    )
    shard_first, shard_second = (
        lax.psum_scatter(
            grad_first.astype(jnp.bfloat16), ("dp", "heads"), scatter_dimension=0, tiled=True
        ).astype(jnp.float32),
        lax.psum_scatter(
            grad_second.astype(jnp.bfloat16), ("dp", "heads"), scatter_dimension=0, tiled=True
        ).astype(jnp.float32),
    )
    offset = lax.axis_index("tensor") * row_count
    local_gates = lax.dynamic_slice_in_dim(gate_values, offset, row_count, 0)
    local_routes = lax.dynamic_slice_in_dim(routes, offset, row_count, 0)
    grad_chosen = local_gates * (grad_gates - jnp.sum(local_gates * grad_gates, -1, keepdims=True))
    columns = jnp.arange(experts, dtype=jnp.int32)[None, :]
    grad_logits = (
        jnp.where(local_routes[:, 0:1] == columns, grad_chosen[:, 0:1], 0.0)
        + jnp.where(local_routes[:, 1:2] == columns, grad_chosen[:, 1:2], 0.0)
    ).astype(jnp.bfloat16)
    grad_normed_two = grad_normed_two + jnp.einsum(
        "re,de->rd", grad_logits, router_w, preferred_element_type=jnp.float32
    )
    router_term = jnp.einsum(
        "rd,re->de", normed_two, grad_logits, preferred_element_type=jnp.float32
    )
    grad_hidden_norm, gain_two_term = general_norm_back(grad_normed_two, unit_two, factor_two, gain_expert)
    grad_hidden = cotangent.astype(jnp.float32) + grad_hidden_norm
    grad_attn = lax.all_gather(grad_hidden.astype(jnp.bfloat16), "heads", axis=0, tiled=True)
    grad_mixed = jnp.einsum(
        "rd,cd->rc", grad_attn, attn_w, preferred_element_type=jnp.float32
    ).astype(jnp.bfloat16)
    out_term = jnp.einsum("rc,rd->cd", mixed_rows, grad_attn, preferred_element_type=jnp.float32)
    grad_query, grad_key, grad_value = lax.map(
        attn_backward, (queries, key_rows, value_rows, to_blocks(grad_mixed), log_total)
    )
    grad_proj = jnp.concatenate(
        [from_blocks(grad_query), from_blocks(grad_key), from_blocks(grad_value)], 1
    )
    grad_normed_one = lax.psum_scatter(
        jnp.einsum("rc,dc->rd", grad_proj, joined_w, preferred_element_type=jnp.float32).astype(
            jnp.bfloat16
        ),
        "heads",
        scatter_dimension=0,
        tiled=True,
    ).astype(jnp.float32)
    proj_term = jnp.einsum("rd,rc->dc", normed_all, grad_proj, preferred_element_type=jnp.float32)
    proj_stack = jnp.stack(
        [
            proj_term[:, :head_cols],
            proj_term[:, head_cols : 2 * head_cols],
            proj_term[:, 2 * head_cols :],
        ],
        0,
    )
    whole_proj = lax.dynamic_update_slice_in_dim(
        jnp.zeros((3, width, width), jnp.float32), proj_stack, head_start, 2
    )
    whole_out = lax.dynamic_update_slice_in_dim(
        jnp.zeros((width, width), jnp.float32), out_term, head_start, 0
    )
    send_qkv = (
        whole_proj.reshape(3, n_dp, n_tensor, row_piece, n_heads, col_piece)
        .transpose(1, 4, 2, 0, 3, 5)
        .reshape(-1, 3, row_piece, col_piece)
    )
    send_out = (
        whole_out.reshape(n_heads, col_piece, n_dp, n_tensor, row_piece)
        .transpose(2, 0, 3, 1, 4)
        .reshape(-1, col_piece, row_piece)
    )
    shard_proj, shard_attn = (
        lax.psum_scatter(send_qkv, ("dp", "heads", "tensor"), scatter_dimension=0, tiled=True),
        lax.psum_scatter(send_out, ("dp", "heads", "tensor"), scatter_dimension=0, tiled=True),
    )
    grad_input_norm, gain_one_term = general_norm_back(grad_normed_one, unit_one, factor_one, gain_attn)
    grad_input = (grad_hidden + grad_input_norm).astype(jnp.bfloat16)
    gain_one_grad, gain_two_grad, router_all = lax.psum(
        (gain_one_term, gain_two_term, router_term), ("dp", "heads", "tensor")
    )
    router_grad = lax.dynamic_slice_in_dim(
        router_all, lax.axis_index(("dp", "heads")) * w_router.shape[0], w_router.shape[0], 0
    )
    local_tau = lax.dynamic_slice_in_dim(tau, lax.axis_index("heads") * own_heads, own_heads, 0)
    clip_factor = jnp.sqrt(local_tau / jnp.maximum(peak_logit, local_tau))
    clipped = (w_qkv[:2].astype(jnp.float32) * jnp.repeat(clip_factor, HEAD_DIM)).astype(
        jnp.bfloat16
    )
    return (
        output,
        grad_input,
        gain_one_grad,
        gain_two_grad,
        shard_proj[0],
        shard_attn[0],
        router_grad,
        shard_first,
        shard_second,
        clipped,
    )


def body(*args):
    inputs, _, routes, _, _, _, w_qkv, _, w_router, w_in, _ = args
    sz = Sizes(
        lax.axis_size("dp"), lax.axis_size("heads"), lax.axis_size("tensor"), inputs, routes, w_qkv, w_router, w_in
    )
    if sz.fits():
        return fast_body(sz, *args)
    return general_body(*args)


def solution(mesh):
    return jax.shard_map(
        body,
        mesh=mesh,
        in_specs=(
            P(("dp", "heads", "tensor"), None),
            P(("dp", "heads", "tensor"), None),
            P(("dp", "heads"), None),
            P(),
            P(),
            P(),
            P(None, ("dp", "tensor"), "heads"),
            P("heads", ("dp", "tensor")),
            P(("dp", "heads"), None),
            P(("dp", "heads"), None, "tensor"),
            P(("dp", "heads"), "tensor", None),
        ),
        out_specs=(
            P(("dp", "heads", "tensor"), None),
            P(("dp", "heads", "tensor"), None),
            P(),
            P(),
            P(None, ("dp", "tensor"), "heads"),
            P("heads", ("dp", "tensor")),
            P(("dp", "heads"), None),
            P(("dp", "heads"), None, "tensor"),
            P(("dp", "heads"), "tensor", None),
            P(None, ("dp", "tensor"), "heads"),
        ),
        check_vma=False,
    )
```

```python
import functools
import jax
import jax.numpy as jnp
from jax import lax
from jax.experimental import pallas as pl
from jax.experimental.pallas import tpu as pltpu
from jax.sharding import PartitionSpec as P

HEADS = 8
HEAD_DIM = 64
SEQ = 197
F32 = jnp.float32
BF16 = jnp.bfloat16
MESH = pl.DeviceIdType.MESH
NEG = -1e30


class Sizes:
    def __init__(self, n_dp, n_heads, n_tensor, inputs, routes, w_qkv, w_router, w_in):
        self.nd, self.nh, self.nt = n_dp, n_heads, n_tensor
        self.groups = n_dp * n_heads
        self.rows, self.width = inputs.shape
        self.pad = -(-self.rows // 16) * 16
        self.block = self.pad * n_tensor
        self.block_rows = routes.shape[0]
        self.own = w_in.shape[0]
        self.hidden = w_in.shape[2]
        self.experts = self.own * self.groups
        self.cap = (self.block_rows * 5 // (16 * self.experts) + 1) * 8
        self.group_slots = self.own * self.cap
        self.slots = self.experts * self.cap
        self.row_piece, self.col_piece = w_qkv.shape[1], w_qkv.shape[2]
        self.band = self.row_piece * n_tensor
        self.router_rows = w_router.shape[0]
        self.parts = 4

    def fits(self):
        return (
            self.rows == SEQ
            and self.block_rows == self.rows * self.nt
            and self.cap == 64
            and self.experts == 32
            and self.group_slots % 128 == 0
            and self.col_piece % 128 == 0
            and self.row_piece % 16 == 0
            and self.router_rows % 16 == 0
            and self.own * self.groups * 4 == 128
            and self.width == HEADS * HEAD_DIM
            and self.block * self.width * 2 <= 2**20
            and self.own * self.width <= self.slots
            and self.hidden <= self.block
            and self.hidden == self.width
            and self.cap % (16 * self.nt) == 0
            and self.width // self.parts % 128 == 0
        )


def nn(a, b):
    return jnp.dot(a, b, preferred_element_type=F32)


def nt(a, b):
    return lax.dot_general(a, b, (((1,), (1,)), ((), ())), preferred_element_type=F32)


def tn(a, b):
    return lax.dot_general(a, b, (((0,), (0,)), ((), ())), preferred_element_type=F32)


def iota(shape, axis):
    return lax.broadcasted_iota(jnp.int32, shape, axis)


def normalize(rows):
    centered = rows - jnp.mean(rows, -1, keepdims=True)
    factor = lax.rsqrt(jnp.mean(centered * centered, -1, keepdims=True) + 1e-06)
    return centered * factor, factor


def norm_back(grad_norm, unit_rows, factor, gain):
    grad_hat = grad_norm * gain
    inner = (
        grad_hat
        - jnp.mean(grad_hat, -1, keepdims=True)
        - unit_rows * jnp.mean(grad_hat * unit_rows, -1, keepdims=True)
    )
    return factor * inner, jnp.sum(grad_norm * unit_rows, 0, keepdims=True)


def split_high_low(values):
    high = values.astype(BF16)
    low = (values - high.astype(F32)).astype(BF16)
    return jnp.concatenate([high, low], 0)


class Place:
    def __init__(self, sz):
        self.sz = sz
        self.d = lax.axis_index("dp")
        self.h = lax.axis_index("heads")
        self.z = lax.axis_index("tensor")
        self.group = self.d * sz.nh + self.h

    def plane(self, group):
        return (group // self.sz.nh, group % self.sz.nh, self.z)

    def line(self, z):
        return (self.d, self.h, z)

    def next_group(self, k):
        return (self.group + k) % self.sz.groups

    def next_z(self, j):
        return (self.z + j) % self.sz.nt

    def enter(self):
        sz = self.sz
        barrier = pltpu.get_barrier_semaphore()
        for k in range(1, sz.groups):
            pl.semaphore_signal(barrier, inc=1, device_id=self.plane(self.next_group(k)), device_id_type=MESH)
        for j in range(1, sz.nt):
            pl.semaphore_signal(barrier, inc=1, device_id=self.line(self.next_z(j)), device_id_type=MESH)
        pl.semaphore_wait(barrier, sz.groups + sz.nt - 2)


def remote(src, dst, send, recv, device):
    return pltpu.make_async_remote_copy(
        src_ref=src, dst_ref=dst, send_sem=send, recv_sem=recv, device_id=device, device_id_type=MESH
    )


def route_table(sz, routes_ref, table):
    table[...] = jnp.full_like(table, -1.0)
    for z in range(sz.nt):
        table[0:2, z * sz.pad : z * sz.pad + sz.rows] = routes_ref[:, z * sz.rows : (z + 1) * sz.rows].astype(F32)


def block_kernel(
    sz, x_ref, cot_ref, routes_ref, gain_one_ref, gain_two_ref, w_qkv_ref, w_out_ref, w_router_ref, tau_ref, first_hbm,
    second_hbm, output_out, grad_input_out, gain_one_out, gain_two_out, qkv_out, out_out, router_out, clipped_out,
    grad_first_out, grad_second_out,
    w_own, w_full, router_own, router_full, router_t, route_rows, route_columns, select, select_t, select_qt,
    cot_block, rows_block, send_a, send_b, cot_slots, slots, grad_slots, values,
    grads_q, grads_line, grads_sum, grads_back, first, second, act, grad_pre, grad_act, grad_second,
    gate_send, gate_recv, gates_at, dgate_send, dgate_recv, dgate_rows,
    qkv, probs, mixed, hidden_at, peak_at, part, part_own, part_send, part_recv, mix_own, mix_send, mix_recv,
    grad_mixed, grad_qkv, core_send, core_recv, w_half, band_send, band_recv, line_send, line_recv,
    small, small_send, small_core, small_x, small_z, rt, rt_core, rt_x, rt_z,
    wz_s, wz_r, wx_s, wx_r, wc_s, wc_r, r_s, r_r, qz_s, qz_r, nz_s, nz_r, qa_s, qa_r, na_s, na_r, ga_s, ga_r,
    d0_s, d0_r, da_s, da_r, va_s, va_r, dg_s, dg_r, pz_s, pz_r, mz_s, mz_r, gc_s, gc_r, gx_s, gx_r, gl_s, gl_r,
    sc_s, sc_r, sx_s, sx_r, dl_s, dl_r, dq_s, dq_r, local_sem,
):
    at = Place(sz)
    d, h, z, me = at.d, at.h, at.z, at.group
    nd, nh, nz, ng = sz.nd, sz.nh, sz.nt, sz.groups
    band, rp, cp, pad, width = sz.band, sz.row_piece, sz.col_piece, sz.pad, sz.width
    many = ng * sz.cap
    parts, part_width = sz.parts, width // sz.parts

    def lanes(c):
        return pl.ds(c * part_width, part_width)

    def rows_at(n, size):
        return pl.ds(pl.multiple_of(n * size, size), size)

    own_block, own_columns = rows_at(z, pad), rows_at(h, cp)

    w_own[0:3] = w_qkv_ref[...]
    w_own[3] = w_out_ref[...]
    router_own[...] = jnp.zeros_like(router_own)
    router_own[:, 0 : sz.router_rows] = w_router_ref[...]
    cot_block[own_block] = jnp.concatenate(
        [cot_ref[...].astype(F32), jnp.zeros((pad - sz.rows, width), F32)], 0
    ).astype(BF16)

    at.enter()

    w_rows = rows_at(d * nz + z, rp)
    w_z = [
        remote(w_own, w_full.at[:, w_rows, own_columns], wz_s.at[j - 1], wz_r.at[j - 1], at.line(at.next_z(j)))
        for j in range(1, nz)
    ]
    for copy in w_z:
        copy.start()
    loads = [
        pltpu.make_async_copy(first_hbm, first, local_sem.at[0]),
        pltpu.make_async_copy(second_hbm, second, local_sem.at[1]),
    ]
    for copy in loads:
        copy.start()
    routers = [
        remote(router_own, router_full.at[me], r_s.at[k - 1], r_r.at[k - 1], at.plane(at.next_group(k)))
        for k in range(1, ng)
    ]
    for copy in routers:
        copy.start()
    w_full[:, w_rows, own_columns] = w_own[...]
    router_full[me] = router_own[...]

    zeros = jnp.zeros((pad - sz.rows, width), F32)
    x_rows = jnp.concatenate([x_ref[...].astype(F32), zeros], 0)
    unit_one, _ = normalize(x_rows)
    normed_one = (unit_one * gain_one_ref[...]).astype(BF16)

    for copy in w_z:
        copy.wait()

    def to_core(i, dp, other):
        place = w_full.at[:, rows_at(dp, band), own_columns]
        return remote(place, place, wc_s.at[i], wc_r.at[i], (d, (h + other) % nh, z))

    w_band = w_full.at[:, rows_at(d, band), own_columns]
    w_x = [
        remote(w_band, w_band, wx_s.at[k - 1], wx_r.at[k - 1], ((d + k) % nd, h, z)) for k in range(1, nd)
    ]
    for copy in w_x:
        copy.start()
    w_c = [to_core((other - 1) * nd, d, other) for other in range(1, nh)]
    for copy in w_c:
        copy.start()

    def along(block, send_sems, recv_sems, c):
        place = block.at[own_block, lanes(c)]
        return [
            remote(place, place, send_sems.at[c, j - 1], recv_sems.at[c, j - 1], at.line(at.next_z(j)))
            for j in range(1, nz)
        ]

    for c in range(parts):
        for copy in along(cot_block, qz_s, qz_r, c):
            copy.start()

    route_table(sz, routes_ref, route_rows)
    route_a, route_b = route_rows[0:1, :], route_rows[1:2, :]
    expert = iota((sz.experts, sz.block), 0).astype(F32)
    named_a, named_b = route_a == expert, route_b == expert
    named = jnp.logical_or(named_a, named_b)
    before = (iota((sz.block, sz.block), 0) < iota((sz.block, sz.block), 1)).astype(BF16)
    rank = nn(named.astype(BF16), before) + expert * float(sz.cap)
    slot_a = jnp.sum(jnp.where(named_a, rank, 0.0), 0, keepdims=True)
    slot_b = jnp.sum(jnp.where(named_b, rank, 0.0), 0, keepdims=True)
    slot_a = jnp.where(route_a < 0.0, -1.0, slot_a)
    slot_b = jnp.where(route_b < 0.0, -1.0, slot_b)
    slot_pair = jnp.concatenate([slot_a, slot_b] * 64, 0)
    route_columns[...] = slot_pair.T

    def fill(g, carry):
        slot = iota((sz.group_slots, sz.block), 0).astype(F32) + (g * sz.group_slots).astype(F32)
        hit = jnp.logical_or(slot == slot_a, slot == slot_b)
        select[rows_at(g, sz.group_slots), :] = jnp.where(hit, 1.0, 0.0).astype(BF16)
        return carry

    lax.fori_loop(0, ng, fill, 0)

    quarter = sz.cap // nz
    few = ng * sz.own * quarter

    def quarter_slot(dims, axis):
        n = iota(dims, axis)
        return (n // quarter * sz.cap + z * quarter + n % quarter).astype(F32)

    def quarter_move(k, send, landing, send_sems, recv_sems):
        g = (me + k) % ng
        return remote(send.at[g], landing.at[me], send_sems.at[k - 1], recv_sems.at[k - 1], at.plane(g))

    def dispatch(c, block, send, out):
        def step(g, carry):
            send[g, :, lanes(c)] = nn(select[rows_at(g, sz.group_slots), :], block[:, lanes(c)]).astype(BF16)
            return carry

        lax.fori_loop(0, ng, step, 0)
        out[me, :, lanes(c)] = send[me, :, lanes(c)]

    def exchange(c, k, send, out, send_sems, recv_sems):
        g = (me + k) % ng
        return remote(
            send.at[g, :, lanes(c)], out.at[me, :, lanes(c)], send_sems.at[c, k], recv_sems.at[c, k], at.plane(g)
        )

    def start_part(c, *flow):
        def step(i, carry):
            exchange(c, ng - 1 - i, *flow).start()
            return carry

        lax.fori_loop(0, ng - 1, step, 0)

    def wait_part(c, *flow):
        def step(i, carry):
            exchange(c, i + 1, *flow).wait()
            return carry

        lax.fori_loop(0, ng - 1, step, 0)

    cot_flow = (send_a, cot_slots, qa_s, qa_r)
    row_flow = (send_b, slots, na_s, na_r)

    def send_cot(c):
        for copy in along(cot_block, qz_s, qz_r, c):
            copy.wait()
        dispatch(c, cot_block, send_a, cot_slots)

    send_cot(0)
    for k in range(1, nd):
        w_x[k - 1].wait_recv()
        for other in range(1, nh):
            copy = to_core((other - 1) * nd + k, (d - k + nd) % nd, other)
            copy.start()
            w_c.append(copy)
    start_part(0, *cot_flow)
    for copy in w_c:
        copy.wait()
    for copy in w_x:
        copy.wait_send()

    for i in range(3):
        qkv[i] = nn(normed_one, w_full[i]).astype(BF16)
    lane = iota((1, 2 * HEAD_DIM), 1)
    halves = (lane < HEAD_DIM, lane >= HEAD_DIM)
    key_valid = iota((1, pad), 1) < sz.rows
    row_valid = iota((pad, 1), 0) < sz.rows
    peak_lane = iota((1, 128), 1)
    peak_at[...] = jnp.full_like(peak_at, NEG)
    scale = HEAD_DIM ** (-0.5)

    def attend(pair, carry):
        columns = rows_at(pair, 2 * HEAD_DIM)
        q_pair, k_pair, v_pair = (qkv[i, :, columns] for i in range(3))
        sides = []
        for side in range(2):
            q_own = jnp.where(halves[side], q_pair, jnp.zeros_like(q_pair))
            scores = jnp.where(key_valid, nt(q_own, k_pair) * scale, NEG)
            row_peak = jnp.max(scores, -1, keepdims=True)
            exponent = jnp.exp(scores - row_peak)
            weights = (exponent / jnp.sum(exponent, -1, keepdims=True)).astype(BF16)
            head = pair * 2 + side
            probs[head] = weights
            sides.append(nn(weights, v_pair))
            peak = jnp.max(jnp.where(row_valid, row_peak, NEG), 0, keepdims=True)
            peak_at[0:1, :] = jnp.where(peak_lane == head, peak, peak_at[0:1, :])
        mixed[:, columns] = jnp.where(halves[0], sides[0], sides[1]).astype(BF16)
        return carry

    pairs = HEADS // 2
    sent = 1
    for turn in range(2):
        until = 1 + ((parts - 1) * (turn + 1)) // 2
        for c in range(sent, until):
            send_cot(c)
            start_part(c, *cot_flow)
        sent = until
        lax.fori_loop(turn * pairs // 2, (turn + 1) * pairs // 2, attend, 0)

    hidden = x_rows + nt(mixed[...], w_full[3])
    hidden_at[...] = hidden
    unit_two, _ = normalize(hidden)
    rows_block[own_block] = jnp.where(row_valid, unit_two * gain_two_ref[...], 0.0).astype(BF16)
    for c in range(parts):
        for copy in along(rows_block, nz_s, nz_r, c):
            copy.start()

    def fill_t(i, carry):
        rows = rows_at(i, pad)
        slot = iota((pad, sz.slots), 1).astype(F32)
        hit = jnp.logical_or(slot == route_columns[rows, 0:1], slot == route_columns[rows, 1:2])
        select_t[rows, :] = jnp.where(hit, 1.0, 0.0).astype(BF16)
        some = quarter_slot((pad, few), 1)
        hit = jnp.logical_or(some == route_columns[rows, 0:1], some == route_columns[rows, 1:2])
        select_qt[rows, :] = jnp.where(hit, 1.0, 0.0).astype(BF16)
        return carry

    lax.fori_loop(0, nz, fill_t, 0)
    for copy in routers:
        copy.wait()
    for g in range(ng):
        router_t[:, g * sz.router_rows : (g + 1) * sz.router_rows] = router_full[g, :, 0 : sz.router_rows]

    def expert_rows(ref, e):
        return ref[:, rows_at(e, sz.cap), :].reshape(many, width)

    def cot_grad(e, carry):
        grad_act[e] = nt(expert_rows(cot_slots, e), second[e])
        return carry

    for c in range(parts):
        for copy in along(rows_block, nz_s, nz_r, c):
            copy.wait()
        dispatch(c, rows_block, send_b, slots)
        start_part(c, *row_flow)
        if c == parts // 2 - 1:
            for i in range(parts):
                wait_part(i, *cot_flow)
            for copy in loads:
                copy.wait()
            lax.fori_loop(0, sz.own, cot_grad, 0)

    logits = jnp.where(named, nt(router_t[...], rows_block[...]), NEG)
    exponent = jnp.where(named, jnp.exp(logits - jnp.max(logits, 0, keepdims=True)), 0.0)
    total = jnp.sum(exponent, 0, keepdims=True)
    gates = exponent / jnp.where(total > 0.0, total, 1.0)
    gates_at[...] = gates
    by_slot = nt(split_high_low(gates), select[...])
    by_slot = by_slot[0 : sz.experts] + by_slot[sz.experts :]
    own_slot = iota((sz.experts, sz.slots), 1) // sz.cap == iota((sz.experts, sz.slots), 0)
    by_slot = jnp.where(own_slot, by_slot, 0.0)
    folded = by_slot[:, 0:128]
    for i in range(1, sz.slots // 128):
        folded = folded + by_slot[:, i * 128 : (i + 1) * 128]
    gate_send[...] = folded
    gate_copies = [
        remote(
            gate_send.at[rows_at(at.next_group(k) * sz.own // 8, 8)], gate_recv.at[me], ga_s.at[k - 1], ga_r.at[k - 1],
            at.plane(at.next_group(k)),
        )
        for k in range(1, ng)
    ]
    for copy in gate_copies:
        copy.start()
    gate_recv[me] = gate_send[rows_at(me * sz.own // 8, 8)]
    for copy in gate_copies:
        copy.wait()
    for c in range(parts):
        wait_part(c, *row_flow)

    def gate_of(e):
        turned = gate_recv[:, pl.ds(me * sz.own % 8 + e, 1), :].reshape(ng, 128).T
        columns = jnp.where((e % 2) == 1, turned[sz.cap : 2 * sz.cap], turned[0 : sz.cap])
        return jnp.concatenate([columns[:, s : s + 1] for s in range(ng)], 0)

    def first_piece(e, k):
        g = (me + k) % ng
        piece = (rows_at(e, sz.cap), lanes(1))
        return remote(
            send_a.at[(g, *piece)], grad_slots.at[(me, *piece)], d0_s.at[e, k], d0_r.at[e, k], at.plane(g)
        )

    def grads_piece(e, j):
        piece = (slice(None), rows_at(e, quarter), slice(None))
        return remote(
            grads_q.at[(at.next_z(j), *piece)], grads_line.at[(j - 1, *piece)], dl_s.at[e, j - 1], dl_r.at[e, j - 1],
            at.line(at.next_z(j)),
        )

    def expert_back(e, carry):
        gate = gate_of(e)
        half_rows = many // 2
        for part_at in range(2):
            some = slice(part_at * half_rows, (part_at + 1) * half_rows)
            groups = slice(part_at * ng // 2, (part_at + 1) * ng // 2)
            pre = nn(slots[groups, rows_at(e, sz.cap), :].reshape(half_rows, width), first[e])
            const, cubic = 0.7978845608028654, 0.044715
            square = pre * pre
            bent = jnp.tanh(const * pre * (1.0 + cubic * square))
            half = 0.5 * (1.0 + bent)
            hidden_units = (pre * half).astype(BF16)
            act[e, some] = hidden_units
            slope = half + 0.5 * pre * (1.0 - bent * bent) * const * (1.0 + 3.0 * cubic * square)
            through = grad_act[e, some]
            dgate = nt(jnp.ones((8, sz.hidden), BF16), (hidden_units.astype(F32) * through).astype(BF16))
            dgate_send[:, some] = jnp.where(iota((8, half_rows), 0) == e, dgate, dgate_send[:, some])
            grads = (through * gate[some] * slope).astype(BF16)
            grad_pre[e, some] = grads
            spread = nt(grads, first[e]).astype(BF16).reshape(ng // 2, sz.cap, width)
            send_a[groups, rows_at(e, sz.cap), :] = spread
            for i in range(nz):
                grads_q[i, groups, rows_at(e, quarter), :] = spread[:, i * quarter : (i + 1) * quarter, 0:part_width]

        def step(i, carry):
            first_piece(e, ng - 1 - i).start()
            return carry

        lax.fori_loop(0, ng - 1, step, 0)
        for j in range(1, nz):
            grads_piece(e, j).start()
        return carry

    dgate_send[...] = jnp.zeros_like(dgate_send)
    lax.fori_loop(0, sz.own, expert_back, 0)
    dgates = [
        remote(
            dgate_send.at[:, rows_at(at.next_group(k) * sz.cap // 128, 128)], dgate_recv.at[me], dg_s.at[k - 1],
            dg_r.at[k - 1], at.plane(at.next_group(k)),
        )
        for k in range(1, ng)
    ]
    for copy in dgates:
        copy.start()
    dgate_recv[me] = dgate_send[:, rows_at(me * sz.cap // 128, 128)]
    grad_flow = (send_a, grad_slots, da_s, da_r)
    value_flow = (send_b, values, va_s, va_r)
    for c in range(2, parts):
        start_part(c, *grad_flow)
    grad_slots[me] = send_a[me]

    def expert_value(e, carry):
        value = nn(act[e], second[e])
        gated = (value * gate_of(e)).astype(BF16).reshape(ng, sz.cap, width)
        send_b[:, rows_at(e, sz.cap), :] = gated
        return carry

    lax.fori_loop(0, sz.own, expert_value, 0)
    values[me] = send_b[me]

    def quarter_total(own, line, sums):
        total = own[z].astype(F32)
        for j in range(1, nz):
            total = total + line[j - 1].astype(F32)
        sums[...] = total.astype(BF16)

    def wait_pieces(e, carry):
        for j in range(1, nz):
            grads_piece(e, j).wait()
        return carry

    def weight_grads(e, carry):
        grad_value = (expert_rows(cot_slots, e).astype(F32) * gate_of(e)).astype(BF16)
        grad_second[e] = tn(act[e], grad_value).astype(BF16)
        select[rows_at(e, width), 0 : sz.hidden] = tn(expert_rows(slots, e), grad_pre[e]).astype(BF16)
        return carry

    for copy in dgates:
        copy.wait()
    mine = iota((8, 128), 1) // sz.cap == me * sz.cap % 128 // sz.cap
    for g in range(ng):
        folded = jnp.where(mine, dgate_recv[g], 0.0)
        folded = folded + pltpu.roll(folded, 64, 1)
        dgate_rows[g * sz.own : (g + 1) * sz.own, :] = folded[0 : sz.own]
    spread = jnp.concatenate([dgate_rows[...]] * (sz.slots // 128), 1)
    own_slot = iota((sz.experts, sz.slots), 1) // sz.cap == iota((sz.experts, sz.slots), 0)
    dgate = nt(split_high_low(jnp.where(own_slot, spread, 0.0)), select_t[...])
    dgate = dgate[0 : sz.experts] + dgate[sz.experts :]
    gates = gates_at[...]
    dlogits = (gates * (dgate - jnp.sum(gates * dgate, 0, keepdims=True))).astype(BF16)
    rt[...] = nn(dlogits, rows_block[...])
    part[...] = tn(dlogits, router_t[...])

    def line_copy(c, j, send, recv, send_sems, recv_sems):
        return remote(
            send.at[j - 1, :, lanes(c)], recv.at[j - 1, :, lanes(c)], send_sems.at[c, j - 1], recv_sems.at[c, j - 1],
            at.line(at.next_z(j)),
        )

    def scatter(c, source, base, own, *flow):
        if source is grads_back:
            places, flat = select_qt, source[...].reshape(few, part_width)
        else:
            places, flat = select_t, source[:, :, lanes(c)].reshape(sz.slots, part_width)
        for j in [*range(1, nz), 0]:
            tokens = rows_at(at.next_z(j), pad)
            sums = nn(places[tokens, :], flat)
            if base is not None:
                sums = sums + base[tokens, lanes(c)]
            if j == 0:
                own[:, lanes(c)] = sums
            else:
                flow[0][j - 1, :, lanes(c)] = sums.astype(BF16)
                line_copy(c, j, *flow).start()

    def gathered(own, *flow):
        for c in range(parts):
            for j in range(1, nz):
                line_copy(c, j, *flow).wait()
        sums = own[...]
        for j in range(1, nz):
            sums = sums + flow[1][j - 1].astype(F32)
        return sums

    part_flow = (part_send, part_recv, pz_s, pz_r)
    mix_flow = (mix_send, mix_recv, mz_s, mz_r)

    def wait_first(e, carry):
        def step(i, carry):
            first_piece(e, i + 1).wait()
            return carry

        return lax.fori_loop(0, ng - 1, step, carry)

    def exchange_quarters():
        lax.fori_loop(0, sz.own, wait_pieces, 0)
        quarter_total(grads_q, grads_line, grads_sum)
        for copy in grads_moves:
            copy.start()
        grads_back[me] = grads_sum[me]

    grads_moves = [quarter_move(k, grads_sum, grads_back, dq_s, dq_r) for k in range(1, ng)]
    order = [1, 2, 0, *range(3, parts)]
    done = 0
    for turn, c in enumerate(order):
        if c == 0:
            for copy in grads_moves:
                copy.wait()
        elif c == 1:
            lax.fori_loop(0, sz.own, wait_first, 0)
        else:
            wait_part(c, *grad_flow)
        if turn == parts - 1:
            for i in range(parts // 2):
                start_part(i, *value_flow)
        scatter(c, grads_back if c == 0 else grad_slots, part, part_own, *part_flow)
        if turn == 0:
            exchange_quarters()
        until = sz.own * (turn + 1) // parts
        lax.fori_loop(done, until, weight_grads, 0)
        done = until
    stores = [
        pltpu.make_async_copy(grad_second, grad_second_out, local_sem.at[2]),
        *[
            pltpu.make_async_copy(
                select.at[e * width : (e + 1) * width, 0 : sz.hidden], grad_first_out.at[e], local_sem.at[3 + e]
            )
            for e in range(sz.own)
        ],
    ]
    for copy in stores:
        copy.start()

    unit_two, factor_two = normalize(hidden_at[...])
    grad_normed = jnp.where(row_valid, gathered(part_own, *part_flow), 0.0)
    grad_hidden, gain_two = norm_back(grad_normed, unit_two, factor_two, gain_two_ref[...])
    grad_hidden = jnp.concatenate([cot_ref[...].astype(F32), zeros], 0) + jnp.where(row_valid, grad_hidden, 0.0)
    part_own[...] = grad_hidden
    grad_attn = grad_hidden.astype(BF16)

    def core_copy(i, other):
        n = 4 * (other - 1) + i
        return remote(
            core_send.at[other - 1, i], core_recv.at[other - 1, i], gc_s.at[n], gc_r.at[n], (d, (h + other) % nh, z)
        )

    def half_sum(i, sums):
        for other in range(1, nh):
            core_copy(i, other).wait()
            sums = sums + core_recv[other - 1, i].astype(F32)
        w_half[i] = sums
        band_send[i] = sums.astype(BF16)

    def band_copy(k, matrices, n):
        to = (d + k) % nd
        n = 2 * (k - 1) + n
        return remote(
            band_send.at[matrices, rows_at(to, band), :], band_recv.at[k - 1, matrices], gx_s.at[n], gx_r.at[n], (to, h, z)
        )

    for other in [*range(1, nh), 0]:
        sums = tn(grad_attn, mixed[:, rows_at((h + other) % nh, cp)])
        if other:
            core_send[other - 1, 3] = sums.astype(BF16)
            core_copy(3, other).start()
        else:
            w_half[3] = sums
    grad_mixed[...] = nn(grad_attn, w_full[3]).astype(BF16)
    half_sum(3, w_half[3])
    out_band = [band_copy(k, pl.ds(3, 1), 0) for k in range(1, nd)]
    for copy in out_band:
        copy.start()

    def attend_back(pair):
        columns = rows_at(pair, 2 * HEAD_DIM)
        q_pair, k_pair, v_pair = (qkv[i, :, columns] for i in range(3))
        g_pair = grad_mixed[:, columns]
        dq, dk, dv = [], [], []
        for side in range(2):
            weights = probs[pair * 2 + side]
            soft = weights.astype(F32)
            g_own = jnp.where(halves[side], g_pair, jnp.zeros_like(g_pair))
            grad_soft = nt(g_own, v_pair)
            inner = jnp.sum(soft * grad_soft, -1, keepdims=True)
            grad_scores = (soft * (grad_soft - inner)).astype(BF16)
            dq.append(nn(grad_scores, k_pair))
            dk.append(tn(grad_scores, q_pair))
            dv.append(tn(weights, g_pair))
        grad_qkv[0, :, columns] = (jnp.where(halves[0], dq[0], dq[1]) * scale).astype(BF16)
        grad_qkv[1, :, columns] = (jnp.where(halves[0], dk[0], dk[1]) * scale).astype(BF16)
        grad_qkv[2, :, columns] = jnp.where(halves[0], dv[0], dv[1]).astype(BF16)

    unit_one, factor_one = normalize(jnp.concatenate([x_ref[...].astype(F32), zeros], 0))
    normed_one = (unit_one * gain_one_ref[...]).astype(BF16)
    core_pairs = cp // (2 * HEAD_DIM)
    for other in [*range(1, nh), 0]:
        core = (h + other) % nh
        for q in range(core_pairs):
            attend_back(core * core_pairs + q)
        for i in range(3):
            sums = tn(normed_one, grad_qkv[i, :, rows_at(core, cp)])
            if other:
                core_send[other - 1, i] = sums.astype(BF16)
                core_copy(i, other).start()
            else:
                half_sum(i, sums)
    qkv_band = [band_copy(k, pl.ds(0, 3), 1) for k in range(1, nd)]
    for copy in qkv_band:
        copy.start()

    def send_mix(c):
        wait_part(c, *value_flow)
        scatter(c, values, None, mix_own, *mix_flow)

    send_mix(0)
    send_mix(1)

    grad_one = jnp.zeros((pad, width), F32)
    for i in range(3):
        grad_one = grad_one + nt(grad_qkv[i], w_full[i])
    grad_one = jnp.where(row_valid, grad_one, 0.0)
    grad_input, gain_one = norm_back(grad_one, unit_one, factor_one, gain_one_ref[...])
    grad_input_out[...] = (part_own[...] + grad_input)[0 : sz.rows].astype(BF16)

    small[...] = jnp.zeros_like(small)
    small[0:1, :] = gain_one
    small[1:2, :] = gain_two
    small[2:3, 0:128] = peak_at[0:1, :]
    peak_row = iota(small.shape, 0) == 2

    def join(a, b):
        return jnp.where(peak_row, jnp.maximum(a, b), a + b)

    small_copies = []
    for other in range(1, nh):
        device, n = (d, (h + other) % nh, z), 2 * (other - 1)
        small_copies += [
            remote(small, small_core.at[other - 1], sc_s.at[n], sc_r.at[n], device),
            remote(rt, rt_core.at[other - 1], sc_s.at[n + 1], sc_r.at[n + 1], device),
        ]
    for copy in small_copies:
        copy.start()
    for copy in small_copies:
        copy.wait()
    for other in range(1, nh):
        small[...] = join(small[...], small_core[other - 1])
        rt[...] = rt[...] + rt_core[other - 1]
    small_send[0] = small[...]
    small_copies = []
    for k in range(1, nd):
        to, n = (d + k) % nd, 2 * (k - 1)
        small_copies += [
            remote(small_send.at[0], small_x.at[k - 1], sx_s.at[n], sx_r.at[n], (to, h, z)),
            remote(rt.at[:, rows_at(to, band)], rt_x.at[k - 1], sx_s.at[n + 1], sx_r.at[n + 1], (to, h, z)),
        ]
    for copy in small_copies:
        copy.start()

    start_part(parts // 2, *value_flow)
    for copy in small_copies:
        copy.wait()
    router_sum = rt[:, rows_at(d, band)]
    for k in range(1, nd):
        small[...] = join(small[...], small_x[k - 1])
        router_sum = router_sum + rt_x[k - 1]
    rt_z[nz - 1] = router_sum
    small_send[1] = small[...]
    for copy in out_band:
        copy.wait()
    for copy in qkv_band:
        copy.wait()
    for i in range(parts // 2 + 1, parts):
        start_part(i, *value_flow)
    for i in range(4):
        sums = w_half[i, rows_at(d, band), :]
        for k in range(1, nd):
            sums = sums + band_recv[k - 1, i].astype(F32)
        w_half[i, 0:band, :] = sums
        line_send[i] = sums.astype(BF16)
    z_copies = []
    for j in range(1, nz):
        to, n = at.next_z(j), 3 * (j - 1)
        device = at.line(to)
        z_copies += [
            remote(line_send.at[:, rows_at(to, rp), :], line_recv.at[j - 1], gl_s.at[n], gl_r.at[n], device),
            remote(small_send.at[1], small_z.at[j - 1], gl_s.at[n + 1], gl_r.at[n + 1], device),
            remote(rt_z.at[nz - 1], rt_z.at[j - 1], gl_s.at[n + 2], gl_r.at[n + 2], device),
        ]
    for copy in z_copies:
        copy.start()
    for c in range(parts // 2, parts):
        send_mix(c)
    mix = gathered(mix_own, *mix_flow)
    output_out[...] = (hidden_at[...] + mix)[0 : sz.rows].astype(BF16)

    for copy in z_copies:
        copy.wait()
    totals = small[...]
    router_sum = rt_z[nz - 1]
    for j in range(1, nz):
        totals = join(totals, small_z[j - 1])
        router_sum = router_sum + rt_z[j - 1]
    gain_one_out[...] = totals[0:1]
    gain_two_out[...] = totals[1:2]
    rr = sz.router_rows
    own_router = router_sum[:, 0:rr]
    for i in range(1, nh):
        own_router = jnp.where(h == i, router_sum[:, i * rr : (i + 1) * rr], own_router)
    router_out[...] = own_router
    tau = tau_ref[...]
    factor = jnp.sqrt(tau / jnp.maximum(totals[2:3, 0:HEADS], tau))
    column = iota((1, cp), 1) // HEAD_DIM + h * (cp // HEAD_DIM)
    scale_row = jnp.zeros((1, cp), F32)
    for head in range(HEADS):
        scale_row = jnp.where(column == head, factor[:, head : head + 1], scale_row)
    for i in range(2):
        clipped_out[i] = (w_qkv_ref[i].astype(F32) * scale_row).astype(BF16)
    for i in range(4):
        sums = w_half[i, rows_at(z, rp), :]
        for j in range(1, nz):
            sums = sums + line_recv[j - 1, i].astype(F32)
        if i < 3:
            qkv_out[i] = sums
        else:
            out_out[...] = sums
    for copy in stores:
        copy.wait()


def finish_kernel(sz, *refs):
    sources, results, held = refs[0:10], refs[10:20], refs[20:28]
    halves_in, full_out, in_sems, out_sems, small_in, small_out = refs[28:]
    pieces = [(i, e) for e in range(sz.own) for i in range(2)]
    loads = [pltpu.make_async_copy(sources[8 + i].at[e], halves_in.at[i, e], in_sems.at[i, e]) for i, e in pieces]
    stores = [pltpu.make_async_copy(full_out.at[i, e], results[8 + i].at[e], out_sems.at[i, e]) for i, e in pieces]
    small_loads = [pltpu.make_async_copy(sources[n], held[n], small_in.at[n]) for n in range(8)]
    small_stores = [pltpu.make_async_copy(held[n], results[n], small_out.at[n]) for n in range(8)]
    for copy in loads + small_loads:
        copy.start()
    for (i, e), load, store in zip(pieces, loads, stores):
        load.wait()
        full_out[i, e] = halves_in[i, e].astype(F32)
        store.start()
    for load, store in zip(small_loads, small_stores):
        load.wait()
        store.start()
    for copy in stores + small_stores:
        copy.wait()


def fast_body(
    sz, inputs, cotangent, routes, gain_attn, gain_expert, tau, w_qkv, w_out_attn, w_router, w_in, w_out
):
    ng, nz, nd, nh, pad, width, own = sz.groups, sz.nt, sz.nd, sz.nh, sz.pad, sz.width, sz.own
    rp, cp, band, parts, block = sz.row_piece, sz.col_piece, sz.band, sz.parts, sz.block
    many, hidden = ng * sz.cap, sz.hidden
    on_chip, anywhere = pl.BlockSpec(memory_space=pltpu.VMEM), pl.BlockSpec(memory_space=pltpu.HBM)

    def shape(dims, dtype):
        return jax.ShapeDtypeStruct(dims, dtype)

    def half(*dims):
        return pltpu.VMEM(dims, BF16)

    def full(*dims):
        return pltpu.VMEM(dims, F32)

    def pair(*dims):
        return [pltpu.SemaphoreType.DMA(dims)] * 2

    slot_buffer = half(ng, sz.group_slots, width)
    line_buffer = half(nz - 1, pad, width)
    quarter_dims = (ng, own * (sz.cap // nz), width // parts)
    quarter_buffer, few = half(*quarter_dims), ng * own * (sz.cap // nz)
    rr = sz.router_rows
    smalls = (
        shape(inputs.shape, BF16), shape(inputs.shape, BF16), shape((1, width), F32), shape((1, width), F32),
        shape((3, rp, cp), F32), shape((rp, cp), F32), shape((sz.experts, rr), F32), shape((2, rp, cp), BF16),
    )
    packed = pl.pallas_call(
        functools.partial(block_kernel, sz),
        out_shape=(*smalls, shape(w_in.shape, BF16), shape(w_out.shape, BF16)),
        in_specs=[on_chip] * 9 + [anywhere] * 2,
        out_specs=(on_chip,) * 8 + (anywhere,) * 2,
        scratch_shapes=[
            half(4, rp, cp), half(4, width, width), half(sz.experts, 128), half(ng, sz.experts, 128),
            half(sz.experts, width), full(8, block), full(block, 128), half(sz.slots, block), half(block, sz.slots), half(block, few),
            half(block, width), half(block, width), *[slot_buffer] * 6,
            half(nz, *quarter_dims), half(nz - 1, *quarter_dims), quarter_buffer,
            quarter_buffer,
            half(own, width, hidden), half(own, hidden, width), half(own, many, hidden), half(own, many, hidden),
            full(own, many, hidden), half(own, hidden, width),
            full(sz.experts, 128), full(ng, 8, 128), full(sz.experts, block), full(8, many),
            full(ng, 8, 128), full(sz.experts, 128),
            half(3, pad, width), half(HEADS, pad, pad), half(pad, width), full(pad, width), full(8, 128),
            full(block, width), full(pad, width), line_buffer, line_buffer, full(pad, width), line_buffer, line_buffer,
            half(pad, width), half(3, pad, width), half(nh - 1, 4, width, cp), half(nh - 1, 4, width, cp),
            full(4, width, cp), half(4, width, cp), half(nd - 1, 4, band, cp), half(4, band, cp),
            half(nz - 1, 4, rp, cp),
            full(8, width), full(2, 8, width), full(nh - 1, 8, width), full(nd - 1, 8, width), full(nz - 1, 8, width),
            full(sz.experts, width), full(nh - 1, sz.experts, width), full(nd - 1, sz.experts, band),
            full(nz, sz.experts, band),
            *pair(nz - 1), *pair(nd - 1), *pair(nd * (nh - 1)), *pair(ng - 1), *pair(parts, nz - 1),
            *pair(parts, nz - 1), *pair(parts, ng), *pair(parts, ng), *pair(ng - 1), *pair(own, ng), *pair(parts, ng),
            *pair(parts, ng), *pair(ng - 1), *pair(parts, nz - 1), *pair(parts, nz - 1), *pair(4 * (nh - 1)),
            *pair(2 * (nd - 1)), *pair(3 * (nz - 1)), *pair(2 * (nh - 1)), *pair(2 * (nd - 1)),
            *pair(own, nz - 1), *pair(ng - 1),
            pltpu.SemaphoreType.DMA((3 + own,)),
        ],
        compiler_params=pltpu.CompilerParams(collective_id=0, has_side_effects=True, vmem_limit_bytes=62 * 2**20),
        name="block",
    )(
        inputs, cotangent, routes.T, gain_attn[None, :], gain_expert[None, :], w_qkv, w_out_attn.T, w_router.T,
        tau[None, :], w_in, w_out,
    )

    both, dma = (2, *w_in.shape), pltpu.SemaphoreType.DMA
    output, grad_input, gain_one, gain_two, grad_qkv, grad_out, grad_router, clipped, grad_first, grad_second = (
        pl.pallas_call(
            functools.partial(finish_kernel, sz),
            out_shape=(*smalls, shape(w_in.shape, F32), shape(w_out.shape, F32)),
            in_specs=[anywhere] * 10,
            out_specs=(anywhere,) * 10,
            scratch_shapes=[
                *[pltpu.VMEM(x.shape, x.dtype) for x in smalls], half(*both), full(*both), dma((2, own)), dma((2, own)),
                dma((8,)), dma((8,)),
            ],
            compiler_params=pltpu.CompilerParams(vmem_limit_bytes=62 * 2**20),
            name="finish",
        )(*packed)
    )
    return (
        output, grad_input, gain_one[0], gain_two[0], grad_qkv, grad_out.T, grad_router.T, grad_first, grad_second,
        clipped,
    )


def gelu_tanh(inputs):
    return (
        0.5
        * inputs
        * (1.0 + jnp.tanh(0.7978845608028654 * (inputs + 0.044715 * inputs * inputs * inputs)))
    )


def unit_and_factor(inputs):
    centered = inputs - jnp.mean(inputs, -1, keepdims=True)
    factor = lax.rsqrt(jnp.mean(centered * centered, -1, keepdims=True) + 1e-06)
    return (centered * factor, factor)


def general_norm_back(grad_norm, unit_rows, factor, gain):
    grad, gain_row = norm_back(grad_norm, unit_rows, factor, gain)
    return grad, gain_row[0]


def attn_forward(block_parts):
    queries, key_rows, value_rows = block_parts
    scores = jnp.einsum(
        "bhqd,bhkd->bhqk", queries, key_rows, preferred_element_type=jnp.float32
    ) * HEAD_DIM ** (-0.5)
    row_peak = jnp.max(scores, -1, keepdims=True)
    exponent = jnp.exp(scores - row_peak)
    summed = jnp.sum(exponent, -1, keepdims=True)
    soft_weights = (exponent / summed).astype(jnp.bfloat16)
    mixed = jnp.einsum(
        "bhqk,bhkd->bhqd", soft_weights, value_rows, preferred_element_type=jnp.float32
    ).astype(jnp.bfloat16)
    return (mixed, (row_peak + jnp.log(summed))[..., 0], jnp.max(row_peak, axis=(0, 2, 3)))


def attn_backward(block_parts):
    queries, key_rows, value_rows, grad_mixed, log_total = block_parts
    score_scale = HEAD_DIM ** (-0.5)
    scores = (
        jnp.einsum("bhqd,bhkd->bhqk", queries, key_rows, preferred_element_type=jnp.float32)
        * score_scale
    )
    soft_weights = jnp.exp(scores - log_total[..., None])
    grad_soft = jnp.einsum(
        "bhqd,bhkd->bhqk", grad_mixed, value_rows, preferred_element_type=jnp.float32
    )
    inner_sum = jnp.sum(soft_weights * grad_soft, -1, keepdims=True)
    grad_scores = (soft_weights * (grad_soft - inner_sum)).astype(jnp.bfloat16)
    grad_query = (
        jnp.einsum("bhqk,bhkd->bhqd", grad_scores, key_rows, preferred_element_type=jnp.float32)
        * score_scale
    ).astype(jnp.bfloat16)
    grad_key = (
        jnp.einsum("bhqk,bhqd->bhkd", grad_scores, queries, preferred_element_type=jnp.float32)
        * score_scale
    ).astype(jnp.bfloat16)
    grad_value = jnp.einsum(
        "bhqk,bhqd->bhkd",
        soft_weights.astype(jnp.bfloat16),
        grad_mixed,
        preferred_element_type=jnp.float32,
    ).astype(jnp.bfloat16)
    return (grad_query, grad_key, grad_value)


def general_body(
    inputs, cotangent, routes, gain_attn, gain_expert, tau, w_qkv, w_out_attn, w_router, w_in, w_out
):
    row_count, width = inputs.shape
    n_dp = lax.axis_size("dp")
    n_heads = lax.axis_size("heads")
    n_tensor = lax.axis_size("tensor")
    row_piece = w_qkv.shape[1]
    col_piece = w_qkv.shape[2]
    own_heads = col_piece // HEAD_DIM
    head_start = lax.axis_index("heads") * col_piece
    x_float = inputs.astype(jnp.float32)
    unit_one, factor_one = unit_and_factor(x_float)
    normed_one = (unit_one * gain_attn).astype(jnp.bfloat16)
    stack_qkv, stack_out = (
        lax.all_gather(w_qkv[None], ("dp", "heads", "tensor"), axis=0, tiled=True),
        lax.all_gather(w_out_attn[None], ("dp", "heads", "tensor"), axis=0, tiled=True),
    )
    full_qkv = (
        stack_qkv.reshape(n_dp, n_heads, n_tensor, 3, row_piece, col_piece)
        .transpose(3, 0, 2, 4, 1, 5)
        .reshape(3, width, width)
    )
    full_out = (
        stack_out.reshape(n_dp, n_heads, n_tensor, col_piece, row_piece)
        .transpose(1, 3, 0, 2, 4)
        .reshape(width, width)
    )
    proj_w = lax.dynamic_slice_in_dim(full_qkv, head_start, col_piece, 2)
    attn_w = lax.dynamic_slice_in_dim(full_out, head_start, col_piece, 0)
    normed_all = lax.all_gather(normed_one, "heads", axis=0, tiled=True)
    head_cols = attn_w.shape[0]
    local_heads = head_cols // HEAD_DIM
    joined_w = jnp.concatenate([proj_w[0], proj_w[1], proj_w[2]], 1)
    projected = jnp.dot(normed_all, joined_w, preferred_element_type=jnp.float32).astype(
        jnp.bfloat16
    )
    images = normed_all.shape[0] // SEQ
    per_block = 4 if images % 4 == 0 else 3 if images % 3 == 0 else 2 if images % 2 == 0 else 1
    block_shape = (images // per_block, per_block, SEQ, local_heads, HEAD_DIM)

    def to_blocks(row_matrix):
        return row_matrix.reshape(block_shape).transpose(0, 1, 3, 2, 4)

    def from_blocks(block_array):
        return block_array.transpose(0, 1, 3, 2, 4).reshape(-1, head_cols)

    queries = to_blocks(projected[:, :head_cols])
    key_rows = to_blocks(projected[:, head_cols : 2 * head_cols])
    value_rows = to_blocks(projected[:, 2 * head_cols :])
    mixed, log_total, head_peaks = lax.map(attn_forward, (queries, key_rows, value_rows))
    mixed_rows = from_blocks(mixed)
    block_peak = jnp.max(head_peaks, 0)
    attn_out = lax.psum_scatter(
        jnp.dot(mixed_rows, attn_w, preferred_element_type=jnp.float32),
        "heads",
        scatter_dimension=0,
        tiled=True,
    )
    peak_full = lax.dynamic_update_slice_in_dim(
        jnp.full((HEADS,), -1e30, jnp.float32), block_peak, lax.axis_index("heads") * local_heads, 0
    )
    hidden = x_float + attn_out
    peak_all = lax.pmax(peak_full, ("dp", "heads", "tensor"))
    peak_logit = lax.dynamic_slice_in_dim(
        peak_all, lax.axis_index("heads") * own_heads, own_heads, 0
    )
    unit_two, factor_two = unit_and_factor(hidden)
    normed_two = (unit_two * gain_expert).astype(jnp.bfloat16)
    group_rows, group_cot = (
        lax.all_gather(normed_two, "tensor", axis=0, tiled=True),
        lax.all_gather(cotangent, "tensor", axis=0, tiled=True),
    )
    first_w, second_w, router_w = (
        lax.all_gather(w_in, ("dp", "heads"), axis=0, tiled=True),
        lax.all_gather(w_out, ("dp", "heads"), axis=0, tiled=True),
        lax.all_gather(w_router, ("dp", "heads"), axis=0, tiled=True),
    )
    logits = jnp.dot(group_rows, router_w, preferred_element_type=jnp.float32)
    chosen = jnp.take_along_axis(logits, routes, 1)
    exponent = jnp.exp(chosen - jnp.max(chosen, -1, keepdims=True))
    gate_values = exponent / jnp.sum(exponent, -1, keepdims=True)
    group_count = routes.shape[0]
    experts = router_w.shape[1]
    capacity = (group_count * 5 // (16 * experts) + 1) * 8
    flat_ids = routes.reshape(-1)
    ordering = jnp.argsort(flat_ids, stable=True)
    sorted_ids = flat_ids[ordering]
    counts = jnp.sum(
        (flat_ids[:, None] == jnp.arange(experts, dtype=jnp.int32)[None, :]).astype(jnp.int32), 0
    )
    expert_ids = jnp.arange(experts, dtype=jnp.int32)
    starts = jnp.sum(jnp.where(expert_ids[None, :] < expert_ids[:, None], counts[None, :], 0), 1)
    slot_rank = jnp.arange(2 * group_count, dtype=jnp.int32) - starts[sorted_ids]
    slot_table = (
        jnp.full((experts * capacity,), 2 * group_count, jnp.int32)
        .at[sorted_ids * capacity + slot_rank]
        .set(ordering)
    )
    slot_token = slot_table // 2
    padded_rows = jnp.concatenate([group_rows, jnp.zeros((1, width), jnp.bfloat16)], 0)
    slot_in = padded_rows[slot_token].reshape(experts, capacity, width)
    slot_gate = jnp.concatenate([gate_values.reshape(-1), jnp.zeros((1,), jnp.float32)], 0)[
        slot_table
    ]
    pre_gelu = jnp.einsum("ecd,edf->ecf", slot_in, first_w, preferred_element_type=jnp.float32)
    activated = gelu_tanh(pre_gelu).astype(jnp.bfloat16)
    slot_out = jnp.einsum(
        "ecf,efd->ecd", activated, second_w, preferred_element_type=jnp.float32
    ).reshape(-1, width)
    partial_value = (
        jnp.zeros((group_count + 1, width), jnp.float32)
        .at[slot_token]
        .add(slot_gate[:, None] * slot_out)[:group_count]
    )
    expert_mix = lax.psum_scatter(
        partial_value.astype(jnp.bfloat16), "tensor", scatter_dimension=0, tiled=True
    ).astype(jnp.float32)
    output = (hidden + expert_mix).astype(jnp.bfloat16)
    padded_cot = jnp.concatenate([group_cot, jnp.zeros((1, width), jnp.bfloat16)], 0)
    slot_cot = padded_cot[slot_token].astype(jnp.float32)
    grad_slot_out = (
        (slot_gate[:, None] * slot_cot).astype(jnp.bfloat16).reshape(experts, capacity, width)
    )
    gate_part = (
        jnp.zeros((2 * group_count + 1,), jnp.float32)
        .at[slot_table]
        .add(jnp.sum(slot_cot * slot_out, -1))[: 2 * group_count]
        .reshape(group_count, 2)
    )
    grad_act = jnp.einsum(
        "ecd,efd->ecf", grad_slot_out, second_w, preferred_element_type=jnp.float32
    )
    grad_pre = jax.vjp(gelu_tanh, pre_gelu)[1](grad_act)[0].astype(jnp.bfloat16)
    grad_first = jnp.einsum("ecd,ecf->edf", slot_in, grad_pre, preferred_element_type=jnp.float32)
    grad_second = jnp.einsum(
        "ecf,ecd->efd", activated, grad_slot_out, preferred_element_type=jnp.float32
    )
    grad_slots = jnp.einsum(
        "ecf,edf->ecd", grad_pre, first_w, preferred_element_type=jnp.float32
    ).reshape(-1, width)
    grad_part = (
        jnp.zeros((group_count + 1, width), jnp.float32)
        .at[slot_token]
        .add(grad_slots)[:group_count]
    )
    grad_normed_two, grad_gates = (
        lax.psum_scatter(
            grad_part.astype(jnp.bfloat16), "tensor", scatter_dimension=0, tiled=True
        ).astype(jnp.float32),
        lax.psum_scatter(
            gate_part.astype(jnp.bfloat16), "tensor", scatter_dimension=0, tiled=True
        ).astype(jnp.float32),
    )
    shard_first, shard_second = (
        lax.psum_scatter(
            grad_first.astype(jnp.bfloat16), ("dp", "heads"), scatter_dimension=0, tiled=True
        ).astype(jnp.float32),
        lax.psum_scatter(
            grad_second.astype(jnp.bfloat16), ("dp", "heads"), scatter_dimension=0, tiled=True
        ).astype(jnp.float32),
    )
    offset = lax.axis_index("tensor") * row_count
    local_gates = lax.dynamic_slice_in_dim(gate_values, offset, row_count, 0)
    local_routes = lax.dynamic_slice_in_dim(routes, offset, row_count, 0)
    grad_chosen = local_gates * (grad_gates - jnp.sum(local_gates * grad_gates, -1, keepdims=True))
    columns = jnp.arange(experts, dtype=jnp.int32)[None, :]
    grad_logits = (
        jnp.where(local_routes[:, 0:1] == columns, grad_chosen[:, 0:1], 0.0)
        + jnp.where(local_routes[:, 1:2] == columns, grad_chosen[:, 1:2], 0.0)
    ).astype(jnp.bfloat16)
    grad_normed_two = grad_normed_two + jnp.einsum(
        "re,de->rd", grad_logits, router_w, preferred_element_type=jnp.float32
    )
    router_term = jnp.einsum(
        "rd,re->de", normed_two, grad_logits, preferred_element_type=jnp.float32
    )
    grad_hidden_norm, gain_two_term = general_norm_back(grad_normed_two, unit_two, factor_two, gain_expert)
    grad_hidden = cotangent.astype(jnp.float32) + grad_hidden_norm
    grad_attn = lax.all_gather(grad_hidden.astype(jnp.bfloat16), "heads", axis=0, tiled=True)
    grad_mixed = jnp.einsum(
        "rd,cd->rc", grad_attn, attn_w, preferred_element_type=jnp.float32
    ).astype(jnp.bfloat16)
    out_term = jnp.einsum("rc,rd->cd", mixed_rows, grad_attn, preferred_element_type=jnp.float32)
    grad_query, grad_key, grad_value = lax.map(
        attn_backward, (queries, key_rows, value_rows, to_blocks(grad_mixed), log_total)
    )
    grad_proj = jnp.concatenate(
        [from_blocks(grad_query), from_blocks(grad_key), from_blocks(grad_value)], 1
    )
    grad_normed_one = lax.psum_scatter(
        jnp.einsum("rc,dc->rd", grad_proj, joined_w, preferred_element_type=jnp.float32).astype(
            jnp.bfloat16
        ),
        "heads",
        scatter_dimension=0,
        tiled=True,
    ).astype(jnp.float32)
    proj_term = jnp.einsum("rd,rc->dc", normed_all, grad_proj, preferred_element_type=jnp.float32)
    proj_stack = jnp.stack(
        [
            proj_term[:, :head_cols],
            proj_term[:, head_cols : 2 * head_cols],
            proj_term[:, 2 * head_cols :],
        ],
        0,
    )
    whole_proj = lax.dynamic_update_slice_in_dim(
        jnp.zeros((3, width, width), jnp.float32), proj_stack, head_start, 2
    )
    whole_out = lax.dynamic_update_slice_in_dim(
        jnp.zeros((width, width), jnp.float32), out_term, head_start, 0
    )
    send_qkv = (
        whole_proj.reshape(3, n_dp, n_tensor, row_piece, n_heads, col_piece)
        .transpose(1, 4, 2, 0, 3, 5)
        .reshape(-1, 3, row_piece, col_piece)
    )
    send_out = (
        whole_out.reshape(n_heads, col_piece, n_dp, n_tensor, row_piece)
        .transpose(2, 0, 3, 1, 4)
        .reshape(-1, col_piece, row_piece)
    )
    shard_proj, shard_attn = (
        lax.psum_scatter(send_qkv, ("dp", "heads", "tensor"), scatter_dimension=0, tiled=True),
        lax.psum_scatter(send_out, ("dp", "heads", "tensor"), scatter_dimension=0, tiled=True),
    )
    grad_input_norm, gain_one_term = general_norm_back(grad_normed_one, unit_one, factor_one, gain_attn)
    grad_input = (grad_hidden + grad_input_norm).astype(jnp.bfloat16)
    gain_one_grad, gain_two_grad, router_all = lax.psum(
        (gain_one_term, gain_two_term, router_term), ("dp", "heads", "tensor")
    )
    router_grad = lax.dynamic_slice_in_dim(
        router_all, lax.axis_index(("dp", "heads")) * w_router.shape[0], w_router.shape[0], 0
    )
    local_tau = lax.dynamic_slice_in_dim(tau, lax.axis_index("heads") * own_heads, own_heads, 0)
    clip_factor = jnp.sqrt(local_tau / jnp.maximum(peak_logit, local_tau))
    clipped = (w_qkv[:2].astype(jnp.float32) * jnp.repeat(clip_factor, HEAD_DIM)).astype(
        jnp.bfloat16
    )
    return (
        output,
        grad_input,
        gain_one_grad,
        gain_two_grad,
        shard_proj[0],
        shard_attn[0],
        router_grad,
        shard_first,
        shard_second,
        clipped,
    )


def body(*args):
    inputs, _, routes, _, _, _, w_qkv, _, w_router, w_in, _ = args
    sz = Sizes(
        lax.axis_size("dp"), lax.axis_size("heads"), lax.axis_size("tensor"), inputs, routes, w_qkv, w_router, w_in
    )
    if sz.fits():
        return fast_body(sz, *args)
    return general_body(*args)


def solution(mesh):
    return jax.shard_map(
        body,
        mesh=mesh,
        in_specs=(
            P(("dp", "heads", "tensor"), None),
            P(("dp", "heads", "tensor"), None),
            P(("dp", "heads"), None),
            P(),
            P(),
            P(),
            P(None, ("dp", "tensor"), "heads"),
            P("heads", ("dp", "tensor")),
            P(("dp", "heads"), None),
            P(("dp", "heads"), None, "tensor"),
            P(("dp", "heads"), "tensor", None),
        ),
        out_specs=(
            P(("dp", "heads", "tensor"), None),
            P(("dp", "heads", "tensor"), None),
            P(),
            P(),
            P(None, ("dp", "tensor"), "heads"),
            P("heads", ("dp", "tensor")),
            P(("dp", "heads"), None),
            P(("dp", "heads"), None, "tensor"),
            P(("dp", "heads"), "tensor", None),
            P(None, ("dp", "tensor"), "heads"),
        ),
        check_vma=False,
    )
```

```python
import functools
import jax
import jax.numpy as jnp
from jax import lax
from jax.experimental import pallas as pl
from jax.experimental.pallas import tpu as pltpu
from jax.sharding import PartitionSpec as P

HEADS = 8
HEAD_DIM = 64
SEQ = 197
F32 = jnp.float32
BF16 = jnp.bfloat16
MESH = pl.DeviceIdType.MESH
NEG = -1e30


class Sizes:
    def __init__(self, n_dp, n_heads, n_tensor, inputs, routes, w_qkv, w_router, w_in):
        self.nd, self.nh, self.nt = n_dp, n_heads, n_tensor
        self.groups = n_dp * n_heads
        self.rows, self.width = inputs.shape
        self.pad = -(-self.rows // 16) * 16
        self.block = self.pad * n_tensor
        self.block_rows = routes.shape[0]
        self.own = w_in.shape[0]
        self.hidden = w_in.shape[2]
        self.experts = self.own * self.groups
        self.cap = (self.block_rows * 5 // (16 * self.experts) + 1) * 8
        self.group_slots = self.own * self.cap
        self.slots = self.experts * self.cap
        self.row_piece, self.col_piece = w_qkv.shape[1], w_qkv.shape[2]
        self.band = self.row_piece * n_tensor
        self.router_rows = w_router.shape[0]
        self.parts = 4

    def fits(self):
        return (
            self.rows == SEQ
            and self.nt == 4
            and self.parts == 4
            and self.block_rows == self.rows * self.nt
            and self.cap == 64
            and self.experts == 32
            and self.group_slots % 128 == 0
            and self.col_piece % 128 == 0
            and self.row_piece % 16 == 0
            and self.router_rows % 16 == 0
            and self.own * self.groups * 4 == 128
            and self.width == HEADS * HEAD_DIM
            and self.block * self.width * 2 <= 2**20
            and self.own * self.width <= self.slots
            and self.hidden <= self.block
            and self.hidden == self.width
            and self.cap % (16 * self.nt) == 0
            and self.width // self.parts % 128 == 0
        )


def nn(a, b):
    return jnp.dot(a, b, preferred_element_type=F32)


def nt(a, b):
    return lax.dot_general(a, b, (((1,), (1,)), ((), ())), preferred_element_type=F32)


def tn(a, b):
    return lax.dot_general(a, b, (((0,), (0,)), ((), ())), preferred_element_type=F32)


def iota(shape, axis):
    return lax.broadcasted_iota(jnp.int32, shape, axis)


def normalize(rows):
    centered = rows - jnp.mean(rows, -1, keepdims=True)
    factor = lax.rsqrt(jnp.mean(centered * centered, -1, keepdims=True) + 1e-06)
    return centered * factor, factor


def norm_back(grad_norm, unit_rows, factor, gain):
    grad_hat = grad_norm * gain
    inner = (
        grad_hat
        - jnp.mean(grad_hat, -1, keepdims=True)
        - unit_rows * jnp.mean(grad_hat * unit_rows, -1, keepdims=True)
    )
    return factor * inner, jnp.sum(grad_norm * unit_rows, 0, keepdims=True)


def split_high_low(values):
    high = values.astype(BF16)
    low = (values - high.astype(F32)).astype(BF16)
    return jnp.concatenate([high, low], 0)


class Place:
    def __init__(self, sz):
        self.sz = sz
        self.d = lax.axis_index("dp")
        self.h = lax.axis_index("heads")
        self.z = lax.axis_index("tensor")
        self.group = self.d * sz.nh + self.h

    def plane(self, group):
        return (group // self.sz.nh, group % self.sz.nh, self.z)

    def line(self, z):
        return (self.d, self.h, z)

    def next_group(self, k):
        return (self.group + k) % self.sz.groups

    def next_z(self, j):
        return (self.z + j) % self.sz.nt

    def inner(self):
        return (self.z + 1) % 4 // 2

    def mates(self):
        return self.z + 1 - 2 * (self.z % 2), (self.z + 2) % 4, 3 - self.z

    def enter(self):
        sz = self.sz
        barrier = pltpu.get_barrier_semaphore()
        for k in range(1, sz.groups):
            pl.semaphore_signal(barrier, inc=1, device_id=self.plane(self.next_group(k)), device_id_type=MESH)
        for j in range(1, sz.nt):
            pl.semaphore_signal(barrier, inc=1, device_id=self.line(self.next_z(j)), device_id_type=MESH)
        pl.semaphore_wait(barrier, sz.groups + sz.nt - 2)


def remote(src, dst, send, recv, device):
    return pltpu.make_async_remote_copy(
        src_ref=src, dst_ref=dst, send_sem=send, recv_sem=recv, device_id=device, device_id_type=MESH
    )


def drain(send_sem, recv_sem, sent, landed):
    pltpu.make_async_copy(sent, sent, send_sem).wait()
    pltpu.make_async_copy(landed, landed, recv_sem).wait()


def route_table(sz, routes_ref, table):
    table[...] = jnp.full_like(table, -1.0)
    for z in range(sz.nt):
        table[0:2, z * sz.pad : z * sz.pad + sz.rows] = routes_ref[:, z * sz.rows : (z + 1) * sz.rows].astype(F32)


def block_kernel(
    sz, x_ref, cot_ref, routes_ref, gain_one_ref, gain_two_ref, w_qkv_ref, w_out_ref, w_router_ref, tau_ref, first_hbm,
    second_hbm, output_out, grad_input_out, gain_one_out, gain_two_out, qkv_out, out_out, router_out, clipped_out,
    grad_first_out, grad_second_out,
    w_own, w_full, router_own, router_full, router_t, route_rows, route_columns, select, select_t, select_qt,
    cot_block, rows_block, send_a, send_b, cot_slots, slots, grad_slots, values,
    grads_q, grads_line, grads_sum, grads_back, first, second, act, grad_pre, grad_act, grad_second,
    gate_send, gate_recv, gates_at, dgate_send, dgate_recv, dgate_rows,
    qkv, probs, mixed, hidden_at, peak_at, part, part_own, part_send, part_recv, mix_own, mix_send, mix_recv,
    grad_mixed, grad_qkv, core_send, core_recv, w_half, band_send, band_recv, line_send, line_recv,
    small, small_send, small_core, small_x, small_z, rt, rt_core, rt_x, rt_z,
    wz_s, wz_r, wx_s, wx_r, wc_s, wc_r, r_s, r_r, qz_s, qz_r, nz_s, nz_r, qa_s, qa_r, na_s, na_r, ga_s, ga_r,
    d0_s, d0_r, da_s, da_r, va_s, va_r, dg_s, dg_r, pz_s, pz_r, mz_s, mz_r, gc_s, gc_r, gx_s, gx_r, gl_s, gl_r,
    sc_s, sc_r, sx_s, sx_r, dl_s, dl_r, dq_s, dq_r, pr_r, mr_r,
    local_sem,
):
    at = Place(sz)
    d, h, z, me = at.d, at.h, at.z, at.group
    nd, nh, nz, ng = sz.nd, sz.nh, sz.nt, sz.groups
    band, rp, cp, pad, width = sz.band, sz.row_piece, sz.col_piece, sz.pad, sz.width
    many = ng * sz.cap
    parts, part_width = sz.parts, width // sz.parts

    def lanes(c):
        return pl.ds(c * part_width, part_width)

    def rows_at(n, size):
        return pl.ds(pl.multiple_of(n * size, size), size)

    own_block, own_columns = rows_at(z, pad), rows_at(h, cp)

    w_own[0:3] = w_qkv_ref[...]
    w_own[3] = w_out_ref[...]
    router_own[...] = jnp.zeros_like(router_own)
    router_own[:, 0 : sz.router_rows] = w_router_ref[...]
    cot_block[own_block] = jnp.concatenate(
        [cot_ref[...].astype(F32), jnp.zeros((pad - sz.rows, width), F32)], 0
    ).astype(BF16)

    part_recv[2] = jnp.zeros((pad, width), BF16)
    mix_recv[2] = jnp.zeros((pad, width), BF16)

    at.enter()

    w_rows = rows_at(d * nz + z, rp)
    w_z = [
        remote(w_own, w_full.at[:, w_rows, own_columns], wz_s.at[0], wz_r.at[0], at.line(at.next_z(j)))
        for j in range(1, nz)
    ]
    for copy in w_z:
        copy.start()
    loads = [
        pltpu.make_async_copy(first_hbm, first, local_sem.at[0]),
        pltpu.make_async_copy(second_hbm, second, local_sem.at[1]),
    ]
    for copy in loads:
        copy.start()
    routers = [
        remote(router_own, router_full.at[me], r_s.at[0], r_r.at[0], at.plane(at.next_group(k)))
        for k in range(1, ng)
    ]
    for copy in routers:
        copy.start()
    w_full[:, w_rows, own_columns] = w_own[...]
    router_full[me] = router_own[...]

    zeros = jnp.zeros((pad - sz.rows, width), F32)
    x_rows = jnp.concatenate([x_ref[...].astype(F32), zeros], 0)
    unit_one, _ = normalize(x_rows)
    normed_one = (unit_one * gain_one_ref[...]).astype(BF16)

    others = pl.ds(0, ng - 1)
    three = w_full.at[:, pl.ds(0, (nz - 1) * rp), own_columns]
    drain(wz_s.at[0], wz_r.at[0], three, three)

    def to_core(dp, other):
        place = w_full.at[:, rows_at(dp, band), own_columns]
        return remote(place, place, wc_s.at[other - 1], wc_r.at[other - 1], (d, (h + other) % nh, z))

    w_band = w_full.at[:, rows_at(d, band), own_columns]
    w_x = [
        remote(w_band, w_band, wx_s.at[k - 1], wx_r.at[k - 1], ((d + k) % nd, h, z)) for k in range(1, nd)
    ]
    for copy in w_x:
        copy.start()
    w_c = [to_core(d, other) for other in range(1, nh)]
    for copy in w_c:
        copy.start()

    def along(block, send_sems, recv_sems, c):
        place = block.at[own_block, lanes(c)]
        return [
            remote(place, place, send_sems.at[c], recv_sems.at[c], at.line(at.next_z(j)))
            for j in range(1, nz)
        ]

    def wait_along(block, send_sems, recv_sems, c):
        place = block.at[pl.ds(0, (nz - 1) * pad), lanes(c)]
        drain(send_sems.at[c], recv_sems.at[c], place, place)

    for c in range(parts):
        for copy in along(cot_block, qz_s, qz_r, c):
            copy.start()

    route_table(sz, routes_ref, route_rows)
    route_a, route_b = route_rows[0:1, :], route_rows[1:2, :]
    expert = iota((sz.experts, sz.block), 0).astype(F32)
    named_a, named_b = route_a == expert, route_b == expert
    named = jnp.logical_or(named_a, named_b)
    before = (iota((sz.block, sz.block), 0) < iota((sz.block, sz.block), 1)).astype(BF16)
    rank = nn(named.astype(BF16), before) + expert * float(sz.cap)
    slot_a = jnp.sum(jnp.where(named_a, rank, 0.0), 0, keepdims=True)
    slot_b = jnp.sum(jnp.where(named_b, rank, 0.0), 0, keepdims=True)
    slot_a = jnp.where(route_a < 0.0, -1.0, slot_a)
    slot_b = jnp.where(route_b < 0.0, -1.0, slot_b)
    slot_pair = jnp.concatenate([slot_a, slot_b] * 64, 0)
    route_columns[...] = slot_pair.T

    def fill(g, carry):
        slot = iota((sz.group_slots, sz.block), 0).astype(F32) + (g * sz.group_slots).astype(F32)
        hit = jnp.logical_or(slot == slot_a, slot == slot_b)
        select[rows_at(g, sz.group_slots), :] = jnp.where(hit, 1.0, 0.0).astype(BF16)
        return carry

    lax.fori_loop(0, ng, fill, 0)

    quarter = sz.cap // nz
    few = ng * sz.own * quarter

    def quarter_slot(dims, axis):
        n = iota(dims, axis)
        return (n // quarter * sz.cap + z * quarter + n % quarter).astype(F32)

    def quarter_move(k, send, landing, send_sems, recv_sems):
        g = (me + k) % ng
        return remote(send.at[g], landing.at[me], send_sems.at[0], recv_sems.at[0], at.plane(g))

    def dispatch(c, block, send, out):
        def step(g, carry):
            send[g, :, lanes(c)] = nn(select[rows_at(g, sz.group_slots), :], block[:, lanes(c)]).astype(BF16)
            return carry

        lax.fori_loop(0, ng, step, 0)
        out[me, :, lanes(c)] = send[me, :, lanes(c)]

    def exchange(c, k, send, out, send_sems, recv_sems):
        g = (me + k) % ng
        return remote(
            send.at[g, :, lanes(c)], out.at[me, :, lanes(c)], send_sems.at[c], recv_sems.at[c], at.plane(g)
        )

    def start_part(c, *flow):
        def step(i, carry):
            exchange(c, ng - 1 - i, *flow).start()
            return carry

        lax.fori_loop(0, ng - 1, step, 0)

    def wait_part(c, send, out, send_sems, recv_sems):
        drain(send_sems.at[c], recv_sems.at[c], send.at[others, :, lanes(c)], out.at[others, :, lanes(c)])

    cot_flow = (send_a, cot_slots, qa_s, qa_r)
    row_flow = (send_b, slots, na_s, na_r)

    def send_cot(c):
        wait_along(cot_block, qz_s, qz_r, c)
        dispatch(c, cot_block, send_a, cot_slots)

    send_cot(0)
    for k in range(1, nd):
        w_x[k - 1].wait_recv()
        for other in range(1, nh):
            to_core((d - k + nd) % nd, other).start()
    start_part(0, *cot_flow)
    for other in range(1, nh):
        columns = w_full.at[:, :, own_columns]
        drain(wc_s.at[other - 1], wc_r.at[other - 1], columns, columns)
    for copy in w_x:
        copy.wait_send()

    for i in range(3):
        qkv[i] = nn(normed_one, w_full[i]).astype(BF16)
    lane = iota((1, 2 * HEAD_DIM), 1)
    halves = (lane < HEAD_DIM, lane >= HEAD_DIM)
    key_valid = iota((1, pad), 1) < sz.rows
    row_valid = iota((pad, 1), 0) < sz.rows
    peak_lane = iota((1, 128), 1)
    peak_at[...] = jnp.full_like(peak_at, NEG)
    scale = HEAD_DIM ** (-0.5)

    def attend(pair, carry):
        columns = rows_at(pair, 2 * HEAD_DIM)
        q_pair, k_pair, v_pair = (qkv[i, :, columns] for i in range(3))
        sides = []
        for side in range(2):
            q_own = jnp.where(halves[side], q_pair, jnp.zeros_like(q_pair))
            scores = jnp.where(key_valid, nt(q_own, k_pair) * scale, NEG)
            row_peak = jnp.max(scores, -1, keepdims=True)
            exponent = jnp.exp(scores - row_peak)
            weights = (exponent / jnp.sum(exponent, -1, keepdims=True)).astype(BF16)
            head = pair * 2 + side
            probs[head] = weights
            sides.append(nn(weights, v_pair))
            peak = jnp.max(jnp.where(row_valid, row_peak, NEG), 0, keepdims=True)
            peak_at[0:1, :] = jnp.where(peak_lane == head, peak, peak_at[0:1, :])
        mixed[:, columns] = jnp.where(halves[0], sides[0], sides[1]).astype(BF16)
        return carry

    pairs = HEADS // 2
    sent = 1
    for turn in range(2):
        until = 1 + ((parts - 1) * (turn + 1)) // 2
        for c in range(sent, until):
            send_cot(c)
            start_part(c, *cot_flow)
        sent = until
        lax.fori_loop(turn * pairs // 2, (turn + 1) * pairs // 2, attend, 0)

    hidden = x_rows + nt(mixed[...], w_full[3])
    hidden_at[...] = hidden
    unit_two, _ = normalize(hidden)
    rows_block[own_block] = jnp.where(row_valid, unit_two * gain_two_ref[...], 0.0).astype(BF16)
    for c in range(parts):
        for copy in along(rows_block, nz_s, nz_r, c):
            copy.start()

    def fill_t(i, carry):
        rows = rows_at(i, pad)
        slot = iota((pad, sz.slots), 1).astype(F32)
        hit = jnp.logical_or(slot == route_columns[rows, 0:1], slot == route_columns[rows, 1:2])
        select_t[rows, :] = jnp.where(hit, 1.0, 0.0).astype(BF16)
        some = quarter_slot((pad, few), 1)
        hit = jnp.logical_or(some == route_columns[rows, 0:1], some == route_columns[rows, 1:2])
        select_qt[rows, :] = jnp.where(hit, 1.0, 0.0).astype(BF16)
        return carry

    lax.fori_loop(0, nz, fill_t, 0)
    drain(r_s.at[0], r_r.at[0], router_full.at[others], router_full.at[others])
    for g in range(ng):
        router_t[:, g * sz.router_rows : (g + 1) * sz.router_rows] = router_full[g, :, 0 : sz.router_rows]

    def expert_rows(ref, e):
        return ref[:, rows_at(e, sz.cap), :].reshape(many, width)

    def cot_grad(e, carry):
        grad_act[e] = nt(expert_rows(cot_slots, e), second[e])
        return carry

    for c in range(parts):
        wait_along(rows_block, nz_s, nz_r, c)
        dispatch(c, rows_block, send_b, slots)
        start_part(c, *row_flow)
        if c == parts // 2 - 1:
            for i in range(parts):
                wait_part(i, *cot_flow)
            for copy in loads:
                copy.wait()
            lax.fori_loop(0, sz.own, cot_grad, 0)

    logits = jnp.where(named, nt(router_t[...], rows_block[...]), NEG)
    exponent = jnp.where(named, jnp.exp(logits - jnp.max(logits, 0, keepdims=True)), 0.0)
    total = jnp.sum(exponent, 0, keepdims=True)
    gates = exponent / jnp.where(total > 0.0, total, 1.0)
    gates_at[...] = gates
    by_slot = nt(split_high_low(gates), select[...])
    by_slot = by_slot[0 : sz.experts] + by_slot[sz.experts :]
    own_slot = iota((sz.experts, sz.slots), 1) // sz.cap == iota((sz.experts, sz.slots), 0)
    by_slot = jnp.where(own_slot, by_slot, 0.0)
    folded = by_slot[:, 0:128]
    for i in range(1, sz.slots // 128):
        folded = folded + by_slot[:, i * 128 : (i + 1) * 128]
    gate_send[...] = folded
    gate_copies = [
        remote(
            gate_send.at[rows_at(at.next_group(k) * sz.own // 8, 8)], gate_recv.at[me], ga_s.at[0], ga_r.at[0],
            at.plane(at.next_group(k)),
        )
        for k in range(1, ng)
    ]
    for copy in gate_copies:
        copy.start()
    gate_recv[me] = gate_send[rows_at(me * sz.own // 8, 8)]
    drain(ga_s.at[0], ga_r.at[0], gate_recv.at[others], gate_recv.at[others])
    for c in range(parts):
        wait_part(c, *row_flow)

    def gate_of(e):
        turned = gate_recv[:, pl.ds(me * sz.own % 8 + e, 1), :].reshape(ng, 128).T
        columns = jnp.where((e % 2) == 1, turned[sz.cap : 2 * sz.cap], turned[0 : sz.cap])
        return jnp.concatenate([columns[:, s : s + 1] for s in range(ng)], 0)

    def first_piece(e, k):
        g = (me + k) % ng
        piece = (rows_at(e, sz.cap), lanes(1))
        return remote(
            send_a.at[(g, *piece)], grad_slots.at[(me, *piece)], d0_s.at[e], d0_r.at[e], at.plane(g)
        )

    def grads_piece(e, j):
        piece = (slice(None), rows_at(e, quarter), slice(None))
        return remote(
            grads_q.at[(at.next_z(j), *piece)], grads_line.at[(j - 1, *piece)], dl_s.at[0], dl_r.at[0],
            at.line(at.next_z(j)),
        )

    def expert_back(e, carry):
        gate = gate_of(e)
        half_rows = many // 2
        for part_at in range(2):
            some = slice(part_at * half_rows, (part_at + 1) * half_rows)
            groups = slice(part_at * ng // 2, (part_at + 1) * ng // 2)
            pre = nn(slots[groups, rows_at(e, sz.cap), :].reshape(half_rows, width), first[e])
            const, cubic = 0.7978845608028654, 0.044715
            square = pre * pre
            bent = jnp.tanh(const * pre * (1.0 + cubic * square))
            half = 0.5 * (1.0 + bent)
            hidden_units = (pre * half).astype(BF16)
            act[e, some] = hidden_units
            slope = half + 0.5 * pre * (1.0 - bent * bent) * const * (1.0 + 3.0 * cubic * square)
            through = grad_act[e, some]
            dgate = nt(jnp.ones((8, sz.hidden), BF16), (hidden_units.astype(F32) * through).astype(BF16))
            dgate_send[:, some] = jnp.where(iota((8, half_rows), 0) == e, dgate, dgate_send[:, some])
            grads = (through * gate[some] * slope).astype(BF16)
            grad_pre[e, some] = grads
            spread = nt(grads, first[e]).astype(BF16).reshape(ng // 2, sz.cap, width)
            send_a[groups, rows_at(e, sz.cap), :] = spread
            for i in range(nz):
                grads_q[i, groups, rows_at(e, quarter), :] = spread[:, i * quarter : (i + 1) * quarter, 0:part_width]

        def step(i, carry):
            first_piece(e, ng - 1 - i).start()
            return carry

        lax.fori_loop(0, ng - 1, step, 0)
        for j in range(1, nz):
            grads_piece(e, j).start()
        return carry

    dgate_send[...] = jnp.zeros_like(dgate_send)
    lax.fori_loop(0, sz.own, expert_back, 0)
    dgates = [
        remote(
            dgate_send.at[:, rows_at(at.next_group(k) * sz.cap // 128, 128)], dgate_recv.at[me], dg_s.at[0],
            dg_r.at[0], at.plane(at.next_group(k)),
        )
        for k in range(1, ng)
    ]
    for copy in dgates:
        copy.start()
    dgate_recv[me] = dgate_send[:, rows_at(me * sz.cap // 128, 128)]
    grad_flow = (send_a, grad_slots, da_s, da_r)
    value_flow = (send_b, values, va_s, va_r)
    for c in range(2, parts):
        start_part(c, *grad_flow)
    grad_slots[me] = send_a[me]

    def expert_value(e, carry):
        value = nn(act[e], second[e])
        gated = (value * gate_of(e)).astype(BF16).reshape(ng, sz.cap, width)
        send_b[:, rows_at(e, sz.cap), :] = gated
        return carry

    lax.fori_loop(0, sz.own, expert_value, 0)
    values[me] = send_b[me]

    def quarter_total(own, line, sums):
        total = own[z].astype(F32)
        for j in range(1, nz):
            total = total + line[j - 1].astype(F32)
        sums[...] = total.astype(BF16)


    def weight_grads(e, carry):
        grad_value = (expert_rows(cot_slots, e).astype(F32) * gate_of(e)).astype(BF16)
        grad_second[e] = tn(act[e], grad_value).astype(BF16)
        select[rows_at(e, width), 0 : sz.hidden] = tn(expert_rows(slots, e), grad_pre[e]).astype(BF16)
        return carry

    drain(dg_s.at[0], dg_r.at[0], dgate_recv.at[others], dgate_recv.at[others])
    mine = iota((8, 128), 1) // sz.cap == me * sz.cap % 128 // sz.cap
    for g in range(ng):
        folded = jnp.where(mine, dgate_recv[g], 0.0)
        folded = folded + pltpu.roll(folded, 64, 1)
        dgate_rows[g * sz.own : (g + 1) * sz.own, :] = folded[0 : sz.own]
    spread = jnp.concatenate([dgate_rows[...]] * (sz.slots // 128), 1)
    own_slot = iota((sz.experts, sz.slots), 1) // sz.cap == iota((sz.experts, sz.slots), 0)
    dgate = nt(split_high_low(jnp.where(own_slot, spread, 0.0)), select_t[...])
    dgate = dgate[0 : sz.experts] + dgate[sz.experts :]
    gates = gates_at[...]
    dlogits = (gates * (dgate - jnp.sum(gates * dgate, 0, keepdims=True))).astype(BF16)
    rt[...] = nn(dlogits, rows_block[...])
    part[...] = tn(dlogits, router_t[...])

    inner = at.inner()
    beside, across, mirror = at.mates()

    def line_copy(c, slot, send, recv, send_sems, recv_sems, relay_sems, last):
        if slot < 2:
            return remote(
                send.at[slot, :, lanes(c)], recv.at[slot, :, lanes(c)], send_sems.at[c], recv_sems.at[c],
                at.line((beside, across)[slot]),
            )
        by_way = 1 - inner if c != last else 0
        to = mirror + by_way * (beside - mirror)
        return remote(
            send.at[2, :, lanes(c)], recv.at[2 + by_way, :, lanes(c)], send_sems.at[c], relay_sems.at[c, by_way], at.line(to)
        )

    def scatter(c, source, base, own, *flow):
        if source is grads_back:
            places, flat = select_qt, source[...].reshape(few, part_width)
        else:
            places, flat = select_t, source[:, :, lanes(c)].reshape(sz.slots, part_width)
        for slot, target in ((2, mirror), (1, across), (0, beside), (None, z)):
            tokens = rows_at(target, pad)
            sums = nn(places[tokens, :], flat)
            if base is not None:
                sums = sums + base[tokens, lanes(c)]
            if slot is None:
                own[:, lanes(c)] = sums
                continue
            flow[0][slot, :, lanes(c)] = sums.astype(BF16)
            if slot == 1 and c != flow[-1]:

                @pl.when(inner == 0)
                def _():
                    line_copy(c, 1, *flow).start()
            else:
                line_copy(c, slot, *flow).start()

    def relay(c, send, recv, send_sems, recv_sems, relay_sems, last):
        @pl.when(inner == 1)
        def _():
            landed = recv.at[3, :, lanes(c)]
            pltpu.make_async_copy(landed, landed, relay_sems.at[c, 1]).wait()
            send[1, :, lanes(c)] = (send[1, :, lanes(c)].astype(F32) + recv[3, :, lanes(c)].astype(F32)).astype(BF16)
            line_copy(c, 1, send, recv, send_sems, recv_sems, relay_sems, last).start()

    def gathered(own, send, recv, send_sems, recv_sems, relay_sems, last):
        for c in range(parts):
            drain(send_sems.at[c], recv_sems.at[c], send.at[:, :, lanes(c)], recv.at[pl.ds(0, 2), :, lanes(c)])

            @pl.when(inner == 1 if c != last else True)
            def _(c=c):
                landed = recv.at[2, :, lanes(c)]
                pltpu.make_async_copy(landed, landed, relay_sems.at[c, 0]).wait()

        sums = own[...]
        for slot in range(3):
            sums = sums + recv[slot].astype(F32)
        return sums

    part_flow = (part_send, part_recv, pz_s, pz_r, pr_r, 0)
    mix_flow = (mix_send, mix_recv, mz_s, mz_r, mr_r, parts - 1)

    def wait_first(e, carry):
        piece = (others, rows_at(e, sz.cap), lanes(1))
        drain(d0_s.at[e], d0_r.at[e], send_a.at[piece], grad_slots.at[piece])
        return carry

    def exchange_quarters():
        drain(dl_s.at[0], dl_r.at[0], grads_line, grads_line)
        quarter_total(grads_q, grads_line, grads_sum)
        for copy in grads_moves:
            copy.start()
        grads_back[me] = grads_sum[me]

    grads_moves = [quarter_move(k, grads_sum, grads_back, dq_s, dq_r) for k in range(1, ng)]
    order = [*range(1, parts), 0]
    done = 0
    for turn, c in enumerate(order):
        if c == 0:
            drain(dq_s.at[0], dq_r.at[0], grads_back.at[others], grads_back.at[others])
        elif c == 1:
            lax.fori_loop(0, sz.own, wait_first, 0)
        else:
            wait_part(c, *grad_flow)
        if c == parts - 1:
            for i in range(parts):
                start_part(i, *value_flow)
        scatter(c, grads_back if c == 0 else grad_slots, part, part_own, *part_flow)
        if turn == 0:
            exchange_quarters()
        until = sz.own * (turn + 1) // parts
        lax.fori_loop(done, until, weight_grads, 0)
        done = until
        if turn > 0:
            relay(order[turn - 1], *part_flow)
    stores = [
        pltpu.make_async_copy(grad_second, grad_second_out, local_sem.at[2]),
        *[
            pltpu.make_async_copy(
                select.at[e * width : (e + 1) * width, 0 : sz.hidden], grad_first_out.at[e], local_sem.at[3 + e]
            )
            for e in range(sz.own)
        ],
    ]
    for copy in stores:
        copy.start()

    unit_two, factor_two = normalize(hidden_at[...])
    grad_normed = jnp.where(row_valid, gathered(part_own, *part_flow), 0.0)
    grad_hidden, gain_two = norm_back(grad_normed, unit_two, factor_two, gain_two_ref[...])
    grad_hidden = jnp.concatenate([cot_ref[...].astype(F32), zeros], 0) + jnp.where(row_valid, grad_hidden, 0.0)
    part_own[...] = grad_hidden
    grad_attn = grad_hidden.astype(BF16)

    def core_copy(i, other):
        n = 4 * (other - 1) + i
        return remote(
            core_send.at[other - 1, i], core_recv.at[other - 1, i], gc_s.at[n], gc_r.at[n], (d, (h + other) % nh, z)
        )

    def half_sum(i, sums):
        for other in range(1, nh):
            core_copy(i, other).wait()
            sums = sums + core_recv[other - 1, i].astype(F32)
        w_half[i] = sums
        band_send[i] = sums.astype(BF16)

    def band_copy(k, i):
        to = (d + k) % nd
        return remote(
            band_send.at[i, rows_at(to, band), :], band_recv.at[k - 1, i], gx_s.at[i], gx_r.at[i], (to, h, z)
        )

    for other in [*range(1, nh), 0]:
        sums = tn(grad_attn, mixed[:, rows_at((h + other) % nh, cp)])
        if other:
            core_send[other - 1, 3] = sums.astype(BF16)
            core_copy(3, other).start()
        else:
            w_half[3] = sums
    grad_mixed[...] = nn(grad_attn, w_full[3]).astype(BF16)
    half_sum(3, w_half[3])
    for k in range(1, nd):
        band_copy(k, 3).start()

    def send_mix(c):
        wait_part(c, *value_flow)
        scatter(c, values, None, mix_own, *mix_flow)
        if c:
            relay(c - 1, *mix_flow)

    for c in range(parts // 2):
        send_mix(c)

    def attend_back(pair):
        columns = rows_at(pair, 2 * HEAD_DIM)
        q_pair, k_pair, v_pair = (qkv[i, :, columns] for i in range(3))
        g_pair = grad_mixed[:, columns]
        dq, dk, dv = [], [], []
        for side in range(2):
            weights = probs[pair * 2 + side]
            soft = weights.astype(F32)
            g_own = jnp.where(halves[side], g_pair, jnp.zeros_like(g_pair))
            grad_soft = nt(g_own, v_pair)
            inner = jnp.sum(soft * grad_soft, -1, keepdims=True)
            grad_scores = (soft * (grad_soft - inner)).astype(BF16)
            dq.append(nn(grad_scores, k_pair))
            dk.append(tn(grad_scores, q_pair))
            dv.append(tn(weights, g_pair))
        grad_qkv[0, :, columns] = (jnp.where(halves[0], dq[0], dq[1]) * scale).astype(BF16)
        grad_qkv[1, :, columns] = (jnp.where(halves[0], dk[0], dk[1]) * scale).astype(BF16)
        grad_qkv[2, :, columns] = jnp.where(halves[0], dv[0], dv[1]).astype(BF16)

    unit_one, factor_one = normalize(jnp.concatenate([x_ref[...].astype(F32), zeros], 0))
    normed_one = (unit_one * gain_one_ref[...]).astype(BF16)
    core_pairs = cp // (2 * HEAD_DIM)
    for other in [*range(1, nh), 0]:
        core = (h + other) % nh
        for q in range(core_pairs):
            attend_back(core * core_pairs + q)
        for i in range(3):
            sums = tn(normed_one, grad_qkv[i, :, rows_at(core, cp)])
            if other:
                core_send[other - 1, i] = sums.astype(BF16)
                core_copy(i, other).start()
            else:
                half_sum(i, sums)
        if other == nh - 1:
            send_mix(2)
    for i in range(3):
        for k in range(1, nd):
            band_copy(k, i).start()
    send_mix(3)

    grad_one = jnp.zeros((pad, width), F32)
    for i in range(3):
        grad_one = grad_one + nt(grad_qkv[i], w_full[i])
    grad_one = jnp.where(row_valid, grad_one, 0.0)
    grad_input, gain_one = norm_back(grad_one, unit_one, factor_one, gain_one_ref[...])
    grad_input_out[...] = (part_own[...] + grad_input)[0 : sz.rows].astype(BF16)

    small[...] = jnp.zeros_like(small)
    small[0:1, :] = gain_one
    small[1:2, :] = gain_two
    small[2:3, 0:128] = peak_at[0:1, :]
    peak_row = iota(small.shape, 0) == 2

    def join(a, b):
        return jnp.where(peak_row, jnp.maximum(a, b), a + b)

    small_copies = []
    for other in range(1, nh):
        device, n = (d, (h + other) % nh, z), 2 * (other - 1)
        small_copies += [
            remote(small, small_core.at[other - 1], sc_s.at[n], sc_r.at[n], device),
            remote(rt, rt_core.at[other - 1], sc_s.at[n + 1], sc_r.at[n + 1], device),
        ]
    for copy in small_copies:
        copy.start()
    for copy in small_copies:
        copy.wait()
    for other in range(1, nh):
        small[...] = join(small[...], small_core[other - 1])
        rt[...] = rt[...] + rt_core[other - 1]
    small_send[0] = small[...]
    small_copies = []
    for k in range(1, nd):
        to = (d + k) % nd
        small_copies += [
            remote(small_send.at[0], small_x.at[k - 1], sx_s.at[0], sx_r.at[0], (to, h, z)),
            remote(rt.at[:, rows_at(to, band)], rt_x.at[k - 1], sx_s.at[1], sx_r.at[1], (to, h, z)),
        ]
    for copy in small_copies:
        copy.start()

    def line_piece(i, j):
        to = at.next_z(j)
        return remote(line_send.at[i, rows_at(to, rp), :], line_recv.at[j - 1, i], gl_s.at[i], gl_r.at[i], at.line(to))

    for i in (3, 0, 1, 2):
        drain(gx_s.at[i], gx_r.at[i], band_recv.at[:, i], band_recv.at[:, i])
        sums = w_half[i, rows_at(d, band), :]
        for k in range(1, nd):
            sums = sums + band_recv[k - 1, i].astype(F32)
        w_half[i, 0:band, :] = sums
        line_send[i] = sums.astype(BF16)
        for j in range(1, nz):
            line_piece(i, j).start()
    drain(sx_s.at[0], sx_r.at[0], small_x, small_x)
    drain(sx_s.at[1], sx_r.at[1], rt_x, rt_x)
    router_sum = rt[:, rows_at(d, band)]
    for k in range(1, nd):
        small[...] = join(small[...], small_x[k - 1])
        router_sum = router_sum + rt_x[k - 1]
    rt_z[nz - 1] = router_sum
    small_send[1] = small[...]
    for j in range(1, nz):
        device = at.line(at.next_z(j))
        remote(small_send.at[1], small_z.at[j - 1], gl_s.at[4], gl_r.at[4], device).start()
        remote(rt_z.at[nz - 1], rt_z.at[j - 1], gl_s.at[5], gl_r.at[5], device).start()

    mix = gathered(mix_own, *mix_flow)
    output_out[...] = (hidden_at[...] + mix)[0 : sz.rows].astype(BF16)

    for i in range(4):
        drain(gl_s.at[i], gl_r.at[i], line_recv.at[:, i], line_recv.at[:, i])
    for n, landed in ((4, small_z), (5, rt_z.at[pl.ds(0, nz - 1)])):
        drain(gl_s.at[n], gl_r.at[n], landed, landed)
    totals = small[...]
    router_sum = rt_z[nz - 1]
    for j in range(1, nz):
        totals = join(totals, small_z[j - 1])
        router_sum = router_sum + rt_z[j - 1]
    gain_one_out[...] = totals[0:1]
    gain_two_out[...] = totals[1:2]
    rr = sz.router_rows
    own_router = router_sum[:, 0:rr]
    for i in range(1, nh):
        own_router = jnp.where(h == i, router_sum[:, i * rr : (i + 1) * rr], own_router)
    router_out[...] = own_router
    tau = tau_ref[...]
    factor = jnp.sqrt(tau / jnp.maximum(totals[2:3, 0:HEADS], tau))
    column = iota((1, cp), 1) // HEAD_DIM + h * (cp // HEAD_DIM)
    scale_row = jnp.zeros((1, cp), F32)
    for head in range(HEADS):
        scale_row = jnp.where(column == head, factor[:, head : head + 1], scale_row)
    for i in range(2):
        clipped_out[i] = (w_qkv_ref[i].astype(F32) * scale_row).astype(BF16)
    for i in range(4):
        sums = w_half[i, rows_at(z, rp), :]
        for j in range(1, nz):
            sums = sums + line_recv[j - 1, i].astype(F32)
        if i < 3:
            qkv_out[i] = sums
        else:
            out_out[...] = sums
    for copy in stores:
        copy.wait()


def finish_kernel(sz, *refs):
    sources, results, held = refs[0:10], refs[10:20], refs[20:28]
    halves_in, full_out, in_sems, out_sems, small_in, small_out = refs[28:]
    pieces = [(i, e) for e in range(sz.own) for i in range(2)]
    loads = [pltpu.make_async_copy(sources[8 + i].at[e], halves_in.at[i, e], in_sems.at[i, e]) for i, e in pieces]
    stores = [pltpu.make_async_copy(full_out.at[i, e], results[8 + i].at[e], out_sems.at[i, e]) for i, e in pieces]
    small_loads = [pltpu.make_async_copy(sources[n], held[n], small_in.at[n]) for n in range(8)]
    small_stores = [pltpu.make_async_copy(held[n], results[n], small_out.at[n]) for n in range(8)]
    for copy in loads + small_loads:
        copy.start()
    for (i, e), load, store in zip(pieces, loads, stores):
        load.wait()
        full_out[i, e] = halves_in[i, e].astype(F32)
        store.start()
    for load, store in zip(small_loads, small_stores):
        load.wait()
        store.start()
    for copy in stores + small_stores:
        copy.wait()


def fast_body(
    sz, inputs, cotangent, routes, gain_attn, gain_expert, tau, w_qkv, w_out_attn, w_router, w_in, w_out
):
    ng, nz, nd, nh, pad, width, own = sz.groups, sz.nt, sz.nd, sz.nh, sz.pad, sz.width, sz.own
    rp, cp, band, parts, block = sz.row_piece, sz.col_piece, sz.band, sz.parts, sz.block
    many, hidden = ng * sz.cap, sz.hidden
    on_chip, anywhere = pl.BlockSpec(memory_space=pltpu.VMEM), pl.BlockSpec(memory_space=pltpu.HBM)

    def shape(dims, dtype):
        return jax.ShapeDtypeStruct(dims, dtype)

    def half(*dims):
        return pltpu.VMEM(dims, BF16)

    def full(*dims):
        return pltpu.VMEM(dims, F32)

    def pair(*dims):
        return [pltpu.SemaphoreType.DMA(dims)] * 2

    slot_buffer = half(ng, sz.group_slots, width)
    line_buffer = half(nz - 1, pad, width)
    quarter_dims = (ng, own * (sz.cap // nz), width // parts)
    quarter_buffer, few = half(*quarter_dims), ng * own * (sz.cap // nz)
    rr = sz.router_rows
    smalls = (
        shape(inputs.shape, BF16), shape(inputs.shape, BF16), shape((1, width), F32), shape((1, width), F32),
        shape((3, rp, cp), F32), shape((rp, cp), F32), shape((sz.experts, rr), F32), shape((2, rp, cp), BF16),
    )
    packed = pl.pallas_call(
        functools.partial(block_kernel, sz),
        out_shape=(*smalls, shape(w_in.shape, BF16), shape(w_out.shape, BF16)),
        in_specs=[on_chip] * 9 + [anywhere] * 2,
        out_specs=(on_chip,) * 8 + (anywhere,) * 2,
        scratch_shapes=[
            half(4, rp, cp), half(4, width, width), half(sz.experts, 128), half(ng, sz.experts, 128),
            half(sz.experts, width), full(8, block), full(block, 128), half(sz.slots, block), half(block, sz.slots), half(block, few),
            half(block, width), half(block, width), *[slot_buffer] * 6,
            half(nz, *quarter_dims), half(nz - 1, *quarter_dims), quarter_buffer,
            quarter_buffer,
            half(own, width, hidden), half(own, hidden, width), half(own, many, hidden), half(own, many, hidden),
            full(own, many, hidden), half(own, hidden, width),
            full(sz.experts, 128), full(ng, 8, 128), full(sz.experts, block), full(8, many),
            full(ng, 8, 128), full(sz.experts, 128),
            half(3, pad, width), half(HEADS, pad, pad), half(pad, width), full(pad, width), full(8, 128),
            full(block, width), full(pad, width), line_buffer, half(nz, pad, width), full(pad, width), line_buffer,
            half(nz, pad, width),
            half(pad, width), half(3, pad, width), half(nh - 1, 4, width, cp), half(nh - 1, 4, width, cp),
            full(4, width, cp), half(4, width, cp), half(nd - 1, 4, band, cp), half(4, band, cp),
            half(nz - 1, 4, rp, cp),
            full(8, width), full(2, 8, width), full(nh - 1, 8, width), full(nd - 1, 8, width), full(nz - 1, 8, width),
            full(sz.experts, width), full(nh - 1, sz.experts, width), full(nd - 1, sz.experts, band),
            full(nz, sz.experts, band),
            *pair(1), *pair(nd - 1), *pair(nh - 1), *pair(1), *pair(parts), *pair(parts), *pair(parts), *pair(parts),
            *pair(1), *pair(own), *pair(parts), *pair(parts), *pair(1), *pair(parts), *pair(parts), *pair(4 * (nh - 1)),
            *pair(4), *pair(6), *pair(2 * (nh - 1)), *pair(2), *pair(1), *pair(1),
            *pair(parts, 2),
            pltpu.SemaphoreType.DMA((3 + own,)),
        ],
        compiler_params=pltpu.CompilerParams(collective_id=0, has_side_effects=True, vmem_limit_bytes=62 * 2**20),
        name="block",
    )(
        inputs, cotangent, routes.T, gain_attn[None, :], gain_expert[None, :], w_qkv, w_out_attn.T, w_router.T,
        tau[None, :], w_in, w_out,
    )

    both, dma = (2, *w_in.shape), pltpu.SemaphoreType.DMA
    output, grad_input, gain_one, gain_two, grad_qkv, grad_out, grad_router, clipped, grad_first, grad_second = (
        pl.pallas_call(
            functools.partial(finish_kernel, sz),
            out_shape=(*smalls, shape(w_in.shape, F32), shape(w_out.shape, F32)),
            in_specs=[anywhere] * 10,
            out_specs=(anywhere,) * 10,
            scratch_shapes=[
                *[pltpu.VMEM(x.shape, x.dtype) for x in smalls], half(*both), full(*both), dma((2, own)), dma((2, own)),
                dma((8,)), dma((8,)),
            ],
            compiler_params=pltpu.CompilerParams(vmem_limit_bytes=62 * 2**20),
            name="finish",
        )(*packed)
    )
    return (
        output, grad_input, gain_one[0], gain_two[0], grad_qkv, grad_out.T, grad_router.T, grad_first, grad_second,
        clipped,
    )


def gelu_tanh(inputs):
    return (
        0.5
        * inputs
        * (1.0 + jnp.tanh(0.7978845608028654 * (inputs + 0.044715 * inputs * inputs * inputs)))
    )


def unit_and_factor(inputs):
    centered = inputs - jnp.mean(inputs, -1, keepdims=True)
    factor = lax.rsqrt(jnp.mean(centered * centered, -1, keepdims=True) + 1e-06)
    return (centered * factor, factor)


def general_norm_back(grad_norm, unit_rows, factor, gain):
    grad, gain_row = norm_back(grad_norm, unit_rows, factor, gain)
    return grad, gain_row[0]


def attn_forward(block_parts):
    queries, key_rows, value_rows = block_parts
    scores = jnp.einsum(
        "bhqd,bhkd->bhqk", queries, key_rows, preferred_element_type=jnp.float32
    ) * HEAD_DIM ** (-0.5)
    row_peak = jnp.max(scores, -1, keepdims=True)
    exponent = jnp.exp(scores - row_peak)
    summed = jnp.sum(exponent, -1, keepdims=True)
    soft_weights = (exponent / summed).astype(jnp.bfloat16)
    mixed = jnp.einsum(
        "bhqk,bhkd->bhqd", soft_weights, value_rows, preferred_element_type=jnp.float32
    ).astype(jnp.bfloat16)
    return (mixed, (row_peak + jnp.log(summed))[..., 0], jnp.max(row_peak, axis=(0, 2, 3)))


def attn_backward(block_parts):
    queries, key_rows, value_rows, grad_mixed, log_total = block_parts
    score_scale = HEAD_DIM ** (-0.5)
    scores = (
        jnp.einsum("bhqd,bhkd->bhqk", queries, key_rows, preferred_element_type=jnp.float32)
        * score_scale
    )
    soft_weights = jnp.exp(scores - log_total[..., None])
    grad_soft = jnp.einsum(
        "bhqd,bhkd->bhqk", grad_mixed, value_rows, preferred_element_type=jnp.float32
    )
    inner_sum = jnp.sum(soft_weights * grad_soft, -1, keepdims=True)
    grad_scores = (soft_weights * (grad_soft - inner_sum)).astype(jnp.bfloat16)
    grad_query = (
        jnp.einsum("bhqk,bhkd->bhqd", grad_scores, key_rows, preferred_element_type=jnp.float32)
        * score_scale
    ).astype(jnp.bfloat16)
    grad_key = (
        jnp.einsum("bhqk,bhqd->bhkd", grad_scores, queries, preferred_element_type=jnp.float32)
        * score_scale
    ).astype(jnp.bfloat16)
    grad_value = jnp.einsum(
        "bhqk,bhqd->bhkd",
        soft_weights.astype(jnp.bfloat16),
        grad_mixed,
        preferred_element_type=jnp.float32,
    ).astype(jnp.bfloat16)
    return (grad_query, grad_key, grad_value)


def general_body(
    inputs, cotangent, routes, gain_attn, gain_expert, tau, w_qkv, w_out_attn, w_router, w_in, w_out
):
    row_count, width = inputs.shape
    n_dp = lax.axis_size("dp")
    n_heads = lax.axis_size("heads")
    n_tensor = lax.axis_size("tensor")
    row_piece = w_qkv.shape[1]
    col_piece = w_qkv.shape[2]
    own_heads = col_piece // HEAD_DIM
    head_start = lax.axis_index("heads") * col_piece
    x_float = inputs.astype(jnp.float32)
    unit_one, factor_one = unit_and_factor(x_float)
    normed_one = (unit_one * gain_attn).astype(jnp.bfloat16)
    stack_qkv, stack_out = (
        lax.all_gather(w_qkv[None], ("dp", "heads", "tensor"), axis=0, tiled=True),
        lax.all_gather(w_out_attn[None], ("dp", "heads", "tensor"), axis=0, tiled=True),
    )
    full_qkv = (
        stack_qkv.reshape(n_dp, n_heads, n_tensor, 3, row_piece, col_piece)
        .transpose(3, 0, 2, 4, 1, 5)
        .reshape(3, width, width)
    )
    full_out = (
        stack_out.reshape(n_dp, n_heads, n_tensor, col_piece, row_piece)
        .transpose(1, 3, 0, 2, 4)
        .reshape(width, width)
    )
    proj_w = lax.dynamic_slice_in_dim(full_qkv, head_start, col_piece, 2)
    attn_w = lax.dynamic_slice_in_dim(full_out, head_start, col_piece, 0)
    normed_all = lax.all_gather(normed_one, "heads", axis=0, tiled=True)
    head_cols = attn_w.shape[0]
    local_heads = head_cols // HEAD_DIM
    joined_w = jnp.concatenate([proj_w[0], proj_w[1], proj_w[2]], 1)
    projected = jnp.dot(normed_all, joined_w, preferred_element_type=jnp.float32).astype(
        jnp.bfloat16
    )
    images = normed_all.shape[0] // SEQ
    per_block = 4 if images % 4 == 0 else 3 if images % 3 == 0 else 2 if images % 2 == 0 else 1
    block_shape = (images // per_block, per_block, SEQ, local_heads, HEAD_DIM)

    def to_blocks(row_matrix):
        return row_matrix.reshape(block_shape).transpose(0, 1, 3, 2, 4)

    def from_blocks(block_array):
        return block_array.transpose(0, 1, 3, 2, 4).reshape(-1, head_cols)

    queries = to_blocks(projected[:, :head_cols])
    key_rows = to_blocks(projected[:, head_cols : 2 * head_cols])
    value_rows = to_blocks(projected[:, 2 * head_cols :])
    mixed, log_total, head_peaks = lax.map(attn_forward, (queries, key_rows, value_rows))
    mixed_rows = from_blocks(mixed)
    block_peak = jnp.max(head_peaks, 0)
    attn_out = lax.psum_scatter(
        jnp.dot(mixed_rows, attn_w, preferred_element_type=jnp.float32),
        "heads",
        scatter_dimension=0,
        tiled=True,
    )
    peak_full = lax.dynamic_update_slice_in_dim(
        jnp.full((HEADS,), -1e30, jnp.float32), block_peak, lax.axis_index("heads") * local_heads, 0
    )
    hidden = x_float + attn_out
    peak_all = lax.pmax(peak_full, ("dp", "heads", "tensor"))
    peak_logit = lax.dynamic_slice_in_dim(
        peak_all, lax.axis_index("heads") * own_heads, own_heads, 0
    )
    unit_two, factor_two = unit_and_factor(hidden)
    normed_two = (unit_two * gain_expert).astype(jnp.bfloat16)
    group_rows, group_cot = (
        lax.all_gather(normed_two, "tensor", axis=0, tiled=True),
        lax.all_gather(cotangent, "tensor", axis=0, tiled=True),
    )
    first_w, second_w, router_w = (
        lax.all_gather(w_in, ("dp", "heads"), axis=0, tiled=True),
        lax.all_gather(w_out, ("dp", "heads"), axis=0, tiled=True),
        lax.all_gather(w_router, ("dp", "heads"), axis=0, tiled=True),
    )
    logits = jnp.dot(group_rows, router_w, preferred_element_type=jnp.float32)
    chosen = jnp.take_along_axis(logits, routes, 1)
    exponent = jnp.exp(chosen - jnp.max(chosen, -1, keepdims=True))
    gate_values = exponent / jnp.sum(exponent, -1, keepdims=True)
    group_count = routes.shape[0]
    experts = router_w.shape[1]
    capacity = (group_count * 5 // (16 * experts) + 1) * 8
    flat_ids = routes.reshape(-1)
    ordering = jnp.argsort(flat_ids, stable=True)
    sorted_ids = flat_ids[ordering]
    counts = jnp.sum(
        (flat_ids[:, None] == jnp.arange(experts, dtype=jnp.int32)[None, :]).astype(jnp.int32), 0
    )
    expert_ids = jnp.arange(experts, dtype=jnp.int32)
    starts = jnp.sum(jnp.where(expert_ids[None, :] < expert_ids[:, None], counts[None, :], 0), 1)
    slot_rank = jnp.arange(2 * group_count, dtype=jnp.int32) - starts[sorted_ids]
    slot_table = (
        jnp.full((experts * capacity,), 2 * group_count, jnp.int32)
        .at[sorted_ids * capacity + slot_rank]
        .set(ordering)
    )
    slot_token = slot_table // 2
    padded_rows = jnp.concatenate([group_rows, jnp.zeros((1, width), jnp.bfloat16)], 0)
    slot_in = padded_rows[slot_token].reshape(experts, capacity, width)
    slot_gate = jnp.concatenate([gate_values.reshape(-1), jnp.zeros((1,), jnp.float32)], 0)[
        slot_table
    ]
    pre_gelu = jnp.einsum("ecd,edf->ecf", slot_in, first_w, preferred_element_type=jnp.float32)
    activated = gelu_tanh(pre_gelu).astype(jnp.bfloat16)
    slot_out = jnp.einsum(
        "ecf,efd->ecd", activated, second_w, preferred_element_type=jnp.float32
    ).reshape(-1, width)
    partial_value = (
        jnp.zeros((group_count + 1, width), jnp.float32)
        .at[slot_token]
        .add(slot_gate[:, None] * slot_out)[:group_count]
    )
    expert_mix = lax.psum_scatter(
        partial_value.astype(jnp.bfloat16), "tensor", scatter_dimension=0, tiled=True
    ).astype(jnp.float32)
    output = (hidden + expert_mix).astype(jnp.bfloat16)
    padded_cot = jnp.concatenate([group_cot, jnp.zeros((1, width), jnp.bfloat16)], 0)
    slot_cot = padded_cot[slot_token].astype(jnp.float32)
    grad_slot_out = (
        (slot_gate[:, None] * slot_cot).astype(jnp.bfloat16).reshape(experts, capacity, width)
    )
    gate_part = (
        jnp.zeros((2 * group_count + 1,), jnp.float32)
        .at[slot_table]
        .add(jnp.sum(slot_cot * slot_out, -1))[: 2 * group_count]
        .reshape(group_count, 2)
    )
    grad_act = jnp.einsum(
        "ecd,efd->ecf", grad_slot_out, second_w, preferred_element_type=jnp.float32
    )
    grad_pre = jax.vjp(gelu_tanh, pre_gelu)[1](grad_act)[0].astype(jnp.bfloat16)
    grad_first = jnp.einsum("ecd,ecf->edf", slot_in, grad_pre, preferred_element_type=jnp.float32)
    grad_second = jnp.einsum(
        "ecf,ecd->efd", activated, grad_slot_out, preferred_element_type=jnp.float32
    )
    grad_slots = jnp.einsum(
        "ecf,edf->ecd", grad_pre, first_w, preferred_element_type=jnp.float32
    ).reshape(-1, width)
    grad_part = (
        jnp.zeros((group_count + 1, width), jnp.float32)
        .at[slot_token]
        .add(grad_slots)[:group_count]
    )
    grad_normed_two, grad_gates = (
        lax.psum_scatter(
            grad_part.astype(jnp.bfloat16), "tensor", scatter_dimension=0, tiled=True
        ).astype(jnp.float32),
        lax.psum_scatter(
            gate_part.astype(jnp.bfloat16), "tensor", scatter_dimension=0, tiled=True
        ).astype(jnp.float32),
    )
    shard_first, shard_second = (
        lax.psum_scatter(
            grad_first.astype(jnp.bfloat16), ("dp", "heads"), scatter_dimension=0, tiled=True
        ).astype(jnp.float32),
        lax.psum_scatter(
            grad_second.astype(jnp.bfloat16), ("dp", "heads"), scatter_dimension=0, tiled=True
        ).astype(jnp.float32),
    )
    offset = lax.axis_index("tensor") * row_count
    local_gates = lax.dynamic_slice_in_dim(gate_values, offset, row_count, 0)
    local_routes = lax.dynamic_slice_in_dim(routes, offset, row_count, 0)
    grad_chosen = local_gates * (grad_gates - jnp.sum(local_gates * grad_gates, -1, keepdims=True))
    columns = jnp.arange(experts, dtype=jnp.int32)[None, :]
    grad_logits = (
        jnp.where(local_routes[:, 0:1] == columns, grad_chosen[:, 0:1], 0.0)
        + jnp.where(local_routes[:, 1:2] == columns, grad_chosen[:, 1:2], 0.0)
    ).astype(jnp.bfloat16)
    grad_normed_two = grad_normed_two + jnp.einsum(
        "re,de->rd", grad_logits, router_w, preferred_element_type=jnp.float32
    )
    router_term = jnp.einsum(
        "rd,re->de", normed_two, grad_logits, preferred_element_type=jnp.float32
    )
    grad_hidden_norm, gain_two_term = general_norm_back(grad_normed_two, unit_two, factor_two, gain_expert)
    grad_hidden = cotangent.astype(jnp.float32) + grad_hidden_norm
    grad_attn = lax.all_gather(grad_hidden.astype(jnp.bfloat16), "heads", axis=0, tiled=True)
    grad_mixed = jnp.einsum(
        "rd,cd->rc", grad_attn, attn_w, preferred_element_type=jnp.float32
    ).astype(jnp.bfloat16)
    out_term = jnp.einsum("rc,rd->cd", mixed_rows, grad_attn, preferred_element_type=jnp.float32)
    grad_query, grad_key, grad_value = lax.map(
        attn_backward, (queries, key_rows, value_rows, to_blocks(grad_mixed), log_total)
    )
    grad_proj = jnp.concatenate(
        [from_blocks(grad_query), from_blocks(grad_key), from_blocks(grad_value)], 1
    )
    grad_normed_one = lax.psum_scatter(
        jnp.einsum("rc,dc->rd", grad_proj, joined_w, preferred_element_type=jnp.float32).astype(
            jnp.bfloat16
        ),
        "heads",
        scatter_dimension=0,
        tiled=True,
    ).astype(jnp.float32)
    proj_term = jnp.einsum("rd,rc->dc", normed_all, grad_proj, preferred_element_type=jnp.float32)
    proj_stack = jnp.stack(
        [
            proj_term[:, :head_cols],
            proj_term[:, head_cols : 2 * head_cols],
            proj_term[:, 2 * head_cols :],
        ],
        0,
    )
    whole_proj = lax.dynamic_update_slice_in_dim(
        jnp.zeros((3, width, width), jnp.float32), proj_stack, head_start, 2
    )
    whole_out = lax.dynamic_update_slice_in_dim(
        jnp.zeros((width, width), jnp.float32), out_term, head_start, 0
    )
    send_qkv = (
        whole_proj.reshape(3, n_dp, n_tensor, row_piece, n_heads, col_piece)
        .transpose(1, 4, 2, 0, 3, 5)
        .reshape(-1, 3, row_piece, col_piece)
    )
    send_out = (
        whole_out.reshape(n_heads, col_piece, n_dp, n_tensor, row_piece)
        .transpose(2, 0, 3, 1, 4)
        .reshape(-1, col_piece, row_piece)
    )
    shard_proj, shard_attn = (
        lax.psum_scatter(send_qkv, ("dp", "heads", "tensor"), scatter_dimension=0, tiled=True),
        lax.psum_scatter(send_out, ("dp", "heads", "tensor"), scatter_dimension=0, tiled=True),
    )
    grad_input_norm, gain_one_term = general_norm_back(grad_normed_one, unit_one, factor_one, gain_attn)
    grad_input = (grad_hidden + grad_input_norm).astype(jnp.bfloat16)
    gain_one_grad, gain_two_grad, router_all = lax.psum(
        (gain_one_term, gain_two_term, router_term), ("dp", "heads", "tensor")
    )
    router_grad = lax.dynamic_slice_in_dim(
        router_all, lax.axis_index(("dp", "heads")) * w_router.shape[0], w_router.shape[0], 0
    )
    local_tau = lax.dynamic_slice_in_dim(tau, lax.axis_index("heads") * own_heads, own_heads, 0)
    clip_factor = jnp.sqrt(local_tau / jnp.maximum(peak_logit, local_tau))
    clipped = (w_qkv[:2].astype(jnp.float32) * jnp.repeat(clip_factor, HEAD_DIM)).astype(
        jnp.bfloat16
    )
    return (
        output,
        grad_input,
        gain_one_grad,
        gain_two_grad,
        shard_proj[0],
        shard_attn[0],
        router_grad,
        shard_first,
        shard_second,
        clipped,
    )


def body(*args):
    inputs, _, routes, _, _, _, w_qkv, _, w_router, w_in, _ = args
    sz = Sizes(
        lax.axis_size("dp"), lax.axis_size("heads"), lax.axis_size("tensor"), inputs, routes, w_qkv, w_router, w_in
    )
    if sz.fits():
        return fast_body(sz, *args)
    return general_body(*args)


def solution(mesh):
    return jax.shard_map(
        body,
        mesh=mesh,
        in_specs=(
            P(("dp", "heads", "tensor"), None),
            P(("dp", "heads", "tensor"), None),
            P(("dp", "heads"), None),
            P(),
            P(),
            P(),
            P(None, ("dp", "tensor"), "heads"),
            P("heads", ("dp", "tensor")),
            P(("dp", "heads"), None),
            P(("dp", "heads"), None, "tensor"),
            P(("dp", "heads"), "tensor", None),
        ),
        out_specs=(
            P(("dp", "heads", "tensor"), None),
            P(("dp", "heads", "tensor"), None),
            P(),
            P(),
            P(None, ("dp", "tensor"), "heads"),
            P("heads", ("dp", "tensor")),
            P(("dp", "heads"), None),
            P(("dp", "heads"), None, "tensor"),
            P(("dp", "heads"), "tensor", None),
            P(None, ("dp", "tensor"), "heads"),
        ),
        check_vma=False,
    )
```

```python
import functools
import jax
import jax.numpy as jnp
from jax import lax
from jax.experimental import pallas as pl
from jax.experimental.pallas import tpu as pltpu
from jax.sharding import PartitionSpec as P

HEADS = 8
HEAD_DIM = 64
SEQ = 197
F32 = jnp.float32
BF16 = jnp.bfloat16
MESH = pl.DeviceIdType.MESH
NEG = -1e30


class Sizes:
    def __init__(self, n_dp, n_heads, n_tensor, inputs, routes, w_qkv, w_router, w_in):
        self.nd, self.nh, self.nt = n_dp, n_heads, n_tensor
        self.groups = n_dp * n_heads
        self.rows, self.width = inputs.shape
        self.pad = -(-self.rows // 16) * 16
        self.block = self.pad * n_tensor
        self.block_rows = routes.shape[0]
        self.own = w_in.shape[0]
        self.hidden = w_in.shape[2]
        self.experts = self.own * self.groups
        self.cap = (self.block_rows * 5 // (16 * self.experts) + 1) * 8
        self.group_slots = self.own * self.cap
        self.slots = self.experts * self.cap
        self.row_piece, self.col_piece = w_qkv.shape[1], w_qkv.shape[2]
        self.band = self.row_piece * n_tensor
        self.router_rows = w_router.shape[0]
        self.parts = 4

    def fits(self):
        return (
            self.rows == SEQ
            and self.nt == 4
            and self.parts == 4
            and self.block_rows == self.rows * self.nt
            and self.cap == 64
            and self.experts == 32
            and self.group_slots % 128 == 0
            and self.col_piece % 128 == 0
            and self.row_piece % 16 == 0
            and self.router_rows % 16 == 0
            and self.own * self.groups * 4 == 128
            and self.width == HEADS * HEAD_DIM
            and self.block * self.width * 2 <= 2**20
            and self.own * self.width <= self.slots
            and self.hidden <= self.block
            and self.hidden == self.width
            and self.cap % (16 * self.nt) == 0
            and self.width // self.parts % 128 == 0
        )


def nn(a, b):
    return jnp.dot(a, b, preferred_element_type=F32)


def nt(a, b):
    return lax.dot_general(a, b, (((1,), (1,)), ((), ())), preferred_element_type=F32)


def tn(a, b):
    return lax.dot_general(a, b, (((0,), (0,)), ((), ())), preferred_element_type=F32)


def iota(shape, axis):
    return lax.broadcasted_iota(jnp.int32, shape, axis)


def normalize(rows):
    centered = rows - jnp.mean(rows, -1, keepdims=True)
    factor = lax.rsqrt(jnp.mean(centered * centered, -1, keepdims=True) + 1e-06)
    return centered * factor, factor


def norm_back(grad_norm, unit_rows, factor, gain):
    grad_hat = grad_norm * gain
    inner = (
        grad_hat
        - jnp.mean(grad_hat, -1, keepdims=True)
        - unit_rows * jnp.mean(grad_hat * unit_rows, -1, keepdims=True)
    )
    return factor * inner, jnp.sum(grad_norm * unit_rows, 0, keepdims=True)


def split_high_low(values):
    high = values.astype(BF16)
    low = (values - high.astype(F32)).astype(BF16)
    return jnp.concatenate([high, low], 0)


class Place:
    def __init__(self, sz):
        self.sz = sz
        self.d = lax.axis_index("dp")
        self.h = lax.axis_index("heads")
        self.z = lax.axis_index("tensor")
        self.group = self.d * sz.nh + self.h

    def plane(self, group):
        return (group // self.sz.nh, group % self.sz.nh, self.z)

    def line(self, z):
        return (self.d, self.h, z)

    def next_group(self, k):
        return (self.group + k) % self.sz.groups

    def next_z(self, j):
        return (self.z + j) % self.sz.nt

    def inner(self):
        return (self.z + 1) % 4 // 2

    def mates(self):
        return self.z + 1 - 2 * (self.z % 2), (self.z + 2) % 4, 3 - self.z

    def enter(self):
        sz = self.sz
        barrier = pltpu.get_barrier_semaphore()
        for k in range(1, sz.groups):
            pl.semaphore_signal(barrier, inc=1, device_id=self.plane(self.next_group(k)), device_id_type=MESH)
        for j in range(1, sz.nt):
            pl.semaphore_signal(barrier, inc=1, device_id=self.line(self.next_z(j)), device_id_type=MESH)
        pl.semaphore_wait(barrier, sz.groups + sz.nt - 2)


def remote(src, dst, send, recv, device):
    return pltpu.make_async_remote_copy(
        src_ref=src, dst_ref=dst, send_sem=send, recv_sem=recv, device_id=device, device_id_type=MESH
    )


def drain(send_sem, recv_sem, sent, landed):
    pltpu.make_async_copy(sent, sent, send_sem).wait()
    pltpu.make_async_copy(landed, landed, recv_sem).wait()


def route_table(sz, routes_ref, table):
    table[...] = jnp.full_like(table, -1.0)
    for z in range(sz.nt):
        table[0:2, z * sz.pad : z * sz.pad + sz.rows] = routes_ref[:, z * sz.rows : (z + 1) * sz.rows].astype(F32)


def block_kernel(
    sz, x_ref, cot_ref, routes_ref, gain_one_ref, gain_two_ref, w_qkv_ref, w_out_ref, w_router_ref, tau_ref, first_hbm,
    second_hbm, output_out, grad_input_out, gain_one_out, gain_two_out, qkv_out, out_out, router_out, clipped_out,
    grad_first_out, grad_second_out,
    w_own, w_full, router_own, router_full, router_t, route_rows, route_columns, select, select_t, select_qt,
    cot_block, rows_block, send_a, send_b, cot_slots, slots, grad_slots, values,
    grads_q, grads_line, grads_sum, grads_back, first, second, act, grad_pre, grad_act, grad_second,
    gate_send, gate_recv, gates_at, dgate_send, dgate_recv, dgate_rows,
    qkv, probs, mixed, hidden_at, peak_at, part, part_own, part_send, part_recv, mix_own, mix_send, mix_recv,
    grad_mixed, grad_qkv, core_send, core_recv, w_half, band_send, band_recv, line_send, line_recv,
    small, small_send, small_core, small_x, small_z, rt, rt_core, rt_x, rt_z,
    wz_s, wz_r, wx_s, wx_r, wc_s, wc_r, r_s, r_r, qz_s, qz_r, nz_s, nz_r, qa_s, qa_r, na_s, na_r, ga_s, ga_r,
    d0_s, d0_r, da_s, da_r, va_s, va_r, dg_s, dg_r, pz_s, pz_r, mz_s, mz_r, gc_s, gc_r, gx_s, gx_r, gl_s, gl_r,
    sc_s, sc_r, sx_s, sx_r, dl_s, dl_r, dq_s, dq_r, pr_r, mr_r,
    local_sem,
):
    at = Place(sz)
    d, h, z, me = at.d, at.h, at.z, at.group
    nd, nh, nz, ng = sz.nd, sz.nh, sz.nt, sz.groups
    band, rp, cp, pad, width = sz.band, sz.row_piece, sz.col_piece, sz.pad, sz.width
    many = ng * sz.cap
    parts, part_width = sz.parts, width // sz.parts

    def lanes(c):
        return pl.ds(c * part_width, part_width)

    def rows_at(n, size):
        return pl.ds(pl.multiple_of(n * size, size), size)

    own_block, own_columns = rows_at(z, pad), rows_at(h, cp)

    w_own[0:3] = w_qkv_ref[...]
    w_own[3] = w_out_ref[...]
    router_own[...] = jnp.zeros_like(router_own)
    router_own[:, 0 : sz.router_rows] = w_router_ref[...]
    cot_block[own_block] = jnp.concatenate(
        [cot_ref[...].astype(F32), jnp.zeros((pad - sz.rows, width), F32)], 0
    ).astype(BF16)

    part_recv[2] = jnp.zeros((pad, width), BF16)
    mix_recv[2] = jnp.zeros((pad, width), BF16)

    at.enter()

    w_rows = rows_at(d * nz + z, rp)
    others = pl.ds(0, ng - 1)

    def send_line(i):
        for j in range(1, nz):
            remote(
                w_own.at[i], w_full.at[i, w_rows, own_columns], wz_s.at[i], wz_r.at[i], at.line(at.next_z(j))
            ).start()

    def along(block, send_sems, recv_sems, c):
        place = block.at[own_block, lanes(c)]
        return [
            remote(place, place, send_sems.at[c], recv_sems.at[c], at.line(at.next_z(j)))
            for j in range(1, nz)
        ]

    def wait_along(block, send_sems, recv_sems, c):
        place = block.at[pl.ds(0, (nz - 1) * pad), lanes(c)]
        drain(send_sems.at[c], recv_sems.at[c], place, place)

    for i in range(3):
        send_line(i)
    for copy in along(cot_block, qz_s, qz_r, 0):
        copy.start()
    send_line(3)
    routers = [
        remote(router_own, router_full.at[me], r_s.at[0], r_r.at[0], at.plane(at.next_group(k)))
        for k in range(1, ng)
    ]
    for copy in routers:
        copy.start()
    loads = [
        pltpu.make_async_copy(first_hbm, first, local_sem.at[0]),
        pltpu.make_async_copy(second_hbm, second, local_sem.at[1]),
    ]
    for copy in loads:
        copy.start()
    w_full[:, w_rows, own_columns] = w_own[...]
    router_full[me] = router_own[...]

    def to_core(i, dp, other):
        place = w_full.at[i, rows_at(dp, band), own_columns]
        n = 4 * (other - 1) + i
        return remote(place, place, wc_s.at[n], wc_r.at[n], (d, (h + other) % nh, z))

    def send_band(i):
        landed = w_full.at[i, pl.ds(0, (nz - 1) * rp), own_columns]
        drain(wz_s.at[i], wz_r.at[i], landed, landed)
        place = w_full.at[i, rows_at(d, band), own_columns]
        for k in range(1, nd):
            remote(place, place, wx_s.at[i], wx_r.at[i], ((d + k) % nd, h, z)).start()
        for other in range(1, nh):
            to_core(i, d, other).start()

    def pass_on(i):
        landed = w_full.at[i, pl.ds(0, (nd - 1) * band), own_columns]
        drain(wx_s.at[i], wx_r.at[i], landed, landed)
        for k in range(1, nd):
            for other in range(1, nh):
                to_core(i, (d + k) % nd, other).start()

    def arrived(i):
        for other in range(1, nh):
            n, columns = 4 * (other - 1) + i, w_full.at[i, :, own_columns]
            drain(wc_s.at[n], wc_r.at[n], columns, columns)

    zeros = jnp.zeros((pad - sz.rows, width), F32)
    x_rows = jnp.concatenate([x_ref[...].astype(F32), zeros], 0)
    unit_one, _ = normalize(x_rows)
    normed_one = (unit_one * gain_one_ref[...]).astype(BF16)
    for i in range(3):
        send_band(i)

    route_table(sz, routes_ref, route_rows)
    route_a, route_b = route_rows[0:1, :], route_rows[1:2, :]
    expert = iota((sz.experts, sz.block), 0).astype(F32)
    named_a, named_b = route_a == expert, route_b == expert
    named = jnp.logical_or(named_a, named_b)
    before = (iota((sz.block, sz.block), 0) < iota((sz.block, sz.block), 1)).astype(BF16)
    rank = nn(named.astype(BF16), before) + expert * float(sz.cap)
    slot_a = jnp.sum(jnp.where(named_a, rank, 0.0), 0, keepdims=True)
    slot_b = jnp.sum(jnp.where(named_b, rank, 0.0), 0, keepdims=True)
    slot_a = jnp.where(route_a < 0.0, -1.0, slot_a)
    slot_b = jnp.where(route_b < 0.0, -1.0, slot_b)
    slot_pair = jnp.concatenate([slot_a, slot_b] * 64, 0)
    route_columns[...] = slot_pair.T

    def fill(g, carry):
        slot = iota((sz.group_slots, sz.block), 0).astype(F32) + (g * sz.group_slots).astype(F32)
        hit = jnp.logical_or(slot == slot_a, slot == slot_b)
        select[rows_at(g, sz.group_slots), :] = jnp.where(hit, 1.0, 0.0).astype(BF16)
        return carry

    lax.fori_loop(0, ng, fill, 0)

    quarter = sz.cap // nz
    few = ng * sz.own * quarter

    def quarter_slot(dims, axis):
        n = iota(dims, axis)
        return (n // quarter * sz.cap + z * quarter + n % quarter).astype(F32)

    def quarter_move(k, send, landing, send_sems, recv_sems):
        g = (me + k) % ng
        return remote(send.at[g], landing.at[me], send_sems.at[0], recv_sems.at[0], at.plane(g))

    def exchange(c, k, send, out, send_sems, recv_sems):
        g = (me + k) % ng
        return remote(
            send.at[g, :, lanes(c)], out.at[me, :, lanes(c)], send_sems.at[c], recv_sems.at[c], at.plane(g)
        )

    def dispatch(c, block, send, out, send_sems, recv_sems):
        def step(i, carry):
            k = ng - 1 - i
            g = (me + k) % ng
            send[g, :, lanes(c)] = nn(select[rows_at(g, sz.group_slots), :], block[:, lanes(c)]).astype(BF16)

            @pl.when(k > 0)
            def _():
                exchange(c, k, send, out, send_sems, recv_sems).start()

            return carry

        lax.fori_loop(0, ng, step, 0)
        out[me, :, lanes(c)] = send[me, :, lanes(c)]

    def start_part(c, *flow):
        def step(i, carry):
            exchange(c, ng - 1 - i, *flow).start()
            return carry

        lax.fori_loop(0, ng - 1, step, 0)

    def wait_part(c, send, out, send_sems, recv_sems):
        drain(send_sems.at[c], recv_sems.at[c], send.at[others, :, lanes(c)], out.at[others, :, lanes(c)])

    cot_flow = (send_a, cot_slots, qa_s, qa_r)
    row_flow = (send_b, slots, na_s, na_r)

    def send_cot(c):
        wait_along(cot_block, qz_s, qz_r, c)
        dispatch(c, cot_block, *cot_flow)

    send_band(3)
    for c in range(1, parts):
        for copy in along(cot_block, qz_s, qz_r, c):
            copy.start()
    pass_on(0)
    send_cot(0)
    pass_on(1)
    pass_on(2)

    for i in range(3):
        arrived(i)
        qkv[i] = nn(normed_one, w_full[i]).astype(BF16)
    pass_on(3)
    lane = iota((1, 2 * HEAD_DIM), 1)
    halves = (lane < HEAD_DIM, lane >= HEAD_DIM)
    key_valid = iota((1, pad), 1) < sz.rows
    row_valid = iota((pad, 1), 0) < sz.rows
    peak_lane = iota((1, 128), 1)
    peak_at[...] = jnp.full_like(peak_at, NEG)
    scale = HEAD_DIM ** (-0.5)

    def attend(pair, carry):
        columns = rows_at(pair, 2 * HEAD_DIM)
        q_pair, k_pair, v_pair = (qkv[i, :, columns] for i in range(3))
        sides = []
        for side in range(2):
            q_own = jnp.where(halves[side], q_pair, jnp.zeros_like(q_pair))
            scores = jnp.where(key_valid, nt(q_own, k_pair) * scale, NEG)
            row_peak = jnp.max(scores, -1, keepdims=True)
            exponent = jnp.exp(scores - row_peak)
            weights = (exponent / jnp.sum(exponent, -1, keepdims=True)).astype(BF16)
            head = pair * 2 + side
            probs[head] = weights
            sides.append(nn(weights, v_pair))
            peak = jnp.max(jnp.where(row_valid, row_peak, NEG), 0, keepdims=True)
            peak_at[0:1, :] = jnp.where(peak_lane == head, peak, peak_at[0:1, :])
        mixed[:, columns] = jnp.where(halves[0], sides[0], sides[1]).astype(BF16)
        return carry

    pairs = HEADS // 2
    sent = 1
    for turn in range(2):
        until = 1 + ((parts - 1) * (turn + 1)) // 2
        for c in range(sent, until):
            send_cot(c)
        sent = until
        lax.fori_loop(turn * pairs // 2, (turn + 1) * pairs // 2, attend, 0)

    arrived(3)
    hidden = x_rows + nt(mixed[...], w_full[3])
    hidden_at[...] = hidden
    unit_two, _ = normalize(hidden)
    rows_block[own_block] = jnp.where(row_valid, unit_two * gain_two_ref[...], 0.0).astype(BF16)
    for c in range(parts):
        for copy in along(rows_block, nz_s, nz_r, c):
            copy.start()

    def fill_t(i, carry):
        rows = rows_at(i, pad)
        slot = iota((pad, sz.slots), 1).astype(F32)
        hit = jnp.logical_or(slot == route_columns[rows, 0:1], slot == route_columns[rows, 1:2])
        select_t[rows, :] = jnp.where(hit, 1.0, 0.0).astype(BF16)
        some = quarter_slot((pad, few), 1)
        hit = jnp.logical_or(some == route_columns[rows, 0:1], some == route_columns[rows, 1:2])
        select_qt[rows, :] = jnp.where(hit, 1.0, 0.0).astype(BF16)
        return carry

    lax.fori_loop(0, nz, fill_t, 0)
    drain(r_s.at[0], r_r.at[0], router_full.at[others], router_full.at[others])
    for g in range(ng):
        router_t[:, g * sz.router_rows : (g + 1) * sz.router_rows] = router_full[g, :, 0 : sz.router_rows]

    def expert_rows(ref, e):
        return ref[:, rows_at(e, sz.cap), :].reshape(many, width)

    def send_gates():
        logits = jnp.where(named, nt(router_t[...], rows_block[...]), NEG)
        exponent = jnp.where(named, jnp.exp(logits - jnp.max(logits, 0, keepdims=True)), 0.0)
        total = jnp.sum(exponent, 0, keepdims=True)
        gates = exponent / jnp.where(total > 0.0, total, 1.0)
        gates_at[...] = gates
        by_slot = nt(split_high_low(gates), select[...])
        by_slot = by_slot[0 : sz.experts] + by_slot[sz.experts :]
        own_slot = iota((sz.experts, sz.slots), 1) // sz.cap == iota((sz.experts, sz.slots), 0)
        by_slot = jnp.where(own_slot, by_slot, 0.0)
        folded = by_slot[:, 0:128]
        for i in range(1, sz.slots // 128):
            folded = folded + by_slot[:, i * 128 : (i + 1) * 128]
        gate_send[...] = folded
        gate_copies = [
            remote(
                gate_send.at[rows_at(at.next_group(k) * sz.own // 8, 8)], gate_recv.at[me], ga_s.at[0], ga_r.at[0],
                at.plane(at.next_group(k)),
            )
            for k in range(1, ng)
        ]
        for copy in gate_copies:
            copy.start()
        gate_recv[me] = gate_send[rows_at(me * sz.own // 8, 8)]

    for c in range(parts):
        wait_along(rows_block, nz_s, nz_r, c)
        if c == parts - 1:
            send_gates()
        dispatch(c, rows_block, *row_flow)

    drain(ga_s.at[0], ga_r.at[0], gate_recv.at[others], gate_recv.at[others])
    def gate_of(e):
        turned = gate_recv[:, pl.ds(me * sz.own % 8 + e, 1), :].reshape(ng, 128).T
        columns = jnp.where((e % 2) == 1, turned[sz.cap : 2 * sz.cap], turned[0 : sz.cap])
        return jnp.concatenate([columns[:, s : s + 1] for s in range(ng)], 0)

    def weigh(e, carry):
        grad_act[e] = nt(expert_rows(cot_slots, e), second[e]) * gate_of(e)
        return carry

    for c in range(parts):
        wait_part(c, *cot_flow)
    for copy in loads:
        copy.wait()
    lax.fori_loop(0, sz.own, weigh, 0)
    for c in range(parts):
        wait_part(c, *row_flow)

    def first_piece(e, g):
        piece = (rows_at(e, sz.cap), lanes(1))
        return remote(
            send_a.at[(g, *piece)], grad_slots.at[(me, *piece)], d0_s.at[e], d0_r.at[e], at.plane(g)
        )

    def grads_piece(e, j):
        piece = (slice(None), rows_at(e, quarter), slice(None))
        return remote(
            grads_q.at[(at.next_z(j), *piece)], grads_line.at[(j - 1, *piece)], dl_s.at[0], dl_r.at[0],
            at.line(at.next_z(j)),
        )

    def expert_back(e, carry):
        half_rows = many // 2
        for part_at in range(2):
            some = slice(part_at * half_rows, (part_at + 1) * half_rows)
            groups = slice(part_at * ng // 2, (part_at + 1) * ng // 2)
            pre = nn(slots[groups, rows_at(e, sz.cap), :].reshape(half_rows, width), first[e])
            const, cubic = 0.7978845608028654, 0.044715
            square = pre * pre
            half = 0.5 * jnp.tanh(pre * (const + const * cubic * square)) + 0.5
            hidden_units = pre * half
            act[e, some] = hidden_units.astype(BF16)
            through = grad_act[e, some]
            dgate = nt(jnp.ones((8, sz.hidden), BF16), (hidden_units * through).astype(BF16))
            dgate_send[:, some] = jnp.where(iota((8, half_rows), 0) == e, dgate, dgate_send[:, some])
            slope = half * (1.0 + (1.0 - half) * (pre * (2.0 * const + 6.0 * const * cubic * square)))
            grads = (through * slope).astype(BF16)
            grad_pre[e, some] = grads
            spread = nt(grads, first[e]).astype(BF16).reshape(ng // 2, sz.cap, width)
            send_a[groups, rows_at(e, sz.cap), :] = spread
            for i in range(nz):
                grads_q[i, groups, rows_at(e, quarter), :] = spread[:, i * quarter : (i + 1) * quarter, 0:part_width]

        def step(i, carry):
            first_piece(e, (me + ng - 1 - i) % ng).start()
            return carry

        lax.fori_loop(0, ng - 1, step, 0)
        for j in range(1, nz):
            grads_piece(e, j).start()
        return carry

    dgate_send[...] = jnp.zeros_like(dgate_send)
    lax.fori_loop(0, sz.own, expert_back, 0)
    dgates = [
        remote(
            dgate_send.at[:, rows_at(at.next_group(k) * sz.cap // 128, 128)], dgate_recv.at[me], dg_s.at[0],
            dg_r.at[0], at.plane(at.next_group(k)),
        )
        for k in range(1, ng)
    ]
    for copy in dgates:
        copy.start()
    dgate_recv[me] = dgate_send[:, rows_at(me * sz.cap // 128, 128)]
    grad_flow = (send_a, grad_slots, da_s, da_r)
    value_flow = (send_b, values, va_s, va_r)
    for c in range(2, parts - 1):
        start_part(c, *grad_flow)
    grad_slots[me] = send_a[me]

    def expert_value(e, carry):
        value = nn(act[e], second[e])
        gated = (value * gate_of(e)).astype(BF16).reshape(ng, sz.cap, width)
        send_b[:, rows_at(e, sz.cap), :] = gated
        return carry

    lax.fori_loop(0, sz.own, expert_value, 0)
    values[me] = send_b[me]

    def quarter_total(own, line, sums):
        total = own[z].astype(F32)
        for j in range(1, nz):
            total = total + line[j - 1].astype(F32)
        sums[...] = total.astype(BF16)


    def weight_grads(e, carry):
        grad_value = (expert_rows(cot_slots, e).astype(F32) * gate_of(e)).astype(BF16)
        grad_second[e] = tn(act[e], grad_value).astype(BF16)
        select[rows_at(e, width), 0 : sz.hidden] = tn(expert_rows(slots, e), grad_pre[e]).astype(BF16)
        return carry

    drain(dg_s.at[0], dg_r.at[0], dgate_recv.at[others], dgate_recv.at[others])
    mine = iota((8, 128), 1) // sz.cap == me * sz.cap % 128 // sz.cap
    for g in range(ng):
        folded = jnp.where(mine, dgate_recv[g], 0.0)
        folded = folded + pltpu.roll(folded, 64, 1)
        dgate_rows[g * sz.own : (g + 1) * sz.own, :] = folded[0 : sz.own]
    spread = jnp.concatenate([dgate_rows[...]] * (sz.slots // 128), 1)
    own_slot = iota((sz.experts, sz.slots), 1) // sz.cap == iota((sz.experts, sz.slots), 0)
    dgate = nt(split_high_low(jnp.where(own_slot, spread, 0.0)), select_t[...])
    dgate = dgate[0 : sz.experts] + dgate[sz.experts :]
    gates = gates_at[...]
    dlogits = (dgate - gates * jnp.sum(dgate, 0, keepdims=True)).astype(BF16)
    rt[...] = nn(dlogits, rows_block[...])
    part[...] = tn(dlogits, router_t[...])

    inner = at.inner()
    beside, across, mirror = at.mates()

    def line_copy(c, slot, send, recv, send_sems, recv_sems, relay_sems, last):
        if slot < 2:
            return remote(
                send.at[slot, :, lanes(c)], recv.at[slot, :, lanes(c)], send_sems.at[c], recv_sems.at[c],
                at.line((beside, across)[slot]),
            )
        by_way = 1 - inner if c != last else 0
        to = mirror + by_way * (beside - mirror)
        return remote(
            send.at[2, :, lanes(c)], recv.at[2 + by_way, :, lanes(c)], send_sems.at[c], relay_sems.at[c, by_way], at.line(to)
        )

    def scatter(c, source, base, own, *flow):
        if source is grads_back:
            places, flat = select_qt, source[...].reshape(few, part_width)
        else:
            places, flat = select_t, source[:, :, lanes(c)].reshape(sz.slots, part_width)
        for slot, target in ((2, mirror), (1, across), (0, beside), (None, z)):
            tokens = rows_at(target, pad)
            sums = nn(places[tokens, :], flat)
            if base is not None:
                sums = sums + base[tokens, lanes(c)]
            if slot is None:
                own[:, lanes(c)] = sums
                continue
            flow[0][slot, :, lanes(c)] = sums.astype(BF16)
            if slot == 1 and c != flow[-1]:

                @pl.when(inner == 0)
                def _():
                    line_copy(c, 1, *flow).start()
            else:
                line_copy(c, slot, *flow).start()

    def relay(c, send, recv, send_sems, recv_sems, relay_sems, last):
        @pl.when(inner == 1)
        def _():
            landed = recv.at[3, :, lanes(c)]
            pltpu.make_async_copy(landed, landed, relay_sems.at[c, 1]).wait()
            send[1, :, lanes(c)] = (send[1, :, lanes(c)].astype(F32) + recv[3, :, lanes(c)].astype(F32)).astype(BF16)
            line_copy(c, 1, send, recv, send_sems, recv_sems, relay_sems, last).start()

    def gathered(own, send, recv, send_sems, recv_sems, relay_sems, last):
        for c in range(parts):
            drain(send_sems.at[c], recv_sems.at[c], send.at[:, :, lanes(c)], recv.at[pl.ds(0, 2), :, lanes(c)])

            @pl.when(inner == 1 if c != last else True)
            def _(c=c):
                landed = recv.at[2, :, lanes(c)]
                pltpu.make_async_copy(landed, landed, relay_sems.at[c, 0]).wait()

        sums = own[...]
        for slot in range(3):
            sums = sums + recv[slot].astype(F32)
        return sums

    part_flow = (part_send, part_recv, pz_s, pz_r, pr_r, parts - 1)
    mix_flow = (mix_send, mix_recv, mz_s, mz_r, mr_r, parts - 1)

    def wait_first(e, carry):
        piece = (others, rows_at(e, sz.cap), lanes(1))
        drain(d0_s.at[e], d0_r.at[e], send_a.at[piece], grad_slots.at[piece])
        return carry

    def exchange_quarters():
        drain(dl_s.at[0], dl_r.at[0], grads_line, grads_line)
        quarter_total(grads_q, grads_line, grads_sum)
        for copy in grads_moves:
            copy.start()
        start_part(parts - 1, *grad_flow)
        start_part(0, *value_flow)
        grads_back[me] = grads_sum[me]

    grads_moves = [quarter_move(k, grads_sum, grads_back, dq_s, dq_r) for k in range(1, ng)]
    order = [*range(1, parts - 1), 0, parts - 1]
    exchange_quarters()
    done = 0
    for turn, c in enumerate(order):
        if c == 0:
            drain(dq_s.at[0], dq_r.at[0], grads_back.at[others], grads_back.at[others])
        elif c == 1:
            lax.fori_loop(0, sz.own, wait_first, 0)
        else:
            wait_part(c, *grad_flow)
        if c == parts - 1:
            for i in range(1, parts):
                start_part(i, *value_flow)
        scatter(c, grads_back if c == 0 else grad_slots, part, part_own, *part_flow)
        until = sz.own * (turn + 1) // parts
        lax.fori_loop(done, until, weight_grads, 0)
        done = until
        if turn > 0:
            relay(order[turn - 1], *part_flow)
    stores = [
        pltpu.make_async_copy(grad_second, grad_second_out, local_sem.at[2]),
        *[
            pltpu.make_async_copy(
                select.at[e * width : (e + 1) * width, 0 : sz.hidden], grad_first_out.at[e], local_sem.at[3 + e]
            )
            for e in range(sz.own)
        ],
    ]
    for copy in stores:
        copy.start()

    def send_mix(c):
        wait_part(c, *value_flow)
        scatter(c, values, None, mix_own, *mix_flow)
        if c:
            relay(c - 1, *mix_flow)

    send_mix(0)
    unit_two, factor_two = normalize(hidden_at[...])
    grad_normed = jnp.where(row_valid, gathered(part_own, *part_flow), 0.0)
    grad_hidden, gain_two = norm_back(grad_normed, unit_two, factor_two, gain_two_ref[...])
    grad_hidden = jnp.concatenate([cot_ref[...].astype(F32), zeros], 0) + jnp.where(row_valid, grad_hidden, 0.0)
    part_own[...] = grad_hidden
    grad_attn = grad_hidden.astype(BF16)

    def core_copy(i, other):
        n = 4 * (other - 1) + i
        return remote(
            core_send.at[other - 1, i], core_recv.at[other - 1, i], gc_s.at[n], gc_r.at[n], (d, (h + other) % nh, z)
        )

    def half_sum(i, sums):
        for other in range(1, nh):
            core_copy(i, other).wait()
            sums = sums + core_recv[other - 1, i].astype(F32)
        w_half[i] = sums
        band_send[i] = sums.astype(BF16)

    def band_copy(k, i):
        to = (d + k) % nd
        return remote(
            band_send.at[i, rows_at(to, band), :], band_recv.at[k - 1, i], gx_s.at[i], gx_r.at[i], (to, h, z)
        )

    for other in [*range(1, nh), 0]:
        sums = tn(grad_attn, mixed[:, rows_at((h + other) % nh, cp)])
        if other:
            core_send[other - 1, 3] = sums.astype(BF16)
            core_copy(3, other).start()
        else:
            w_half[3] = sums
    grad_mixed[...] = nn(grad_attn, w_full[3]).astype(BF16)
    half_sum(3, w_half[3])
    for k in range(1, nd):
        band_copy(k, 3).start()

    for c in range(1, parts // 2):
        send_mix(c)

    def attend_back(pair):
        columns = rows_at(pair, 2 * HEAD_DIM)
        q_pair, k_pair, v_pair = (qkv[i, :, columns] for i in range(3))
        g_pair = grad_mixed[:, columns]
        dq, dk, dv = [], [], []
        for side in range(2):
            weights = probs[pair * 2 + side]
            soft = weights.astype(F32)
            g_own = jnp.where(halves[side], g_pair, jnp.zeros_like(g_pair))
            grad_soft = nt(g_own, v_pair)
            inner = jnp.sum(soft * grad_soft, -1, keepdims=True)
            grad_scores = (soft * (grad_soft - inner)).astype(BF16)
            dq.append(nn(grad_scores, k_pair))
            dk.append(tn(grad_scores, q_pair))
            dv.append(tn(weights, g_pair))
        grad_qkv[0, :, columns] = (jnp.where(halves[0], dq[0], dq[1]) * scale).astype(BF16)
        grad_qkv[1, :, columns] = (jnp.where(halves[0], dk[0], dk[1]) * scale).astype(BF16)
        grad_qkv[2, :, columns] = jnp.where(halves[0], dv[0], dv[1]).astype(BF16)

    unit_one, factor_one = normalize(jnp.concatenate([x_ref[...].astype(F32), zeros], 0))
    normed_one = (unit_one * gain_one_ref[...]).astype(BF16)
    core_pairs = cp // (2 * HEAD_DIM)
    for other in [*range(1, nh), 0]:
        core = (h + other) % nh
        for q in range(core_pairs):
            attend_back(core * core_pairs + q)
        for i in range(3):
            sums = tn(normed_one, grad_qkv[i, :, rows_at(core, cp)])
            if other:
                core_send[other - 1, i] = sums.astype(BF16)
                core_copy(i, other).start()
            else:
                half_sum(i, sums)
        if other == nh - 1:
            send_mix(2)
    for i in range(2):
        for k in range(1, nd):
            band_copy(k, i).start()

    grad_one = jnp.zeros((pad, width), F32)
    for i in range(3):
        grad_one = grad_one + nt(grad_qkv[i], w_full[i])
    grad_one = jnp.where(row_valid, grad_one, 0.0)
    grad_input, gain_one = norm_back(grad_one, unit_one, factor_one, gain_one_ref[...])
    grad_input_out[...] = (part_own[...] + grad_input)[0 : sz.rows].astype(BF16)

    small[...] = jnp.zeros_like(small)
    small[0:1, :] = gain_one
    small[1:2, :] = gain_two
    small[2:3, 0:128] = peak_at[0:1, :]
    peak_row = iota(small.shape, 0) == 2

    def join(a, b):
        return jnp.where(peak_row, jnp.maximum(a, b), a + b)

    small_copies = []
    for other in range(1, nh):
        device, n = (d, (h + other) % nh, z), 2 * (other - 1)
        small_copies += [
            remote(small, small_core.at[other - 1], sc_s.at[n], sc_r.at[n], device),
            remote(rt, rt_core.at[other - 1], sc_s.at[n + 1], sc_r.at[n + 1], device),
        ]
    for copy in small_copies:
        copy.start()
    for copy in small_copies:
        copy.wait()
    for other in range(1, nh):
        small[...] = join(small[...], small_core[other - 1])
        rt[...] = rt[...] + rt_core[other - 1]
    small_send[0] = small[...]
    small_copies = []
    for k in range(1, nd):
        to = (d + k) % nd
        small_copies += [
            remote(small_send.at[0], small_x.at[k - 1], sx_s.at[0], sx_r.at[0], (to, h, z)),
            remote(rt.at[:, rows_at(to, band)], rt_x.at[k - 1], sx_s.at[1], sx_r.at[1], (to, h, z)),
        ]
    for copy in small_copies:
        copy.start()
    for k in range(1, nd):
        band_copy(k, 2).start()
    send_mix(3)

    def line_piece(i, j):
        to = at.next_z(j)
        return remote(line_send.at[i, rows_at(to, rp), :], line_recv.at[j - 1, i], gl_s.at[i], gl_r.at[i], at.line(to))

    def end_band(i):
        drain(gx_s.at[i], gx_r.at[i], band_recv.at[:, i], band_recv.at[:, i])
        sums = w_half[i, rows_at(d, band), :]
        for k in range(1, nd):
            sums = sums + band_recv[k - 1, i].astype(F32)
        w_half[i, 0:band, :] = sums
        line_send[i] = sums.astype(BF16)
        for j in range(1, nz):
            line_piece(i, j).start()

    for i in (3, 0, 1):
        end_band(i)
    drain(sx_s.at[0], sx_r.at[0], small_x, small_x)
    drain(sx_s.at[1], sx_r.at[1], rt_x, rt_x)
    router_sum = rt[:, rows_at(d, band)]
    for k in range(1, nd):
        small[...] = join(small[...], small_x[k - 1])
        router_sum = router_sum + rt_x[k - 1]
    rt_z[nz - 1] = router_sum
    small_send[1] = small[...]
    for j in range(1, nz):
        device = at.line(at.next_z(j))
        remote(small_send.at[1], small_z.at[j - 1], gl_s.at[4], gl_r.at[4], device).start()
        remote(rt_z.at[nz - 1], rt_z.at[j - 1], gl_s.at[5], gl_r.at[5], device).start()
    end_band(2)

    mix = gathered(mix_own, *mix_flow)
    output_out[...] = (hidden_at[...] + mix)[0 : sz.rows].astype(BF16)

    for i in range(4):
        drain(gl_s.at[i], gl_r.at[i], line_recv.at[:, i], line_recv.at[:, i])
    for n, landed in ((4, small_z), (5, rt_z.at[pl.ds(0, nz - 1)])):
        drain(gl_s.at[n], gl_r.at[n], landed, landed)
    totals = small[...]
    router_sum = rt_z[nz - 1]
    for j in range(1, nz):
        totals = join(totals, small_z[j - 1])
        router_sum = router_sum + rt_z[j - 1]
    gain_one_out[...] = totals[0:1]
    gain_two_out[...] = totals[1:2]
    rr = sz.router_rows
    own_router = router_sum[:, 0:rr]
    for i in range(1, nh):
        own_router = jnp.where(h == i, router_sum[:, i * rr : (i + 1) * rr], own_router)
    router_out[...] = own_router
    tau = tau_ref[...]
    factor = jnp.sqrt(tau / jnp.maximum(totals[2:3, 0:HEADS], tau))
    column = iota((1, cp), 1) // HEAD_DIM + h * (cp // HEAD_DIM)
    scale_row = jnp.zeros((1, cp), F32)
    for head in range(HEADS):
        scale_row = jnp.where(column == head, factor[:, head : head + 1], scale_row)
    for i in range(2):
        clipped_out[i] = (w_qkv_ref[i].astype(F32) * scale_row).astype(BF16)
    for i in range(4):
        sums = w_half[i, rows_at(z, rp), :]
        for j in range(1, nz):
            sums = sums + line_recv[j - 1, i].astype(F32)
        if i < 3:
            qkv_out[i] = sums
        else:
            out_out[...] = sums
    for copy in stores:
        copy.wait()


def finish_kernel(sz, *refs):
    sources, results, held = refs[0:10], refs[10:20], refs[20:28]
    halves_in, full_out, in_sems, out_sems, small_in, small_out = refs[28:]
    pieces = [(i, e) for e in range(sz.own) for i in range(2)]
    loads = [pltpu.make_async_copy(sources[8 + i].at[e], halves_in.at[i, e], in_sems.at[i, e]) for i, e in pieces]
    stores = [pltpu.make_async_copy(full_out.at[i, e], results[8 + i].at[e], out_sems.at[i, e]) for i, e in pieces]
    small_loads = [pltpu.make_async_copy(sources[n], held[n], small_in.at[n]) for n in range(8)]
    small_stores = [pltpu.make_async_copy(held[n], results[n], small_out.at[n]) for n in range(8)]
    for copy in loads + small_loads:
        copy.start()
    for (i, e), load, store in zip(pieces, loads, stores):
        load.wait()
        full_out[i, e] = halves_in[i, e].astype(F32)
        store.start()
    for load, store in zip(small_loads, small_stores):
        load.wait()
        store.start()
    for copy in stores + small_stores:
        copy.wait()


def fast_body(
    sz, inputs, cotangent, routes, gain_attn, gain_expert, tau, w_qkv, w_out_attn, w_router, w_in, w_out
):
    ng, nz, nd, nh, pad, width, own = sz.groups, sz.nt, sz.nd, sz.nh, sz.pad, sz.width, sz.own
    rp, cp, band, parts, block = sz.row_piece, sz.col_piece, sz.band, sz.parts, sz.block
    many, hidden = ng * sz.cap, sz.hidden
    on_chip, anywhere = pl.BlockSpec(memory_space=pltpu.VMEM), pl.BlockSpec(memory_space=pltpu.HBM)

    def shape(dims, dtype):
        return jax.ShapeDtypeStruct(dims, dtype)

    def half(*dims):
        return pltpu.VMEM(dims, BF16)

    def full(*dims):
        return pltpu.VMEM(dims, F32)

    def pair(*dims):
        return [pltpu.SemaphoreType.DMA(dims)] * 2

    slot_buffer = half(ng, sz.group_slots, width)
    line_buffer = half(nz - 1, pad, width)
    quarter_dims = (ng, own * (sz.cap // nz), width // parts)
    quarter_buffer, few = half(*quarter_dims), ng * own * (sz.cap // nz)
    rr = sz.router_rows
    smalls = (
        shape(inputs.shape, BF16), shape(inputs.shape, BF16), shape((1, width), F32), shape((1, width), F32),
        shape((3, rp, cp), F32), shape((rp, cp), F32), shape((sz.experts, rr), F32), shape((2, rp, cp), BF16),
    )
    packed = pl.pallas_call(
        functools.partial(block_kernel, sz),
        out_shape=(*smalls, shape(w_in.shape, BF16), shape(w_out.shape, BF16)),
        in_specs=[on_chip] * 9 + [anywhere] * 2,
        out_specs=(on_chip,) * 8 + (anywhere,) * 2,
        scratch_shapes=[
            half(4, rp, cp), half(4, width, width), half(sz.experts, 128), half(ng, sz.experts, 128),
            half(sz.experts, width), full(8, block), full(block, 128), half(sz.slots, block), half(block, sz.slots), half(block, few),
            half(block, width), half(block, width), *[slot_buffer] * 6,
            half(nz, *quarter_dims), half(nz - 1, *quarter_dims), quarter_buffer,
            quarter_buffer,
            half(own, width, hidden), half(own, hidden, width), half(own, many, hidden), half(own, many, hidden),
            full(own, many, hidden), half(own, hidden, width),
            full(sz.experts, 128), full(ng, 8, 128), full(sz.experts, block), full(8, many),
            full(ng, 8, 128), full(sz.experts, 128),
            half(3, pad, width), half(HEADS, pad, pad), half(pad, width), full(pad, width), full(8, 128),
            full(block, width), full(pad, width), line_buffer, half(nz, pad, width), full(pad, width), line_buffer,
            half(nz, pad, width),
            half(pad, width), half(3, pad, width), half(nh - 1, 4, width, cp), half(nh - 1, 4, width, cp),
            full(4, width, cp), half(4, width, cp), half(nd - 1, 4, band, cp), half(4, band, cp),
            half(nz - 1, 4, rp, cp),
            full(8, width), full(2, 8, width), full(nh - 1, 8, width), full(nd - 1, 8, width), full(nz - 1, 8, width),
            full(sz.experts, width), full(nh - 1, sz.experts, width), full(nd - 1, sz.experts, band),
            full(nz, sz.experts, band),
            *pair(4), *pair(4), *pair(4 * (nh - 1)), *pair(1), *pair(parts), *pair(parts), *pair(parts), *pair(parts),
            *pair(1), *pair(own), *pair(parts), *pair(parts), *pair(1), *pair(parts), *pair(parts), *pair(4 * (nh - 1)),
            *pair(4), *pair(6), *pair(2 * (nh - 1)), *pair(2), *pair(1), *pair(1),
            *pair(parts, 2),
            pltpu.SemaphoreType.DMA((3 + own,)),
        ],
        compiler_params=pltpu.CompilerParams(collective_id=0, has_side_effects=True, vmem_limit_bytes=62 * 2**20),
        name="block",
    )(
        inputs, cotangent, routes.T, gain_attn[None, :], gain_expert[None, :], w_qkv, w_out_attn.T, w_router.T,
        tau[None, :], w_in, w_out,
    )

    both, dma = (2, *w_in.shape), pltpu.SemaphoreType.DMA
    output, grad_input, gain_one, gain_two, grad_qkv, grad_out, grad_router, clipped, grad_first, grad_second = (
        pl.pallas_call(
            functools.partial(finish_kernel, sz),
            out_shape=(*smalls, shape(w_in.shape, F32), shape(w_out.shape, F32)),
            in_specs=[anywhere] * 10,
            out_specs=(anywhere,) * 10,
            scratch_shapes=[
                *[pltpu.VMEM(x.shape, x.dtype) for x in smalls], half(*both), full(*both), dma((2, own)), dma((2, own)),
                dma((8,)), dma((8,)),
            ],
            compiler_params=pltpu.CompilerParams(vmem_limit_bytes=62 * 2**20),
            name="finish",
        )(*packed)
    )
    return (
        output, grad_input, gain_one[0], gain_two[0], grad_qkv, grad_out.T, grad_router.T, grad_first, grad_second,
        clipped,
    )


def gelu_tanh(inputs):
    return (
        0.5
        * inputs
        * (1.0 + jnp.tanh(0.7978845608028654 * (inputs + 0.044715 * inputs * inputs * inputs)))
    )


def unit_and_factor(inputs):
    centered = inputs - jnp.mean(inputs, -1, keepdims=True)
    factor = lax.rsqrt(jnp.mean(centered * centered, -1, keepdims=True) + 1e-06)
    return (centered * factor, factor)


def general_norm_back(grad_norm, unit_rows, factor, gain):
    grad, gain_row = norm_back(grad_norm, unit_rows, factor, gain)
    return grad, gain_row[0]


def attn_forward(block_parts):
    queries, key_rows, value_rows = block_parts
    scores = jnp.einsum(
        "bhqd,bhkd->bhqk", queries, key_rows, preferred_element_type=jnp.float32
    ) * HEAD_DIM ** (-0.5)
    row_peak = jnp.max(scores, -1, keepdims=True)
    exponent = jnp.exp(scores - row_peak)
    summed = jnp.sum(exponent, -1, keepdims=True)
    soft_weights = (exponent / summed).astype(jnp.bfloat16)
    mixed = jnp.einsum(
        "bhqk,bhkd->bhqd", soft_weights, value_rows, preferred_element_type=jnp.float32
    ).astype(jnp.bfloat16)
    return (mixed, (row_peak + jnp.log(summed))[..., 0], jnp.max(row_peak, axis=(0, 2, 3)))


def attn_backward(block_parts):
    queries, key_rows, value_rows, grad_mixed, log_total = block_parts
    score_scale = HEAD_DIM ** (-0.5)
    scores = (
        jnp.einsum("bhqd,bhkd->bhqk", queries, key_rows, preferred_element_type=jnp.float32)
        * score_scale
    )
    soft_weights = jnp.exp(scores - log_total[..., None])
    grad_soft = jnp.einsum(
        "bhqd,bhkd->bhqk", grad_mixed, value_rows, preferred_element_type=jnp.float32
    )
    inner_sum = jnp.sum(soft_weights * grad_soft, -1, keepdims=True)
    grad_scores = (soft_weights * (grad_soft - inner_sum)).astype(jnp.bfloat16)
    grad_query = (
        jnp.einsum("bhqk,bhkd->bhqd", grad_scores, key_rows, preferred_element_type=jnp.float32)
        * score_scale
    ).astype(jnp.bfloat16)
    grad_key = (
        jnp.einsum("bhqk,bhqd->bhkd", grad_scores, queries, preferred_element_type=jnp.float32)
        * score_scale
    ).astype(jnp.bfloat16)
    grad_value = jnp.einsum(
        "bhqk,bhqd->bhkd",
        soft_weights.astype(jnp.bfloat16),
        grad_mixed,
        preferred_element_type=jnp.float32,
    ).astype(jnp.bfloat16)
    return (grad_query, grad_key, grad_value)


def general_body(
    inputs, cotangent, routes, gain_attn, gain_expert, tau, w_qkv, w_out_attn, w_router, w_in, w_out
):
    row_count, width = inputs.shape
    n_dp = lax.axis_size("dp")
    n_heads = lax.axis_size("heads")
    n_tensor = lax.axis_size("tensor")
    row_piece = w_qkv.shape[1]
    col_piece = w_qkv.shape[2]
    own_heads = col_piece // HEAD_DIM
    head_start = lax.axis_index("heads") * col_piece
    x_float = inputs.astype(jnp.float32)
    unit_one, factor_one = unit_and_factor(x_float)
    normed_one = (unit_one * gain_attn).astype(jnp.bfloat16)
    stack_qkv, stack_out = (
        lax.all_gather(w_qkv[None], ("dp", "heads", "tensor"), axis=0, tiled=True),
        lax.all_gather(w_out_attn[None], ("dp", "heads", "tensor"), axis=0, tiled=True),
    )
    full_qkv = (
        stack_qkv.reshape(n_dp, n_heads, n_tensor, 3, row_piece, col_piece)
        .transpose(3, 0, 2, 4, 1, 5)
        .reshape(3, width, width)
    )
    full_out = (
        stack_out.reshape(n_dp, n_heads, n_tensor, col_piece, row_piece)
        .transpose(1, 3, 0, 2, 4)
        .reshape(width, width)
    )
    proj_w = lax.dynamic_slice_in_dim(full_qkv, head_start, col_piece, 2)
    attn_w = lax.dynamic_slice_in_dim(full_out, head_start, col_piece, 0)
    normed_all = lax.all_gather(normed_one, "heads", axis=0, tiled=True)
    head_cols = attn_w.shape[0]
    local_heads = head_cols // HEAD_DIM
    joined_w = jnp.concatenate([proj_w[0], proj_w[1], proj_w[2]], 1)
    projected = jnp.dot(normed_all, joined_w, preferred_element_type=jnp.float32).astype(
        jnp.bfloat16
    )
    images = normed_all.shape[0] // SEQ
    per_block = 4 if images % 4 == 0 else 3 if images % 3 == 0 else 2 if images % 2 == 0 else 1
    block_shape = (images // per_block, per_block, SEQ, local_heads, HEAD_DIM)

    def to_blocks(row_matrix):
        return row_matrix.reshape(block_shape).transpose(0, 1, 3, 2, 4)

    def from_blocks(block_array):
        return block_array.transpose(0, 1, 3, 2, 4).reshape(-1, head_cols)

    queries = to_blocks(projected[:, :head_cols])
    key_rows = to_blocks(projected[:, head_cols : 2 * head_cols])
    value_rows = to_blocks(projected[:, 2 * head_cols :])
    mixed, log_total, head_peaks = lax.map(attn_forward, (queries, key_rows, value_rows))
    mixed_rows = from_blocks(mixed)
    block_peak = jnp.max(head_peaks, 0)
    attn_out = lax.psum_scatter(
        jnp.dot(mixed_rows, attn_w, preferred_element_type=jnp.float32),
        "heads",
        scatter_dimension=0,
        tiled=True,
    )
    peak_full = lax.dynamic_update_slice_in_dim(
        jnp.full((HEADS,), -1e30, jnp.float32), block_peak, lax.axis_index("heads") * local_heads, 0
    )
    hidden = x_float + attn_out
    peak_all = lax.pmax(peak_full, ("dp", "heads", "tensor"))
    peak_logit = lax.dynamic_slice_in_dim(
        peak_all, lax.axis_index("heads") * own_heads, own_heads, 0
    )
    unit_two, factor_two = unit_and_factor(hidden)
    normed_two = (unit_two * gain_expert).astype(jnp.bfloat16)
    group_rows, group_cot = (
        lax.all_gather(normed_two, "tensor", axis=0, tiled=True),
        lax.all_gather(cotangent, "tensor", axis=0, tiled=True),
    )
    first_w, second_w, router_w = (
        lax.all_gather(w_in, ("dp", "heads"), axis=0, tiled=True),
        lax.all_gather(w_out, ("dp", "heads"), axis=0, tiled=True),
        lax.all_gather(w_router, ("dp", "heads"), axis=0, tiled=True),
    )
    logits = jnp.dot(group_rows, router_w, preferred_element_type=jnp.float32)
    chosen = jnp.take_along_axis(logits, routes, 1)
    exponent = jnp.exp(chosen - jnp.max(chosen, -1, keepdims=True))
    gate_values = exponent / jnp.sum(exponent, -1, keepdims=True)
    group_count = routes.shape[0]
    experts = router_w.shape[1]
    capacity = (group_count * 5 // (16 * experts) + 1) * 8
    flat_ids = routes.reshape(-1)
    ordering = jnp.argsort(flat_ids, stable=True)
    sorted_ids = flat_ids[ordering]
    counts = jnp.sum(
        (flat_ids[:, None] == jnp.arange(experts, dtype=jnp.int32)[None, :]).astype(jnp.int32), 0
    )
    expert_ids = jnp.arange(experts, dtype=jnp.int32)
    starts = jnp.sum(jnp.where(expert_ids[None, :] < expert_ids[:, None], counts[None, :], 0), 1)
    slot_rank = jnp.arange(2 * group_count, dtype=jnp.int32) - starts[sorted_ids]
    slot_table = (
        jnp.full((experts * capacity,), 2 * group_count, jnp.int32)
        .at[sorted_ids * capacity + slot_rank]
        .set(ordering)
    )
    slot_token = slot_table // 2
    padded_rows = jnp.concatenate([group_rows, jnp.zeros((1, width), jnp.bfloat16)], 0)
    slot_in = padded_rows[slot_token].reshape(experts, capacity, width)
    slot_gate = jnp.concatenate([gate_values.reshape(-1), jnp.zeros((1,), jnp.float32)], 0)[
        slot_table
    ]
    pre_gelu = jnp.einsum("ecd,edf->ecf", slot_in, first_w, preferred_element_type=jnp.float32)
    activated = gelu_tanh(pre_gelu).astype(jnp.bfloat16)
    slot_out = jnp.einsum(
        "ecf,efd->ecd", activated, second_w, preferred_element_type=jnp.float32
    ).reshape(-1, width)
    partial_value = (
        jnp.zeros((group_count + 1, width), jnp.float32)
        .at[slot_token]
        .add(slot_gate[:, None] * slot_out)[:group_count]
    )
    expert_mix = lax.psum_scatter(
        partial_value.astype(jnp.bfloat16), "tensor", scatter_dimension=0, tiled=True
    ).astype(jnp.float32)
    output = (hidden + expert_mix).astype(jnp.bfloat16)
    padded_cot = jnp.concatenate([group_cot, jnp.zeros((1, width), jnp.bfloat16)], 0)
    slot_cot = padded_cot[slot_token].astype(jnp.float32)
    grad_slot_out = (
        (slot_gate[:, None] * slot_cot).astype(jnp.bfloat16).reshape(experts, capacity, width)
    )
    gate_part = (
        jnp.zeros((2 * group_count + 1,), jnp.float32)
        .at[slot_table]
        .add(jnp.sum(slot_cot * slot_out, -1))[: 2 * group_count]
        .reshape(group_count, 2)
    )
    grad_act = jnp.einsum(
        "ecd,efd->ecf", grad_slot_out, second_w, preferred_element_type=jnp.float32
    )
    grad_pre = jax.vjp(gelu_tanh, pre_gelu)[1](grad_act)[0].astype(jnp.bfloat16)
    grad_first = jnp.einsum("ecd,ecf->edf", slot_in, grad_pre, preferred_element_type=jnp.float32)
    grad_second = jnp.einsum(
        "ecf,ecd->efd", activated, grad_slot_out, preferred_element_type=jnp.float32
    )
    grad_slots = jnp.einsum(
        "ecf,edf->ecd", grad_pre, first_w, preferred_element_type=jnp.float32
    ).reshape(-1, width)
    grad_part = (
        jnp.zeros((group_count + 1, width), jnp.float32)
        .at[slot_token]
        .add(grad_slots)[:group_count]
    )
    grad_normed_two, grad_gates = (
        lax.psum_scatter(
            grad_part.astype(jnp.bfloat16), "tensor", scatter_dimension=0, tiled=True
        ).astype(jnp.float32),
        lax.psum_scatter(
            gate_part.astype(jnp.bfloat16), "tensor", scatter_dimension=0, tiled=True
        ).astype(jnp.float32),
    )
    shard_first, shard_second = (
        lax.psum_scatter(
            grad_first.astype(jnp.bfloat16), ("dp", "heads"), scatter_dimension=0, tiled=True
        ).astype(jnp.float32),
        lax.psum_scatter(
            grad_second.astype(jnp.bfloat16), ("dp", "heads"), scatter_dimension=0, tiled=True
        ).astype(jnp.float32),
    )
    offset = lax.axis_index("tensor") * row_count
    local_gates = lax.dynamic_slice_in_dim(gate_values, offset, row_count, 0)
    local_routes = lax.dynamic_slice_in_dim(routes, offset, row_count, 0)
    grad_chosen = local_gates * (grad_gates - jnp.sum(local_gates * grad_gates, -1, keepdims=True))
    columns = jnp.arange(experts, dtype=jnp.int32)[None, :]
    grad_logits = (
        jnp.where(local_routes[:, 0:1] == columns, grad_chosen[:, 0:1], 0.0)
        + jnp.where(local_routes[:, 1:2] == columns, grad_chosen[:, 1:2], 0.0)
    ).astype(jnp.bfloat16)
    grad_normed_two = grad_normed_two + jnp.einsum(
        "re,de->rd", grad_logits, router_w, preferred_element_type=jnp.float32
    )
    router_term = jnp.einsum(
        "rd,re->de", normed_two, grad_logits, preferred_element_type=jnp.float32
    )
    grad_hidden_norm, gain_two_term = general_norm_back(grad_normed_two, unit_two, factor_two, gain_expert)
    grad_hidden = cotangent.astype(jnp.float32) + grad_hidden_norm
    grad_attn = lax.all_gather(grad_hidden.astype(jnp.bfloat16), "heads", axis=0, tiled=True)
    grad_mixed = jnp.einsum(
        "rd,cd->rc", grad_attn, attn_w, preferred_element_type=jnp.float32
    ).astype(jnp.bfloat16)
    out_term = jnp.einsum("rc,rd->cd", mixed_rows, grad_attn, preferred_element_type=jnp.float32)
    grad_query, grad_key, grad_value = lax.map(
        attn_backward, (queries, key_rows, value_rows, to_blocks(grad_mixed), log_total)
    )
    grad_proj = jnp.concatenate(
        [from_blocks(grad_query), from_blocks(grad_key), from_blocks(grad_value)], 1
    )
    grad_normed_one = lax.psum_scatter(
        jnp.einsum("rc,dc->rd", grad_proj, joined_w, preferred_element_type=jnp.float32).astype(
            jnp.bfloat16
        ),
        "heads",
        scatter_dimension=0,
        tiled=True,
    ).astype(jnp.float32)
    proj_term = jnp.einsum("rd,rc->dc", normed_all, grad_proj, preferred_element_type=jnp.float32)
    proj_stack = jnp.stack(
        [
            proj_term[:, :head_cols],
            proj_term[:, head_cols : 2 * head_cols],
            proj_term[:, 2 * head_cols :],
        ],
        0,
    )
    whole_proj = lax.dynamic_update_slice_in_dim(
        jnp.zeros((3, width, width), jnp.float32), proj_stack, head_start, 2
    )
    whole_out = lax.dynamic_update_slice_in_dim(
        jnp.zeros((width, width), jnp.float32), out_term, head_start, 0
    )
    send_qkv = (
        whole_proj.reshape(3, n_dp, n_tensor, row_piece, n_heads, col_piece)
        .transpose(1, 4, 2, 0, 3, 5)
        .reshape(-1, 3, row_piece, col_piece)
    )
    send_out = (
        whole_out.reshape(n_heads, col_piece, n_dp, n_tensor, row_piece)
        .transpose(2, 0, 3, 1, 4)
        .reshape(-1, col_piece, row_piece)
    )
    shard_proj, shard_attn = (
        lax.psum_scatter(send_qkv, ("dp", "heads", "tensor"), scatter_dimension=0, tiled=True),
        lax.psum_scatter(send_out, ("dp", "heads", "tensor"), scatter_dimension=0, tiled=True),
    )
    grad_input_norm, gain_one_term = general_norm_back(grad_normed_one, unit_one, factor_one, gain_attn)
    grad_input = (grad_hidden + grad_input_norm).astype(jnp.bfloat16)
    gain_one_grad, gain_two_grad, router_all = lax.psum(
        (gain_one_term, gain_two_term, router_term), ("dp", "heads", "tensor")
    )
    router_grad = lax.dynamic_slice_in_dim(
        router_all, lax.axis_index(("dp", "heads")) * w_router.shape[0], w_router.shape[0], 0
    )
    local_tau = lax.dynamic_slice_in_dim(tau, lax.axis_index("heads") * own_heads, own_heads, 0)
    clip_factor = jnp.sqrt(local_tau / jnp.maximum(peak_logit, local_tau))
    clipped = (w_qkv[:2].astype(jnp.float32) * jnp.repeat(clip_factor, HEAD_DIM)).astype(
        jnp.bfloat16
    )
    return (
        output,
        grad_input,
        gain_one_grad,
        gain_two_grad,
        shard_proj[0],
        shard_attn[0],
        router_grad,
        shard_first,
        shard_second,
        clipped,
    )


def body(*args):
    inputs, _, routes, _, _, _, w_qkv, _, w_router, w_in, _ = args
    sz = Sizes(
        lax.axis_size("dp"), lax.axis_size("heads"), lax.axis_size("tensor"), inputs, routes, w_qkv, w_router, w_in
    )
    if sz.fits():
        return fast_body(sz, *args)
    return general_body(*args)


def solution(mesh):
    return jax.shard_map(
        body,
        mesh=mesh,
        in_specs=(
            P(("dp", "heads", "tensor"), None),
            P(("dp", "heads", "tensor"), None),
            P(("dp", "heads"), None),
            P(),
            P(),
            P(),
            P(None, ("dp", "tensor"), "heads"),
            P("heads", ("dp", "tensor")),
            P(("dp", "heads"), None),
            P(("dp", "heads"), None, "tensor"),
            P(("dp", "heads"), "tensor", None),
        ),
        out_specs=(
            P(("dp", "heads", "tensor"), None),
            P(("dp", "heads", "tensor"), None),
            P(),
            P(),
            P(None, ("dp", "tensor"), "heads"),
            P("heads", ("dp", "tensor")),
            P(("dp", "heads"), None),
            P(("dp", "heads"), None, "tensor"),
            P(("dp", "heads"), "tensor", None),
            P(None, ("dp", "tensor"), "heads"),
        ),
        check_vma=False,
    )
```

```python
import functools
import jax
import jax.numpy as jnp
from jax import lax
from jax.experimental import pallas as pl
from jax.experimental.pallas import tpu as pltpu
from jax.sharding import PartitionSpec as P

HEADS = 8
HEAD_DIM = 64
SEQ = 197
F32 = jnp.float32
BF16 = jnp.bfloat16
MESH = pl.DeviceIdType.MESH
NEG = -1e30


class Sizes:
    def __init__(self, n_dp, n_heads, n_tensor, inputs, routes, w_qkv, w_router, w_in):
        self.nd, self.nh, self.nt = n_dp, n_heads, n_tensor
        self.groups = n_dp * n_heads
        self.rows, self.width = inputs.shape
        self.pad = -(-self.rows // 16) * 16
        self.block = self.pad * n_tensor
        self.block_rows = routes.shape[0]
        self.own = w_in.shape[0]
        self.hidden = w_in.shape[2]
        self.experts = self.own * self.groups
        self.cap = (self.block_rows * 5 // (16 * self.experts) + 1) * 8
        self.group_slots = self.own * self.cap
        self.slots = self.experts * self.cap
        self.row_piece, self.col_piece = w_qkv.shape[1], w_qkv.shape[2]
        self.band = self.row_piece * n_tensor
        self.router_rows = w_router.shape[0]
        self.parts = 4

    def fits(self):
        return (
            self.rows == SEQ
            and self.nt == 4
            and self.parts == 4
            and self.block_rows == self.rows * self.nt
            and self.cap == 64
            and self.experts == 32
            and self.group_slots % 128 == 0
            and self.col_piece % 128 == 0
            and self.row_piece % 16 == 0
            and self.router_rows % 16 == 0
            and self.own * self.groups * 4 == 128
            and self.width == HEADS * HEAD_DIM
            and self.block * self.width * 2 <= 2**20
            and self.own * self.width <= self.slots
            and self.hidden <= self.block
            and self.hidden == self.width
            and self.cap % (16 * self.nt) == 0
            and self.width // self.parts % 128 == 0
        )


def nn(a, b):
    return jnp.dot(a, b, preferred_element_type=F32)


def nt(a, b):
    return lax.dot_general(a, b, (((1,), (1,)), ((), ())), preferred_element_type=F32)


def tn(a, b):
    return lax.dot_general(a, b, (((0,), (0,)), ((), ())), preferred_element_type=F32)


def iota(shape, axis):
    return lax.broadcasted_iota(jnp.int32, shape, axis)


def normalize(rows):
    centered = rows - jnp.mean(rows, -1, keepdims=True)
    factor = lax.rsqrt(jnp.mean(centered * centered, -1, keepdims=True) + 1e-06)
    return centered * factor, factor


def norm_back(grad_norm, unit_rows, factor, gain):
    grad_hat = grad_norm * gain
    inner = (
        grad_hat
        - jnp.mean(grad_hat, -1, keepdims=True)
        - unit_rows * jnp.mean(grad_hat * unit_rows, -1, keepdims=True)
    )
    return factor * inner, jnp.sum(grad_norm * unit_rows, 0, keepdims=True)


def split_high_low(values):
    high = values.astype(BF16)
    low = (values - high.astype(F32)).astype(BF16)
    return jnp.concatenate([high, low], 0)


class Place:
    def __init__(self, sz):
        self.sz = sz
        self.d = lax.axis_index("dp")
        self.h = lax.axis_index("heads")
        self.z = lax.axis_index("tensor")
        self.group = self.d * sz.nh + self.h

    def plane(self, group):
        return (group // self.sz.nh, group % self.sz.nh, self.z)

    def line(self, z):
        return (self.d, self.h, z)

    def next_group(self, k):
        return (self.group + k) % self.sz.groups

    def next_z(self, j):
        return (self.z + j) % self.sz.nt

    def inner(self):
        return (self.z + 1) % 4 // 2

    def mates(self):
        return self.z + 1 - 2 * (self.z % 2), (self.z + 2) % 4, 3 - self.z

    def enter(self):
        sz = self.sz
        barrier = pltpu.get_barrier_semaphore()
        for k in range(1, sz.groups):
            pl.semaphore_signal(barrier, inc=1, device_id=self.plane(self.next_group(k)), device_id_type=MESH)
        for j in range(1, sz.nt):
            pl.semaphore_signal(barrier, inc=1, device_id=self.line(self.next_z(j)), device_id_type=MESH)
        pl.semaphore_wait(barrier, sz.groups + sz.nt - 2)


def remote(src, dst, send, recv, device):
    return pltpu.make_async_remote_copy(
        src_ref=src, dst_ref=dst, send_sem=send, recv_sem=recv, device_id=device, device_id_type=MESH
    )


def drain(send_sem, recv_sem, sent, landed):
    pltpu.make_async_copy(sent, sent, send_sem).wait()
    pltpu.make_async_copy(landed, landed, recv_sem).wait()


def route_table(sz, routes_ref, table):
    table[...] = jnp.full_like(table, -1.0)
    for z in range(sz.nt):
        table[0:2, z * sz.pad : z * sz.pad + sz.rows] = routes_ref[:, z * sz.rows : (z + 1) * sz.rows].astype(F32)


def block_kernel(
    sz, x_ref, cot_ref, routes_ref, gain_one_ref, gain_two_ref, w_qkv_ref, w_out_ref, w_router_ref, tau_ref, first_hbm,
    second_hbm, output_out, grad_input_out, gain_one_out, gain_two_out, qkv_out, out_out, router_out, clipped_out,
    grad_first_out, grad_second_out,
    w_own, w_full, router_own, router_full, router_t, route_rows, route_columns, select, select_t, select_q, select_qt,
    cot_block, rows_block, send_a, send_b, cot_slots, slots, grad_slots, values,
    rows_q, rows_line, grads_q, grads_line, grads_sum, grads_back, first, second, act, grad_pre, grad_act, grad_second,
    gate_send, gate_recv, gates_at, dgate_send, dgate_recv, dgate_rows,
    qkv, probs, mixed, hidden_at, peak_at, part, part_own, part_send, part_recv, mix_own, mix_send, mix_recv,
    grad_mixed, grad_qkv, core_send, core_recv, w_half, band_send, band_recv, line_send, line_recv,
    small, small_send, small_core, small_x, small_z, rt, rt_core, rt_x, rt_z,
    wz_s, wz_r, wx_s, wx_r, wc_s, wc_r, r_s, r_r, qz_s, qz_r, nz_s, nz_r, qa_s, qa_r, na_s, na_r, ga_s, ga_r,
    d0_s, d0_r, da_s, da_r, va_s, va_r, dg_s, dg_r, pz_s, pz_r, mz_s, mz_r, gc_s, gc_r, gx_s, gx_r, gl_s, gl_r,
    sc_s, sc_r, sx_s, sx_r, dl_s, dl_r, dq_s, dq_r, nq_s, nq_r, nl_s, nl_r, pr_r, mr_r,
    local_sem,
):
    at = Place(sz)
    d, h, z, me = at.d, at.h, at.z, at.group
    nd, nh, nz, ng = sz.nd, sz.nh, sz.nt, sz.groups
    band, rp, cp, pad, width = sz.band, sz.row_piece, sz.col_piece, sz.pad, sz.width
    many = ng * sz.cap
    parts, part_width = sz.parts, width // sz.parts

    def lanes(c):
        return pl.ds(c * part_width, part_width)

    def rows_at(n, size):
        return pl.ds(pl.multiple_of(n * size, size), size)

    own_block, own_columns = rows_at(z, pad), rows_at(h, cp)

    w_own[0:3] = w_qkv_ref[...]
    w_own[3] = w_out_ref[...]
    router_own[...] = jnp.zeros_like(router_own)
    router_own[:, 0 : sz.router_rows] = w_router_ref[...]
    cot_block[own_block] = jnp.concatenate(
        [cot_ref[...].astype(F32), jnp.zeros((pad - sz.rows, width), F32)], 0
    ).astype(BF16)

    part_recv[2] = jnp.zeros((pad, width), BF16)
    mix_recv[2] = jnp.zeros((pad, width), BF16)

    at.enter()

    w_rows = rows_at(d * nz + z, rp)
    others = pl.ds(0, ng - 1)

    def send_line(i):
        for j in range(1, nz):
            remote(
                w_own.at[i], w_full.at[i, w_rows, own_columns], wz_s.at[i], wz_r.at[i], at.line(at.next_z(j))
            ).start()

    def along(block, send_sems, recv_sems, c):
        place = block.at[own_block, lanes(c)]
        return [
            remote(place, place, send_sems.at[c], recv_sems.at[c], at.line(at.next_z(j)))
            for j in range(1, nz)
        ]

    def wait_along(block, send_sems, recv_sems, c):
        place = block.at[pl.ds(0, (nz - 1) * pad), lanes(c)]
        drain(send_sems.at[c], recv_sems.at[c], place, place)

    for i in range(3):
        send_line(i)
    for copy in along(cot_block, qz_s, qz_r, 0):
        copy.start()
    send_line(3)
    routers = [
        remote(router_own, router_full.at[me], r_s.at[0], r_r.at[0], at.plane(at.next_group(k)))
        for k in range(1, ng)
    ]
    for copy in routers:
        copy.start()
    loads = [
        pltpu.make_async_copy(first_hbm, first, local_sem.at[0]),
        pltpu.make_async_copy(second_hbm, second, local_sem.at[1]),
    ]
    for copy in loads:
        copy.start()
    w_full[:, w_rows, own_columns] = w_own[...]
    router_full[me] = router_own[...]

    def to_core(i, dp, other):
        place = w_full.at[i, rows_at(dp, band), own_columns]
        n = 4 * (other - 1) + i
        return remote(place, place, wc_s.at[n], wc_r.at[n], (d, (h + other) % nh, z))

    def send_band(i):
        landed = w_full.at[i, pl.ds(0, (nz - 1) * rp), own_columns]
        drain(wz_s.at[i], wz_r.at[i], landed, landed)
        place = w_full.at[i, rows_at(d, band), own_columns]
        for k in range(1, nd):
            remote(place, place, wx_s.at[i], wx_r.at[i], ((d + k) % nd, h, z)).start()
        for other in range(1, nh):
            to_core(i, d, other).start()

    def pass_on(i):
        landed = w_full.at[i, pl.ds(0, (nd - 1) * band), own_columns]
        drain(wx_s.at[i], wx_r.at[i], landed, landed)
        for k in range(1, nd):
            for other in range(1, nh):
                to_core(i, (d + k) % nd, other).start()

    def arrived(i):
        for other in range(1, nh):
            n, columns = 4 * (other - 1) + i, w_full.at[i, :, own_columns]
            drain(wc_s.at[n], wc_r.at[n], columns, columns)

    zeros = jnp.zeros((pad - sz.rows, width), F32)
    x_rows = jnp.concatenate([x_ref[...].astype(F32), zeros], 0)
    unit_one, _ = normalize(x_rows)
    normed_one = (unit_one * gain_one_ref[...]).astype(BF16)
    for i in range(3):
        send_band(i)

    route_table(sz, routes_ref, route_rows)
    route_a, route_b = route_rows[0:1, :], route_rows[1:2, :]
    expert = iota((sz.experts, sz.block), 0).astype(F32)
    named_a, named_b = route_a == expert, route_b == expert
    named = jnp.logical_or(named_a, named_b)
    before = (iota((sz.block, sz.block), 0) < iota((sz.block, sz.block), 1)).astype(BF16)
    rank = nn(named.astype(BF16), before) + expert * float(sz.cap)
    slot_a = jnp.sum(jnp.where(named_a, rank, 0.0), 0, keepdims=True)
    slot_b = jnp.sum(jnp.where(named_b, rank, 0.0), 0, keepdims=True)
    slot_a = jnp.where(route_a < 0.0, -1.0, slot_a)
    slot_b = jnp.where(route_b < 0.0, -1.0, slot_b)
    slot_pair = jnp.concatenate([slot_a, slot_b] * 64, 0)
    route_columns[...] = slot_pair.T

    def fill(g, carry):
        slot = iota((sz.group_slots, sz.block), 0).astype(F32) + (g * sz.group_slots).astype(F32)
        hit = jnp.logical_or(slot == slot_a, slot == slot_b)
        select[rows_at(g, sz.group_slots), :] = jnp.where(hit, 1.0, 0.0).astype(BF16)
        return carry

    lax.fori_loop(0, ng, fill, 0)

    quarter = sz.cap // nz
    few = ng * sz.own * quarter

    def quarter_slot(dims, axis):
        n = iota(dims, axis)
        return (n // quarter * sz.cap + z * quarter + n % quarter).astype(F32)

    some_slot = quarter_slot((few, sz.block), 0)
    select_q[...] = jnp.where(jnp.logical_or(some_slot == slot_a, some_slot == slot_b), 1.0, 0.0).astype(BF16)

    def quarter_move(k, send, landing, send_sems, recv_sems):
        g = (me + k) % ng
        return remote(send.at[g], landing.at[me], send_sems.at[0], recv_sems.at[0], at.plane(g))

    def exchange(c, k, send, out, send_sems, recv_sems):
        g = (me + k) % ng
        return remote(
            send.at[g, :, lanes(c)], out.at[me, :, lanes(c)], send_sems.at[c], recv_sems.at[c], at.plane(g)
        )

    def dispatch(c, block, send, out, send_sems, recv_sems):
        def step(i, carry):
            k = ng - 1 - i
            g = (me + k) % ng
            send[g, :, lanes(c)] = nn(select[rows_at(g, sz.group_slots), :], block[:, lanes(c)]).astype(BF16)

            @pl.when(k > 0)
            def _():
                exchange(c, k, send, out, send_sems, recv_sems).start()

            return carry

        lax.fori_loop(0, ng, step, 0)
        out[me, :, lanes(c)] = send[me, :, lanes(c)]

    def start_part(c, *flow):
        def step(i, carry):
            exchange(c, ng - 1 - i, *flow).start()
            return carry

        lax.fori_loop(0, ng - 1, step, 0)

    def wait_part(c, send, out, send_sems, recv_sems):
        drain(send_sems.at[c], recv_sems.at[c], send.at[others, :, lanes(c)], out.at[others, :, lanes(c)])

    cot_flow = (send_a, cot_slots, qa_s, qa_r)
    row_flow = (send_b, slots, na_s, na_r)

    def send_cot(c):
        wait_along(cot_block, qz_s, qz_r, c)
        dispatch(c, cot_block, *cot_flow)

    send_band(3)
    for c in range(1, parts):
        for copy in along(cot_block, qz_s, qz_r, c):
            copy.start()
    pass_on(0)
    send_cot(0)
    pass_on(1)
    pass_on(2)

    for i in range(3):
        arrived(i)
        qkv[i] = nn(normed_one, w_full[i]).astype(BF16)
    pass_on(3)
    lane = iota((1, 2 * HEAD_DIM), 1)
    halves = (lane < HEAD_DIM, lane >= HEAD_DIM)
    key_valid = iota((1, pad), 1) < sz.rows
    row_valid = iota((pad, 1), 0) < sz.rows
    peak_lane = iota((1, 128), 1)
    peak_at[...] = jnp.full_like(peak_at, NEG)
    scale = HEAD_DIM ** (-0.5)

    def attend(pair, carry):
        columns = rows_at(pair, 2 * HEAD_DIM)
        q_pair, k_pair, v_pair = (qkv[i, :, columns] for i in range(3))
        sides = []
        for side in range(2):
            q_own = jnp.where(halves[side], q_pair, jnp.zeros_like(q_pair))
            scores = jnp.where(key_valid, nt(q_own, k_pair) * scale, NEG)
            row_peak = jnp.max(scores, -1, keepdims=True)
            exponent = jnp.exp(scores - row_peak)
            weights = (exponent / jnp.sum(exponent, -1, keepdims=True)).astype(BF16)
            head = pair * 2 + side
            probs[head] = weights
            sides.append(nn(weights, v_pair))
            peak = jnp.max(jnp.where(row_valid, row_peak, NEG), 0, keepdims=True)
            peak_at[0:1, :] = jnp.where(peak_lane == head, peak, peak_at[0:1, :])
        mixed[:, columns] = jnp.where(halves[0], sides[0], sides[1]).astype(BF16)
        return carry

    pairs = HEADS // 2
    lax.fori_loop(0, pairs // 2, attend, 0)
    send_cot(1)
    lax.fori_loop(pairs // 2, pairs, attend, 0)

    arrived(3)
    hidden = x_rows + nt(mixed[...], w_full[3])
    hidden_at[...] = hidden
    unit_two, _ = normalize(hidden)
    rows_block[own_block] = jnp.where(row_valid, unit_two * gain_two_ref[...], 0.0).astype(BF16)
    for c in range(parts):
        for copy in along(rows_block, nz_s, nz_r, c):
            copy.start()

    for c in range(2, parts):
        send_cot(c)

    def fill_t(i, carry):
        rows = rows_at(i, pad)
        slot = iota((pad, sz.slots), 1).astype(F32)
        hit = jnp.logical_or(slot == route_columns[rows, 0:1], slot == route_columns[rows, 1:2])
        select_t[rows, :] = jnp.where(hit, 1.0, 0.0).astype(BF16)
        some = quarter_slot((pad, few), 1)
        hit = jnp.logical_or(some == route_columns[rows, 0:1], some == route_columns[rows, 1:2])
        select_qt[rows, :] = jnp.where(hit, 1.0, 0.0).astype(BF16)
        return carry

    lax.fori_loop(0, nz, fill_t, 0)
    drain(r_s.at[0], r_r.at[0], router_full.at[others], router_full.at[others])
    for g in range(ng):
        router_t[:, g * sz.router_rows : (g + 1) * sz.router_rows] = router_full[g, :, 0 : sz.router_rows]

    def expert_rows(ref, e):
        return ref[:, rows_at(e, sz.cap), :].reshape(many, width)

    def send_gates():
        logits = jnp.where(named, nt(router_t[...], rows_block[...]), NEG)
        exponent = jnp.where(named, jnp.exp(logits - jnp.max(logits, 0, keepdims=True)), 0.0)
        total = jnp.sum(exponent, 0, keepdims=True)
        gates = exponent / jnp.where(total > 0.0, total, 1.0)
        gates_at[...] = gates
        by_slot = nt(split_high_low(gates), select[...])
        by_slot = by_slot[0 : sz.experts] + by_slot[sz.experts :]
        own_slot = iota((sz.experts, sz.slots), 1) // sz.cap == iota((sz.experts, sz.slots), 0)
        by_slot = jnp.where(own_slot, by_slot, 0.0)
        folded = by_slot[:, 0:128]
        for i in range(1, sz.slots // 128):
            folded = folded + by_slot[:, i * 128 : (i + 1) * 128]
        gate_send[...] = folded
        gate_copies = [
            remote(
                gate_send.at[rows_at(at.next_group(k) * sz.own // 8, 8)], gate_recv.at[me], ga_s.at[0], ga_r.at[0],
                at.plane(at.next_group(k)),
            )
            for k in range(1, ng)
        ]
        for copy in gate_copies:
            copy.start()
        gate_recv[me] = gate_send[rows_at(me * sz.own // 8, 8)]

    for c in range(parts):
        wait_along(rows_block, nz_s, nz_r, c)
        if c == 0:
            rows_q[...] = nn(select_q[...], rows_block[:, lanes(0)]).astype(BF16).reshape(rows_q.shape)
            for k in range(1, ng):
                quarter_move(k, rows_q, rows_line.at[z], nq_s, nq_r).start()
            rows_line[z, me] = rows_q[me]
            continue
        if c == parts - 1:
            drain(nq_s.at[0], nq_r.at[0], rows_q.at[others], rows_q.at[others])
            for j in range(1, nz):
                remote(rows_line.at[z], rows_line.at[z], nl_s.at[0], nl_r.at[0], at.line(at.next_z(j))).start()
            send_gates()
        dispatch(c, rows_block, *row_flow)

    drain(ga_s.at[0], ga_r.at[0], gate_recv.at[others], gate_recv.at[others])
    def gate_of(e):
        turned = gate_recv[:, pl.ds(me * sz.own % 8 + e, 1), :].reshape(ng, 128).T
        columns = jnp.where((e % 2) == 1, turned[sz.cap : 2 * sz.cap], turned[0 : sz.cap])
        return jnp.concatenate([columns[:, s : s + 1] for s in range(ng)], 0)

    def weigh(e, carry):
        grad_act[e] = nt(expert_rows(cot_slots, e), second[e]) * gate_of(e)
        return carry

    for c in range(parts):
        wait_part(c, *cot_flow)
    for copy in loads:
        copy.wait()
    lax.fori_loop(0, sz.own, weigh, 0)
    lines = rows_line.at[pl.ds(0, nz - 1)]
    drain(nl_s.at[0], nl_r.at[0], lines, lines)
    for i in range(nz):
        for e in range(sz.own):
            slots[:, e * sz.cap + i * quarter : e * sz.cap + (i + 1) * quarter, lanes(0)] = rows_line[
                i, :, e * quarter : (e + 1) * quarter, :
            ]
    for c in range(1, parts):
        wait_part(c, *row_flow)

    def first_piece(e, g):
        piece = (rows_at(e, sz.cap), lanes(1))
        return remote(
            send_a.at[(g, *piece)], grad_slots.at[(me, *piece)], d0_s.at[e], d0_r.at[e], at.plane(g)
        )

    def grads_piece(e, j):
        piece = (slice(None), rows_at(e, quarter), slice(None))
        return remote(
            grads_q.at[(at.next_z(j), *piece)], grads_line.at[(j - 1, *piece)], dl_s.at[0], dl_r.at[0],
            at.line(at.next_z(j)),
        )

    def expert_back(e, carry):
        half_rows = many // 2
        for part_at in range(2):
            some = slice(part_at * half_rows, (part_at + 1) * half_rows)
            groups = slice(part_at * ng // 2, (part_at + 1) * ng // 2)
            pre = nn(slots[groups, rows_at(e, sz.cap), :].reshape(half_rows, width), first[e])
            const, cubic = 0.7978845608028654, 0.044715
            square = pre * pre
            half = 0.5 * jnp.tanh(pre * (const + const * cubic * square)) + 0.5
            hidden_units = pre * half
            act[e, some] = hidden_units.astype(BF16)
            through = grad_act[e, some]
            dgate = nt(jnp.ones((8, sz.hidden), BF16), (hidden_units * through).astype(BF16))
            dgate_send[:, some] = jnp.where(iota((8, half_rows), 0) == e, dgate, dgate_send[:, some])
            slope = half * (1.0 + (1.0 - half) * (pre * (2.0 * const + 6.0 * const * cubic * square)))
            grads = (through * slope).astype(BF16)
            grad_pre[e, some] = grads
            spread = nt(grads, first[e]).astype(BF16).reshape(ng // 2, sz.cap, width)
            send_a[groups, rows_at(e, sz.cap), :] = spread
            for i in range(nz):
                grads_q[i, groups, rows_at(e, quarter), :] = spread[:, i * quarter : (i + 1) * quarter, 0:part_width]

        def step(i, carry):
            first_piece(e, (me + ng - 1 - i) % ng).start()
            return carry

        lax.fori_loop(0, ng - 1, step, 0)
        for j in range(1, nz):
            grads_piece(e, j).start()
        return carry

    dgate_send[...] = jnp.zeros_like(dgate_send)
    lax.fori_loop(0, sz.own, expert_back, 0)
    dgates = [
        remote(
            dgate_send.at[:, rows_at(at.next_group(k) * sz.cap // 128, 128)], dgate_recv.at[me], dg_s.at[0],
            dg_r.at[0], at.plane(at.next_group(k)),
        )
        for k in range(1, ng)
    ]
    for copy in dgates:
        copy.start()
    dgate_recv[me] = dgate_send[:, rows_at(me * sz.cap // 128, 128)]
    grad_flow = (send_a, grad_slots, da_s, da_r)
    value_flow = (send_b, values, va_s, va_r)
    for c in range(2, parts):
        start_part(c, *grad_flow)
    grad_slots[me] = send_a[me]

    def expert_value(e, carry):
        value = nn(act[e], second[e])
        gated = (value * gate_of(e)).astype(BF16).reshape(ng, sz.cap, width)
        send_b[:, rows_at(e, sz.cap), :] = gated
        return carry

    lax.fori_loop(0, sz.own, expert_value, 0)
    values[me] = send_b[me]

    def quarter_total(own, line, sums):
        total = own[z].astype(F32)
        for j in range(1, nz):
            total = total + line[j - 1].astype(F32)
        sums[...] = total.astype(BF16)


    def weight_grads(e, carry):
        grad_value = (expert_rows(cot_slots, e).astype(F32) * gate_of(e)).astype(BF16)
        grad_second[e] = tn(act[e], grad_value).astype(BF16)
        select[rows_at(e, width), 0 : sz.hidden] = tn(expert_rows(slots, e), grad_pre[e]).astype(BF16)
        return carry

    drain(dg_s.at[0], dg_r.at[0], dgate_recv.at[others], dgate_recv.at[others])
    mine = iota((8, 128), 1) // sz.cap == me * sz.cap % 128 // sz.cap
    for g in range(ng):
        folded = jnp.where(mine, dgate_recv[g], 0.0)
        folded = folded + pltpu.roll(folded, 64, 1)
        dgate_rows[g * sz.own : (g + 1) * sz.own, :] = folded[0 : sz.own]
    spread = jnp.concatenate([dgate_rows[...]] * (sz.slots // 128), 1)
    own_slot = iota((sz.experts, sz.slots), 1) // sz.cap == iota((sz.experts, sz.slots), 0)
    dgate = nt(split_high_low(jnp.where(own_slot, spread, 0.0)), select_t[...])
    dgate = dgate[0 : sz.experts] + dgate[sz.experts :]
    gates = gates_at[...]
    dlogits = (dgate - gates * jnp.sum(dgate, 0, keepdims=True)).astype(BF16)
    rt[...] = nn(dlogits, rows_block[...])
    part[...] = tn(dlogits, router_t[...])

    inner = at.inner()
    beside, across, mirror = at.mates()

    def line_copy(c, slot, send, recv, send_sems, recv_sems, relay_sems, last):
        if slot < 2:
            return remote(
                send.at[slot, :, lanes(c)], recv.at[slot, :, lanes(c)], send_sems.at[c], recv_sems.at[c],
                at.line((beside, across)[slot]),
            )
        by_way = 1 - inner if c != last else 0
        to = mirror + by_way * (beside - mirror)
        return remote(
            send.at[2, :, lanes(c)], recv.at[2 + by_way, :, lanes(c)], send_sems.at[c], relay_sems.at[c, by_way], at.line(to)
        )

    def scatter(c, source, base, own, *flow):
        if source is grads_back:
            places, flat = select_qt, source[...].reshape(few, part_width)
        else:
            places, flat = select_t, source[:, :, lanes(c)].reshape(sz.slots, part_width)
        for slot, target in ((2, mirror), (1, across), (0, beside), (None, z)):
            tokens = rows_at(target, pad)
            sums = nn(places[tokens, :], flat)
            if base is not None:
                sums = sums + base[tokens, lanes(c)]
            if slot is None:
                own[:, lanes(c)] = sums
                continue
            flow[0][slot, :, lanes(c)] = sums.astype(BF16)
            if slot == 1 and c != flow[-1]:

                @pl.when(inner == 0)
                def _():
                    line_copy(c, 1, *flow).start()
            else:
                line_copy(c, slot, *flow).start()

    def relay(c, send, recv, send_sems, recv_sems, relay_sems, last):
        @pl.when(inner == 1)
        def _():
            landed = recv.at[3, :, lanes(c)]
            pltpu.make_async_copy(landed, landed, relay_sems.at[c, 1]).wait()
            send[1, :, lanes(c)] = (send[1, :, lanes(c)].astype(F32) + recv[3, :, lanes(c)].astype(F32)).astype(BF16)
            line_copy(c, 1, send, recv, send_sems, recv_sems, relay_sems, last).start()

    def gathered(own, send, recv, send_sems, recv_sems, relay_sems, last):
        for c in range(parts):
            drain(send_sems.at[c], recv_sems.at[c], send.at[:, :, lanes(c)], recv.at[pl.ds(0, 2), :, lanes(c)])

            @pl.when(inner == 1 if c != last else True)
            def _(c=c):
                landed = recv.at[2, :, lanes(c)]
                pltpu.make_async_copy(landed, landed, relay_sems.at[c, 0]).wait()

        sums = own[...]
        for slot in range(3):
            sums = sums + recv[slot].astype(F32)
        return sums

    part_flow = (part_send, part_recv, pz_s, pz_r, pr_r, 0)
    mix_flow = (mix_send, mix_recv, mz_s, mz_r, mr_r, parts - 1)

    def wait_first(e, carry):
        piece = (others, rows_at(e, sz.cap), lanes(1))
        drain(d0_s.at[e], d0_r.at[e], send_a.at[piece], grad_slots.at[piece])
        return carry

    def exchange_quarters():
        drain(dl_s.at[0], dl_r.at[0], grads_line, grads_line)
        quarter_total(grads_q, grads_line, grads_sum)
        for copy in grads_moves:
            copy.start()
        for i in range(2):
            start_part(i, *value_flow)
        grads_back[me] = grads_sum[me]

    grads_moves = [quarter_move(k, grads_sum, grads_back, dq_s, dq_r) for k in range(1, ng)]
    order = [*range(1, parts), 0]
    exchange_quarters()
    done = 0
    for turn, c in enumerate(order):
        if c == 0:
            drain(dq_s.at[0], dq_r.at[0], grads_back.at[others], grads_back.at[others])
        elif c == 1:
            lax.fori_loop(0, sz.own, wait_first, 0)
        else:
            wait_part(c, *grad_flow)
        if c == parts - 1:
            for i in range(2, parts):
                start_part(i, *value_flow)
        scatter(c, grads_back if c == 0 else grad_slots, part, part_own, *part_flow)
        until = sz.own * (turn + 1) // parts
        lax.fori_loop(done, until, weight_grads, 0)
        done = until
        if turn > 0:
            relay(order[turn - 1], *part_flow)
    stores = [
        pltpu.make_async_copy(grad_second, grad_second_out, local_sem.at[2]),
        *[
            pltpu.make_async_copy(
                select.at[e * width : (e + 1) * width, 0 : sz.hidden], grad_first_out.at[e], local_sem.at[3 + e]
            )
            for e in range(sz.own)
        ],
    ]
    for copy in stores:
        copy.start()

    def send_mix(c):
        wait_part(c, *value_flow)
        scatter(c, values, None, mix_own, *mix_flow)
        if c:
            relay(c - 1, *mix_flow)

    send_mix(0)
    unit_two, factor_two = normalize(hidden_at[...])
    grad_normed = jnp.where(row_valid, gathered(part_own, *part_flow), 0.0)
    grad_hidden, gain_two = norm_back(grad_normed, unit_two, factor_two, gain_two_ref[...])
    grad_hidden = jnp.concatenate([cot_ref[...].astype(F32), zeros], 0) + jnp.where(row_valid, grad_hidden, 0.0)
    part_own[...] = grad_hidden
    grad_attn = grad_hidden.astype(BF16)

    def core_copy(i, other):
        n = 4 * (other - 1) + i
        return remote(
            core_send.at[other - 1, i], core_recv.at[other - 1, i], gc_s.at[n], gc_r.at[n], (d, (h + other) % nh, z)
        )

    def half_sum(i, sums):
        for other in range(1, nh):
            core_copy(i, other).wait()
            sums = sums + core_recv[other - 1, i].astype(F32)
        w_half[i] = sums
        band_send[i] = sums.astype(BF16)

    def band_copy(k, i):
        to = (d + k) % nd
        return remote(
            band_send.at[i, rows_at(to, band), :], band_recv.at[k - 1, i], gx_s.at[i], gx_r.at[i], (to, h, z)
        )

    for other in [*range(1, nh), 0]:
        sums = tn(grad_attn, mixed[:, rows_at((h + other) % nh, cp)])
        if other:
            core_send[other - 1, 3] = sums.astype(BF16)
            core_copy(3, other).start()
        else:
            w_half[3] = sums
    grad_mixed[...] = nn(grad_attn, w_full[3]).astype(BF16)
    half_sum(3, w_half[3])
    for k in range(1, nd):
        band_copy(k, 3).start()


    send_mix(1)

    def attend_back(pair):
        columns = rows_at(pair, 2 * HEAD_DIM)
        q_pair, k_pair, v_pair = (qkv[i, :, columns] for i in range(3))
        g_pair = grad_mixed[:, columns]
        dq, dk, dv = [], [], []
        for side in range(2):
            weights = probs[pair * 2 + side]
            soft = weights.astype(F32)
            g_own = jnp.where(halves[side], g_pair, jnp.zeros_like(g_pair))
            grad_soft = nt(g_own, v_pair)
            inner = jnp.sum(soft * grad_soft, -1, keepdims=True)
            grad_scores = (soft * (grad_soft - inner)).astype(BF16)
            dq.append(nn(grad_scores, k_pair))
            dk.append(tn(grad_scores, q_pair))
            dv.append(tn(weights, g_pair))
        grad_qkv[0, :, columns] = (jnp.where(halves[0], dq[0], dq[1]) * scale).astype(BF16)
        grad_qkv[1, :, columns] = (jnp.where(halves[0], dk[0], dk[1]) * scale).astype(BF16)
        grad_qkv[2, :, columns] = jnp.where(halves[0], dv[0], dv[1]).astype(BF16)

    unit_one, factor_one = normalize(jnp.concatenate([x_ref[...].astype(F32), zeros], 0))
    normed_one = (unit_one * gain_one_ref[...]).astype(BF16)
    core_pairs = cp // (2 * HEAD_DIM)
    for other in [*range(1, nh), 0]:
        core = (h + other) % nh
        for q in range(core_pairs):
            attend_back(core * core_pairs + q)
        for i in range(3):
            sums = tn(normed_one, grad_qkv[i, :, rows_at(core, cp)])
            if other:
                core_send[other - 1, i] = sums.astype(BF16)
                core_copy(i, other).start()
            else:
                half_sum(i, sums)
        if other == nh - 1:
            send_mix(2)
    for i in range(2):
        for k in range(1, nd):
            band_copy(k, i).start()

    grad_one = jnp.zeros((pad, width), F32)
    for i in range(3):
        grad_one = grad_one + nt(grad_qkv[i], w_full[i])
    grad_one = jnp.where(row_valid, grad_one, 0.0)
    grad_input, gain_one = norm_back(grad_one, unit_one, factor_one, gain_one_ref[...])
    grad_input_out[...] = (part_own[...] + grad_input)[0 : sz.rows].astype(BF16)

    small[...] = jnp.zeros_like(small)
    small[0:1, :] = gain_one
    small[1:2, :] = gain_two
    small[2:3, 0:128] = peak_at[0:1, :]
    peak_row = iota(small.shape, 0) == 2

    def join(a, b):
        return jnp.where(peak_row, jnp.maximum(a, b), a + b)

    small_copies = []
    for other in range(1, nh):
        device, n = (d, (h + other) % nh, z), 2 * (other - 1)
        small_copies += [
            remote(small, small_core.at[other - 1], sc_s.at[n], sc_r.at[n], device),
            remote(rt, rt_core.at[other - 1], sc_s.at[n + 1], sc_r.at[n + 1], device),
        ]
    for copy in small_copies:
        copy.start()
    for copy in small_copies:
        copy.wait()
    for other in range(1, nh):
        small[...] = join(small[...], small_core[other - 1])
        rt[...] = rt[...] + rt_core[other - 1]
    small_send[0] = small[...]
    small_copies = []
    for k in range(1, nd):
        to = (d + k) % nd
        small_copies += [
            remote(small_send.at[0], small_x.at[k - 1], sx_s.at[0], sx_r.at[0], (to, h, z)),
            remote(rt.at[:, rows_at(to, band)], rt_x.at[k - 1], sx_s.at[1], sx_r.at[1], (to, h, z)),
        ]
    for copy in small_copies:
        copy.start()
    for k in range(1, nd):
        band_copy(k, 2).start()
    send_mix(3)

    def line_piece(i, j):
        to = at.next_z(j)
        return remote(line_send.at[i, rows_at(to, rp), :], line_recv.at[j - 1, i], gl_s.at[i], gl_r.at[i], at.line(to))

    def end_band(i):
        drain(gx_s.at[i], gx_r.at[i], band_recv.at[:, i], band_recv.at[:, i])
        sums = w_half[i, rows_at(d, band), :]
        for k in range(1, nd):
            sums = sums + band_recv[k - 1, i].astype(F32)
        w_half[i, 0:band, :] = sums
        line_send[i] = sums.astype(BF16)
        for j in range(1, nz):
            line_piece(i, j).start()

    for i in (3, 0, 1):
        end_band(i)
    drain(sx_s.at[0], sx_r.at[0], small_x, small_x)
    drain(sx_s.at[1], sx_r.at[1], rt_x, rt_x)
    router_sum = rt[:, rows_at(d, band)]
    for k in range(1, nd):
        small[...] = join(small[...], small_x[k - 1])
        router_sum = router_sum + rt_x[k - 1]
    rt_z[nz - 1] = router_sum
    small_send[1] = small[...]
    for j in range(1, nz):
        device = at.line(at.next_z(j))
        remote(small_send.at[1], small_z.at[j - 1], gl_s.at[4], gl_r.at[4], device).start()
        remote(rt_z.at[nz - 1], rt_z.at[j - 1], gl_s.at[5], gl_r.at[5], device).start()
    end_band(2)

    mix = gathered(mix_own, *mix_flow)
    output_out[...] = (hidden_at[...] + mix)[0 : sz.rows].astype(BF16)

    for i in range(4):
        drain(gl_s.at[i], gl_r.at[i], line_recv.at[:, i], line_recv.at[:, i])
    for n, landed in ((4, small_z), (5, rt_z.at[pl.ds(0, nz - 1)])):
        drain(gl_s.at[n], gl_r.at[n], landed, landed)
    totals = small[...]
    router_sum = rt_z[nz - 1]
    for j in range(1, nz):
        totals = join(totals, small_z[j - 1])
        router_sum = router_sum + rt_z[j - 1]
    gain_one_out[...] = totals[0:1]
    gain_two_out[...] = totals[1:2]
    rr = sz.router_rows
    own_router = router_sum[:, 0:rr]
    for i in range(1, nh):
        own_router = jnp.where(h == i, router_sum[:, i * rr : (i + 1) * rr], own_router)
    router_out[...] = own_router
    tau = tau_ref[...]
    factor = jnp.sqrt(tau / jnp.maximum(totals[2:3, 0:HEADS], tau))
    column = iota((1, cp), 1) // HEAD_DIM + h * (cp // HEAD_DIM)
    scale_row = jnp.zeros((1, cp), F32)
    for head in range(HEADS):
        scale_row = jnp.where(column == head, factor[:, head : head + 1], scale_row)
    for i in range(2):
        clipped_out[i] = (w_qkv_ref[i].astype(F32) * scale_row).astype(BF16)
    for i in range(4):
        sums = w_half[i, rows_at(z, rp), :]
        for j in range(1, nz):
            sums = sums + line_recv[j - 1, i].astype(F32)
        if i < 3:
            qkv_out[i] = sums
        else:
            out_out[...] = sums
    for copy in stores:
        copy.wait()


def finish_kernel(sz, *refs):
    sources, results, held = refs[0:10], refs[10:20], refs[20:28]
    halves_in, full_out, in_sems, out_sems, small_in, small_out = refs[28:]
    pieces = [(i, e) for e in range(sz.own) for i in range(2)]
    loads = [pltpu.make_async_copy(sources[8 + i].at[e], halves_in.at[i, e], in_sems.at[i, e]) for i, e in pieces]
    stores = [pltpu.make_async_copy(full_out.at[i, e], results[8 + i].at[e], out_sems.at[i, e]) for i, e in pieces]
    small_loads = [pltpu.make_async_copy(sources[n], held[n], small_in.at[n]) for n in range(8)]
    small_stores = [pltpu.make_async_copy(held[n], results[n], small_out.at[n]) for n in range(8)]
    for copy in loads + small_loads:
        copy.start()
    for (i, e), load, store in zip(pieces, loads, stores):
        load.wait()
        full_out[i, e] = halves_in[i, e].astype(F32)
        store.start()
    for load, store in zip(small_loads, small_stores):
        load.wait()
        store.start()
    for copy in stores + small_stores:
        copy.wait()


def fast_body(
    sz, inputs, cotangent, routes, gain_attn, gain_expert, tau, w_qkv, w_out_attn, w_router, w_in, w_out
):
    ng, nz, nd, nh, pad, width, own = sz.groups, sz.nt, sz.nd, sz.nh, sz.pad, sz.width, sz.own
    rp, cp, band, parts, block = sz.row_piece, sz.col_piece, sz.band, sz.parts, sz.block
    many, hidden = ng * sz.cap, sz.hidden
    on_chip, anywhere = pl.BlockSpec(memory_space=pltpu.VMEM), pl.BlockSpec(memory_space=pltpu.HBM)

    def shape(dims, dtype):
        return jax.ShapeDtypeStruct(dims, dtype)

    def half(*dims):
        return pltpu.VMEM(dims, BF16)

    def full(*dims):
        return pltpu.VMEM(dims, F32)

    def pair(*dims):
        return [pltpu.SemaphoreType.DMA(dims)] * 2

    slot_buffer = half(ng, sz.group_slots, width)
    line_buffer = half(nz - 1, pad, width)
    quarter_dims = (ng, own * (sz.cap // nz), width // parts)
    quarter_buffer, few = half(*quarter_dims), ng * own * (sz.cap // nz)
    rr = sz.router_rows
    smalls = (
        shape(inputs.shape, BF16), shape(inputs.shape, BF16), shape((1, width), F32), shape((1, width), F32),
        shape((3, rp, cp), F32), shape((rp, cp), F32), shape((sz.experts, rr), F32), shape((2, rp, cp), BF16),
    )
    packed = pl.pallas_call(
        functools.partial(block_kernel, sz),
        out_shape=(*smalls, shape(w_in.shape, BF16), shape(w_out.shape, BF16)),
        in_specs=[on_chip] * 9 + [anywhere] * 2,
        out_specs=(on_chip,) * 8 + (anywhere,) * 2,
        scratch_shapes=[
            half(4, rp, cp), half(4, width, width), half(sz.experts, 128), half(ng, sz.experts, 128),
            half(sz.experts, width), full(8, block), full(block, 128), half(sz.slots, block), half(block, sz.slots), half(few, block), half(block, few),
            half(block, width), half(block, width), *[slot_buffer] * 6,
            quarter_buffer, half(nz, *quarter_dims), half(nz, *quarter_dims), half(nz - 1, *quarter_dims), quarter_buffer,
            quarter_buffer,
            half(own, width, hidden), half(own, hidden, width), half(own, many, hidden), half(own, many, hidden),
            full(own, many, hidden), half(own, hidden, width),
            full(sz.experts, 128), full(ng, 8, 128), full(sz.experts, block), full(8, many),
            full(ng, 8, 128), full(sz.experts, 128),
            half(3, pad, width), half(HEADS, pad, pad), half(pad, width), full(pad, width), full(8, 128),
            full(block, width), full(pad, width), line_buffer, half(nz, pad, width), full(pad, width), line_buffer,
            half(nz, pad, width),
            half(pad, width), half(3, pad, width), half(nh - 1, 4, width, cp), half(nh - 1, 4, width, cp),
            full(4, width, cp), half(4, width, cp), half(nd - 1, 4, band, cp), half(4, band, cp),
            half(nz - 1, 4, rp, cp),
            full(8, width), full(2, 8, width), full(nh - 1, 8, width), full(nd - 1, 8, width), full(nz - 1, 8, width),
            full(sz.experts, width), full(nh - 1, sz.experts, width), full(nd - 1, sz.experts, band),
            full(nz, sz.experts, band),
            *pair(4), *pair(4), *pair(4 * (nh - 1)), *pair(1), *pair(parts), *pair(parts), *pair(parts), *pair(parts),
            *pair(1), *pair(own), *pair(parts), *pair(parts), *pair(1), *pair(parts), *pair(parts), *pair(4 * (nh - 1)),
            *pair(4), *pair(6), *pair(2 * (nh - 1)), *pair(2), *pair(1), *pair(1), *pair(1), *pair(1),
            *pair(parts, 2),
            pltpu.SemaphoreType.DMA((3 + own,)),
        ],
        compiler_params=pltpu.CompilerParams(collective_id=0, has_side_effects=True, vmem_limit_bytes=62 * 2**20),
        name="block",
    )(
        inputs, cotangent, routes.T, gain_attn[None, :], gain_expert[None, :], w_qkv, w_out_attn.T, w_router.T,
        tau[None, :], w_in, w_out,
    )

    both, dma = (2, *w_in.shape), pltpu.SemaphoreType.DMA
    output, grad_input, gain_one, gain_two, grad_qkv, grad_out, grad_router, clipped, grad_first, grad_second = (
        pl.pallas_call(
            functools.partial(finish_kernel, sz),
            out_shape=(*smalls, shape(w_in.shape, F32), shape(w_out.shape, F32)),
            in_specs=[anywhere] * 10,
            out_specs=(anywhere,) * 10,
            scratch_shapes=[
                *[pltpu.VMEM(x.shape, x.dtype) for x in smalls], half(*both), full(*both), dma((2, own)), dma((2, own)),
                dma((8,)), dma((8,)),
            ],
            compiler_params=pltpu.CompilerParams(vmem_limit_bytes=62 * 2**20),
            name="finish",
        )(*packed)
    )
    return (
        output, grad_input, gain_one[0], gain_two[0], grad_qkv, grad_out.T, grad_router.T, grad_first, grad_second,
        clipped,
    )


def gelu_tanh(inputs):
    return (
        0.5
        * inputs
        * (1.0 + jnp.tanh(0.7978845608028654 * (inputs + 0.044715 * inputs * inputs * inputs)))
    )


def unit_and_factor(inputs):
    centered = inputs - jnp.mean(inputs, -1, keepdims=True)
    factor = lax.rsqrt(jnp.mean(centered * centered, -1, keepdims=True) + 1e-06)
    return (centered * factor, factor)


def general_norm_back(grad_norm, unit_rows, factor, gain):
    grad, gain_row = norm_back(grad_norm, unit_rows, factor, gain)
    return grad, gain_row[0]


def attn_forward(block_parts):
    queries, key_rows, value_rows = block_parts
    scores = jnp.einsum(
        "bhqd,bhkd->bhqk", queries, key_rows, preferred_element_type=jnp.float32
    ) * HEAD_DIM ** (-0.5)
    row_peak = jnp.max(scores, -1, keepdims=True)
    exponent = jnp.exp(scores - row_peak)
    summed = jnp.sum(exponent, -1, keepdims=True)
    soft_weights = (exponent / summed).astype(jnp.bfloat16)
    mixed = jnp.einsum(
        "bhqk,bhkd->bhqd", soft_weights, value_rows, preferred_element_type=jnp.float32
    ).astype(jnp.bfloat16)
    return (mixed, (row_peak + jnp.log(summed))[..., 0], jnp.max(row_peak, axis=(0, 2, 3)))


def attn_backward(block_parts):
    queries, key_rows, value_rows, grad_mixed, log_total = block_parts
    score_scale = HEAD_DIM ** (-0.5)
    scores = (
        jnp.einsum("bhqd,bhkd->bhqk", queries, key_rows, preferred_element_type=jnp.float32)
        * score_scale
    )
    soft_weights = jnp.exp(scores - log_total[..., None])
    grad_soft = jnp.einsum(
        "bhqd,bhkd->bhqk", grad_mixed, value_rows, preferred_element_type=jnp.float32
    )
    inner_sum = jnp.sum(soft_weights * grad_soft, -1, keepdims=True)
    grad_scores = (soft_weights * (grad_soft - inner_sum)).astype(jnp.bfloat16)
    grad_query = (
        jnp.einsum("bhqk,bhkd->bhqd", grad_scores, key_rows, preferred_element_type=jnp.float32)
        * score_scale
    ).astype(jnp.bfloat16)
    grad_key = (
        jnp.einsum("bhqk,bhqd->bhkd", grad_scores, queries, preferred_element_type=jnp.float32)
        * score_scale
    ).astype(jnp.bfloat16)
    grad_value = jnp.einsum(
        "bhqk,bhqd->bhkd",
        soft_weights.astype(jnp.bfloat16),
        grad_mixed,
        preferred_element_type=jnp.float32,
    ).astype(jnp.bfloat16)
    return (grad_query, grad_key, grad_value)


def general_body(
    inputs, cotangent, routes, gain_attn, gain_expert, tau, w_qkv, w_out_attn, w_router, w_in, w_out
):
    row_count, width = inputs.shape
    n_dp = lax.axis_size("dp")
    n_heads = lax.axis_size("heads")
    n_tensor = lax.axis_size("tensor")
    row_piece = w_qkv.shape[1]
    col_piece = w_qkv.shape[2]
    own_heads = col_piece // HEAD_DIM
    head_start = lax.axis_index("heads") * col_piece
    x_float = inputs.astype(jnp.float32)
    unit_one, factor_one = unit_and_factor(x_float)
    normed_one = (unit_one * gain_attn).astype(jnp.bfloat16)
    stack_qkv, stack_out = (
        lax.all_gather(w_qkv[None], ("dp", "heads", "tensor"), axis=0, tiled=True),
        lax.all_gather(w_out_attn[None], ("dp", "heads", "tensor"), axis=0, tiled=True),
    )
    full_qkv = (
        stack_qkv.reshape(n_dp, n_heads, n_tensor, 3, row_piece, col_piece)
        .transpose(3, 0, 2, 4, 1, 5)
        .reshape(3, width, width)
    )
    full_out = (
        stack_out.reshape(n_dp, n_heads, n_tensor, col_piece, row_piece)
        .transpose(1, 3, 0, 2, 4)
        .reshape(width, width)
    )
    proj_w = lax.dynamic_slice_in_dim(full_qkv, head_start, col_piece, 2)
    attn_w = lax.dynamic_slice_in_dim(full_out, head_start, col_piece, 0)
    normed_all = lax.all_gather(normed_one, "heads", axis=0, tiled=True)
    head_cols = attn_w.shape[0]
    local_heads = head_cols // HEAD_DIM
    joined_w = jnp.concatenate([proj_w[0], proj_w[1], proj_w[2]], 1)
    projected = jnp.dot(normed_all, joined_w, preferred_element_type=jnp.float32).astype(
        jnp.bfloat16
    )
    images = normed_all.shape[0] // SEQ
    per_block = 4 if images % 4 == 0 else 3 if images % 3 == 0 else 2 if images % 2 == 0 else 1
    block_shape = (images // per_block, per_block, SEQ, local_heads, HEAD_DIM)

    def to_blocks(row_matrix):
        return row_matrix.reshape(block_shape).transpose(0, 1, 3, 2, 4)

    def from_blocks(block_array):
        return block_array.transpose(0, 1, 3, 2, 4).reshape(-1, head_cols)

    queries = to_blocks(projected[:, :head_cols])
    key_rows = to_blocks(projected[:, head_cols : 2 * head_cols])
    value_rows = to_blocks(projected[:, 2 * head_cols :])
    mixed, log_total, head_peaks = lax.map(attn_forward, (queries, key_rows, value_rows))
    mixed_rows = from_blocks(mixed)
    block_peak = jnp.max(head_peaks, 0)
    attn_out = lax.psum_scatter(
        jnp.dot(mixed_rows, attn_w, preferred_element_type=jnp.float32),
        "heads",
        scatter_dimension=0,
        tiled=True,
    )
    peak_full = lax.dynamic_update_slice_in_dim(
        jnp.full((HEADS,), -1e30, jnp.float32), block_peak, lax.axis_index("heads") * local_heads, 0
    )
    hidden = x_float + attn_out
    peak_all = lax.pmax(peak_full, ("dp", "heads", "tensor"))
    peak_logit = lax.dynamic_slice_in_dim(
        peak_all, lax.axis_index("heads") * own_heads, own_heads, 0
    )
    unit_two, factor_two = unit_and_factor(hidden)
    normed_two = (unit_two * gain_expert).astype(jnp.bfloat16)
    group_rows, group_cot = (
        lax.all_gather(normed_two, "tensor", axis=0, tiled=True),
        lax.all_gather(cotangent, "tensor", axis=0, tiled=True),
    )
    first_w, second_w, router_w = (
        lax.all_gather(w_in, ("dp", "heads"), axis=0, tiled=True),
        lax.all_gather(w_out, ("dp", "heads"), axis=0, tiled=True),
        lax.all_gather(w_router, ("dp", "heads"), axis=0, tiled=True),
    )
    logits = jnp.dot(group_rows, router_w, preferred_element_type=jnp.float32)
    chosen = jnp.take_along_axis(logits, routes, 1)
    exponent = jnp.exp(chosen - jnp.max(chosen, -1, keepdims=True))
    gate_values = exponent / jnp.sum(exponent, -1, keepdims=True)
    group_count = routes.shape[0]
    experts = router_w.shape[1]
    capacity = (group_count * 5 // (16 * experts) + 1) * 8
    flat_ids = routes.reshape(-1)
    ordering = jnp.argsort(flat_ids, stable=True)
    sorted_ids = flat_ids[ordering]
    counts = jnp.sum(
        (flat_ids[:, None] == jnp.arange(experts, dtype=jnp.int32)[None, :]).astype(jnp.int32), 0
    )
    expert_ids = jnp.arange(experts, dtype=jnp.int32)
    starts = jnp.sum(jnp.where(expert_ids[None, :] < expert_ids[:, None], counts[None, :], 0), 1)
    slot_rank = jnp.arange(2 * group_count, dtype=jnp.int32) - starts[sorted_ids]
    slot_table = (
        jnp.full((experts * capacity,), 2 * group_count, jnp.int32)
        .at[sorted_ids * capacity + slot_rank]
        .set(ordering)
    )
    slot_token = slot_table // 2
    padded_rows = jnp.concatenate([group_rows, jnp.zeros((1, width), jnp.bfloat16)], 0)
    slot_in = padded_rows[slot_token].reshape(experts, capacity, width)
    slot_gate = jnp.concatenate([gate_values.reshape(-1), jnp.zeros((1,), jnp.float32)], 0)[
        slot_table
    ]
    pre_gelu = jnp.einsum("ecd,edf->ecf", slot_in, first_w, preferred_element_type=jnp.float32)
    activated = gelu_tanh(pre_gelu).astype(jnp.bfloat16)
    slot_out = jnp.einsum(
        "ecf,efd->ecd", activated, second_w, preferred_element_type=jnp.float32
    ).reshape(-1, width)
    partial_value = (
        jnp.zeros((group_count + 1, width), jnp.float32)
        .at[slot_token]
        .add(slot_gate[:, None] * slot_out)[:group_count]
    )
    expert_mix = lax.psum_scatter(
        partial_value.astype(jnp.bfloat16), "tensor", scatter_dimension=0, tiled=True
    ).astype(jnp.float32)
    output = (hidden + expert_mix).astype(jnp.bfloat16)
    padded_cot = jnp.concatenate([group_cot, jnp.zeros((1, width), jnp.bfloat16)], 0)
    slot_cot = padded_cot[slot_token].astype(jnp.float32)
    grad_slot_out = (
        (slot_gate[:, None] * slot_cot).astype(jnp.bfloat16).reshape(experts, capacity, width)
    )
    gate_part = (
        jnp.zeros((2 * group_count + 1,), jnp.float32)
        .at[slot_table]
        .add(jnp.sum(slot_cot * slot_out, -1))[: 2 * group_count]
        .reshape(group_count, 2)
    )
    grad_act = jnp.einsum(
        "ecd,efd->ecf", grad_slot_out, second_w, preferred_element_type=jnp.float32
    )
    grad_pre = jax.vjp(gelu_tanh, pre_gelu)[1](grad_act)[0].astype(jnp.bfloat16)
    grad_first = jnp.einsum("ecd,ecf->edf", slot_in, grad_pre, preferred_element_type=jnp.float32)
    grad_second = jnp.einsum(
        "ecf,ecd->efd", activated, grad_slot_out, preferred_element_type=jnp.float32
    )
    grad_slots = jnp.einsum(
        "ecf,edf->ecd", grad_pre, first_w, preferred_element_type=jnp.float32
    ).reshape(-1, width)
    grad_part = (
        jnp.zeros((group_count + 1, width), jnp.float32)
        .at[slot_token]
        .add(grad_slots)[:group_count]
    )
    grad_normed_two, grad_gates = (
        lax.psum_scatter(
            grad_part.astype(jnp.bfloat16), "tensor", scatter_dimension=0, tiled=True
        ).astype(jnp.float32),
        lax.psum_scatter(
            gate_part.astype(jnp.bfloat16), "tensor", scatter_dimension=0, tiled=True
        ).astype(jnp.float32),
    )
    shard_first, shard_second = (
        lax.psum_scatter(
            grad_first.astype(jnp.bfloat16), ("dp", "heads"), scatter_dimension=0, tiled=True
        ).astype(jnp.float32),
        lax.psum_scatter(
            grad_second.astype(jnp.bfloat16), ("dp", "heads"), scatter_dimension=0, tiled=True
        ).astype(jnp.float32),
    )
    offset = lax.axis_index("tensor") * row_count
    local_gates = lax.dynamic_slice_in_dim(gate_values, offset, row_count, 0)
    local_routes = lax.dynamic_slice_in_dim(routes, offset, row_count, 0)
    grad_chosen = local_gates * (grad_gates - jnp.sum(local_gates * grad_gates, -1, keepdims=True))
    columns = jnp.arange(experts, dtype=jnp.int32)[None, :]
    grad_logits = (
        jnp.where(local_routes[:, 0:1] == columns, grad_chosen[:, 0:1], 0.0)
        + jnp.where(local_routes[:, 1:2] == columns, grad_chosen[:, 1:2], 0.0)
    ).astype(jnp.bfloat16)
    grad_normed_two = grad_normed_two + jnp.einsum(
        "re,de->rd", grad_logits, router_w, preferred_element_type=jnp.float32
    )
    router_term = jnp.einsum(
        "rd,re->de", normed_two, grad_logits, preferred_element_type=jnp.float32
    )
    grad_hidden_norm, gain_two_term = general_norm_back(grad_normed_two, unit_two, factor_two, gain_expert)
    grad_hidden = cotangent.astype(jnp.float32) + grad_hidden_norm
    grad_attn = lax.all_gather(grad_hidden.astype(jnp.bfloat16), "heads", axis=0, tiled=True)
    grad_mixed = jnp.einsum(
        "rd,cd->rc", grad_attn, attn_w, preferred_element_type=jnp.float32
    ).astype(jnp.bfloat16)
    out_term = jnp.einsum("rc,rd->cd", mixed_rows, grad_attn, preferred_element_type=jnp.float32)
    grad_query, grad_key, grad_value = lax.map(
        attn_backward, (queries, key_rows, value_rows, to_blocks(grad_mixed), log_total)
    )
    grad_proj = jnp.concatenate(
        [from_blocks(grad_query), from_blocks(grad_key), from_blocks(grad_value)], 1
    )
    grad_normed_one = lax.psum_scatter(
        jnp.einsum("rc,dc->rd", grad_proj, joined_w, preferred_element_type=jnp.float32).astype(
            jnp.bfloat16
        ),
        "heads",
        scatter_dimension=0,
        tiled=True,
    ).astype(jnp.float32)
    proj_term = jnp.einsum("rd,rc->dc", normed_all, grad_proj, preferred_element_type=jnp.float32)
    proj_stack = jnp.stack(
        [
            proj_term[:, :head_cols],
            proj_term[:, head_cols : 2 * head_cols],
            proj_term[:, 2 * head_cols :],
        ],
        0,
    )
    whole_proj = lax.dynamic_update_slice_in_dim(
        jnp.zeros((3, width, width), jnp.float32), proj_stack, head_start, 2
    )
    whole_out = lax.dynamic_update_slice_in_dim(
        jnp.zeros((width, width), jnp.float32), out_term, head_start, 0
    )
    send_qkv = (
        whole_proj.reshape(3, n_dp, n_tensor, row_piece, n_heads, col_piece)
        .transpose(1, 4, 2, 0, 3, 5)
        .reshape(-1, 3, row_piece, col_piece)
    )
    send_out = (
        whole_out.reshape(n_heads, col_piece, n_dp, n_tensor, row_piece)
        .transpose(2, 0, 3, 1, 4)
        .reshape(-1, col_piece, row_piece)
    )
    shard_proj, shard_attn = (
        lax.psum_scatter(send_qkv, ("dp", "heads", "tensor"), scatter_dimension=0, tiled=True),
        lax.psum_scatter(send_out, ("dp", "heads", "tensor"), scatter_dimension=0, tiled=True),
    )
    grad_input_norm, gain_one_term = general_norm_back(grad_normed_one, unit_one, factor_one, gain_attn)
    grad_input = (grad_hidden + grad_input_norm).astype(jnp.bfloat16)
    gain_one_grad, gain_two_grad, router_all = lax.psum(
        (gain_one_term, gain_two_term, router_term), ("dp", "heads", "tensor")
    )
    router_grad = lax.dynamic_slice_in_dim(
        router_all, lax.axis_index(("dp", "heads")) * w_router.shape[0], w_router.shape[0], 0
    )
    local_tau = lax.dynamic_slice_in_dim(tau, lax.axis_index("heads") * own_heads, own_heads, 0)
    clip_factor = jnp.sqrt(local_tau / jnp.maximum(peak_logit, local_tau))
    clipped = (w_qkv[:2].astype(jnp.float32) * jnp.repeat(clip_factor, HEAD_DIM)).astype(
        jnp.bfloat16
    )
    return (
        output,
        grad_input,
        gain_one_grad,
        gain_two_grad,
        shard_proj[0],
        shard_attn[0],
        router_grad,
        shard_first,
        shard_second,
        clipped,
    )


def body(*args):
    inputs, _, routes, _, _, _, w_qkv, _, w_router, w_in, _ = args
    sz = Sizes(
        lax.axis_size("dp"), lax.axis_size("heads"), lax.axis_size("tensor"), inputs, routes, w_qkv, w_router, w_in
    )
    if sz.fits():
        return fast_body(sz, *args)
    return general_body(*args)


def solution(mesh):
    return jax.shard_map(
        body,
        mesh=mesh,
        in_specs=(
            P(("dp", "heads", "tensor"), None),
            P(("dp", "heads", "tensor"), None),
            P(("dp", "heads"), None),
            P(),
            P(),
            P(),
            P(None, ("dp", "tensor"), "heads"),
            P("heads", ("dp", "tensor")),
            P(("dp", "heads"), None),
            P(("dp", "heads"), None, "tensor"),
            P(("dp", "heads"), "tensor", None),
        ),
        out_specs=(
            P(("dp", "heads", "tensor"), None),
            P(("dp", "heads", "tensor"), None),
            P(),
            P(),
            P(None, ("dp", "tensor"), "heads"),
            P("heads", ("dp", "tensor")),
            P(("dp", "heads"), None),
            P(("dp", "heads"), None, "tensor"),
            P(("dp", "heads"), "tensor", None),
            P(None, ("dp", "tensor"), "heads"),
        ),
        check_vma=False,
    )
```

```python
import functools
import jax
import jax.numpy as jnp
from jax import lax
from jax.experimental import pallas as pl
from jax.experimental.pallas import tpu as pltpu
from jax.sharding import PartitionSpec as P

HEADS = 8
HEAD_DIM = 64
SEQ = 197
F32 = jnp.float32
BF16 = jnp.bfloat16
MESH = pl.DeviceIdType.MESH
NEG = -1e30


class Sizes:
    def __init__(self, n_dp, n_heads, n_tensor, inputs, routes, w_qkv, w_router, w_in):
        self.nd, self.nh, self.nt = n_dp, n_heads, n_tensor
        self.groups = n_dp * n_heads
        self.rows, self.width = inputs.shape
        self.pad = -(-self.rows // 16) * 16
        self.block = self.pad * n_tensor
        self.block_rows = routes.shape[0]
        self.own = w_in.shape[0]
        self.hidden = w_in.shape[2]
        self.experts = self.own * self.groups
        self.cap = (self.block_rows * 5 // (16 * self.experts) + 1) * 8
        self.group_slots = self.own * self.cap
        self.slots = self.experts * self.cap
        self.row_piece, self.col_piece = w_qkv.shape[1], w_qkv.shape[2]
        self.band = self.row_piece * n_tensor
        self.router_rows = w_router.shape[0]
        self.parts = 4

    def fits(self):
        return (
            self.rows == SEQ
            and self.nt == 4
            and self.parts == 4
            and self.block_rows == self.rows * self.nt
            and self.cap == 64
            and self.experts == 32
            and self.group_slots % 128 == 0
            and self.col_piece % 128 == 0
            and self.row_piece % 16 == 0
            and self.router_rows % 16 == 0
            and self.own * self.groups * 4 == 128
            and self.width == HEADS * HEAD_DIM
            and self.block * self.width * 2 <= 2**20
            and self.own * self.width <= self.slots
            and self.hidden <= self.block
            and self.hidden == self.width
            and self.cap % (16 * self.nt) == 0
            and self.width // self.parts % 128 == 0
        )


def nn(a, b):
    return jnp.dot(a, b, preferred_element_type=F32)


def nt(a, b):
    return lax.dot_general(a, b, (((1,), (1,)), ((), ())), preferred_element_type=F32)


def tn(a, b):
    return lax.dot_general(a, b, (((0,), (0,)), ((), ())), preferred_element_type=F32)


def iota(shape, axis):
    return lax.broadcasted_iota(jnp.int32, shape, axis)


def normalize(rows):
    centered = rows - jnp.mean(rows, -1, keepdims=True)
    factor = lax.rsqrt(jnp.mean(centered * centered, -1, keepdims=True) + 1e-06)
    return centered * factor, factor


def norm_back(grad_norm, unit_rows, factor, gain):
    grad_hat = grad_norm * gain
    inner = (
        grad_hat
        - jnp.mean(grad_hat, -1, keepdims=True)
        - unit_rows * jnp.mean(grad_hat * unit_rows, -1, keepdims=True)
    )
    return factor * inner, jnp.sum(grad_norm * unit_rows, 0, keepdims=True)


def split_high_low(values):
    high = values.astype(BF16)
    low = (values - high.astype(F32)).astype(BF16)
    return jnp.concatenate([high, low], 0)


class Place:
    def __init__(self, sz):
        self.sz = sz
        self.d = lax.axis_index("dp")
        self.h = lax.axis_index("heads")
        self.z = lax.axis_index("tensor")
        self.group = self.d * sz.nh + self.h

    def plane(self, group):
        return (group // self.sz.nh, group % self.sz.nh, self.z)

    def line(self, z):
        return (self.d, self.h, z)

    def next_group(self, k):
        return (self.group + k) % self.sz.groups

    def next_z(self, j):
        return (self.z + j) % self.sz.nt

    def inner(self):
        return (self.z + 1) % 4 // 2

    def mates(self):
        return self.z + 1 - 2 * (self.z % 2), (self.z + 2) % 4, 3 - self.z

    def enter(self):
        sz = self.sz
        barrier = pltpu.get_barrier_semaphore()
        for k in range(1, sz.groups):
            pl.semaphore_signal(barrier, inc=1, device_id=self.plane(self.next_group(k)), device_id_type=MESH)
        for j in range(1, sz.nt):
            pl.semaphore_signal(barrier, inc=1, device_id=self.line(self.next_z(j)), device_id_type=MESH)
        pl.semaphore_wait(barrier, sz.groups + sz.nt - 2)


def remote(src, dst, send, recv, device):
    return pltpu.make_async_remote_copy(
        src_ref=src, dst_ref=dst, send_sem=send, recv_sem=recv, device_id=device, device_id_type=MESH
    )


def drain(send_sem, recv_sem, sent, landed):
    pltpu.make_async_copy(sent, sent, send_sem).wait()
    pltpu.make_async_copy(landed, landed, recv_sem).wait()


def route_table(sz, routes_ref, table):
    table[...] = jnp.full_like(table, -1.0)
    for z in range(sz.nt):
        table[0:2, z * sz.pad : z * sz.pad + sz.rows] = routes_ref[:, z * sz.rows : (z + 1) * sz.rows].astype(F32)


def block_kernel(
    sz, x_ref, cot_ref, routes_ref, gain_one_ref, gain_two_ref, w_qkv_ref, w_out_ref, w_router_ref, tau_ref, first_hbm,
    second_hbm, output_out, grad_input_out, gain_one_out, gain_two_out, qkv_out, out_out, router_out, clipped_out,
    grad_first_out, grad_second_out,
    w_own, w_full, router_own, router_full, router_t, route_rows, route_columns, select, select_t, select_q, select_qt,
    cot_block, rows_block, send_a, send_b, cot_slots, slots, grad_slots, values,
    rows_q, rows_line, grads_q, grads_line, grads_sum, grads_back, first, second, act, grad_pre, grad_act,
    gate_send, gate_recv, gates_at, dgate_send, dgate_recv, dgate_rows,
    qkv, probs, mixed, hidden_at, peak_at, part, part_own, part_send, part_recv, mix_own, mix_send, mix_recv,
    grad_mixed, grad_qkv, core_send, core_recv, w_half, band_send, band_recv, line_send, line_recv,
    small, small_send, small_core, small_x, small_z, rt, rt_core, rt_x, rt_z,
    wz_s, wz_r, wx_s, wx_r, wc_s, wc_r, r_s, r_r, qz_s, qz_r, nz_s, nz_r, qa_s, qa_r, na_s, na_r, ga_s, ga_r,
    d0_s, d0_r, da_s, da_r, va_s, va_r, dg_s, dg_r, pz_s, pz_r, mz_s, mz_r, gc_s, gc_r, gx_s, gx_r, gl_s, gl_r,
    sc_s, sc_r, sx_s, sx_r, dl_s, dl_r, dq_s, dq_r, nq_s, nq_r, nl_s, nl_r, pr_r, mr_r,
    local_sem,
):
    at = Place(sz)
    d, h, z, me = at.d, at.h, at.z, at.group
    nd, nh, nz, ng = sz.nd, sz.nh, sz.nt, sz.groups
    band, rp, cp, pad, width = sz.band, sz.row_piece, sz.col_piece, sz.pad, sz.width
    many = ng * sz.cap
    parts, part_width = sz.parts, width // sz.parts

    def lanes(c):
        return pl.ds(c * part_width, part_width)

    def rows_at(n, size):
        return pl.ds(pl.multiple_of(n * size, size), size)

    own_block, own_columns = rows_at(z, pad), rows_at(h, cp)

    w_own[0:3] = w_qkv_ref[...]
    w_own[3] = w_out_ref[...]
    router_own[...] = jnp.zeros_like(router_own)
    router_own[:, 0 : sz.router_rows] = w_router_ref[...]
    cot_block[own_block] = jnp.concatenate(
        [cot_ref[...].astype(F32), jnp.zeros((pad - sz.rows, width), F32)], 0
    ).astype(BF16)

    part_recv[2] = jnp.zeros((pad, width), BF16)
    mix_recv[2] = jnp.zeros((pad, width), BF16)

    at.enter()

    w_rows = rows_at(d * nz + z, rp)
    others = pl.ds(0, ng - 1)

    def send_line(i):
        for j in range(1, nz):
            remote(
                w_own.at[i], w_full.at[i, w_rows, own_columns], wz_s.at[i], wz_r.at[i], at.line(at.next_z(j))
            ).start()

    def along(block, send_sems, recv_sems, c):
        place = block.at[own_block, lanes(c)]
        return [
            remote(place, place, send_sems.at[c], recv_sems.at[c], at.line(at.next_z(j)))
            for j in range(1, nz)
        ]

    def wait_along(block, send_sems, recv_sems, c):
        place = block.at[pl.ds(0, (nz - 1) * pad), lanes(c)]
        drain(send_sems.at[c], recv_sems.at[c], place, place)

    for i in range(3):
        send_line(i)
    for copy in along(cot_block, qz_s, qz_r, 0):
        copy.start()
    send_line(3)
    routers = [
        remote(router_own, router_full.at[me], r_s.at[0], r_r.at[0], at.plane(at.next_group(k)))
        for k in range(1, ng)
    ]
    for copy in routers:
        copy.start()
    loads = [
        pltpu.make_async_copy(first_hbm, first, local_sem.at[0]),
        pltpu.make_async_copy(second_hbm, second, local_sem.at[1]),
    ]
    for copy in loads:
        copy.start()
    w_full[:, w_rows, own_columns] = w_own[...]
    router_full[me] = router_own[...]

    def to_core(i, dp, other):
        place = w_full.at[i, rows_at(dp, band), own_columns]
        n = 4 * (other - 1) + i
        return remote(place, place, wc_s.at[n], wc_r.at[n], (d, (h + other) % nh, z))

    def send_band(i):
        landed = w_full.at[i, pl.ds(0, (nz - 1) * rp), own_columns]
        drain(wz_s.at[i], wz_r.at[i], landed, landed)
        place = w_full.at[i, rows_at(d, band), own_columns]
        for k in range(1, nd):
            remote(place, place, wx_s.at[i], wx_r.at[i], ((d + k) % nd, h, z)).start()
        for other in range(1, nh):
            to_core(i, d, other).start()

    def pass_on(i):
        landed = w_full.at[i, pl.ds(0, (nd - 1) * band), own_columns]
        drain(wx_s.at[i], wx_r.at[i], landed, landed)
        for k in range(1, nd):
            for other in range(1, nh):
                to_core(i, (d + k) % nd, other).start()

    def arrived(i):
        for other in range(1, nh):
            n, columns = 4 * (other - 1) + i, w_full.at[i, :, own_columns]
            drain(wc_s.at[n], wc_r.at[n], columns, columns)

    zeros = jnp.zeros((pad - sz.rows, width), F32)
    x_rows = jnp.concatenate([x_ref[...].astype(F32), zeros], 0)
    unit_one, _ = normalize(x_rows)
    normed_one = (unit_one * gain_one_ref[...]).astype(BF16)
    for i in range(3):
        send_band(i)

    route_table(sz, routes_ref, route_rows)
    route_a, route_b = route_rows[0:1, :], route_rows[1:2, :]
    expert = iota((sz.experts, sz.block), 0).astype(F32)
    named_a, named_b = route_a == expert, route_b == expert
    named = jnp.logical_or(named_a, named_b)
    before = (iota((sz.block, sz.block), 0) < iota((sz.block, sz.block), 1)).astype(BF16)
    rank = nn(named.astype(BF16), before) + expert * float(sz.cap)
    slot_a = jnp.sum(jnp.where(named_a, rank, 0.0), 0, keepdims=True)
    slot_b = jnp.sum(jnp.where(named_b, rank, 0.0), 0, keepdims=True)
    slot_a = jnp.where(route_a < 0.0, -1.0, slot_a)
    slot_b = jnp.where(route_b < 0.0, -1.0, slot_b)
    slot_pair = jnp.concatenate([slot_a, slot_b] * 64, 0)
    route_columns[...] = slot_pair.T

    def fill(g, carry):
        slot = iota((sz.group_slots, sz.block), 0).astype(F32) + (g * sz.group_slots).astype(F32)
        hit = jnp.logical_or(slot == slot_a, slot == slot_b)
        select[rows_at(g, sz.group_slots), :] = jnp.where(hit, 1.0, 0.0).astype(BF16)
        return carry

    lax.fori_loop(0, ng, fill, 0)

    quarter = sz.cap // nz
    few = ng * sz.own * quarter

    def quarter_slot(dims, axis):
        n = iota(dims, axis)
        return (n // quarter * sz.cap + z * quarter + n % quarter).astype(F32)

    some_slot = quarter_slot((few, sz.block), 0)
    select_q[...] = jnp.where(jnp.logical_or(some_slot == slot_a, some_slot == slot_b), 1.0, 0.0).astype(BF16)

    def quarter_move(k, send, landing, send_sems, recv_sems):
        g = (me + k) % ng
        return remote(send.at[g], landing.at[me], send_sems.at[0], recv_sems.at[0], at.plane(g))

    def exchange(c, k, send, out, send_sems, recv_sems):
        g = (me + k) % ng
        return remote(
            send.at[g, :, lanes(c)], out.at[me, :, lanes(c)], send_sems.at[c], recv_sems.at[c], at.plane(g)
        )

    def dispatch(c, block, send, out, send_sems, recv_sems):
        def step(i, carry):
            k = ng - 1 - i
            g = (me + k) % ng
            send[g, :, lanes(c)] = nn(select[rows_at(g, sz.group_slots), :], block[:, lanes(c)]).astype(BF16)

            @pl.when(k > 0)
            def _():
                exchange(c, k, send, out, send_sems, recv_sems).start()

            return carry

        lax.fori_loop(0, ng, step, 0)
        out[me, :, lanes(c)] = send[me, :, lanes(c)]

    def start_part(c, *flow):
        def step(i, carry):
            exchange(c, ng - 1 - i, *flow).start()
            return carry

        lax.fori_loop(0, ng - 1, step, 0)

    def wait_part(c, send, out, send_sems, recv_sems):
        drain(send_sems.at[c], recv_sems.at[c], send.at[others, :, lanes(c)], out.at[others, :, lanes(c)])

    cot_flow = (send_a, cot_slots, qa_s, qa_r)
    row_flow = (send_b, slots, na_s, na_r)

    def send_cot(c):
        wait_along(cot_block, qz_s, qz_r, c)
        dispatch(c, cot_block, *cot_flow)

    send_band(3)
    for c in range(1, parts):
        for copy in along(cot_block, qz_s, qz_r, c):
            copy.start()
    pass_on(0)
    send_cot(0)
    pass_on(1)
    pass_on(2)

    for i in range(3):
        arrived(i)
        qkv[i] = nn(normed_one, w_full[i]).astype(BF16)
    pass_on(3)
    lane = iota((1, 2 * HEAD_DIM), 1)
    halves = (lane < HEAD_DIM, lane >= HEAD_DIM)
    key_valid = iota((1, pad), 1) < sz.rows
    row_valid = iota((pad, 1), 0) < sz.rows
    peak_lane = iota((1, 128), 1)
    peak_at[...] = jnp.full_like(peak_at, NEG)
    scale = HEAD_DIM ** (-0.5)

    def attend(pair, carry):
        columns = rows_at(pair, 2 * HEAD_DIM)
        q_pair, k_pair, v_pair = (qkv[i, :, columns] for i in range(3))
        sides = []
        for side in range(2):
            q_own = jnp.where(halves[side], q_pair, jnp.zeros_like(q_pair))
            scores = jnp.where(key_valid, nt(q_own, k_pair) * scale, NEG)
            row_peak = jnp.max(scores, -1, keepdims=True)
            exponent = jnp.exp(scores - row_peak)
            weights = (exponent / jnp.sum(exponent, -1, keepdims=True)).astype(BF16)
            head = pair * 2 + side
            probs[head] = weights
            sides.append(nn(weights, v_pair))
            peak = jnp.max(jnp.where(row_valid, row_peak, NEG), 0, keepdims=True)
            peak_at[0:1, :] = jnp.where(peak_lane == head, peak, peak_at[0:1, :])
        mixed[:, columns] = jnp.where(halves[0], sides[0], sides[1]).astype(BF16)
        return carry

    pairs = HEADS // 2
    lax.fori_loop(0, pairs // 2, attend, 0)
    send_cot(1)
    lax.fori_loop(pairs // 2, pairs, attend, 0)

    arrived(3)
    hidden = x_rows + nt(mixed[...], w_full[3])
    hidden_at[...] = hidden
    unit_two, _ = normalize(hidden)
    rows_block[own_block] = jnp.where(row_valid, unit_two * gain_two_ref[...], 0.0).astype(BF16)
    for c in range(parts):
        for copy in along(rows_block, nz_s, nz_r, c):
            copy.start()

    for c in range(2, parts):
        send_cot(c)

    def fill_t(i, carry):
        rows = rows_at(i, pad)
        slot = iota((pad, sz.slots), 1).astype(F32)
        hit = jnp.logical_or(slot == route_columns[rows, 0:1], slot == route_columns[rows, 1:2])
        select_t[rows, :] = jnp.where(hit, 1.0, 0.0).astype(BF16)
        some = quarter_slot((pad, few), 1)
        hit = jnp.logical_or(some == route_columns[rows, 0:1], some == route_columns[rows, 1:2])
        select_qt[rows, :] = jnp.where(hit, 1.0, 0.0).astype(BF16)
        return carry

    lax.fori_loop(0, nz, fill_t, 0)
    drain(r_s.at[0], r_r.at[0], router_full.at[others], router_full.at[others])
    for g in range(ng):
        router_t[:, g * sz.router_rows : (g + 1) * sz.router_rows] = router_full[g, :, 0 : sz.router_rows]

    def expert_rows(ref, e):
        return ref[:, rows_at(e, sz.cap), :].reshape(many, width)

    def send_gates():
        logits = jnp.where(named, nt(router_t[...], rows_block[...]), NEG)
        exponent = jnp.where(named, jnp.exp(logits - jnp.max(logits, 0, keepdims=True)), 0.0)
        total = jnp.sum(exponent, 0, keepdims=True)
        gates = exponent / jnp.where(total > 0.0, total, 1.0)
        gates_at[...] = gates
        by_slot = nt(split_high_low(gates), select[...])
        by_slot = by_slot[0 : sz.experts] + by_slot[sz.experts :]
        own_slot = iota((sz.experts, sz.slots), 1) // sz.cap == iota((sz.experts, sz.slots), 0)
        by_slot = jnp.where(own_slot, by_slot, 0.0)
        folded = by_slot[:, 0:128]
        for i in range(1, sz.slots // 128):
            folded = folded + by_slot[:, i * 128 : (i + 1) * 128]
        gate_send[...] = folded
        gate_copies = [
            remote(
                gate_send.at[rows_at(at.next_group(k) * sz.own // 8, 8)], gate_recv.at[me], ga_s.at[0], ga_r.at[0],
                at.plane(at.next_group(k)),
            )
            for k in range(1, ng)
        ]
        for copy in gate_copies:
            copy.start()
        gate_recv[me] = gate_send[rows_at(me * sz.own // 8, 8)]

    for c in range(parts):
        wait_along(rows_block, nz_s, nz_r, c)
        if c == 0:
            rows_q[...] = nn(select_q[...], rows_block[:, lanes(0)]).astype(BF16).reshape(rows_q.shape)
            for k in range(1, ng):
                quarter_move(k, rows_q, rows_line.at[z], nq_s, nq_r).start()
            rows_line[z, me] = rows_q[me]
            continue
        if c == parts - 1:
            drain(nq_s.at[0], nq_r.at[0], rows_q.at[others], rows_q.at[others])
            for j in range(1, nz):
                remote(rows_line.at[z], rows_line.at[z], nl_s.at[0], nl_r.at[0], at.line(at.next_z(j))).start()
            send_gates()
        dispatch(c, rows_block, *row_flow)

    drain(ga_s.at[0], ga_r.at[0], gate_recv.at[others], gate_recv.at[others])
    def gate_of(e):
        turned = gate_recv[:, pl.ds(me * sz.own % 8 + e, 1), :].reshape(ng, 128).T
        columns = jnp.where((e % 2) == 1, turned[sz.cap : 2 * sz.cap], turned[0 : sz.cap])
        return jnp.concatenate([columns[:, s : s + 1] for s in range(ng)], 0)

    def weigh(e, carry):
        grad_act[e] = nt(expert_rows(cot_slots, e), second[e]) * gate_of(e)
        return carry

    for c in range(parts):
        wait_part(c, *cot_flow)
    for copy in loads:
        copy.wait()
    lax.fori_loop(0, sz.own, weigh, 0)
    lines = rows_line.at[pl.ds(0, nz - 1)]
    drain(nl_s.at[0], nl_r.at[0], lines, lines)
    for i in range(nz):
        for e in range(sz.own):
            slots[:, e * sz.cap + i * quarter : e * sz.cap + (i + 1) * quarter, lanes(0)] = rows_line[
                i, :, e * quarter : (e + 1) * quarter, :
            ]
    for c in range(1, parts):
        wait_part(c, *row_flow)

    def first_piece(e, g):
        piece = (rows_at(e, sz.cap), lanes(1))
        return remote(
            send_a.at[(g, *piece)], grad_slots.at[(me, *piece)], d0_s.at[e], d0_r.at[e], at.plane(g)
        )

    def grads_piece(e, j):
        piece = (slice(None), rows_at(e, quarter), slice(None))
        return remote(
            grads_q.at[(at.next_z(j), *piece)], grads_line.at[(j - 1, *piece)], dl_s.at[0], dl_r.at[0],
            at.line(at.next_z(j)),
        )

    def expert_back(e, carry):
        half_rows = many // 2
        for part_at in range(2):
            some = slice(part_at * half_rows, (part_at + 1) * half_rows)
            groups = slice(part_at * ng // 2, (part_at + 1) * ng // 2)
            pre = nn(slots[groups, rows_at(e, sz.cap), :].reshape(half_rows, width), first[e])
            const, cubic = 0.7978845608028654, 0.044715
            square = pre * pre
            half = 0.5 * jnp.tanh(pre * (const + const * cubic * square)) + 0.5
            hidden_units = pre * half
            act[e, some] = hidden_units.astype(BF16)
            through = grad_act[e, some]
            dgate = nt(jnp.ones((8, sz.hidden), BF16), (hidden_units * through).astype(BF16))
            dgate_send[:, some] = jnp.where(iota((8, half_rows), 0) == e, dgate, dgate_send[:, some])
            slope = half * (1.0 + (1.0 - half) * (pre * (2.0 * const + 6.0 * const * cubic * square)))
            grads = (through * slope).astype(BF16)
            grad_pre[e, some] = grads
            spread = nt(grads, first[e]).astype(BF16).reshape(ng // 2, sz.cap, width)
            send_a[groups, rows_at(e, sz.cap), :] = spread
            for i in range(nz):
                grads_q[i, groups, rows_at(e, quarter), :] = spread[:, i * quarter : (i + 1) * quarter, 0:part_width]

        def step(i, carry):
            first_piece(e, (me + ng - 1 - i) % ng).start()
            return carry

        lax.fori_loop(0, ng - 1, step, 0)
        for j in range(1, nz):
            grads_piece(e, j).start()
        return carry

    dgate_send[...] = jnp.zeros_like(dgate_send)
    lax.fori_loop(0, sz.own, expert_back, 0)
    dgates = [
        remote(
            dgate_send.at[:, rows_at(at.next_group(k) * sz.cap // 128, 128)], dgate_recv.at[me], dg_s.at[0],
            dg_r.at[0], at.plane(at.next_group(k)),
        )
        for k in range(1, ng)
    ]
    for copy in dgates:
        copy.start()
    dgate_recv[me] = dgate_send[:, rows_at(me * sz.cap // 128, 128)]
    grad_flow = (send_a, grad_slots, da_s, da_r)
    value_flow = (send_b, values, va_s, va_r)
    for c in range(2, parts):
        start_part(c, *grad_flow)
    grad_slots[me] = send_a[me]

    def expert_value(e, carry):
        value = nn(act[e], second[e])
        gated = (value * gate_of(e)).astype(BF16).reshape(ng, sz.cap, width)
        send_b[:, rows_at(e, sz.cap), :] = gated
        return carry

    lax.fori_loop(0, sz.own, expert_value, 0)
    values[me] = send_b[me]

    def quarter_total(own, line, sums):
        total = own[z].astype(F32)
        for j in range(1, nz):
            total = total + line[j - 1].astype(F32)
        sums[...] = total.astype(BF16)


    def weight_grads(e, carry):
        grad_value = (expert_rows(cot_slots, e).astype(F32) * gate_of(e)).astype(BF16)
        grad_second_out[e] = tn(act[e], grad_value).astype(BF16)
        grad_first_out[e] = tn(expert_rows(slots, e), grad_pre[e]).astype(BF16)
        return carry

    drain(dg_s.at[0], dg_r.at[0], dgate_recv.at[others], dgate_recv.at[others])
    mine = iota((8, 128), 1) // sz.cap == me * sz.cap % 128 // sz.cap
    for g in range(ng):
        folded = jnp.where(mine, dgate_recv[g], 0.0)
        folded = folded + pltpu.roll(folded, 64, 1)
        dgate_rows[g * sz.own : (g + 1) * sz.own, :] = folded[0 : sz.own]
    spread = jnp.concatenate([dgate_rows[...]] * (sz.slots // 128), 1)
    own_slot = iota((sz.experts, sz.slots), 1) // sz.cap == iota((sz.experts, sz.slots), 0)
    dgate = nt(split_high_low(jnp.where(own_slot, spread, 0.0)), select_t[...])
    dgate = dgate[0 : sz.experts] + dgate[sz.experts :]
    gates = gates_at[...]
    dlogits = (dgate - gates * jnp.sum(dgate, 0, keepdims=True)).astype(BF16)
    rt[...] = nn(dlogits, rows_block[...])
    part[...] = tn(dlogits, router_t[...])

    inner = at.inner()
    beside, across, mirror = at.mates()

    def line_copy(c, slot, send, recv, send_sems, recv_sems, relay_sems, last):
        if slot < 2:
            return remote(
                send.at[slot, :, lanes(c)], recv.at[slot, :, lanes(c)], send_sems.at[c], recv_sems.at[c],
                at.line((beside, across)[slot]),
            )
        by_way = 1 - inner if c != last else 0
        to = mirror + by_way * (beside - mirror)
        return remote(
            send.at[2, :, lanes(c)], recv.at[2 + by_way, :, lanes(c)], send_sems.at[c], relay_sems.at[c, by_way], at.line(to)
        )

    def scatter(c, source, base, own, *flow):
        if source is grads_back:
            places, flat = select_qt, source[...].reshape(few, part_width)
        else:
            places, flat = select_t, source[:, :, lanes(c)].reshape(sz.slots, part_width)
        for slot, target in ((2, mirror), (1, across), (0, beside), (None, z)):
            tokens = rows_at(target, pad)
            sums = nn(places[tokens, :], flat)
            if base is not None:
                sums = sums + base[tokens, lanes(c)]
            if slot is None:
                own[:, lanes(c)] = sums
                continue
            flow[0][slot, :, lanes(c)] = sums.astype(BF16)
            if slot == 1 and c != flow[-1]:

                @pl.when(inner == 0)
                def _():
                    line_copy(c, 1, *flow).start()
            else:
                line_copy(c, slot, *flow).start()

    def relay(c, send, recv, send_sems, recv_sems, relay_sems, last):
        @pl.when(inner == 1)
        def _():
            landed = recv.at[3, :, lanes(c)]
            pltpu.make_async_copy(landed, landed, relay_sems.at[c, 1]).wait()
            send[1, :, lanes(c)] = (send[1, :, lanes(c)].astype(F32) + recv[3, :, lanes(c)].astype(F32)).astype(BF16)
            line_copy(c, 1, send, recv, send_sems, recv_sems, relay_sems, last).start()

    def gathered(own, send, recv, send_sems, recv_sems, relay_sems, last):
        for c in range(parts):
            drain(send_sems.at[c], recv_sems.at[c], send.at[:, :, lanes(c)], recv.at[pl.ds(0, 2), :, lanes(c)])

            @pl.when(inner == 1 if c != last else True)
            def _(c=c):
                landed = recv.at[2, :, lanes(c)]
                pltpu.make_async_copy(landed, landed, relay_sems.at[c, 0]).wait()

        sums = own[...]
        for slot in range(3):
            sums = sums + recv[slot].astype(F32)
        return sums

    part_flow = (part_send, part_recv, pz_s, pz_r, pr_r, 0)
    mix_flow = (mix_send, mix_recv, mz_s, mz_r, mr_r, parts - 1)

    def wait_first(e, carry):
        piece = (others, rows_at(e, sz.cap), lanes(1))
        drain(d0_s.at[e], d0_r.at[e], send_a.at[piece], grad_slots.at[piece])
        return carry

    def exchange_quarters():
        drain(dl_s.at[0], dl_r.at[0], grads_line, grads_line)
        quarter_total(grads_q, grads_line, grads_sum)
        for copy in grads_moves:
            copy.start()
        for i in range(2):
            start_part(i, *value_flow)
        grads_back[me] = grads_sum[me]

    grads_moves = [quarter_move(k, grads_sum, grads_back, dq_s, dq_r) for k in range(1, ng)]
    order = [*range(1, parts), 0]
    exchange_quarters()
    done = 0
    for turn, c in enumerate(order):
        if c == 0:
            drain(dq_s.at[0], dq_r.at[0], grads_back.at[others], grads_back.at[others])
        elif c == 1:
            lax.fori_loop(0, sz.own, wait_first, 0)
        else:
            wait_part(c, *grad_flow)
        if c == parts - 1:
            for i in range(2, parts):
                start_part(i, *value_flow)
        scatter(c, grads_back if c == 0 else grad_slots, part, part_own, *part_flow)
        until = sz.own * (turn + 1) // parts
        lax.fori_loop(done, until, weight_grads, 0)
        done = until
        if turn > 0:
            relay(order[turn - 1], *part_flow)
    def send_mix(c):
        wait_part(c, *value_flow)
        scatter(c, values, None, mix_own, *mix_flow)
        if c:
            relay(c - 1, *mix_flow)

    send_mix(0)
    unit_two, factor_two = normalize(hidden_at[...])
    grad_normed = jnp.where(row_valid, gathered(part_own, *part_flow), 0.0)
    grad_hidden, gain_two = norm_back(grad_normed, unit_two, factor_two, gain_two_ref[...])
    grad_hidden = jnp.concatenate([cot_ref[...].astype(F32), zeros], 0) + jnp.where(row_valid, grad_hidden, 0.0)
    part_own[...] = grad_hidden
    grad_attn = grad_hidden.astype(BF16)

    def core_copy(i, other):
        n = 4 * (other - 1) + i
        return remote(
            core_send.at[other - 1, i], core_recv.at[other - 1, i], gc_s.at[n], gc_r.at[n], (d, (h + other) % nh, z)
        )

    def half_sum(i, sums):
        for other in range(1, nh):
            core_copy(i, other).wait()
            sums = sums + core_recv[other - 1, i].astype(F32)
        w_half[i] = sums
        band_send[i] = sums.astype(BF16)

    def band_copy(k, i):
        to = (d + k) % nd
        return remote(
            band_send.at[i, rows_at(to, band), :], band_recv.at[k - 1, i], gx_s.at[i], gx_r.at[i], (to, h, z)
        )

    for other in [*range(1, nh), 0]:
        sums = tn(grad_attn, mixed[:, rows_at((h + other) % nh, cp)])
        if other:
            core_send[other - 1, 3] = sums.astype(BF16)
            core_copy(3, other).start()
        else:
            w_half[3] = sums
    grad_mixed[...] = nn(grad_attn, w_full[3]).astype(BF16)
    half_sum(3, w_half[3])
    for k in range(1, nd):
        band_copy(k, 3).start()


    send_mix(1)

    def attend_back(pair):
        columns = rows_at(pair, 2 * HEAD_DIM)
        q_pair, k_pair, v_pair = (qkv[i, :, columns] for i in range(3))
        g_pair = grad_mixed[:, columns]
        dq, dk, dv = [], [], []
        for side in range(2):
            weights = probs[pair * 2 + side]
            soft = weights.astype(F32)
            g_own = jnp.where(halves[side], g_pair, jnp.zeros_like(g_pair))
            grad_soft = nt(g_own, v_pair)
            inner = jnp.sum(soft * grad_soft, -1, keepdims=True)
            grad_scores = (soft * (grad_soft - inner)).astype(BF16)
            dq.append(nn(grad_scores, k_pair))
            dk.append(tn(grad_scores, q_pair))
            dv.append(tn(weights, g_pair))
        grad_qkv[0, :, columns] = (jnp.where(halves[0], dq[0], dq[1]) * scale).astype(BF16)
        grad_qkv[1, :, columns] = (jnp.where(halves[0], dk[0], dk[1]) * scale).astype(BF16)
        grad_qkv[2, :, columns] = jnp.where(halves[0], dv[0], dv[1]).astype(BF16)

    unit_one, factor_one = normalize(jnp.concatenate([x_ref[...].astype(F32), zeros], 0))
    normed_one = (unit_one * gain_one_ref[...]).astype(BF16)
    core_pairs = cp // (2 * HEAD_DIM)
    for other in [*range(1, nh), 0]:
        core = (h + other) % nh
        for q in range(core_pairs):
            attend_back(core * core_pairs + q)
        for i in range(3):
            sums = tn(normed_one, grad_qkv[i, :, rows_at(core, cp)])
            if other:
                core_send[other - 1, i] = sums.astype(BF16)
                core_copy(i, other).start()
            else:
                half_sum(i, sums)
        if other == nh - 1:
            send_mix(2)
    for i in range(2):
        for k in range(1, nd):
            band_copy(k, i).start()

    grad_one = jnp.zeros((pad, width), F32)
    for i in range(3):
        grad_one = grad_one + nt(grad_qkv[i], w_full[i])
    grad_one = jnp.where(row_valid, grad_one, 0.0)
    grad_input, gain_one = norm_back(grad_one, unit_one, factor_one, gain_one_ref[...])
    grad_input_out[...] = (part_own[...] + grad_input)[0 : sz.rows].astype(BF16)

    small[...] = jnp.zeros_like(small)
    small[0:1, :] = gain_one
    small[1:2, :] = gain_two
    small[2:3, 0:128] = peak_at[0:1, :]
    peak_row = iota(small.shape, 0) == 2

    def join(a, b):
        return jnp.where(peak_row, jnp.maximum(a, b), a + b)

    small_copies = []
    for other in range(1, nh):
        device, n = (d, (h + other) % nh, z), 2 * (other - 1)
        small_copies += [
            remote(small, small_core.at[other - 1], sc_s.at[n], sc_r.at[n], device),
            remote(rt, rt_core.at[other - 1], sc_s.at[n + 1], sc_r.at[n + 1], device),
        ]
    for copy in small_copies:
        copy.start()
    for copy in small_copies:
        copy.wait()
    for other in range(1, nh):
        small[...] = join(small[...], small_core[other - 1])
        rt[...] = rt[...] + rt_core[other - 1]
    small_send[0] = small[...]
    small_copies = []
    for k in range(1, nd):
        to = (d + k) % nd
        small_copies += [
            remote(small_send.at[0], small_x.at[k - 1], sx_s.at[0], sx_r.at[0], (to, h, z)),
            remote(rt.at[:, rows_at(to, band)], rt_x.at[k - 1], sx_s.at[1], sx_r.at[1], (to, h, z)),
        ]
    for copy in small_copies:
        copy.start()
    for k in range(1, nd):
        band_copy(k, 2).start()
    send_mix(3)

    def line_piece(i, j):
        to = at.next_z(j)
        return remote(line_send.at[i, rows_at(to, rp), :], line_recv.at[j - 1, i], gl_s.at[i], gl_r.at[i], at.line(to))

    def end_band(i):
        drain(gx_s.at[i], gx_r.at[i], band_recv.at[:, i], band_recv.at[:, i])
        sums = w_half[i, rows_at(d, band), :]
        for k in range(1, nd):
            sums = sums + band_recv[k - 1, i].astype(F32)
        w_half[i, 0:band, :] = sums
        line_send[i] = sums.astype(BF16)
        for j in range(1, nz):
            line_piece(i, j).start()

    for i in (3, 0, 1):
        end_band(i)
    drain(sx_s.at[0], sx_r.at[0], small_x, small_x)
    drain(sx_s.at[1], sx_r.at[1], rt_x, rt_x)
    router_sum = rt[:, rows_at(d, band)]
    for k in range(1, nd):
        small[...] = join(small[...], small_x[k - 1])
        router_sum = router_sum + rt_x[k - 1]
    rt_z[nz - 1] = router_sum
    small_send[1] = small[...]
    for j in range(1, nz):
        device = at.line(at.next_z(j))
        remote(small_send.at[1], small_z.at[j - 1], gl_s.at[4], gl_r.at[4], device).start()
        remote(rt_z.at[nz - 1], rt_z.at[j - 1], gl_s.at[5], gl_r.at[5], device).start()
    end_band(2)

    mix = gathered(mix_own, *mix_flow)
    output_out[...] = (hidden_at[...] + mix)[0 : sz.rows].astype(BF16)

    for i in range(4):
        drain(gl_s.at[i], gl_r.at[i], line_recv.at[:, i], line_recv.at[:, i])
    for n, landed in ((4, small_z), (5, rt_z.at[pl.ds(0, nz - 1)])):
        drain(gl_s.at[n], gl_r.at[n], landed, landed)
    totals = small[...]
    router_sum = rt_z[nz - 1]
    for j in range(1, nz):
        totals = join(totals, small_z[j - 1])
        router_sum = router_sum + rt_z[j - 1]
    gain_one_out[...] = totals[0:1]
    gain_two_out[...] = totals[1:2]
    rr = sz.router_rows
    own_router = router_sum[:, 0:rr]
    for i in range(1, nh):
        own_router = jnp.where(h == i, router_sum[:, i * rr : (i + 1) * rr], own_router)
    router_out[...] = own_router
    tau = tau_ref[...]
    factor = jnp.sqrt(tau / jnp.maximum(totals[2:3, 0:HEADS], tau))
    column = iota((1, cp), 1) // HEAD_DIM + h * (cp // HEAD_DIM)
    scale_row = jnp.zeros((1, cp), F32)
    for head in range(HEADS):
        scale_row = jnp.where(column == head, factor[:, head : head + 1], scale_row)
    for i in range(2):
        clipped_out[i] = (w_qkv_ref[i].astype(F32) * scale_row).astype(BF16)
    for i in range(4):
        sums = w_half[i, rows_at(z, rp), :]
        for j in range(1, nz):
            sums = sums + line_recv[j - 1, i].astype(F32)
        if i < 3:
            qkv_out[i] = sums
        else:
            out_out[...] = sums


def finish_kernel(sz, *refs):
    sources, results = refs[0:10], refs[10:20]
    full_out, out_sems, small_out = refs[20:]
    small_stores = [pltpu.make_async_copy(sources[n], results[n], small_out.at[n]) for n in range(8)]
    for copy in small_stores:
        copy.start()
    stores = []
    for e in range(sz.own):
        for i in range(2):
            full_out[i, e] = sources[8 + i][e].astype(F32)
            stores.append(pltpu.make_async_copy(full_out.at[i, e], results[8 + i].at[e], out_sems.at[i, e]))
            stores[-1].start()
    for copy in stores + small_stores:
        copy.wait()


def fast_body(
    sz, inputs, cotangent, routes, gain_attn, gain_expert, tau, w_qkv, w_out_attn, w_router, w_in, w_out
):
    ng, nz, nd, nh, pad, width, own = sz.groups, sz.nt, sz.nd, sz.nh, sz.pad, sz.width, sz.own
    rp, cp, band, parts, block = sz.row_piece, sz.col_piece, sz.band, sz.parts, sz.block
    many, hidden = ng * sz.cap, sz.hidden
    on_chip, anywhere = pl.BlockSpec(memory_space=pltpu.VMEM), pl.BlockSpec(memory_space=pltpu.HBM)

    def shape(dims, dtype):
        return jax.ShapeDtypeStruct(dims, dtype)

    def half(*dims):
        return pltpu.VMEM(dims, BF16)

    def full(*dims):
        return pltpu.VMEM(dims, F32)

    def pair(*dims):
        return [pltpu.SemaphoreType.DMA(dims)] * 2

    slot_buffer = half(ng, sz.group_slots, width)
    line_buffer = half(nz - 1, pad, width)
    quarter_dims = (ng, own * (sz.cap // nz), width // parts)
    quarter_buffer, few = half(*quarter_dims), ng * own * (sz.cap // nz)
    rr = sz.router_rows
    smalls = (
        shape(inputs.shape, BF16), shape(inputs.shape, BF16), shape((1, width), F32), shape((1, width), F32),
        shape((3, rp, cp), F32), shape((rp, cp), F32), shape((sz.experts, rr), F32), shape((2, rp, cp), BF16),
    )
    packed = pl.pallas_call(
        functools.partial(block_kernel, sz),
        out_shape=(*[pltpu.VMEM(x.shape, x.dtype) for x in smalls], half(*w_in.shape), half(*w_out.shape)),
        in_specs=[on_chip] * 9 + [anywhere] * 2,
        out_specs=(on_chip,) * 10,
        scratch_shapes=[
            half(4, rp, cp), half(4, width, width), half(sz.experts, 128), half(ng, sz.experts, 128),
            half(sz.experts, width), full(8, block), full(block, 128), half(sz.slots, block), half(block, sz.slots), half(few, block), half(block, few),
            half(block, width), half(block, width), *[slot_buffer] * 6,
            quarter_buffer, half(nz, *quarter_dims), half(nz, *quarter_dims), half(nz - 1, *quarter_dims), quarter_buffer,
            quarter_buffer,
            half(own, width, hidden), half(own, hidden, width), half(own, many, hidden), half(own, many, hidden),
            full(own, many, hidden),
            full(sz.experts, 128), full(ng, 8, 128), full(sz.experts, block), full(8, many),
            full(ng, 8, 128), full(sz.experts, 128),
            half(3, pad, width), half(HEADS, pad, pad), half(pad, width), full(pad, width), full(8, 128),
            full(block, width), full(pad, width), line_buffer, half(nz, pad, width), full(pad, width), line_buffer,
            half(nz, pad, width),
            half(pad, width), half(3, pad, width), half(nh - 1, 4, width, cp), half(nh - 1, 4, width, cp),
            full(4, width, cp), half(4, width, cp), half(nd - 1, 4, band, cp), half(4, band, cp),
            half(nz - 1, 4, rp, cp),
            full(8, width), full(2, 8, width), full(nh - 1, 8, width), full(nd - 1, 8, width), full(nz - 1, 8, width),
            full(sz.experts, width), full(nh - 1, sz.experts, width), full(nd - 1, sz.experts, band),
            full(nz, sz.experts, band),
            *pair(4), *pair(4), *pair(4 * (nh - 1)), *pair(1), *pair(parts), *pair(parts), *pair(parts), *pair(parts),
            *pair(1), *pair(own), *pair(parts), *pair(parts), *pair(1), *pair(parts), *pair(parts), *pair(4 * (nh - 1)),
            *pair(4), *pair(6), *pair(2 * (nh - 1)), *pair(2), *pair(1), *pair(1), *pair(1), *pair(1),
            *pair(parts, 2),
            pltpu.SemaphoreType.DMA((2,)),
        ],
        compiler_params=pltpu.CompilerParams(collective_id=0, has_side_effects=True, vmem_limit_bytes=57 * 2**20),
        name="block",
    )(
        inputs, cotangent, routes.T, gain_attn[None, :], gain_expert[None, :], w_qkv, w_out_attn.T, w_router.T,
        tau[None, :], w_in, w_out,
    )

    both, dma = (2, *w_in.shape), pltpu.SemaphoreType.DMA
    output, grad_input, gain_one, gain_two, grad_qkv, grad_out, grad_router, clipped, grad_first, grad_second = (
        pl.pallas_call(
            functools.partial(finish_kernel, sz),
            out_shape=(*smalls, shape(w_in.shape, F32), shape(w_out.shape, F32)),
            in_specs=[on_chip] * 10,
            out_specs=(anywhere,) * 10,
            scratch_shapes=[full(*both), dma((2, own)), dma((8,))],
            compiler_params=pltpu.CompilerParams(vmem_limit_bytes=48 * 2**20),
            name="finish",
        )(*[pltpu.with_memory_space_constraint(x, pltpu.VMEM) for x in packed])
    )
    return (
        output, grad_input, gain_one[0], gain_two[0], grad_qkv, grad_out.T, grad_router.T, grad_first, grad_second,
        clipped,
    )


def gelu_tanh(inputs):
    return (
        0.5
        * inputs
        * (1.0 + jnp.tanh(0.7978845608028654 * (inputs + 0.044715 * inputs * inputs * inputs)))
    )


def unit_and_factor(inputs):
    centered = inputs - jnp.mean(inputs, -1, keepdims=True)
    factor = lax.rsqrt(jnp.mean(centered * centered, -1, keepdims=True) + 1e-06)
    return (centered * factor, factor)


def general_norm_back(grad_norm, unit_rows, factor, gain):
    grad, gain_row = norm_back(grad_norm, unit_rows, factor, gain)
    return grad, gain_row[0]


def attn_forward(block_parts):
    queries, key_rows, value_rows = block_parts
    scores = jnp.einsum(
        "bhqd,bhkd->bhqk", queries, key_rows, preferred_element_type=jnp.float32
    ) * HEAD_DIM ** (-0.5)
    row_peak = jnp.max(scores, -1, keepdims=True)
    exponent = jnp.exp(scores - row_peak)
    summed = jnp.sum(exponent, -1, keepdims=True)
    soft_weights = (exponent / summed).astype(jnp.bfloat16)
    mixed = jnp.einsum(
        "bhqk,bhkd->bhqd", soft_weights, value_rows, preferred_element_type=jnp.float32
    ).astype(jnp.bfloat16)
    return (mixed, (row_peak + jnp.log(summed))[..., 0], jnp.max(row_peak, axis=(0, 2, 3)))


def attn_backward(block_parts):
    queries, key_rows, value_rows, grad_mixed, log_total = block_parts
    score_scale = HEAD_DIM ** (-0.5)
    scores = (
        jnp.einsum("bhqd,bhkd->bhqk", queries, key_rows, preferred_element_type=jnp.float32)
        * score_scale
    )
    soft_weights = jnp.exp(scores - log_total[..., None])
    grad_soft = jnp.einsum(
        "bhqd,bhkd->bhqk", grad_mixed, value_rows, preferred_element_type=jnp.float32
    )
    inner_sum = jnp.sum(soft_weights * grad_soft, -1, keepdims=True)
    grad_scores = (soft_weights * (grad_soft - inner_sum)).astype(jnp.bfloat16)
    grad_query = (
        jnp.einsum("bhqk,bhkd->bhqd", grad_scores, key_rows, preferred_element_type=jnp.float32)
        * score_scale
    ).astype(jnp.bfloat16)
    grad_key = (
        jnp.einsum("bhqk,bhqd->bhkd", grad_scores, queries, preferred_element_type=jnp.float32)
        * score_scale
    ).astype(jnp.bfloat16)
    grad_value = jnp.einsum(
        "bhqk,bhqd->bhkd",
        soft_weights.astype(jnp.bfloat16),
        grad_mixed,
        preferred_element_type=jnp.float32,
    ).astype(jnp.bfloat16)
    return (grad_query, grad_key, grad_value)


def general_body(
    inputs, cotangent, routes, gain_attn, gain_expert, tau, w_qkv, w_out_attn, w_router, w_in, w_out
):
    row_count, width = inputs.shape
    n_dp = lax.axis_size("dp")
    n_heads = lax.axis_size("heads")
    n_tensor = lax.axis_size("tensor")
    row_piece = w_qkv.shape[1]
    col_piece = w_qkv.shape[2]
    own_heads = col_piece // HEAD_DIM
    head_start = lax.axis_index("heads") * col_piece
    x_float = inputs.astype(jnp.float32)
    unit_one, factor_one = unit_and_factor(x_float)
    normed_one = (unit_one * gain_attn).astype(jnp.bfloat16)
    stack_qkv, stack_out = (
        lax.all_gather(w_qkv[None], ("dp", "heads", "tensor"), axis=0, tiled=True),
        lax.all_gather(w_out_attn[None], ("dp", "heads", "tensor"), axis=0, tiled=True),
    )
    full_qkv = (
        stack_qkv.reshape(n_dp, n_heads, n_tensor, 3, row_piece, col_piece)
        .transpose(3, 0, 2, 4, 1, 5)
        .reshape(3, width, width)
    )
    full_out = (
        stack_out.reshape(n_dp, n_heads, n_tensor, col_piece, row_piece)
        .transpose(1, 3, 0, 2, 4)
        .reshape(width, width)
    )
    proj_w = lax.dynamic_slice_in_dim(full_qkv, head_start, col_piece, 2)
    attn_w = lax.dynamic_slice_in_dim(full_out, head_start, col_piece, 0)
    normed_all = lax.all_gather(normed_one, "heads", axis=0, tiled=True)
    head_cols = attn_w.shape[0]
    local_heads = head_cols // HEAD_DIM
    joined_w = jnp.concatenate([proj_w[0], proj_w[1], proj_w[2]], 1)
    projected = jnp.dot(normed_all, joined_w, preferred_element_type=jnp.float32).astype(
        jnp.bfloat16
    )
    images = normed_all.shape[0] // SEQ
    per_block = 4 if images % 4 == 0 else 3 if images % 3 == 0 else 2 if images % 2 == 0 else 1
    block_shape = (images // per_block, per_block, SEQ, local_heads, HEAD_DIM)

    def to_blocks(row_matrix):
        return row_matrix.reshape(block_shape).transpose(0, 1, 3, 2, 4)

    def from_blocks(block_array):
        return block_array.transpose(0, 1, 3, 2, 4).reshape(-1, head_cols)

    queries = to_blocks(projected[:, :head_cols])
    key_rows = to_blocks(projected[:, head_cols : 2 * head_cols])
    value_rows = to_blocks(projected[:, 2 * head_cols :])
    mixed, log_total, head_peaks = lax.map(attn_forward, (queries, key_rows, value_rows))
    mixed_rows = from_blocks(mixed)
    block_peak = jnp.max(head_peaks, 0)
    attn_out = lax.psum_scatter(
        jnp.dot(mixed_rows, attn_w, preferred_element_type=jnp.float32),
        "heads",
        scatter_dimension=0,
        tiled=True,
    )
    peak_full = lax.dynamic_update_slice_in_dim(
        jnp.full((HEADS,), -1e30, jnp.float32), block_peak, lax.axis_index("heads") * local_heads, 0
    )
    hidden = x_float + attn_out
    peak_all = lax.pmax(peak_full, ("dp", "heads", "tensor"))
    peak_logit = lax.dynamic_slice_in_dim(
        peak_all, lax.axis_index("heads") * own_heads, own_heads, 0
    )
    unit_two, factor_two = unit_and_factor(hidden)
    normed_two = (unit_two * gain_expert).astype(jnp.bfloat16)
    group_rows, group_cot = (
        lax.all_gather(normed_two, "tensor", axis=0, tiled=True),
        lax.all_gather(cotangent, "tensor", axis=0, tiled=True),
    )
    first_w, second_w, router_w = (
        lax.all_gather(w_in, ("dp", "heads"), axis=0, tiled=True),
        lax.all_gather(w_out, ("dp", "heads"), axis=0, tiled=True),
        lax.all_gather(w_router, ("dp", "heads"), axis=0, tiled=True),
    )
    logits = jnp.dot(group_rows, router_w, preferred_element_type=jnp.float32)
    chosen = jnp.take_along_axis(logits, routes, 1)
    exponent = jnp.exp(chosen - jnp.max(chosen, -1, keepdims=True))
    gate_values = exponent / jnp.sum(exponent, -1, keepdims=True)
    group_count = routes.shape[0]
    experts = router_w.shape[1]
    capacity = (group_count * 5 // (16 * experts) + 1) * 8
    flat_ids = routes.reshape(-1)
    ordering = jnp.argsort(flat_ids, stable=True)
    sorted_ids = flat_ids[ordering]
    counts = jnp.sum(
        (flat_ids[:, None] == jnp.arange(experts, dtype=jnp.int32)[None, :]).astype(jnp.int32), 0
    )
    expert_ids = jnp.arange(experts, dtype=jnp.int32)
    starts = jnp.sum(jnp.where(expert_ids[None, :] < expert_ids[:, None], counts[None, :], 0), 1)
    slot_rank = jnp.arange(2 * group_count, dtype=jnp.int32) - starts[sorted_ids]
    slot_table = (
        jnp.full((experts * capacity,), 2 * group_count, jnp.int32)
        .at[sorted_ids * capacity + slot_rank]
        .set(ordering)
    )
    slot_token = slot_table // 2
    padded_rows = jnp.concatenate([group_rows, jnp.zeros((1, width), jnp.bfloat16)], 0)
    slot_in = padded_rows[slot_token].reshape(experts, capacity, width)
    slot_gate = jnp.concatenate([gate_values.reshape(-1), jnp.zeros((1,), jnp.float32)], 0)[
        slot_table
    ]
    pre_gelu = jnp.einsum("ecd,edf->ecf", slot_in, first_w, preferred_element_type=jnp.float32)
    activated = gelu_tanh(pre_gelu).astype(jnp.bfloat16)
    slot_out = jnp.einsum(
        "ecf,efd->ecd", activated, second_w, preferred_element_type=jnp.float32
    ).reshape(-1, width)
    partial_value = (
        jnp.zeros((group_count + 1, width), jnp.float32)
        .at[slot_token]
        .add(slot_gate[:, None] * slot_out)[:group_count]
    )
    expert_mix = lax.psum_scatter(
        partial_value.astype(jnp.bfloat16), "tensor", scatter_dimension=0, tiled=True
    ).astype(jnp.float32)
    output = (hidden + expert_mix).astype(jnp.bfloat16)
    padded_cot = jnp.concatenate([group_cot, jnp.zeros((1, width), jnp.bfloat16)], 0)
    slot_cot = padded_cot[slot_token].astype(jnp.float32)
    grad_slot_out = (
        (slot_gate[:, None] * slot_cot).astype(jnp.bfloat16).reshape(experts, capacity, width)
    )
    gate_part = (
        jnp.zeros((2 * group_count + 1,), jnp.float32)
        .at[slot_table]
        .add(jnp.sum(slot_cot * slot_out, -1))[: 2 * group_count]
        .reshape(group_count, 2)
    )
    grad_act = jnp.einsum(
        "ecd,efd->ecf", grad_slot_out, second_w, preferred_element_type=jnp.float32
    )
    grad_pre = jax.vjp(gelu_tanh, pre_gelu)[1](grad_act)[0].astype(jnp.bfloat16)
    grad_first = jnp.einsum("ecd,ecf->edf", slot_in, grad_pre, preferred_element_type=jnp.float32)
    grad_second = jnp.einsum(
        "ecf,ecd->efd", activated, grad_slot_out, preferred_element_type=jnp.float32
    )
    grad_slots = jnp.einsum(
        "ecf,edf->ecd", grad_pre, first_w, preferred_element_type=jnp.float32
    ).reshape(-1, width)
    grad_part = (
        jnp.zeros((group_count + 1, width), jnp.float32)
        .at[slot_token]
        .add(grad_slots)[:group_count]
    )
    grad_normed_two, grad_gates = (
        lax.psum_scatter(
            grad_part.astype(jnp.bfloat16), "tensor", scatter_dimension=0, tiled=True
        ).astype(jnp.float32),
        lax.psum_scatter(
            gate_part.astype(jnp.bfloat16), "tensor", scatter_dimension=0, tiled=True
        ).astype(jnp.float32),
    )
    shard_first, shard_second = (
        lax.psum_scatter(
            grad_first.astype(jnp.bfloat16), ("dp", "heads"), scatter_dimension=0, tiled=True
        ).astype(jnp.float32),
        lax.psum_scatter(
            grad_second.astype(jnp.bfloat16), ("dp", "heads"), scatter_dimension=0, tiled=True
        ).astype(jnp.float32),
    )
    offset = lax.axis_index("tensor") * row_count
    local_gates = lax.dynamic_slice_in_dim(gate_values, offset, row_count, 0)
    local_routes = lax.dynamic_slice_in_dim(routes, offset, row_count, 0)
    grad_chosen = local_gates * (grad_gates - jnp.sum(local_gates * grad_gates, -1, keepdims=True))
    columns = jnp.arange(experts, dtype=jnp.int32)[None, :]
    grad_logits = (
        jnp.where(local_routes[:, 0:1] == columns, grad_chosen[:, 0:1], 0.0)
        + jnp.where(local_routes[:, 1:2] == columns, grad_chosen[:, 1:2], 0.0)
    ).astype(jnp.bfloat16)
    grad_normed_two = grad_normed_two + jnp.einsum(
        "re,de->rd", grad_logits, router_w, preferred_element_type=jnp.float32
    )
    router_term = jnp.einsum(
        "rd,re->de", normed_two, grad_logits, preferred_element_type=jnp.float32
    )
    grad_hidden_norm, gain_two_term = general_norm_back(grad_normed_two, unit_two, factor_two, gain_expert)
    grad_hidden = cotangent.astype(jnp.float32) + grad_hidden_norm
    grad_attn = lax.all_gather(grad_hidden.astype(jnp.bfloat16), "heads", axis=0, tiled=True)
    grad_mixed = jnp.einsum(
        "rd,cd->rc", grad_attn, attn_w, preferred_element_type=jnp.float32
    ).astype(jnp.bfloat16)
    out_term = jnp.einsum("rc,rd->cd", mixed_rows, grad_attn, preferred_element_type=jnp.float32)
    grad_query, grad_key, grad_value = lax.map(
        attn_backward, (queries, key_rows, value_rows, to_blocks(grad_mixed), log_total)
    )
    grad_proj = jnp.concatenate(
        [from_blocks(grad_query), from_blocks(grad_key), from_blocks(grad_value)], 1
    )
    grad_normed_one = lax.psum_scatter(
        jnp.einsum("rc,dc->rd", grad_proj, joined_w, preferred_element_type=jnp.float32).astype(
            jnp.bfloat16
        ),
        "heads",
        scatter_dimension=0,
        tiled=True,
    ).astype(jnp.float32)
    proj_term = jnp.einsum("rd,rc->dc", normed_all, grad_proj, preferred_element_type=jnp.float32)
    proj_stack = jnp.stack(
        [
            proj_term[:, :head_cols],
            proj_term[:, head_cols : 2 * head_cols],
            proj_term[:, 2 * head_cols :],
        ],
        0,
    )
    whole_proj = lax.dynamic_update_slice_in_dim(
        jnp.zeros((3, width, width), jnp.float32), proj_stack, head_start, 2
    )
    whole_out = lax.dynamic_update_slice_in_dim(
        jnp.zeros((width, width), jnp.float32), out_term, head_start, 0
    )
    send_qkv = (
        whole_proj.reshape(3, n_dp, n_tensor, row_piece, n_heads, col_piece)
        .transpose(1, 4, 2, 0, 3, 5)
        .reshape(-1, 3, row_piece, col_piece)
    )
    send_out = (
        whole_out.reshape(n_heads, col_piece, n_dp, n_tensor, row_piece)
        .transpose(2, 0, 3, 1, 4)
        .reshape(-1, col_piece, row_piece)
    )
    shard_proj, shard_attn = (
        lax.psum_scatter(send_qkv, ("dp", "heads", "tensor"), scatter_dimension=0, tiled=True),
        lax.psum_scatter(send_out, ("dp", "heads", "tensor"), scatter_dimension=0, tiled=True),
    )
    grad_input_norm, gain_one_term = general_norm_back(grad_normed_one, unit_one, factor_one, gain_attn)
    grad_input = (grad_hidden + grad_input_norm).astype(jnp.bfloat16)
    gain_one_grad, gain_two_grad, router_all = lax.psum(
        (gain_one_term, gain_two_term, router_term), ("dp", "heads", "tensor")
    )
    router_grad = lax.dynamic_slice_in_dim(
        router_all, lax.axis_index(("dp", "heads")) * w_router.shape[0], w_router.shape[0], 0
    )
    local_tau = lax.dynamic_slice_in_dim(tau, lax.axis_index("heads") * own_heads, own_heads, 0)
    clip_factor = jnp.sqrt(local_tau / jnp.maximum(peak_logit, local_tau))
    clipped = (w_qkv[:2].astype(jnp.float32) * jnp.repeat(clip_factor, HEAD_DIM)).astype(
        jnp.bfloat16
    )
    return (
        output,
        grad_input,
        gain_one_grad,
        gain_two_grad,
        shard_proj[0],
        shard_attn[0],
        router_grad,
        shard_first,
        shard_second,
        clipped,
    )


def body(*args):
    inputs, _, routes, _, _, _, w_qkv, _, w_router, w_in, _ = args
    sz = Sizes(
        lax.axis_size("dp"), lax.axis_size("heads"), lax.axis_size("tensor"), inputs, routes, w_qkv, w_router, w_in
    )
    if sz.fits():
        return fast_body(sz, *args)
    return general_body(*args)


def solution(mesh):
    return jax.shard_map(
        body,
        mesh=mesh,
        in_specs=(
            P(("dp", "heads", "tensor"), None),
            P(("dp", "heads", "tensor"), None),
            P(("dp", "heads"), None),
            P(),
            P(),
            P(),
            P(None, ("dp", "tensor"), "heads"),
            P("heads", ("dp", "tensor")),
            P(("dp", "heads"), None),
            P(("dp", "heads"), None, "tensor"),
            P(("dp", "heads"), "tensor", None),
        ),
        out_specs=(
            P(("dp", "heads", "tensor"), None),
            P(("dp", "heads", "tensor"), None),
            P(),
            P(),
            P(None, ("dp", "tensor"), "heads"),
            P("heads", ("dp", "tensor")),
            P(("dp", "heads"), None),
            P(("dp", "heads"), None, "tensor"),
            P(("dp", "heads"), "tensor", None),
            P(None, ("dp", "tensor"), "heads"),
        ),
        check_vma=False,
    )
```

```python
import functools
import jax
import jax.numpy as jnp
from jax import lax
from jax.experimental import pallas as pl
from jax.experimental.pallas import tpu as pltpu
from jax.sharding import PartitionSpec as P

HEADS = 8
HEAD_DIM = 64
SEQ = 197
F32 = jnp.float32
BF16 = jnp.bfloat16
MESH = pl.DeviceIdType.MESH
NEG = -1e30


class Sizes:
    def __init__(self, n_dp, n_heads, n_tensor, inputs, routes, w_qkv, w_router, w_in):
        self.nd, self.nh, self.nt = n_dp, n_heads, n_tensor
        self.groups = n_dp * n_heads
        self.rows, self.width = inputs.shape
        self.pad = -(-self.rows // 16) * 16
        self.block = self.pad * n_tensor
        self.block_rows = routes.shape[0]
        self.own = w_in.shape[0]
        self.hidden = w_in.shape[2]
        self.experts = self.own * self.groups
        self.cap = (self.block_rows * 5 // (16 * self.experts) + 1) * 8
        self.group_slots = self.own * self.cap
        self.slots = self.experts * self.cap
        self.row_piece, self.col_piece = w_qkv.shape[1], w_qkv.shape[2]
        self.band = self.row_piece * n_tensor
        self.router_rows = w_router.shape[0]
        self.parts = 4

    def fits(self):
        return (
            self.rows == SEQ
            and self.nt == 4
            and self.parts == 4
            and self.block_rows == self.rows * self.nt
            and self.cap == 64
            and self.experts == 32
            and self.group_slots % 128 == 0
            and self.col_piece % 128 == 0
            and self.row_piece % 16 == 0
            and self.router_rows % 16 == 0
            and self.own * self.groups * 4 == 128
            and self.width == HEADS * HEAD_DIM
            and self.block * self.width * 2 <= 2**20
            and self.own * self.width <= self.slots
            and self.hidden <= self.block
            and self.hidden == self.width
            and self.cap % (16 * self.nt) == 0
            and self.width // self.parts % 128 == 0
        )


def nn(a, b):
    return jnp.dot(a, b, preferred_element_type=F32)


def nt(a, b):
    return lax.dot_general(a, b, (((1,), (1,)), ((), ())), preferred_element_type=F32)


def tn(a, b):
    return lax.dot_general(a, b, (((0,), (0,)), ((), ())), preferred_element_type=F32)


def iota(shape, axis):
    return lax.broadcasted_iota(jnp.int32, shape, axis)


def normalize(rows):
    centered = rows - jnp.mean(rows, -1, keepdims=True)
    factor = lax.rsqrt(jnp.mean(centered * centered, -1, keepdims=True) + 1e-06)
    return centered * factor, factor


def norm_back(grad_norm, unit_rows, factor, gain):
    grad_hat = grad_norm * gain
    inner = (
        grad_hat
        - jnp.mean(grad_hat, -1, keepdims=True)
        - unit_rows * jnp.mean(grad_hat * unit_rows, -1, keepdims=True)
    )
    return factor * inner, jnp.sum(grad_norm * unit_rows, 0, keepdims=True)


def split_high_low(values):
    high = values.astype(BF16)
    low = (values - high.astype(F32)).astype(BF16)
    return jnp.concatenate([high, low], 0)


class Place:
    def __init__(self, sz):
        self.sz = sz
        self.d = lax.axis_index("dp")
        self.h = lax.axis_index("heads")
        self.z = lax.axis_index("tensor")
        self.group = self.d * sz.nh + self.h

    def plane(self, group):
        return (group // self.sz.nh, group % self.sz.nh, self.z)

    def line(self, z):
        return (self.d, self.h, z)

    def next_group(self, k):
        return (self.group + k) % self.sz.groups

    def next_z(self, j):
        return (self.z + j) % self.sz.nt

    def inner(self):
        return (self.z + 1) % 4 // 2

    def mates(self):
        return self.z + 1 - 2 * (self.z % 2), (self.z + 2) % 4, 3 - self.z

    def enter(self):
        sz = self.sz
        barrier = pltpu.get_barrier_semaphore()
        for k in range(1, sz.groups):
            pl.semaphore_signal(barrier, inc=1, device_id=self.plane(self.next_group(k)), device_id_type=MESH)
        for j in range(1, sz.nt):
            pl.semaphore_signal(barrier, inc=1, device_id=self.line(self.next_z(j)), device_id_type=MESH)
        pl.semaphore_wait(barrier, sz.groups + sz.nt - 2)


def remote(src, dst, send, recv, device):
    return pltpu.make_async_remote_copy(
        src_ref=src, dst_ref=dst, send_sem=send, recv_sem=recv, device_id=device, device_id_type=MESH
    )


def drain(send_sem, recv_sem, sent, landed):
    pltpu.make_async_copy(sent, sent, send_sem).wait()
    pltpu.make_async_copy(landed, landed, recv_sem).wait()


def route_table(sz, routes_ref, table):
    table[...] = jnp.full_like(table, -1.0)
    for z in range(sz.nt):
        table[0:2, z * sz.pad : z * sz.pad + sz.rows] = routes_ref[:, z * sz.rows : (z + 1) * sz.rows].astype(F32)


def block_kernel(
    sz, x_ref, cot_ref, routes_ref, gain_one_ref, gain_two_ref, w_qkv_ref, w_out_ref, w_router_ref, tau_ref, first_hbm,
    second_hbm, output_out, grad_input_out, gain_one_out, gain_two_out, qkv_out, out_out, router_out, clipped_out,
    grad_first_out, grad_second_out,
    w_own, w_full, router_own, router_full, router_t, route_rows, route_columns, select, select_t, select_q, select_qt,
    cot_block, rows_block, send_a, send_b, cot_slots, slots, grad_slots, values,
    rows_q, rows_line, grads_q, grads_line, grads_sum, grads_back, first, second, act, grad_pre, grad_act,
    gate_send, gate_recv, gates_at, dgate_send, dgate_recv, dgate_rows,
    qkv, probs, mixed, hidden_at, peak_at, part, part_own, part_send, part_recv, mix_own, mix_send, mix_recv,
    grad_mixed, grad_qkv, core_send, core_recv, w_half, band_send, band_recv, line_send, line_recv,
    small, small_send, small_core, small_x, small_z, rt, rt_core, rt_x, rt_z,
    wz_s, wz_r, wx_s, wx_r, wc_s, wc_r, r_s, r_r, qz_s, qz_r, nz_s, nz_r, qa_s, qa_r, na_s, na_r, ga_s, ga_r,
    d0_s, d0_r, da_s, da_r, va_s, va_r, dg_s, dg_r, pz_s, pz_r, mz_s, mz_r, gc_s, gc_r, gx_s, gx_r, gl_s, gl_r,
    sc_s, sc_r, sx_s, sx_r, dl_s, dl_r, dq_s, dq_r, nq_s, nq_r, nl_s, nl_r, nb_s, nb_r, pr_r, mr_r,
    local_sem,
):
    at = Place(sz)
    d, h, z, me = at.d, at.h, at.z, at.group
    nd, nh, nz, ng = sz.nd, sz.nh, sz.nt, sz.groups
    band, rp, cp, pad, width = sz.band, sz.row_piece, sz.col_piece, sz.pad, sz.width
    many = ng * sz.cap
    parts, part_width = sz.parts, width // sz.parts

    def lanes(c):
        return pl.ds(c * part_width, part_width)

    def rows_at(n, size):
        return pl.ds(pl.multiple_of(n * size, size), size)

    own_block, own_columns = rows_at(z, pad), rows_at(h, cp)
    inner = at.inner()
    beside, across, mirror = at.mates()

    w_own[0:3] = w_qkv_ref[...]
    w_own[3] = w_out_ref[...]
    router_own[...] = jnp.zeros_like(router_own)
    router_own[:, 0 : sz.router_rows] = w_router_ref[...]
    cot_block[own_block] = jnp.concatenate(
        [cot_ref[...].astype(F32), jnp.zeros((pad - sz.rows, width), F32)], 0
    ).astype(BF16)

    part_recv[2] = jnp.zeros((pad, width), BF16)
    mix_recv[2] = jnp.zeros((pad, width), BF16)

    at.enter()

    w_rows = rows_at(d * nz + z, rp)
    others = pl.ds(0, ng - 1)

    def send_line(i):
        for j in range(1, nz):
            remote(
                w_own.at[i], w_full.at[i, w_rows, own_columns], wz_s.at[i], wz_r.at[i], at.line(at.next_z(j))
            ).start()

    def along(block, send_sems, recv_sems, c):
        place = block.at[own_block, lanes(c)]
        return [
            remote(place, place, send_sems.at[c], recv_sems.at[c], at.line(at.next_z(j)))
            for j in range(1, nz)
        ]

    def wait_along(block, send_sems, recv_sems, c):
        place = block.at[pl.ds(0, (nz - 1) * pad), lanes(c)]
        drain(send_sems.at[c], recv_sems.at[c], place, place)

    for i in range(3):
        send_line(i)
    for copy in along(cot_block, qz_s, qz_r, 0):
        copy.start()
    send_line(3)
    routers = [
        remote(router_own, router_full.at[me], r_s.at[0], r_r.at[0], at.plane(at.next_group(k)))
        for k in range(1, ng)
    ]
    for copy in routers:
        copy.start()
    loads = [
        pltpu.make_async_copy(first_hbm, first, local_sem.at[0]),
        pltpu.make_async_copy(second_hbm, second, local_sem.at[1]),
    ]
    for copy in loads:
        copy.start()
    w_full[:, w_rows, own_columns] = w_own[...]
    router_full[me] = router_own[...]

    def to_core(i, dp, other):
        place = w_full.at[i, rows_at(dp, band), own_columns]
        n = 4 * (other - 1) + i
        return remote(place, place, wc_s.at[n], wc_r.at[n], (d, (h + other) % nh, z))

    def send_band(i):
        landed = w_full.at[i, pl.ds(0, (nz - 1) * rp), own_columns]
        drain(wz_s.at[i], wz_r.at[i], landed, landed)
        place = w_full.at[i, rows_at(d, band), own_columns]
        for k in range(1, nd):
            remote(place, place, wx_s.at[i], wx_r.at[i], ((d + k) % nd, h, z)).start()
        for other in range(1, nh):
            to_core(i, d, other).start()

    def pass_on(i):
        landed = w_full.at[i, pl.ds(0, (nd - 1) * band), own_columns]
        drain(wx_s.at[i], wx_r.at[i], landed, landed)
        for k in range(1, nd):
            for other in range(1, nh):
                to_core(i, (d + k) % nd, other).start()

    def arrived(i):
        for other in range(1, nh):
            n, columns = 4 * (other - 1) + i, w_full.at[i, :, own_columns]
            drain(wc_s.at[n], wc_r.at[n], columns, columns)

    zeros = jnp.zeros((pad - sz.rows, width), F32)
    x_rows = jnp.concatenate([x_ref[...].astype(F32), zeros], 0)
    unit_one, _ = normalize(x_rows)
    normed_one = (unit_one * gain_one_ref[...]).astype(BF16)
    for i in range(3):
        send_band(i)

    route_table(sz, routes_ref, route_rows)
    route_a, route_b = route_rows[0:1, :], route_rows[1:2, :]
    expert = iota((sz.experts, sz.block), 0).astype(F32)
    named_a, named_b = route_a == expert, route_b == expert
    named = jnp.logical_or(named_a, named_b)
    before = (iota((sz.block, sz.block), 0) < iota((sz.block, sz.block), 1)).astype(BF16)
    rank = nn(named.astype(BF16), before) + expert * float(sz.cap)
    slot_a = jnp.sum(jnp.where(named_a, rank, 0.0), 0, keepdims=True)
    slot_b = jnp.sum(jnp.where(named_b, rank, 0.0), 0, keepdims=True)
    slot_a = jnp.where(route_a < 0.0, -1.0, slot_a)
    slot_b = jnp.where(route_b < 0.0, -1.0, slot_b)
    slot_pair = jnp.concatenate([slot_a, slot_b] * 64, 0)
    route_columns[...] = slot_pair.T

    def fill(g, carry):
        slot = iota((sz.group_slots, sz.block), 0).astype(F32) + (g * sz.group_slots).astype(F32)
        hit = jnp.logical_or(slot == slot_a, slot == slot_b)
        select[rows_at(g, sz.group_slots), :] = jnp.where(hit, 1.0, 0.0).astype(BF16)
        return carry

    lax.fori_loop(0, ng, fill, 0)

    quarter = sz.cap // nz
    few = ng * sz.own * quarter

    def quarter_slot(dims, axis):
        n = iota(dims, axis)
        return (n // quarter * sz.cap + z * quarter + n % quarter).astype(F32)

    some_slot = quarter_slot((few, sz.block), 0)
    select_q[...] = jnp.where(jnp.logical_or(some_slot == slot_a, some_slot == slot_b), 1.0, 0.0).astype(BF16)

    def quarter_move(k, send, landing, send_sems, recv_sems):
        g = (me + k) % ng
        return remote(send.at[g], landing.at[me], send_sems.at[0], recv_sems.at[0], at.plane(g))

    def exchange(c, k, send, out, send_sems, recv_sems):
        g = (me + k) % ng
        return remote(
            send.at[g, :, lanes(c)], out.at[me, :, lanes(c)], send_sems.at[c], recv_sems.at[c], at.plane(g)
        )

    def dispatch(c, block, send, out, send_sems, recv_sems):
        def step(i, carry):
            k = ng - 1 - i
            g = (me + k) % ng
            send[g, :, lanes(c)] = nn(select[rows_at(g, sz.group_slots), :], block[:, lanes(c)]).astype(BF16)

            @pl.when(k > 0)
            def _():
                exchange(c, k, send, out, send_sems, recv_sems).start()

            return carry

        lax.fori_loop(0, ng, step, 0)
        out[me, :, lanes(c)] = send[me, :, lanes(c)]

    def start_part(c, *flow):
        def step(i, carry):
            exchange(c, ng - 1 - i, *flow).start()
            return carry

        lax.fori_loop(0, ng - 1, step, 0)

    def wait_part(c, send, out, send_sems, recv_sems):
        drain(send_sems.at[c], recv_sems.at[c], send.at[others, :, lanes(c)], out.at[others, :, lanes(c)])

    cot_flow = (send_a, cot_slots, qa_s, qa_r)
    row_flow = (send_b, slots, na_s, na_r)

    def send_cot(c):
        wait_along(cot_block, qz_s, qz_r, c)
        dispatch(c, cot_block, *cot_flow)

    send_band(3)
    for c in range(1, parts):
        for copy in along(cot_block, qz_s, qz_r, c):
            copy.start()
    pass_on(0)
    send_cot(0)
    pass_on(1)
    pass_on(2)

    for i in range(3):
        arrived(i)
        qkv[i] = nn(normed_one, w_full[i]).astype(BF16)
    pass_on(3)
    lane = iota((1, 2 * HEAD_DIM), 1)
    halves = (lane < HEAD_DIM, lane >= HEAD_DIM)
    key_valid = iota((1, pad), 1) < sz.rows
    row_valid = iota((pad, 1), 0) < sz.rows
    peak_lane = iota((1, 128), 1)
    peak_at[...] = jnp.full_like(peak_at, NEG)
    scale = HEAD_DIM ** (-0.5)

    def attend(pair, carry):
        columns = rows_at(pair, 2 * HEAD_DIM)
        q_pair, k_pair, v_pair = (qkv[i, :, columns] for i in range(3))
        sides = []
        for side in range(2):
            q_own = jnp.where(halves[side], q_pair, jnp.zeros_like(q_pair))
            scores = jnp.where(key_valid, nt(q_own, k_pair) * scale, NEG)
            row_peak = jnp.max(scores, -1, keepdims=True)
            exponent = jnp.exp(scores - row_peak)
            weights = (exponent / jnp.sum(exponent, -1, keepdims=True)).astype(BF16)
            head = pair * 2 + side
            probs[head] = weights
            sides.append(nn(weights, v_pair))
            peak = jnp.max(jnp.where(row_valid, row_peak, NEG), 0, keepdims=True)
            peak_at[0:1, :] = jnp.where(peak_lane == head, peak, peak_at[0:1, :])
        mixed[:, columns] = jnp.where(halves[0], sides[0], sides[1]).astype(BF16)
        return carry

    pairs = HEADS // 2
    lax.fori_loop(0, pairs // 2, attend, 0)
    send_cot(1)
    lax.fori_loop(pairs // 2, pairs, attend, 0)

    arrived(3)
    hidden = x_rows + nt(mixed[...], w_full[3])
    hidden_at[...] = hidden
    unit_two, _ = normalize(hidden)
    rows_block[own_block] = jnp.where(row_valid, unit_two * gain_two_ref[...], 0.0).astype(BF16)

    def row_copy(c, owner, to, recv_sems):
        place = rows_block.at[rows_at(owner, pad), lanes(c)]
        return remote(place, place, nz_s.at[c], recv_sems.at[c], at.line(to))

    for c in range(parts):
        row_copy(c, z, across, nb_r).start()
        row_copy(c, z, beside, nz_r).start()

        @pl.when(inner == 1)
        def _(c=c):
            row_copy(c, z, mirror, nz_r).start()

    def row_bytes(c, pieces):
        return rows_block.at[pl.ds(0, pieces * pad), lanes(c)]

    def wait_rows(c):
        pltpu.make_async_copy(row_bytes(c, 1), row_bytes(c, 1), nb_r.at[c]).wait()

        @pl.when(inner == 1)
        def _():
            row_copy(c, across, beside, nz_r).start()

        pltpu.make_async_copy(row_bytes(c, 2), row_bytes(c, 2), nz_r.at[c]).wait()

        @pl.when(inner == 1)
        def _():
            pltpu.make_async_copy(row_bytes(c, 4), row_bytes(c, 4), nz_s.at[c]).wait()

        @pl.when(inner == 0)
        def _():
            pltpu.make_async_copy(row_bytes(c, 2), row_bytes(c, 2), nz_s.at[c]).wait()

    for c in range(2, parts):
        send_cot(c)

    def fill_t(i, carry):
        rows = rows_at(i, pad)
        slot = iota((pad, sz.slots), 1).astype(F32)
        hit = jnp.logical_or(slot == route_columns[rows, 0:1], slot == route_columns[rows, 1:2])
        select_t[rows, :] = jnp.where(hit, 1.0, 0.0).astype(BF16)
        some = quarter_slot((pad, few), 1)
        hit = jnp.logical_or(some == route_columns[rows, 0:1], some == route_columns[rows, 1:2])
        select_qt[rows, :] = jnp.where(hit, 1.0, 0.0).astype(BF16)
        return carry

    lax.fori_loop(0, nz, fill_t, 0)
    drain(r_s.at[0], r_r.at[0], router_full.at[others], router_full.at[others])
    for g in range(ng):
        router_t[:, g * sz.router_rows : (g + 1) * sz.router_rows] = router_full[g, :, 0 : sz.router_rows]

    def expert_rows(ref, e):
        return ref[:, rows_at(e, sz.cap), :].reshape(many, width)

    def send_gates():
        logits = jnp.where(named, nt(router_t[...], rows_block[...]), NEG)
        exponent = jnp.where(named, jnp.exp(logits - jnp.max(logits, 0, keepdims=True)), 0.0)
        total = jnp.sum(exponent, 0, keepdims=True)
        gates = exponent / jnp.where(total > 0.0, total, 1.0)
        gates_at[...] = gates
        by_slot = nt(split_high_low(gates), select[...])
        by_slot = by_slot[0 : sz.experts] + by_slot[sz.experts :]
        own_slot = iota((sz.experts, sz.slots), 1) // sz.cap == iota((sz.experts, sz.slots), 0)
        by_slot = jnp.where(own_slot, by_slot, 0.0)
        folded = by_slot[:, 0:128]
        for i in range(1, sz.slots // 128):
            folded = folded + by_slot[:, i * 128 : (i + 1) * 128]
        gate_send[...] = folded
        gate_copies = [
            remote(
                gate_send.at[rows_at(at.next_group(k) * sz.own // 8, 8)], gate_recv.at[me], ga_s.at[0], ga_r.at[0],
                at.plane(at.next_group(k)),
            )
            for k in range(1, ng)
        ]
        for copy in gate_copies:
            copy.start()
        gate_recv[me] = gate_send[rows_at(me * sz.own // 8, 8)]

    for c in range(parts):
        wait_rows(c)
        if c == 0:
            rows_q[...] = nn(select_q[...], rows_block[:, lanes(0)]).astype(BF16).reshape(rows_q.shape)
            for k in range(1, ng):
                quarter_move(k, rows_q, rows_line.at[z], nq_s, nq_r).start()
            rows_line[z, me] = rows_q[me]
            continue
        if c == parts - 1:
            drain(nq_s.at[0], nq_r.at[0], rows_q.at[others], rows_q.at[others])
            for j in range(1, nz):
                remote(rows_line.at[z], rows_line.at[z], nl_s.at[0], nl_r.at[0], at.line(at.next_z(j))).start()
            send_gates()
        dispatch(c, rows_block, *row_flow)

    drain(ga_s.at[0], ga_r.at[0], gate_recv.at[others], gate_recv.at[others])
    def gate_of(e):
        turned = gate_recv[:, pl.ds(me * sz.own % 8 + e, 1), :].reshape(ng, 128).T
        columns = jnp.where((e % 2) == 1, turned[sz.cap : 2 * sz.cap], turned[0 : sz.cap])
        return jnp.concatenate([columns[:, s : s + 1] for s in range(ng)], 0)

    def weigh(e, carry):
        grad_act[e] = nt(expert_rows(cot_slots, e), second[e]) * gate_of(e)
        return carry

    for c in range(parts):
        wait_part(c, *cot_flow)
    for copy in loads:
        copy.wait()
    lax.fori_loop(0, sz.own, weigh, 0)
    lines = rows_line.at[pl.ds(0, nz - 1)]
    drain(nl_s.at[0], nl_r.at[0], lines, lines)
    for i in range(nz):
        for e in range(sz.own):
            slots[:, e * sz.cap + i * quarter : e * sz.cap + (i + 1) * quarter, lanes(0)] = rows_line[
                i, :, e * quarter : (e + 1) * quarter, :
            ]
    for c in range(1, parts):
        wait_part(c, *row_flow)

    def first_piece(e, g):
        piece = (rows_at(e, sz.cap), lanes(1))
        return remote(
            send_a.at[(g, *piece)], grad_slots.at[(me, *piece)], d0_s.at[e], d0_r.at[e], at.plane(g)
        )

    def grads_piece(e, j):
        piece = (slice(None), rows_at(e, quarter), slice(None))
        return remote(
            grads_q.at[(at.next_z(j), *piece)], grads_line.at[(j - 1, *piece)], dl_s.at[0], dl_r.at[0],
            at.line(at.next_z(j)),
        )

    def expert_back(e, carry):
        half_rows = many // 2
        for part_at in range(2):
            some = slice(part_at * half_rows, (part_at + 1) * half_rows)
            groups = slice(part_at * ng // 2, (part_at + 1) * ng // 2)
            pre = nn(slots[groups, rows_at(e, sz.cap), :].reshape(half_rows, width), first[e])
            const, cubic = 0.7978845608028654, 0.044715
            square = pre * pre
            half = 0.5 * jnp.tanh(pre * (const + const * cubic * square)) + 0.5
            hidden_units = pre * half
            act[e, some] = hidden_units.astype(BF16)
            through = grad_act[e, some]
            dgate = nt(jnp.ones((8, sz.hidden), BF16), (hidden_units * through).astype(BF16))
            dgate_send[:, some] = jnp.where(iota((8, half_rows), 0) == e, dgate, dgate_send[:, some])
            slope = half * (1.0 + (1.0 - half) * (pre * (2.0 * const + 6.0 * const * cubic * square)))
            grads = (through * slope).astype(BF16)
            grad_pre[e, some] = grads
            spread = nt(grads, first[e]).astype(BF16).reshape(ng // 2, sz.cap, width)
            send_a[groups, rows_at(e, sz.cap), :] = spread
            for i in range(nz):
                grads_q[i, groups, rows_at(e, quarter), :] = spread[:, i * quarter : (i + 1) * quarter, 0:part_width]

        def step(i, carry):
            first_piece(e, (me + ng - 1 - i) % ng).start()
            return carry

        lax.fori_loop(0, ng - 1, step, 0)
        for j in range(1, nz):
            grads_piece(e, j).start()
        return carry

    dgate_send[...] = jnp.zeros_like(dgate_send)
    lax.fori_loop(0, sz.own, expert_back, 0)
    dgates = [
        remote(
            dgate_send.at[:, rows_at(at.next_group(k) * sz.cap // 128, 128)], dgate_recv.at[me], dg_s.at[0],
            dg_r.at[0], at.plane(at.next_group(k)),
        )
        for k in range(1, ng)
    ]
    for copy in dgates:
        copy.start()
    dgate_recv[me] = dgate_send[:, rows_at(me * sz.cap // 128, 128)]
    grad_flow = (send_a, grad_slots, da_s, da_r)
    value_flow = (send_b, values, va_s, va_r)
    for c in range(2, parts):
        start_part(c, *grad_flow)
    grad_slots[me] = send_a[me]

    def expert_value(e, carry):
        value = nn(act[e], second[e])
        gated = (value * gate_of(e)).astype(BF16).reshape(ng, sz.cap, width)
        send_b[:, rows_at(e, sz.cap), :] = gated
        return carry

    lax.fori_loop(0, sz.own, expert_value, 0)
    values[me] = send_b[me]

    def quarter_total(own, line, sums):
        total = own[z].astype(F32)
        for j in range(1, nz):
            total = total + line[j - 1].astype(F32)
        sums[...] = total.astype(BF16)


    def weight_grads(e, carry):
        grad_value = (expert_rows(cot_slots, e).astype(F32) * gate_of(e)).astype(BF16)
        grad_second_out[e] = tn(act[e], grad_value).astype(BF16)
        grad_first_out[e] = tn(expert_rows(slots, e), grad_pre[e]).astype(BF16)
        return carry

    drain(dg_s.at[0], dg_r.at[0], dgate_recv.at[others], dgate_recv.at[others])
    mine = iota((8, 128), 1) // sz.cap == me * sz.cap % 128 // sz.cap
    for g in range(ng):
        folded = jnp.where(mine, dgate_recv[g], 0.0)
        folded = folded + pltpu.roll(folded, 64, 1)
        dgate_rows[g * sz.own : (g + 1) * sz.own, :] = folded[0 : sz.own]
    spread = jnp.concatenate([dgate_rows[...]] * (sz.slots // 128), 1)
    own_slot = iota((sz.experts, sz.slots), 1) // sz.cap == iota((sz.experts, sz.slots), 0)
    dgate = nt(split_high_low(jnp.where(own_slot, spread, 0.0)), select_t[...])
    dgate = dgate[0 : sz.experts] + dgate[sz.experts :]
    gates = gates_at[...]
    dlogits = (dgate - gates * jnp.sum(dgate, 0, keepdims=True)).astype(BF16)
    rt[...] = nn(dlogits, rows_block[...])
    part[...] = tn(dlogits, router_t[...])

    def line_copy(c, slot, send, recv, send_sems, recv_sems, relay_sems, last):
        if slot < 2:
            return remote(
                send.at[slot, :, lanes(c)], recv.at[slot, :, lanes(c)], send_sems.at[c], recv_sems.at[c],
                at.line((beside, across)[slot]),
            )
        by_way = 1 - inner if c != last else 0
        to = mirror + by_way * (beside - mirror)
        return remote(
            send.at[2, :, lanes(c)], recv.at[2 + by_way, :, lanes(c)], send_sems.at[c], relay_sems.at[c, by_way], at.line(to)
        )

    def scatter(c, source, base, own, *flow):
        if source is grads_back:
            places, flat = select_qt, source[...].reshape(few, part_width)
        else:
            places, flat = select_t, source[:, :, lanes(c)].reshape(sz.slots, part_width)
        for slot, target in ((2, mirror), (1, across), (0, beside), (None, z)):
            tokens = rows_at(target, pad)
            sums = nn(places[tokens, :], flat)
            if base is not None:
                sums = sums + base[tokens, lanes(c)]
            if slot is None:
                own[:, lanes(c)] = sums
                continue
            flow[0][slot, :, lanes(c)] = sums.astype(BF16)
            if slot == 1 and c != flow[-1]:

                @pl.when(inner == 0)
                def _():
                    line_copy(c, 1, *flow).start()
            else:
                line_copy(c, slot, *flow).start()

    def relay(c, send, recv, send_sems, recv_sems, relay_sems, last):
        @pl.when(inner == 1)
        def _():
            landed = recv.at[3, :, lanes(c)]
            pltpu.make_async_copy(landed, landed, relay_sems.at[c, 1]).wait()
            send[1, :, lanes(c)] = (send[1, :, lanes(c)].astype(F32) + recv[3, :, lanes(c)].astype(F32)).astype(BF16)
            line_copy(c, 1, send, recv, send_sems, recv_sems, relay_sems, last).start()

    def gathered(own, send, recv, send_sems, recv_sems, relay_sems, last):
        for c in range(parts):
            drain(send_sems.at[c], recv_sems.at[c], send.at[:, :, lanes(c)], recv.at[pl.ds(0, 2), :, lanes(c)])

            @pl.when(inner == 1 if c != last else True)
            def _(c=c):
                landed = recv.at[2, :, lanes(c)]
                pltpu.make_async_copy(landed, landed, relay_sems.at[c, 0]).wait()

        sums = own[...]
        for slot in range(3):
            sums = sums + recv[slot].astype(F32)
        return sums

    part_flow = (part_send, part_recv, pz_s, pz_r, pr_r, 0)
    mix_flow = (mix_send, mix_recv, mz_s, mz_r, mr_r, parts - 1)

    def wait_first(e, carry):
        piece = (others, rows_at(e, sz.cap), lanes(1))
        drain(d0_s.at[e], d0_r.at[e], send_a.at[piece], grad_slots.at[piece])
        return carry

    def exchange_quarters():
        drain(dl_s.at[0], dl_r.at[0], grads_line, grads_line)
        quarter_total(grads_q, grads_line, grads_sum)
        for copy in grads_moves:
            copy.start()
        for i in range(2):
            start_part(i, *value_flow)
        grads_back[me] = grads_sum[me]

    grads_moves = [quarter_move(k, grads_sum, grads_back, dq_s, dq_r) for k in range(1, ng)]
    order = [*range(1, parts), 0]
    exchange_quarters()
    done = 0
    for turn, c in enumerate(order):
        if c == 0:
            drain(dq_s.at[0], dq_r.at[0], grads_back.at[others], grads_back.at[others])
        elif c == 1:
            lax.fori_loop(0, sz.own, wait_first, 0)
        else:
            wait_part(c, *grad_flow)
        if c == parts - 1:
            for i in range(2, parts):
                start_part(i, *value_flow)
        scatter(c, grads_back if c == 0 else grad_slots, part, part_own, *part_flow)
        until = sz.own * (turn + 1) // parts
        lax.fori_loop(done, until, weight_grads, 0)
        done = until
        if turn > 0:
            relay(order[turn - 1], *part_flow)
    def send_mix(c):
        wait_part(c, *value_flow)
        scatter(c, values, None, mix_own, *mix_flow)
        if c:
            relay(c - 1, *mix_flow)

    send_mix(0)
    unit_two, factor_two = normalize(hidden_at[...])
    grad_normed = jnp.where(row_valid, gathered(part_own, *part_flow), 0.0)
    grad_hidden, gain_two = norm_back(grad_normed, unit_two, factor_two, gain_two_ref[...])
    grad_hidden = jnp.concatenate([cot_ref[...].astype(F32), zeros], 0) + jnp.where(row_valid, grad_hidden, 0.0)
    part_own[...] = grad_hidden
    grad_attn = grad_hidden.astype(BF16)

    def core_copy(i, other):
        n = 4 * (other - 1) + i
        return remote(
            core_send.at[other - 1, i], core_recv.at[other - 1, i], gc_s.at[n], gc_r.at[n], (d, (h + other) % nh, z)
        )

    def half_sum(i, sums):
        for other in range(1, nh):
            core_copy(i, other).wait()
            sums = sums + core_recv[other - 1, i].astype(F32)
        w_half[i] = sums
        band_send[i] = sums.astype(BF16)

    def band_copy(k, i):
        to = (d + k) % nd
        return remote(
            band_send.at[i, rows_at(to, band), :], band_recv.at[k - 1, i], gx_s.at[i], gx_r.at[i], (to, h, z)
        )

    for other in [*range(1, nh), 0]:
        sums = tn(grad_attn, mixed[:, rows_at((h + other) % nh, cp)])
        if other:
            core_send[other - 1, 3] = sums.astype(BF16)
            core_copy(3, other).start()
        else:
            w_half[3] = sums
    grad_mixed[...] = nn(grad_attn, w_full[3]).astype(BF16)
    half_sum(3, w_half[3])
    for k in range(1, nd):
        band_copy(k, 3).start()


    send_mix(1)

    def attend_back(pair):
        columns = rows_at(pair, 2 * HEAD_DIM)
        q_pair, k_pair, v_pair = (qkv[i, :, columns] for i in range(3))
        g_pair = grad_mixed[:, columns]
        dq, dk, dv = [], [], []
        for side in range(2):
            weights = probs[pair * 2 + side]
            soft = weights.astype(F32)
            g_own = jnp.where(halves[side], g_pair, jnp.zeros_like(g_pair))
            grad_soft = nt(g_own, v_pair)
            inner = jnp.sum(soft * grad_soft, -1, keepdims=True)
            grad_scores = (soft * (grad_soft - inner)).astype(BF16)
            dq.append(nn(grad_scores, k_pair))
            dk.append(tn(grad_scores, q_pair))
            dv.append(tn(weights, g_pair))
        grad_qkv[0, :, columns] = (jnp.where(halves[0], dq[0], dq[1]) * scale).astype(BF16)
        grad_qkv[1, :, columns] = (jnp.where(halves[0], dk[0], dk[1]) * scale).astype(BF16)
        grad_qkv[2, :, columns] = jnp.where(halves[0], dv[0], dv[1]).astype(BF16)

    unit_one, factor_one = normalize(jnp.concatenate([x_ref[...].astype(F32), zeros], 0))
    normed_one = (unit_one * gain_one_ref[...]).astype(BF16)
    core_pairs = cp // (2 * HEAD_DIM)
    for other in [*range(1, nh), 0]:
        core = (h + other) % nh
        for q in range(core_pairs):
            attend_back(core * core_pairs + q)
        for i in range(3):
            sums = tn(normed_one, grad_qkv[i, :, rows_at(core, cp)])
            if other:
                core_send[other - 1, i] = sums.astype(BF16)
                core_copy(i, other).start()
            else:
                half_sum(i, sums)
        if other == nh - 1:
            send_mix(2)
    for i in range(2):
        for k in range(1, nd):
            band_copy(k, i).start()

    grad_one = jnp.zeros((pad, width), F32)
    for i in range(3):
        grad_one = grad_one + nt(grad_qkv[i], w_full[i])
    grad_one = jnp.where(row_valid, grad_one, 0.0)
    grad_input, gain_one = norm_back(grad_one, unit_one, factor_one, gain_one_ref[...])
    grad_input_out[...] = (part_own[...] + grad_input)[0 : sz.rows].astype(BF16)

    small[...] = jnp.zeros_like(small)
    small[0:1, :] = gain_one
    small[1:2, :] = gain_two
    small[2:3, 0:128] = peak_at[0:1, :]
    peak_row = iota(small.shape, 0) == 2

    def join(a, b):
        return jnp.where(peak_row, jnp.maximum(a, b), a + b)

    small_copies = []
    for other in range(1, nh):
        device, n = (d, (h + other) % nh, z), 2 * (other - 1)
        small_copies += [
            remote(small, small_core.at[other - 1], sc_s.at[n], sc_r.at[n], device),
            remote(rt, rt_core.at[other - 1], sc_s.at[n + 1], sc_r.at[n + 1], device),
        ]
    for copy in small_copies:
        copy.start()
    for copy in small_copies:
        copy.wait()
    for other in range(1, nh):
        small[...] = join(small[...], small_core[other - 1])
        rt[...] = rt[...] + rt_core[other - 1]
    small_send[0] = small[...]
    small_copies = []
    for k in range(1, nd):
        to = (d + k) % nd
        small_copies += [
            remote(small_send.at[0], small_x.at[k - 1], sx_s.at[0], sx_r.at[0], (to, h, z)),
            remote(rt.at[:, rows_at(to, band)], rt_x.at[k - 1], sx_s.at[1], sx_r.at[1], (to, h, z)),
        ]
    for copy in small_copies:
        copy.start()
    for k in range(1, nd):
        band_copy(k, 2).start()
    send_mix(3)

    def line_piece(i, j):
        to = at.next_z(j)
        return remote(line_send.at[i, rows_at(to, rp), :], line_recv.at[j - 1, i], gl_s.at[i], gl_r.at[i], at.line(to))

    def end_band(i):
        drain(gx_s.at[i], gx_r.at[i], band_recv.at[:, i], band_recv.at[:, i])
        sums = w_half[i, rows_at(d, band), :]
        for k in range(1, nd):
            sums = sums + band_recv[k - 1, i].astype(F32)
        w_half[i, 0:band, :] = sums
        line_send[i] = sums.astype(BF16)
        for j in range(1, nz):
            line_piece(i, j).start()

    for i in (3, 0, 1):
        end_band(i)
    drain(sx_s.at[0], sx_r.at[0], small_x, small_x)
    drain(sx_s.at[1], sx_r.at[1], rt_x, rt_x)
    router_sum = rt[:, rows_at(d, band)]
    for k in range(1, nd):
        small[...] = join(small[...], small_x[k - 1])
        router_sum = router_sum + rt_x[k - 1]
    rt_z[nz - 1] = router_sum
    small_send[1] = small[...]
    for j in range(1, nz):
        device = at.line(at.next_z(j))
        remote(small_send.at[1], small_z.at[j - 1], gl_s.at[4], gl_r.at[4], device).start()
        remote(rt_z.at[nz - 1], rt_z.at[j - 1], gl_s.at[5], gl_r.at[5], device).start()
    end_band(2)

    mix = gathered(mix_own, *mix_flow)
    output_out[...] = (hidden_at[...] + mix)[0 : sz.rows].astype(BF16)

    for i in range(4):
        drain(gl_s.at[i], gl_r.at[i], line_recv.at[:, i], line_recv.at[:, i])
    for n, landed in ((4, small_z), (5, rt_z.at[pl.ds(0, nz - 1)])):
        drain(gl_s.at[n], gl_r.at[n], landed, landed)
    totals = small[...]
    router_sum = rt_z[nz - 1]
    for j in range(1, nz):
        totals = join(totals, small_z[j - 1])
        router_sum = router_sum + rt_z[j - 1]
    gain_one_out[...] = totals[0:1]
    gain_two_out[...] = totals[1:2]
    rr = sz.router_rows
    own_router = router_sum[:, 0:rr]
    for i in range(1, nh):
        own_router = jnp.where(h == i, router_sum[:, i * rr : (i + 1) * rr], own_router)
    router_out[...] = own_router
    tau = tau_ref[...]
    factor = jnp.sqrt(tau / jnp.maximum(totals[2:3, 0:HEADS], tau))
    column = iota((1, cp), 1) // HEAD_DIM + h * (cp // HEAD_DIM)
    scale_row = jnp.zeros((1, cp), F32)
    for head in range(HEADS):
        scale_row = jnp.where(column == head, factor[:, head : head + 1], scale_row)
    for i in range(2):
        clipped_out[i] = (w_qkv_ref[i].astype(F32) * scale_row).astype(BF16)
    for i in range(4):
        sums = w_half[i, rows_at(z, rp), :]
        for j in range(1, nz):
            sums = sums + line_recv[j - 1, i].astype(F32)
        if i < 3:
            qkv_out[i] = sums
        else:
            out_out[...] = sums


def finish_kernel(sz, *refs):
    sources, results = refs[0:10], refs[10:20]
    full_out, out_sems, small_out = refs[20:]
    small_stores = [pltpu.make_async_copy(sources[n], results[n], small_out.at[n]) for n in range(8)]
    for copy in small_stores:
        copy.start()
    stores = []
    for e in range(sz.own):
        for i in range(2):
            full_out[i, e] = sources[8 + i][e].astype(F32)
            stores.append(pltpu.make_async_copy(full_out.at[i, e], results[8 + i].at[e], out_sems.at[i, e]))
            stores[-1].start()
    for copy in stores + small_stores:
        copy.wait()


def fast_body(
    sz, inputs, cotangent, routes, gain_attn, gain_expert, tau, w_qkv, w_out_attn, w_router, w_in, w_out
):
    ng, nz, nd, nh, pad, width, own = sz.groups, sz.nt, sz.nd, sz.nh, sz.pad, sz.width, sz.own
    rp, cp, band, parts, block = sz.row_piece, sz.col_piece, sz.band, sz.parts, sz.block
    many, hidden = ng * sz.cap, sz.hidden
    on_chip, anywhere = pl.BlockSpec(memory_space=pltpu.VMEM), pl.BlockSpec(memory_space=pltpu.HBM)

    def shape(dims, dtype):
        return jax.ShapeDtypeStruct(dims, dtype)

    def half(*dims):
        return pltpu.VMEM(dims, BF16)

    def full(*dims):
        return pltpu.VMEM(dims, F32)

    def pair(*dims):
        return [pltpu.SemaphoreType.DMA(dims)] * 2

    slot_buffer = half(ng, sz.group_slots, width)
    line_buffer = half(nz - 1, pad, width)
    quarter_dims = (ng, own * (sz.cap // nz), width // parts)
    quarter_buffer, few = half(*quarter_dims), ng * own * (sz.cap // nz)
    rr = sz.router_rows
    smalls = (
        shape(inputs.shape, BF16), shape(inputs.shape, BF16), shape((1, width), F32), shape((1, width), F32),
        shape((3, rp, cp), F32), shape((rp, cp), F32), shape((sz.experts, rr), F32), shape((2, rp, cp), BF16),
    )
    packed = pl.pallas_call(
        functools.partial(block_kernel, sz),
        out_shape=(*[pltpu.VMEM(x.shape, x.dtype) for x in smalls], half(*w_in.shape), half(*w_out.shape)),
        in_specs=[on_chip] * 9 + [anywhere] * 2,
        out_specs=(on_chip,) * 10,
        scratch_shapes=[
            half(4, rp, cp), half(4, width, width), half(sz.experts, 128), half(ng, sz.experts, 128),
            half(sz.experts, width), full(8, block), full(block, 128), half(sz.slots, block), half(block, sz.slots), half(few, block), half(block, few),
            half(block, width), half(block, width), *[slot_buffer] * 6,
            quarter_buffer, half(nz, *quarter_dims), half(nz, *quarter_dims), half(nz - 1, *quarter_dims), quarter_buffer,
            quarter_buffer,
            half(own, width, hidden), half(own, hidden, width), half(own, many, hidden), half(own, many, hidden),
            full(own, many, hidden),
            full(sz.experts, 128), full(ng, 8, 128), full(sz.experts, block), full(8, many),
            full(ng, 8, 128), full(sz.experts, 128),
            half(3, pad, width), half(HEADS, pad, pad), half(pad, width), full(pad, width), full(8, 128),
            full(block, width), full(pad, width), line_buffer, half(nz, pad, width), full(pad, width), line_buffer,
            half(nz, pad, width),
            half(pad, width), half(3, pad, width), half(nh - 1, 4, width, cp), half(nh - 1, 4, width, cp),
            full(4, width, cp), half(4, width, cp), half(nd - 1, 4, band, cp), half(4, band, cp),
            half(nz - 1, 4, rp, cp),
            full(8, width), full(2, 8, width), full(nh - 1, 8, width), full(nd - 1, 8, width), full(nz - 1, 8, width),
            full(sz.experts, width), full(nh - 1, sz.experts, width), full(nd - 1, sz.experts, band),
            full(nz, sz.experts, band),
            *pair(4), *pair(4), *pair(4 * (nh - 1)), *pair(1), *pair(parts), *pair(parts), *pair(parts), *pair(parts),
            *pair(1), *pair(own), *pair(parts), *pair(parts), *pair(1), *pair(parts), *pair(parts), *pair(4 * (nh - 1)),
            *pair(4), *pair(6), *pair(2 * (nh - 1)), *pair(2), *pair(1), *pair(1), *pair(1), *pair(1),
            *pair(parts), *pair(parts, 2),
            pltpu.SemaphoreType.DMA((2,)),
        ],
        compiler_params=pltpu.CompilerParams(collective_id=0, has_side_effects=True, vmem_limit_bytes=57 * 2**20),
        name="block",
    )(
        inputs, cotangent, routes.T, gain_attn[None, :], gain_expert[None, :], w_qkv, w_out_attn.T, w_router.T,
        tau[None, :], w_in, w_out,
    )

    both, dma = (2, *w_in.shape), pltpu.SemaphoreType.DMA
    output, grad_input, gain_one, gain_two, grad_qkv, grad_out, grad_router, clipped, grad_first, grad_second = (
        pl.pallas_call(
            functools.partial(finish_kernel, sz),
            out_shape=(*smalls, shape(w_in.shape, F32), shape(w_out.shape, F32)),
            in_specs=[on_chip] * 10,
            out_specs=(anywhere,) * 10,
            scratch_shapes=[full(*both), dma((2, own)), dma((8,))],
            compiler_params=pltpu.CompilerParams(vmem_limit_bytes=48 * 2**20),
            name="finish",
        )(*[pltpu.with_memory_space_constraint(x, pltpu.VMEM) for x in packed])
    )
    return (
        output, grad_input, gain_one[0], gain_two[0], grad_qkv, grad_out.T, grad_router.T, grad_first, grad_second,
        clipped,
    )


def gelu_tanh(inputs):
    return (
        0.5
        * inputs
        * (1.0 + jnp.tanh(0.7978845608028654 * (inputs + 0.044715 * inputs * inputs * inputs)))
    )


def unit_and_factor(inputs):
    centered = inputs - jnp.mean(inputs, -1, keepdims=True)
    factor = lax.rsqrt(jnp.mean(centered * centered, -1, keepdims=True) + 1e-06)
    return (centered * factor, factor)


def general_norm_back(grad_norm, unit_rows, factor, gain):
    grad, gain_row = norm_back(grad_norm, unit_rows, factor, gain)
    return grad, gain_row[0]


def attn_forward(block_parts):
    queries, key_rows, value_rows = block_parts
    scores = jnp.einsum(
        "bhqd,bhkd->bhqk", queries, key_rows, preferred_element_type=jnp.float32
    ) * HEAD_DIM ** (-0.5)
    row_peak = jnp.max(scores, -1, keepdims=True)
    exponent = jnp.exp(scores - row_peak)
    summed = jnp.sum(exponent, -1, keepdims=True)
    soft_weights = (exponent / summed).astype(jnp.bfloat16)
    mixed = jnp.einsum(
        "bhqk,bhkd->bhqd", soft_weights, value_rows, preferred_element_type=jnp.float32
    ).astype(jnp.bfloat16)
    return (mixed, (row_peak + jnp.log(summed))[..., 0], jnp.max(row_peak, axis=(0, 2, 3)))


def attn_backward(block_parts):
    queries, key_rows, value_rows, grad_mixed, log_total = block_parts
    score_scale = HEAD_DIM ** (-0.5)
    scores = (
        jnp.einsum("bhqd,bhkd->bhqk", queries, key_rows, preferred_element_type=jnp.float32)
        * score_scale
    )
    soft_weights = jnp.exp(scores - log_total[..., None])
    grad_soft = jnp.einsum(
        "bhqd,bhkd->bhqk", grad_mixed, value_rows, preferred_element_type=jnp.float32
    )
    inner_sum = jnp.sum(soft_weights * grad_soft, -1, keepdims=True)
    grad_scores = (soft_weights * (grad_soft - inner_sum)).astype(jnp.bfloat16)
    grad_query = (
        jnp.einsum("bhqk,bhkd->bhqd", grad_scores, key_rows, preferred_element_type=jnp.float32)
        * score_scale
    ).astype(jnp.bfloat16)
    grad_key = (
        jnp.einsum("bhqk,bhqd->bhkd", grad_scores, queries, preferred_element_type=jnp.float32)
        * score_scale
    ).astype(jnp.bfloat16)
    grad_value = jnp.einsum(
        "bhqk,bhqd->bhkd",
        soft_weights.astype(jnp.bfloat16),
        grad_mixed,
        preferred_element_type=jnp.float32,
    ).astype(jnp.bfloat16)
    return (grad_query, grad_key, grad_value)


def general_body(
    inputs, cotangent, routes, gain_attn, gain_expert, tau, w_qkv, w_out_attn, w_router, w_in, w_out
):
    row_count, width = inputs.shape
    n_dp = lax.axis_size("dp")
    n_heads = lax.axis_size("heads")
    n_tensor = lax.axis_size("tensor")
    row_piece = w_qkv.shape[1]
    col_piece = w_qkv.shape[2]
    own_heads = col_piece // HEAD_DIM
    head_start = lax.axis_index("heads") * col_piece
    x_float = inputs.astype(jnp.float32)
    unit_one, factor_one = unit_and_factor(x_float)
    normed_one = (unit_one * gain_attn).astype(jnp.bfloat16)
    stack_qkv, stack_out = (
        lax.all_gather(w_qkv[None], ("dp", "heads", "tensor"), axis=0, tiled=True),
        lax.all_gather(w_out_attn[None], ("dp", "heads", "tensor"), axis=0, tiled=True),
    )
    full_qkv = (
        stack_qkv.reshape(n_dp, n_heads, n_tensor, 3, row_piece, col_piece)
        .transpose(3, 0, 2, 4, 1, 5)
        .reshape(3, width, width)
    )
    full_out = (
        stack_out.reshape(n_dp, n_heads, n_tensor, col_piece, row_piece)
        .transpose(1, 3, 0, 2, 4)
        .reshape(width, width)
    )
    proj_w = lax.dynamic_slice_in_dim(full_qkv, head_start, col_piece, 2)
    attn_w = lax.dynamic_slice_in_dim(full_out, head_start, col_piece, 0)
    normed_all = lax.all_gather(normed_one, "heads", axis=0, tiled=True)
    head_cols = attn_w.shape[0]
    local_heads = head_cols // HEAD_DIM
    joined_w = jnp.concatenate([proj_w[0], proj_w[1], proj_w[2]], 1)
    projected = jnp.dot(normed_all, joined_w, preferred_element_type=jnp.float32).astype(
        jnp.bfloat16
    )
    images = normed_all.shape[0] // SEQ
    per_block = 4 if images % 4 == 0 else 3 if images % 3 == 0 else 2 if images % 2 == 0 else 1
    block_shape = (images // per_block, per_block, SEQ, local_heads, HEAD_DIM)

    def to_blocks(row_matrix):
        return row_matrix.reshape(block_shape).transpose(0, 1, 3, 2, 4)

    def from_blocks(block_array):
        return block_array.transpose(0, 1, 3, 2, 4).reshape(-1, head_cols)

    queries = to_blocks(projected[:, :head_cols])
    key_rows = to_blocks(projected[:, head_cols : 2 * head_cols])
    value_rows = to_blocks(projected[:, 2 * head_cols :])
    mixed, log_total, head_peaks = lax.map(attn_forward, (queries, key_rows, value_rows))
    mixed_rows = from_blocks(mixed)
    block_peak = jnp.max(head_peaks, 0)
    attn_out = lax.psum_scatter(
        jnp.dot(mixed_rows, attn_w, preferred_element_type=jnp.float32),
        "heads",
        scatter_dimension=0,
        tiled=True,
    )
    peak_full = lax.dynamic_update_slice_in_dim(
        jnp.full((HEADS,), -1e30, jnp.float32), block_peak, lax.axis_index("heads") * local_heads, 0
    )
    hidden = x_float + attn_out
    peak_all = lax.pmax(peak_full, ("dp", "heads", "tensor"))
    peak_logit = lax.dynamic_slice_in_dim(
        peak_all, lax.axis_index("heads") * own_heads, own_heads, 0
    )
    unit_two, factor_two = unit_and_factor(hidden)
    normed_two = (unit_two * gain_expert).astype(jnp.bfloat16)
    group_rows, group_cot = (
        lax.all_gather(normed_two, "tensor", axis=0, tiled=True),
        lax.all_gather(cotangent, "tensor", axis=0, tiled=True),
    )
    first_w, second_w, router_w = (
        lax.all_gather(w_in, ("dp", "heads"), axis=0, tiled=True),
        lax.all_gather(w_out, ("dp", "heads"), axis=0, tiled=True),
        lax.all_gather(w_router, ("dp", "heads"), axis=0, tiled=True),
    )
    logits = jnp.dot(group_rows, router_w, preferred_element_type=jnp.float32)
    chosen = jnp.take_along_axis(logits, routes, 1)
    exponent = jnp.exp(chosen - jnp.max(chosen, -1, keepdims=True))
    gate_values = exponent / jnp.sum(exponent, -1, keepdims=True)
    group_count = routes.shape[0]
    experts = router_w.shape[1]
    capacity = (group_count * 5 // (16 * experts) + 1) * 8
    flat_ids = routes.reshape(-1)
    ordering = jnp.argsort(flat_ids, stable=True)
    sorted_ids = flat_ids[ordering]
    counts = jnp.sum(
        (flat_ids[:, None] == jnp.arange(experts, dtype=jnp.int32)[None, :]).astype(jnp.int32), 0
    )
    expert_ids = jnp.arange(experts, dtype=jnp.int32)
    starts = jnp.sum(jnp.where(expert_ids[None, :] < expert_ids[:, None], counts[None, :], 0), 1)
    slot_rank = jnp.arange(2 * group_count, dtype=jnp.int32) - starts[sorted_ids]
    slot_table = (
        jnp.full((experts * capacity,), 2 * group_count, jnp.int32)
        .at[sorted_ids * capacity + slot_rank]
        .set(ordering)
    )
    slot_token = slot_table // 2
    padded_rows = jnp.concatenate([group_rows, jnp.zeros((1, width), jnp.bfloat16)], 0)
    slot_in = padded_rows[slot_token].reshape(experts, capacity, width)
    slot_gate = jnp.concatenate([gate_values.reshape(-1), jnp.zeros((1,), jnp.float32)], 0)[
        slot_table
    ]
    pre_gelu = jnp.einsum("ecd,edf->ecf", slot_in, first_w, preferred_element_type=jnp.float32)
    activated = gelu_tanh(pre_gelu).astype(jnp.bfloat16)
    slot_out = jnp.einsum(
        "ecf,efd->ecd", activated, second_w, preferred_element_type=jnp.float32
    ).reshape(-1, width)
    partial_value = (
        jnp.zeros((group_count + 1, width), jnp.float32)
        .at[slot_token]
        .add(slot_gate[:, None] * slot_out)[:group_count]
    )
    expert_mix = lax.psum_scatter(
        partial_value.astype(jnp.bfloat16), "tensor", scatter_dimension=0, tiled=True
    ).astype(jnp.float32)
    output = (hidden + expert_mix).astype(jnp.bfloat16)
    padded_cot = jnp.concatenate([group_cot, jnp.zeros((1, width), jnp.bfloat16)], 0)
    slot_cot = padded_cot[slot_token].astype(jnp.float32)
    grad_slot_out = (
        (slot_gate[:, None] * slot_cot).astype(jnp.bfloat16).reshape(experts, capacity, width)
    )
    gate_part = (
        jnp.zeros((2 * group_count + 1,), jnp.float32)
        .at[slot_table]
        .add(jnp.sum(slot_cot * slot_out, -1))[: 2 * group_count]
        .reshape(group_count, 2)
    )
    grad_act = jnp.einsum(
        "ecd,efd->ecf", grad_slot_out, second_w, preferred_element_type=jnp.float32
    )
    grad_pre = jax.vjp(gelu_tanh, pre_gelu)[1](grad_act)[0].astype(jnp.bfloat16)
    grad_first = jnp.einsum("ecd,ecf->edf", slot_in, grad_pre, preferred_element_type=jnp.float32)
    grad_second = jnp.einsum(
        "ecf,ecd->efd", activated, grad_slot_out, preferred_element_type=jnp.float32
    )
    grad_slots = jnp.einsum(
        "ecf,edf->ecd", grad_pre, first_w, preferred_element_type=jnp.float32
    ).reshape(-1, width)
    grad_part = (
        jnp.zeros((group_count + 1, width), jnp.float32)
        .at[slot_token]
        .add(grad_slots)[:group_count]
    )
    grad_normed_two, grad_gates = (
        lax.psum_scatter(
            grad_part.astype(jnp.bfloat16), "tensor", scatter_dimension=0, tiled=True
        ).astype(jnp.float32),
        lax.psum_scatter(
            gate_part.astype(jnp.bfloat16), "tensor", scatter_dimension=0, tiled=True
        ).astype(jnp.float32),
    )
    shard_first, shard_second = (
        lax.psum_scatter(
            grad_first.astype(jnp.bfloat16), ("dp", "heads"), scatter_dimension=0, tiled=True
        ).astype(jnp.float32),
        lax.psum_scatter(
            grad_second.astype(jnp.bfloat16), ("dp", "heads"), scatter_dimension=0, tiled=True
        ).astype(jnp.float32),
    )
    offset = lax.axis_index("tensor") * row_count
    local_gates = lax.dynamic_slice_in_dim(gate_values, offset, row_count, 0)
    local_routes = lax.dynamic_slice_in_dim(routes, offset, row_count, 0)
    grad_chosen = local_gates * (grad_gates - jnp.sum(local_gates * grad_gates, -1, keepdims=True))
    columns = jnp.arange(experts, dtype=jnp.int32)[None, :]
    grad_logits = (
        jnp.where(local_routes[:, 0:1] == columns, grad_chosen[:, 0:1], 0.0)
        + jnp.where(local_routes[:, 1:2] == columns, grad_chosen[:, 1:2], 0.0)
    ).astype(jnp.bfloat16)
    grad_normed_two = grad_normed_two + jnp.einsum(
        "re,de->rd", grad_logits, router_w, preferred_element_type=jnp.float32
    )
    router_term = jnp.einsum(
        "rd,re->de", normed_two, grad_logits, preferred_element_type=jnp.float32
    )
    grad_hidden_norm, gain_two_term = general_norm_back(grad_normed_two, unit_two, factor_two, gain_expert)
    grad_hidden = cotangent.astype(jnp.float32) + grad_hidden_norm
    grad_attn = lax.all_gather(grad_hidden.astype(jnp.bfloat16), "heads", axis=0, tiled=True)
    grad_mixed = jnp.einsum(
        "rd,cd->rc", grad_attn, attn_w, preferred_element_type=jnp.float32
    ).astype(jnp.bfloat16)
    out_term = jnp.einsum("rc,rd->cd", mixed_rows, grad_attn, preferred_element_type=jnp.float32)
    grad_query, grad_key, grad_value = lax.map(
        attn_backward, (queries, key_rows, value_rows, to_blocks(grad_mixed), log_total)
    )
    grad_proj = jnp.concatenate(
        [from_blocks(grad_query), from_blocks(grad_key), from_blocks(grad_value)], 1
    )
    grad_normed_one = lax.psum_scatter(
        jnp.einsum("rc,dc->rd", grad_proj, joined_w, preferred_element_type=jnp.float32).astype(
            jnp.bfloat16
        ),
        "heads",
        scatter_dimension=0,
        tiled=True,
    ).astype(jnp.float32)
    proj_term = jnp.einsum("rd,rc->dc", normed_all, grad_proj, preferred_element_type=jnp.float32)
    proj_stack = jnp.stack(
        [
            proj_term[:, :head_cols],
            proj_term[:, head_cols : 2 * head_cols],
            proj_term[:, 2 * head_cols :],
        ],
        0,
    )
    whole_proj = lax.dynamic_update_slice_in_dim(
        jnp.zeros((3, width, width), jnp.float32), proj_stack, head_start, 2
    )
    whole_out = lax.dynamic_update_slice_in_dim(
        jnp.zeros((width, width), jnp.float32), out_term, head_start, 0
    )
    send_qkv = (
        whole_proj.reshape(3, n_dp, n_tensor, row_piece, n_heads, col_piece)
        .transpose(1, 4, 2, 0, 3, 5)
        .reshape(-1, 3, row_piece, col_piece)
    )
    send_out = (
        whole_out.reshape(n_heads, col_piece, n_dp, n_tensor, row_piece)
        .transpose(2, 0, 3, 1, 4)
        .reshape(-1, col_piece, row_piece)
    )
    shard_proj, shard_attn = (
        lax.psum_scatter(send_qkv, ("dp", "heads", "tensor"), scatter_dimension=0, tiled=True),
        lax.psum_scatter(send_out, ("dp", "heads", "tensor"), scatter_dimension=0, tiled=True),
    )
    grad_input_norm, gain_one_term = general_norm_back(grad_normed_one, unit_one, factor_one, gain_attn)
    grad_input = (grad_hidden + grad_input_norm).astype(jnp.bfloat16)
    gain_one_grad, gain_two_grad, router_all = lax.psum(
        (gain_one_term, gain_two_term, router_term), ("dp", "heads", "tensor")
    )
    router_grad = lax.dynamic_slice_in_dim(
        router_all, lax.axis_index(("dp", "heads")) * w_router.shape[0], w_router.shape[0], 0
    )
    local_tau = lax.dynamic_slice_in_dim(tau, lax.axis_index("heads") * own_heads, own_heads, 0)
    clip_factor = jnp.sqrt(local_tau / jnp.maximum(peak_logit, local_tau))
    clipped = (w_qkv[:2].astype(jnp.float32) * jnp.repeat(clip_factor, HEAD_DIM)).astype(
        jnp.bfloat16
    )
    return (
        output,
        grad_input,
        gain_one_grad,
        gain_two_grad,
        shard_proj[0],
        shard_attn[0],
        router_grad,
        shard_first,
        shard_second,
        clipped,
    )


def body(*args):
    inputs, _, routes, _, _, _, w_qkv, _, w_router, w_in, _ = args
    sz = Sizes(
        lax.axis_size("dp"), lax.axis_size("heads"), lax.axis_size("tensor"), inputs, routes, w_qkv, w_router, w_in
    )
    if sz.fits():
        return fast_body(sz, *args)
    return general_body(*args)


def solution(mesh):
    return jax.shard_map(
        body,
        mesh=mesh,
        in_specs=(
            P(("dp", "heads", "tensor"), None),
            P(("dp", "heads", "tensor"), None),
            P(("dp", "heads"), None),
            P(),
            P(),
            P(),
            P(None, ("dp", "tensor"), "heads"),
            P("heads", ("dp", "tensor")),
            P(("dp", "heads"), None),
            P(("dp", "heads"), None, "tensor"),
            P(("dp", "heads"), "tensor", None),
        ),
        out_specs=(
            P(("dp", "heads", "tensor"), None),
            P(("dp", "heads", "tensor"), None),
            P(),
            P(),
            P(None, ("dp", "tensor"), "heads"),
            P("heads", ("dp", "tensor")),
            P(("dp", "heads"), None),
            P(("dp", "heads"), None, "tensor"),
            P(("dp", "heads"), "tensor", None),
            P(None, ("dp", "tensor"), "heads"),
        ),
        check_vma=False,
    )
```

```python
import functools
import jax
import jax.numpy as jnp
from jax import lax
from jax.experimental import pallas as pl
from jax.experimental.pallas import tpu as pltpu
from jax.sharding import PartitionSpec as P

HEADS = 8
HEAD_DIM = 64
SEQ = 197
F32 = jnp.float32
BF16 = jnp.bfloat16
MESH = pl.DeviceIdType.MESH
NEG = -1e30


class Sizes:
    def __init__(self, n_dp, n_heads, n_tensor, inputs, routes, w_qkv, w_router, w_in):
        self.nd, self.nh, self.nt = n_dp, n_heads, n_tensor
        self.groups = n_dp * n_heads
        self.rows, self.width = inputs.shape
        self.pad = -(-self.rows // 16) * 16
        self.block = self.pad * n_tensor
        self.block_rows = routes.shape[0]
        self.own = w_in.shape[0]
        self.hidden = w_in.shape[2]
        self.experts = self.own * self.groups
        self.cap = (self.block_rows * 5 // (16 * self.experts) + 1) * 8
        self.group_slots = self.own * self.cap
        self.slots = self.experts * self.cap
        self.row_piece, self.col_piece = w_qkv.shape[1], w_qkv.shape[2]
        self.band = self.row_piece * n_tensor
        self.router_rows = w_router.shape[0]
        self.parts = 4

    def fits(self):
        return (
            self.rows == SEQ
            and self.nt == 4
            and self.parts == 4
            and self.block_rows == self.rows * self.nt
            and self.cap == 64
            and self.experts == 32
            and self.group_slots % 128 == 0
            and self.col_piece % 128 == 0
            and self.row_piece % 16 == 0
            and self.router_rows % 16 == 0
            and self.own * self.groups * 4 == 128
            and self.width == HEADS * HEAD_DIM
            and self.block * self.width * 2 <= 2**20
            and self.own * self.width <= self.slots
            and self.hidden <= self.block
            and self.hidden == self.width
            and self.cap % (16 * self.nt) == 0
            and self.width // self.parts % 128 == 0
        )


def nn(a, b):
    return jnp.dot(a, b, preferred_element_type=F32)


def nt(a, b):
    return lax.dot_general(a, b, (((1,), (1,)), ((), ())), preferred_element_type=F32)


def tn(a, b):
    return lax.dot_general(a, b, (((0,), (0,)), ((), ())), preferred_element_type=F32)


def iota(shape, axis):
    return lax.broadcasted_iota(jnp.int32, shape, axis)


def normalize(rows):
    centered = rows - jnp.mean(rows, -1, keepdims=True)
    factor = lax.rsqrt(jnp.mean(centered * centered, -1, keepdims=True) + 1e-06)
    return centered * factor, factor


def norm_back(grad_norm, unit_rows, factor, gain):
    grad_hat = grad_norm * gain
    inner = (
        grad_hat
        - jnp.mean(grad_hat, -1, keepdims=True)
        - unit_rows * jnp.mean(grad_hat * unit_rows, -1, keepdims=True)
    )
    return factor * inner, jnp.sum(grad_norm * unit_rows, 0, keepdims=True)


def split_high_low(values):
    high = values.astype(BF16)
    low = (values - high.astype(F32)).astype(BF16)
    return jnp.concatenate([high, low], 0)


class Place:
    def __init__(self, sz):
        self.sz = sz
        self.d = lax.axis_index("dp")
        self.h = lax.axis_index("heads")
        self.z = lax.axis_index("tensor")
        self.group = self.d * sz.nh + self.h

    def plane(self, group):
        return (group // self.sz.nh, group % self.sz.nh, self.z)

    def line(self, z):
        return (self.d, self.h, z)

    def next_group(self, k):
        return (self.group + k) % self.sz.groups

    def next_z(self, j):
        return (self.z + j) % self.sz.nt

    def inner(self):
        return (self.z + 1) % 4 // 2

    def mates(self):
        return self.z + 1 - 2 * (self.z % 2), (self.z + 2) % 4, 3 - self.z

    def enter(self):
        sz = self.sz
        barrier = pltpu.get_barrier_semaphore()
        for k in range(1, sz.groups):
            pl.semaphore_signal(barrier, inc=1, device_id=self.plane(self.next_group(k)), device_id_type=MESH)
        for j in range(1, sz.nt):
            pl.semaphore_signal(barrier, inc=1, device_id=self.line(self.next_z(j)), device_id_type=MESH)
        pl.semaphore_wait(barrier, sz.groups + sz.nt - 2)


def remote(src, dst, send, recv, device):
    return pltpu.make_async_remote_copy(
        src_ref=src, dst_ref=dst, send_sem=send, recv_sem=recv, device_id=device, device_id_type=MESH
    )


def drain(send_sem, recv_sem, sent, landed):
    pltpu.make_async_copy(sent, sent, send_sem).wait()
    pltpu.make_async_copy(landed, landed, recv_sem).wait()


def route_table(sz, routes_ref, table):
    table[...] = jnp.full_like(table, -1.0)
    for z in range(sz.nt):
        table[0:2, z * sz.pad : z * sz.pad + sz.rows] = routes_ref[:, z * sz.rows : (z + 1) * sz.rows].astype(F32)


def block_kernel(
    sz, x_ref, cot_ref, routes_ref, gain_one_ref, gain_two_ref, w_qkv_ref, w_out_ref, w_router_ref, tau_ref, first_hbm,
    second_hbm, output_out, grad_input_out, gain_one_out, gain_two_out, qkv_out, out_out, router_out, clipped_out,
    grad_first_out, grad_second_out,
    w_own, w_full, router_own, router_full, router_t, route_rows, route_columns, select, select_t, select_q, select_qt,
    cot_block, rows_block, send_a, send_b, cot_slots, slots, grad_slots, values,
    rows_q, rows_line, grads_q, grads_line, grads_sum, grads_back, first, second, act, grad_pre, grad_act,
    gate_send, gate_recv, gates_at, dgate_send, dgate_recv, dgate_rows,
    qkv, probs, mixed, hidden_at, peak_at, part, part_own, part_send, part_recv, mix_own, mix_send, mix_recv,
    grad_mixed, grad_qkv, core_send, core_recv, w_half, band_send, band_recv, line_send, line_recv,
    small, small_send, small_core, small_x, small_z, rt, rt_core, rt_x, rt_z,
    wz_s, wz_r, wx_s, wx_r, wc_s, wc_r, r_s, r_r, qz_s, qz_r, nz_s, nz_r, qa_s, qa_r, na_s, na_r, ga_s, ga_r,
    d0_s, d0_r, da_s, da_r, va_s, va_r, dg_s, dg_r, pz_s, pz_r, mz_s, mz_r, gc_s, gc_r, gx_s, gx_r, gl_s, gl_r,
    sc_s, sc_r, sx_s, sx_r, dl_s, dl_r, dq_s, dq_r, nq_s, nq_r, nl_s, nl_r, nb_s, nb_r, pr_r, mr_r,
    local_sem,
):
    at = Place(sz)
    d, h, z, me = at.d, at.h, at.z, at.group
    nd, nh, nz, ng = sz.nd, sz.nh, sz.nt, sz.groups
    band, rp, cp, pad, width = sz.band, sz.row_piece, sz.col_piece, sz.pad, sz.width
    many = ng * sz.cap
    parts, part_width = sz.parts, width // sz.parts

    def lanes(c):
        return pl.ds(c * part_width, part_width)

    def rows_at(n, size):
        return pl.ds(pl.multiple_of(n * size, size), size)

    own_block, own_columns = rows_at(z, pad), rows_at(h, cp)
    inner = at.inner()
    beside, across, mirror = at.mates()

    w_own[0:3] = w_qkv_ref[...]
    w_own[3] = w_out_ref[...]
    router_own[...] = jnp.zeros_like(router_own)
    router_own[:, 0 : sz.router_rows] = w_router_ref[...]
    cot_block[own_block] = jnp.concatenate(
        [cot_ref[...].astype(F32), jnp.zeros((pad - sz.rows, width), F32)], 0
    ).astype(BF16)

    part_recv[2] = jnp.zeros((pad, width), BF16)
    mix_recv[2] = jnp.zeros((pad, width), BF16)

    at.enter()

    w_rows = rows_at(d * nz + z, rp)
    others = pl.ds(0, ng - 1)

    def send_line(i):
        for j in range(1, nz):
            remote(
                w_own.at[i], w_full.at[i, w_rows, own_columns], wz_s.at[i], wz_r.at[i], at.line(at.next_z(j))
            ).start()

    def along(block, send_sems, recv_sems, c):
        place = block.at[own_block, lanes(c)]
        return [
            remote(place, place, send_sems.at[c], recv_sems.at[c], at.line(at.next_z(j)))
            for j in range(1, nz)
        ]

    def wait_along(block, send_sems, recv_sems, c):
        place = block.at[pl.ds(0, (nz - 1) * pad), lanes(c)]
        drain(send_sems.at[c], recv_sems.at[c], place, place)

    for i in range(3):
        send_line(i)
    for copy in along(cot_block, qz_s, qz_r, 0):
        copy.start()
    send_line(3)
    routers = [
        remote(router_own, router_full.at[me], r_s.at[0], r_r.at[0], at.plane(at.next_group(k)))
        for k in range(1, ng)
    ]
    for copy in routers:
        copy.start()
    loads = [
        pltpu.make_async_copy(first_hbm, first, local_sem.at[0]),
        pltpu.make_async_copy(second_hbm, second, local_sem.at[1]),
    ]
    for copy in loads:
        copy.start()
    w_full[:, w_rows, own_columns] = w_own[...]
    router_full[me] = router_own[...]

    def to_core(i, dp, other):
        place = w_full.at[i, rows_at(dp, band), own_columns]
        n = 4 * (other - 1) + i
        return remote(place, place, wc_s.at[n], wc_r.at[n], (d, (h + other) % nh, z))

    def send_band(i):
        landed = w_full.at[i, pl.ds(0, (nz - 1) * rp), own_columns]
        drain(wz_s.at[i], wz_r.at[i], landed, landed)
        place = w_full.at[i, rows_at(d, band), own_columns]
        for k in range(1, nd):
            remote(place, place, wx_s.at[i], wx_r.at[i], ((d + k) % nd, h, z)).start()
        for other in range(1, nh):
            to_core(i, d, other).start()

    def pass_on(i):
        landed = w_full.at[i, pl.ds(0, (nd - 1) * band), own_columns]
        drain(wx_s.at[i], wx_r.at[i], landed, landed)
        for k in range(1, nd):
            for other in range(1, nh):
                to_core(i, (d + k) % nd, other).start()

    def arrived(i):
        for other in range(1, nh):
            n, columns = 4 * (other - 1) + i, w_full.at[i, :, own_columns]
            drain(wc_s.at[n], wc_r.at[n], columns, columns)

    zeros = jnp.zeros((pad - sz.rows, width), F32)
    x_rows = jnp.concatenate([x_ref[...].astype(F32), zeros], 0)
    unit_one, _ = normalize(x_rows)
    normed_one = (unit_one * gain_one_ref[...]).astype(BF16)
    for i in range(3):
        send_band(i)

    route_table(sz, routes_ref, route_rows)
    route_a, route_b = route_rows[0:1, :], route_rows[1:2, :]
    expert = iota((sz.experts, sz.block), 0).astype(F32)
    named_a, named_b = route_a == expert, route_b == expert
    named = jnp.logical_or(named_a, named_b)
    before = (iota((sz.block, sz.block), 0) < iota((sz.block, sz.block), 1)).astype(BF16)
    rank = nn(named.astype(BF16), before) + expert * float(sz.cap)
    slot_a = jnp.sum(jnp.where(named_a, rank, 0.0), 0, keepdims=True)
    slot_b = jnp.sum(jnp.where(named_b, rank, 0.0), 0, keepdims=True)
    slot_a = jnp.where(route_a < 0.0, -1.0, slot_a)
    slot_b = jnp.where(route_b < 0.0, -1.0, slot_b)
    slot_pair = jnp.concatenate([slot_a, slot_b] * 64, 0)
    route_columns[...] = slot_pair.T

    def fill(g, carry):
        slot = iota((sz.group_slots, sz.block), 0).astype(F32) + (g * sz.group_slots).astype(F32)
        hit = jnp.logical_or(slot == slot_a, slot == slot_b)
        select[rows_at(g, sz.group_slots), :] = jnp.where(hit, 1.0, 0.0).astype(BF16)
        return carry

    lax.fori_loop(0, ng, fill, 0)

    quarter = sz.cap // nz
    few = ng * sz.own * quarter

    def quarter_slot(dims, axis):
        n = iota(dims, axis)
        return (n // quarter * sz.cap + z * quarter + n % quarter).astype(F32)

    some_slot = quarter_slot((few, sz.block), 0)
    select_q[...] = jnp.where(jnp.logical_or(some_slot == slot_a, some_slot == slot_b), 1.0, 0.0).astype(BF16)

    def quarter_move(k, send, landing, send_sems, recv_sems):
        g = (me + k) % ng
        return remote(send.at[g], landing.at[me], send_sems.at[0], recv_sems.at[0], at.plane(g))

    def exchange(c, k, send, out, send_sems, recv_sems):
        g = (me + k) % ng
        return remote(
            send.at[g, :, lanes(c)], out.at[me, :, lanes(c)], send_sems.at[c], recv_sems.at[c], at.plane(g)
        )

    def dispatch(c, block, send, out, send_sems, recv_sems):
        def step(i, carry):
            k = ng - 1 - i
            g = (me + k) % ng
            send[g, :, lanes(c)] = nn(select[rows_at(g, sz.group_slots), :], block[:, lanes(c)]).astype(BF16)

            @pl.when(k > 0)
            def _():
                exchange(c, k, send, out, send_sems, recv_sems).start()

            return carry

        lax.fori_loop(0, ng, step, 0)
        out[me, :, lanes(c)] = send[me, :, lanes(c)]

    def start_part(c, *flow):
        def step(i, carry):
            exchange(c, ng - 1 - i, *flow).start()
            return carry

        lax.fori_loop(0, ng - 1, step, 0)

    def wait_part(c, send, out, send_sems, recv_sems):
        drain(send_sems.at[c], recv_sems.at[c], send.at[others, :, lanes(c)], out.at[others, :, lanes(c)])

    cot_flow = (send_a, cot_slots, qa_s, qa_r)
    row_flow = (send_b, slots, na_s, na_r)

    def send_cot(c):
        wait_along(cot_block, qz_s, qz_r, c)
        dispatch(c, cot_block, *cot_flow)

    send_band(3)
    for c in range(1, parts):
        for copy in along(cot_block, qz_s, qz_r, c):
            copy.start()
    send_cot(0)
    pass_on(0)
    pass_on(1)
    pass_on(2)

    for i in range(3):
        arrived(i)
        qkv[i] = nn(normed_one, w_full[i]).astype(BF16)
    pass_on(3)
    lane = iota((1, 2 * HEAD_DIM), 1)
    halves = (lane < HEAD_DIM, lane >= HEAD_DIM)
    key_valid = iota((1, pad), 1) < sz.rows
    row_valid = iota((pad, 1), 0) < sz.rows
    peak_lane = iota((1, 128), 1)
    peak_at[...] = jnp.full_like(peak_at, NEG)
    scale = HEAD_DIM ** (-0.5)

    def attend(pair, carry):
        columns = rows_at(pair, 2 * HEAD_DIM)
        q_pair, k_pair, v_pair = (qkv[i, :, columns] for i in range(3))
        sides = []
        for side in range(2):
            q_own = jnp.where(halves[side], q_pair, jnp.zeros_like(q_pair))
            scores = jnp.where(key_valid, nt(q_own, k_pair) * scale, NEG)
            row_peak = jnp.max(scores, -1, keepdims=True)
            exponent = jnp.exp(scores - row_peak)
            weights = (exponent / jnp.sum(exponent, -1, keepdims=True)).astype(BF16)
            head = pair * 2 + side
            probs[head] = weights
            sides.append(nn(weights, v_pair))
            peak = jnp.max(jnp.where(row_valid, row_peak, NEG), 0, keepdims=True)
            peak_at[0:1, :] = jnp.where(peak_lane == head, peak, peak_at[0:1, :])
        mixed[:, columns] = jnp.where(halves[0], sides[0], sides[1]).astype(BF16)
        return carry

    pairs = HEADS // 2
    lax.fori_loop(0, pairs // 2, attend, 0)
    send_cot(1)
    lax.fori_loop(pairs // 2, pairs, attend, 0)

    arrived(3)
    hidden = x_rows + nt(mixed[...], w_full[3])
    hidden_at[...] = hidden
    unit_two, _ = normalize(hidden)
    rows_block[own_block] = jnp.where(row_valid, unit_two * gain_two_ref[...], 0.0).astype(BF16)

    def row_copy(c, owner, to, recv_sems):
        place = rows_block.at[rows_at(owner, pad), lanes(c)]
        return remote(place, place, nz_s.at[c], recv_sems.at[c], at.line(to))

    for c in range(parts):
        row_copy(c, z, across, nb_r).start()
        row_copy(c, z, beside, nz_r).start()

        @pl.when(inner == 1)
        def _(c=c):
            row_copy(c, z, mirror, nz_r).start()

    def row_bytes(c, pieces):
        return rows_block.at[pl.ds(0, pieces * pad), lanes(c)]

    def wait_rows(c):
        pltpu.make_async_copy(row_bytes(c, 1), row_bytes(c, 1), nb_r.at[c]).wait()

        @pl.when(inner == 1)
        def _():
            row_copy(c, across, beside, nz_r).start()

        pltpu.make_async_copy(row_bytes(c, 2), row_bytes(c, 2), nz_r.at[c]).wait()

        @pl.when(inner == 1)
        def _():
            pltpu.make_async_copy(row_bytes(c, 4), row_bytes(c, 4), nz_s.at[c]).wait()

        @pl.when(inner == 0)
        def _():
            pltpu.make_async_copy(row_bytes(c, 2), row_bytes(c, 2), nz_s.at[c]).wait()

    for c in range(2, parts):
        send_cot(c)

    def fill_t(i, carry):
        rows = rows_at(i, pad)
        slot = iota((pad, sz.slots), 1).astype(F32)
        hit = jnp.logical_or(slot == route_columns[rows, 0:1], slot == route_columns[rows, 1:2])
        select_t[rows, :] = jnp.where(hit, 1.0, 0.0).astype(BF16)
        some = quarter_slot((pad, few), 1)
        hit = jnp.logical_or(some == route_columns[rows, 0:1], some == route_columns[rows, 1:2])
        select_qt[rows, :] = jnp.where(hit, 1.0, 0.0).astype(BF16)
        return carry

    lax.fori_loop(0, nz, fill_t, 0)
    drain(r_s.at[0], r_r.at[0], router_full.at[others], router_full.at[others])
    for g in range(ng):
        router_t[:, g * sz.router_rows : (g + 1) * sz.router_rows] = router_full[g, :, 0 : sz.router_rows]

    def expert_rows(ref, e):
        return ref[:, rows_at(e, sz.cap), :].reshape(many, width)

    def send_gates():
        logits = jnp.where(named, nt(router_t[...], rows_block[...]), NEG)
        exponent = jnp.where(named, jnp.exp(logits - jnp.max(logits, 0, keepdims=True)), 0.0)
        total = jnp.sum(exponent, 0, keepdims=True)
        gates = exponent / jnp.where(total > 0.0, total, 1.0)
        gates_at[...] = gates
        by_slot = nt(split_high_low(gates), select[...])
        by_slot = by_slot[0 : sz.experts] + by_slot[sz.experts :]
        own_slot = iota((sz.experts, sz.slots), 1) // sz.cap == iota((sz.experts, sz.slots), 0)
        by_slot = jnp.where(own_slot, by_slot, 0.0)
        folded = by_slot[:, 0:128]
        for i in range(1, sz.slots // 128):
            folded = folded + by_slot[:, i * 128 : (i + 1) * 128]
        gate_send[...] = folded
        gate_copies = [
            remote(
                gate_send.at[rows_at(at.next_group(k) * sz.own // 8, 8)], gate_recv.at[me], ga_s.at[0], ga_r.at[0],
                at.plane(at.next_group(k)),
            )
            for k in range(1, ng)
        ]
        for copy in gate_copies:
            copy.start()
        gate_recv[me] = gate_send[rows_at(me * sz.own // 8, 8)]

    for c in range(parts):
        wait_rows(c)
        if c == 0:
            rows_q[...] = nn(select_q[...], rows_block[:, lanes(0)]).astype(BF16).reshape(rows_q.shape)
            for k in range(1, ng):
                quarter_move(k, rows_q, rows_line.at[z], nq_s, nq_r).start()
            rows_line[z, me] = rows_q[me]
            continue
        if c == parts - 1:
            drain(nq_s.at[0], nq_r.at[0], rows_q.at[others], rows_q.at[others])
            for j in range(1, nz):
                remote(rows_line.at[z], rows_line.at[z], nl_s.at[0], nl_r.at[0], at.line(at.next_z(j))).start()
            send_gates()
        dispatch(c, rows_block, *row_flow)

    drain(ga_s.at[0], ga_r.at[0], gate_recv.at[others], gate_recv.at[others])
    def gate_of(e):
        turned = gate_recv[:, pl.ds(me * sz.own % 8 + e, 1), :].reshape(ng, 128).T
        columns = jnp.where((e % 2) == 1, turned[sz.cap : 2 * sz.cap], turned[0 : sz.cap])
        return jnp.concatenate([columns[:, s : s + 1] for s in range(ng)], 0)

    def weigh(e, carry):
        grad_act[e] = nt(expert_rows(cot_slots, e), second[e]) * gate_of(e)
        return carry

    for c in range(parts):
        wait_part(c, *cot_flow)
    for copy in loads:
        copy.wait()
    lax.fori_loop(0, sz.own, weigh, 0)
    lines = rows_line.at[pl.ds(0, nz - 1)]
    drain(nl_s.at[0], nl_r.at[0], lines, lines)
    for i in range(nz):
        for e in range(sz.own):
            slots[:, e * sz.cap + i * quarter : e * sz.cap + (i + 1) * quarter, lanes(0)] = rows_line[
                i, :, e * quarter : (e + 1) * quarter, :
            ]
    for c in range(1, parts):
        wait_part(c, *row_flow)

    def first_piece(e, g):
        piece = (rows_at(e, sz.cap), lanes(1))
        return remote(
            send_a.at[(g, *piece)], grad_slots.at[(me, *piece)], d0_s.at[e], d0_r.at[e], at.plane(g)
        )

    def grads_piece(e, j):
        piece = (slice(None), rows_at(e, quarter), slice(None))
        return remote(
            grads_q.at[(at.next_z(j), *piece)], grads_line.at[(j - 1, *piece)], dl_s.at[0], dl_r.at[0],
            at.line(at.next_z(j)),
        )

    def expert_back(e, carry):
        half_rows = many // 2
        for part_at in range(2):
            some = slice(part_at * half_rows, (part_at + 1) * half_rows)
            groups = slice(part_at * ng // 2, (part_at + 1) * ng // 2)
            pre = nn(slots[groups, rows_at(e, sz.cap), :].reshape(half_rows, width), first[e])
            const, cubic = 0.7978845608028654, 0.044715
            square = pre * pre
            half = 0.5 * jnp.tanh(pre * (const + const * cubic * square)) + 0.5
            hidden_units = pre * half
            act[e, some] = hidden_units.astype(BF16)
            through = grad_act[e, some]
            dgate = nt(jnp.ones((8, sz.hidden), BF16), (hidden_units * through).astype(BF16))
            dgate_send[:, some] = jnp.where(iota((8, half_rows), 0) == e, dgate, dgate_send[:, some])
            slope = half * (1.0 + (1.0 - half) * (pre * (2.0 * const + 6.0 * const * cubic * square)))
            grads = (through * slope).astype(BF16)
            grad_pre[e, some] = grads
            spread = nt(grads, first[e]).astype(BF16).reshape(ng // 2, sz.cap, width)
            send_a[groups, rows_at(e, sz.cap), :] = spread
            for i in range(nz):
                grads_q[i, groups, rows_at(e, quarter), :] = spread[:, i * quarter : (i + 1) * quarter, 0:part_width]

        def step(i, carry):
            first_piece(e, (me + ng - 1 - i) % ng).start()
            return carry

        lax.fori_loop(0, ng - 1, step, 0)
        for j in range(1, nz):
            grads_piece(e, j).start()
        return carry

    dgate_send[...] = jnp.zeros_like(dgate_send)
    lax.fori_loop(0, sz.own, expert_back, 0)
    dgates = [
        remote(
            dgate_send.at[:, rows_at(at.next_group(k) * sz.cap // 128, 128)], dgate_recv.at[me], dg_s.at[0],
            dg_r.at[0], at.plane(at.next_group(k)),
        )
        for k in range(1, ng)
    ]
    for copy in dgates:
        copy.start()
    dgate_recv[me] = dgate_send[:, rows_at(me * sz.cap // 128, 128)]
    grad_flow = (send_a, grad_slots, da_s, da_r)
    value_flow = (send_b, values, va_s, va_r)
    for c in range(2, parts):
        start_part(c, *grad_flow)
    grad_slots[me] = send_a[me]

    def expert_value(e, carry):
        value = nn(act[e], second[e])
        gated = (value * gate_of(e)).astype(BF16).reshape(ng, sz.cap, width)
        send_b[:, rows_at(e, sz.cap), :] = gated
        return carry

    lax.fori_loop(0, sz.own, expert_value, 0)
    values[me] = send_b[me]

    def quarter_total(own, line, sums):
        total = own[z].astype(F32)
        for j in range(1, nz):
            total = total + line[j - 1].astype(F32)
        sums[...] = total.astype(BF16)


    def weight_grads(e, carry):
        grad_value = (expert_rows(cot_slots, e).astype(F32) * gate_of(e)).astype(BF16)
        grad_second_out[e] = tn(act[e], grad_value).astype(BF16)
        grad_first_out[e] = tn(expert_rows(slots, e), grad_pre[e]).astype(BF16)
        return carry

    drain(dg_s.at[0], dg_r.at[0], dgate_recv.at[others], dgate_recv.at[others])
    mine = iota((8, 128), 1) // sz.cap == me * sz.cap % 128 // sz.cap
    for g in range(ng):
        folded = jnp.where(mine, dgate_recv[g], 0.0)
        folded = folded + pltpu.roll(folded, 64, 1)
        dgate_rows[g * sz.own : (g + 1) * sz.own, :] = folded[0 : sz.own]
    spread = jnp.concatenate([dgate_rows[...]] * (sz.slots // 128), 1)
    own_slot = iota((sz.experts, sz.slots), 1) // sz.cap == iota((sz.experts, sz.slots), 0)
    dgate = nt(split_high_low(jnp.where(own_slot, spread, 0.0)), select_t[...])
    dgate = dgate[0 : sz.experts] + dgate[sz.experts :]
    gates = gates_at[...]
    dlogits = (dgate - gates * jnp.sum(dgate, 0, keepdims=True)).astype(BF16)
    rt[...] = nn(dlogits, rows_block[...])
    part[...] = tn(dlogits, router_t[...])

    def line_copy(c, slot, send, recv, send_sems, recv_sems, relay_sems, last):
        if slot < 2:
            return remote(
                send.at[slot, :, lanes(c)], recv.at[slot, :, lanes(c)], send_sems.at[c], recv_sems.at[c],
                at.line((beside, across)[slot]),
            )
        by_way = 1 - inner if c != last else 0
        to = mirror + by_way * (beside - mirror)
        return remote(
            send.at[2, :, lanes(c)], recv.at[2 + by_way, :, lanes(c)], send_sems.at[c], relay_sems.at[c, by_way], at.line(to)
        )

    def scatter(c, source, base, own, *flow):
        if source is grads_back:
            places, flat = select_qt, source[...].reshape(few, part_width)
        else:
            places, flat = select_t, source[:, :, lanes(c)].reshape(sz.slots, part_width)
        for slot, target in ((2, mirror), (1, across), (0, beside), (None, z)):
            tokens = rows_at(target, pad)
            sums = nn(places[tokens, :], flat)
            if base is not None:
                sums = sums + base[tokens, lanes(c)]
            if slot is None:
                own[:, lanes(c)] = sums
                continue
            flow[0][slot, :, lanes(c)] = sums.astype(BF16)
            if slot == 1 and c != flow[-1]:

                @pl.when(inner == 0)
                def _():
                    line_copy(c, 1, *flow).start()
            else:
                line_copy(c, slot, *flow).start()

    def relay(c, send, recv, send_sems, recv_sems, relay_sems, last):
        @pl.when(inner == 1)
        def _():
            landed = recv.at[3, :, lanes(c)]
            pltpu.make_async_copy(landed, landed, relay_sems.at[c, 1]).wait()
            send[1, :, lanes(c)] = (send[1, :, lanes(c)].astype(F32) + recv[3, :, lanes(c)].astype(F32)).astype(BF16)
            line_copy(c, 1, send, recv, send_sems, recv_sems, relay_sems, last).start()

    def gathered(own, send, recv, send_sems, recv_sems, relay_sems, last):
        for c in range(parts):
            drain(send_sems.at[c], recv_sems.at[c], send.at[:, :, lanes(c)], recv.at[pl.ds(0, 2), :, lanes(c)])

            @pl.when(inner == 1 if c != last else True)
            def _(c=c):
                landed = recv.at[2, :, lanes(c)]
                pltpu.make_async_copy(landed, landed, relay_sems.at[c, 0]).wait()

        sums = own[...]
        for slot in range(3):
            sums = sums + recv[slot].astype(F32)
        return sums

    part_flow = (part_send, part_recv, pz_s, pz_r, pr_r, 0)
    mix_flow = (mix_send, mix_recv, mz_s, mz_r, mr_r, parts - 1)

    def wait_first(e, carry):
        piece = (others, rows_at(e, sz.cap), lanes(1))
        drain(d0_s.at[e], d0_r.at[e], send_a.at[piece], grad_slots.at[piece])
        return carry

    def exchange_quarters():
        drain(dl_s.at[0], dl_r.at[0], grads_line, grads_line)
        quarter_total(grads_q, grads_line, grads_sum)
        for copy in grads_moves:
            copy.start()
        for i in range(3):
            start_part(i, *value_flow)
        grads_back[me] = grads_sum[me]

    grads_moves = [quarter_move(k, grads_sum, grads_back, dq_s, dq_r) for k in range(1, ng)]
    order = [*range(1, parts), 0]
    exchange_quarters()
    done = 0
    for turn, c in enumerate(order):
        if c == 0:
            drain(dq_s.at[0], dq_r.at[0], grads_back.at[others], grads_back.at[others])
        elif c == 1:
            lax.fori_loop(0, sz.own, wait_first, 0)
        else:
            wait_part(c, *grad_flow)
        if c == parts - 1:
            for i in range(3, parts):
                start_part(i, *value_flow)
        scatter(c, grads_back if c == 0 else grad_slots, part, part_own, *part_flow)
        until = sz.own * (turn + 1) // parts
        lax.fori_loop(done, until, weight_grads, 0)
        done = until
        if turn > 0:
            relay(order[turn - 1], *part_flow)
    def send_mix(c):
        wait_part(c, *value_flow)
        scatter(c, values, None, mix_own, *mix_flow)
        if c:
            relay(c - 1, *mix_flow)

    send_mix(0)
    unit_two, factor_two = normalize(hidden_at[...])
    grad_normed = jnp.where(row_valid, gathered(part_own, *part_flow), 0.0)
    grad_hidden, gain_two = norm_back(grad_normed, unit_two, factor_two, gain_two_ref[...])
    grad_hidden = jnp.concatenate([cot_ref[...].astype(F32), zeros], 0) + jnp.where(row_valid, grad_hidden, 0.0)
    part_own[...] = grad_hidden
    grad_attn = grad_hidden.astype(BF16)

    def core_copy(i, other):
        n = 4 * (other - 1) + i
        return remote(
            core_send.at[other - 1, i], core_recv.at[other - 1, i], gc_s.at[n], gc_r.at[n], (d, (h + other) % nh, z)
        )

    def half_sum(i, sums):
        for other in range(1, nh):
            core_copy(i, other).wait()
            sums = sums + core_recv[other - 1, i].astype(F32)
        w_half[i] = sums
        band_send[i] = sums.astype(BF16)

    def band_copy(k, i):
        to = (d + k) % nd
        return remote(
            band_send.at[i, rows_at(to, band), :], band_recv.at[k - 1, i], gx_s.at[i], gx_r.at[i], (to, h, z)
        )

    for other in [*range(1, nh), 0]:
        sums = tn(grad_attn, mixed[:, rows_at((h + other) % nh, cp)])
        if other:
            core_send[other - 1, 3] = sums.astype(BF16)
            core_copy(3, other).start()
        else:
            w_half[3] = sums
    grad_mixed[...] = nn(grad_attn, w_full[3]).astype(BF16)
    half_sum(3, w_half[3])
    for k in range(1, nd):
        band_copy(k, 3).start()


    send_mix(1)

    def attend_back(pair):
        columns = rows_at(pair, 2 * HEAD_DIM)
        q_pair, k_pair, v_pair = (qkv[i, :, columns] for i in range(3))
        g_pair = grad_mixed[:, columns]
        dq, dk, dv = [], [], []
        for side in range(2):
            weights = probs[pair * 2 + side]
            soft = weights.astype(F32)
            g_own = jnp.where(halves[side], g_pair, jnp.zeros_like(g_pair))
            grad_soft = nt(g_own, v_pair)
            inner = jnp.sum(soft * grad_soft, -1, keepdims=True)
            grad_scores = (soft * (grad_soft - inner)).astype(BF16)
            dq.append(nn(grad_scores, k_pair))
            dk.append(tn(grad_scores, q_pair))
            dv.append(tn(weights, g_pair))
        grad_qkv[0, :, columns] = (jnp.where(halves[0], dq[0], dq[1]) * scale).astype(BF16)
        grad_qkv[1, :, columns] = (jnp.where(halves[0], dk[0], dk[1]) * scale).astype(BF16)
        grad_qkv[2, :, columns] = jnp.where(halves[0], dv[0], dv[1]).astype(BF16)

    unit_one, factor_one = normalize(jnp.concatenate([x_ref[...].astype(F32), zeros], 0))
    normed_one = (unit_one * gain_one_ref[...]).astype(BF16)
    core_pairs = cp // (2 * HEAD_DIM)
    for other in [*range(1, nh), 0]:
        core = (h + other) % nh
        for q in range(core_pairs):
            attend_back(core * core_pairs + q)
        for i in range(3):
            sums = tn(normed_one, grad_qkv[i, :, rows_at(core, cp)])
            if other:
                core_send[other - 1, i] = sums.astype(BF16)
                core_copy(i, other).start()
            else:
                half_sum(i, sums)
        if other == nh - 1:
            send_mix(2)
    for i in range(2):
        for k in range(1, nd):
            band_copy(k, i).start()

    grad_one = jnp.zeros((pad, width), F32)
    for i in range(3):
        grad_one = grad_one + nt(grad_qkv[i], w_full[i])
    grad_one = jnp.where(row_valid, grad_one, 0.0)
    grad_input, gain_one = norm_back(grad_one, unit_one, factor_one, gain_one_ref[...])
    grad_input_out[...] = (part_own[...] + grad_input)[0 : sz.rows].astype(BF16)

    small[...] = jnp.zeros_like(small)
    small[0:1, :] = gain_one
    small[1:2, :] = gain_two
    small[2:3, 0:128] = peak_at[0:1, :]
    peak_row = iota(small.shape, 0) == 2

    def join(a, b):
        return jnp.where(peak_row, jnp.maximum(a, b), a + b)

    small_copies = []
    for other in range(1, nh):
        device, n = (d, (h + other) % nh, z), 2 * (other - 1)
        small_copies += [
            remote(small, small_core.at[other - 1], sc_s.at[n], sc_r.at[n], device),
            remote(rt, rt_core.at[other - 1], sc_s.at[n + 1], sc_r.at[n + 1], device),
        ]
    for copy in small_copies:
        copy.start()
    for copy in small_copies:
        copy.wait()
    for other in range(1, nh):
        small[...] = join(small[...], small_core[other - 1])
        rt[...] = rt[...] + rt_core[other - 1]
    small_send[0] = small[...]
    small_copies = []
    for k in range(1, nd):
        to = (d + k) % nd
        small_copies += [
            remote(small_send.at[0], small_x.at[k - 1], sx_s.at[0], sx_r.at[0], (to, h, z)),
            remote(rt.at[:, rows_at(to, band)], rt_x.at[k - 1], sx_s.at[1], sx_r.at[1], (to, h, z)),
        ]
    for copy in small_copies:
        copy.start()
    for k in range(1, nd):
        band_copy(k, 2).start()
    send_mix(3)

    def line_piece(i, j):
        to = at.next_z(j)
        return remote(line_send.at[i, rows_at(to, rp), :], line_recv.at[j - 1, i], gl_s.at[i], gl_r.at[i], at.line(to))

    def end_band(i):
        drain(gx_s.at[i], gx_r.at[i], band_recv.at[:, i], band_recv.at[:, i])
        sums = w_half[i, rows_at(d, band), :]
        for k in range(1, nd):
            sums = sums + band_recv[k - 1, i].astype(F32)
        w_half[i, 0:band, :] = sums
        line_send[i] = sums.astype(BF16)
        for j in range(1, nz):
            line_piece(i, j).start()

    for i in (3, 0, 1):
        end_band(i)
    drain(sx_s.at[0], sx_r.at[0], small_x, small_x)
    drain(sx_s.at[1], sx_r.at[1], rt_x, rt_x)
    router_sum = rt[:, rows_at(d, band)]
    for k in range(1, nd):
        small[...] = join(small[...], small_x[k - 1])
        router_sum = router_sum + rt_x[k - 1]
    rt_z[nz - 1] = router_sum
    small_send[1] = small[...]
    for j in range(1, nz):
        device = at.line(at.next_z(j))
        remote(small_send.at[1], small_z.at[j - 1], gl_s.at[4], gl_r.at[4], device).start()
        remote(rt_z.at[nz - 1], rt_z.at[j - 1], gl_s.at[5], gl_r.at[5], device).start()
    end_band(2)

    mix = gathered(mix_own, *mix_flow)
    output_out[...] = (hidden_at[...] + mix)[0 : sz.rows].astype(BF16)

    for i in range(4):
        drain(gl_s.at[i], gl_r.at[i], line_recv.at[:, i], line_recv.at[:, i])
    for n, landed in ((4, small_z), (5, rt_z.at[pl.ds(0, nz - 1)])):
        drain(gl_s.at[n], gl_r.at[n], landed, landed)
    totals = small[...]
    router_sum = rt_z[nz - 1]
    for j in range(1, nz):
        totals = join(totals, small_z[j - 1])
        router_sum = router_sum + rt_z[j - 1]
    gain_one_out[...] = totals[0:1]
    gain_two_out[...] = totals[1:2]
    rr = sz.router_rows
    own_router = router_sum[:, 0:rr]
    for i in range(1, nh):
        own_router = jnp.where(h == i, router_sum[:, i * rr : (i + 1) * rr], own_router)
    router_out[...] = own_router
    tau = tau_ref[...]
    factor = jnp.sqrt(tau / jnp.maximum(totals[2:3, 0:HEADS], tau))
    column = iota((1, cp), 1) // HEAD_DIM + h * (cp // HEAD_DIM)
    scale_row = jnp.zeros((1, cp), F32)
    for head in range(HEADS):
        scale_row = jnp.where(column == head, factor[:, head : head + 1], scale_row)
    for i in range(2):
        clipped_out[i] = (w_qkv_ref[i].astype(F32) * scale_row).astype(BF16)
    for i in range(4):
        sums = w_half[i, rows_at(z, rp), :]
        for j in range(1, nz):
            sums = sums + line_recv[j - 1, i].astype(F32)
        if i < 3:
            qkv_out[i] = sums
        else:
            out_out[...] = sums


def finish_kernel(sz, *refs):
    sources, results = refs[0:10], refs[10:20]
    full_out, out_sems, small_out = refs[20:]
    small_stores = [pltpu.make_async_copy(sources[n], results[n], small_out.at[n]) for n in range(8)]
    for copy in small_stores:
        copy.start()
    stores = []
    for e in range(sz.own):
        for i in range(2):
            full_out[i, e] = sources[8 + i][e].astype(F32)
            stores.append(pltpu.make_async_copy(full_out.at[i, e], results[8 + i].at[e], out_sems.at[i, e]))
            stores[-1].start()
    for copy in stores + small_stores:
        copy.wait()


def fast_body(
    sz, inputs, cotangent, routes, gain_attn, gain_expert, tau, w_qkv, w_out_attn, w_router, w_in, w_out
):
    ng, nz, nd, nh, pad, width, own = sz.groups, sz.nt, sz.nd, sz.nh, sz.pad, sz.width, sz.own
    rp, cp, band, parts, block = sz.row_piece, sz.col_piece, sz.band, sz.parts, sz.block
    many, hidden = ng * sz.cap, sz.hidden
    on_chip, anywhere = pl.BlockSpec(memory_space=pltpu.VMEM), pl.BlockSpec(memory_space=pltpu.HBM)

    def shape(dims, dtype):
        return jax.ShapeDtypeStruct(dims, dtype)

    def half(*dims):
        return pltpu.VMEM(dims, BF16)

    def full(*dims):
        return pltpu.VMEM(dims, F32)

    def pair(*dims):
        return [pltpu.SemaphoreType.DMA(dims)] * 2

    slot_buffer = half(ng, sz.group_slots, width)
    line_buffer = half(nz - 1, pad, width)
    quarter_dims = (ng, own * (sz.cap // nz), width // parts)
    quarter_buffer, few = half(*quarter_dims), ng * own * (sz.cap // nz)
    rr = sz.router_rows
    smalls = (
        shape(inputs.shape, BF16), shape(inputs.shape, BF16), shape((1, width), F32), shape((1, width), F32),
        shape((3, rp, cp), F32), shape((rp, cp), F32), shape((sz.experts, rr), F32), shape((2, rp, cp), BF16),
    )
    packed = pl.pallas_call(
        functools.partial(block_kernel, sz),
        out_shape=(*[pltpu.VMEM(x.shape, x.dtype) for x in smalls], half(*w_in.shape), half(*w_out.shape)),
        in_specs=[on_chip] * 9 + [anywhere] * 2,
        out_specs=(on_chip,) * 10,
        scratch_shapes=[
            half(4, rp, cp), half(4, width, width), half(sz.experts, 128), half(ng, sz.experts, 128),
            half(sz.experts, width), full(8, block), full(block, 128), half(sz.slots, block), half(block, sz.slots), half(few, block), half(block, few),
            half(block, width), half(block, width), *[slot_buffer] * 6,
            quarter_buffer, half(nz, *quarter_dims), half(nz, *quarter_dims), half(nz - 1, *quarter_dims), quarter_buffer,
            quarter_buffer,
            half(own, width, hidden), half(own, hidden, width), half(own, many, hidden), half(own, many, hidden),
            full(own, many, hidden),
            full(sz.experts, 128), full(ng, 8, 128), full(sz.experts, block), full(8, many),
            full(ng, 8, 128), full(sz.experts, 128),
            half(3, pad, width), half(HEADS, pad, pad), half(pad, width), full(pad, width), full(8, 128),
            full(block, width), full(pad, width), line_buffer, half(nz, pad, width), full(pad, width), line_buffer,
            half(nz, pad, width),
            half(pad, width), half(3, pad, width), half(nh - 1, 4, width, cp), half(nh - 1, 4, width, cp),
            full(4, width, cp), half(4, width, cp), half(nd - 1, 4, band, cp), half(4, band, cp),
            half(nz - 1, 4, rp, cp),
            full(8, width), full(2, 8, width), full(nh - 1, 8, width), full(nd - 1, 8, width), full(nz - 1, 8, width),
            full(sz.experts, width), full(nh - 1, sz.experts, width), full(nd - 1, sz.experts, band),
            full(nz, sz.experts, band),
            *pair(4), *pair(4), *pair(4 * (nh - 1)), *pair(1), *pair(parts), *pair(parts), *pair(parts), *pair(parts),
            *pair(1), *pair(own), *pair(parts), *pair(parts), *pair(1), *pair(parts), *pair(parts), *pair(4 * (nh - 1)),
            *pair(4), *pair(6), *pair(2 * (nh - 1)), *pair(2), *pair(1), *pair(1), *pair(1), *pair(1),
            *pair(parts), *pair(parts, 2),
            pltpu.SemaphoreType.DMA((2,)),
        ],
        compiler_params=pltpu.CompilerParams(collective_id=0, has_side_effects=True, vmem_limit_bytes=57 * 2**20),
        name="block",
    )(
        inputs, cotangent, routes.T, gain_attn[None, :], gain_expert[None, :], w_qkv, w_out_attn.T, w_router.T,
        tau[None, :], w_in, w_out,
    )

    both, dma = (2, *w_in.shape), pltpu.SemaphoreType.DMA
    output, grad_input, gain_one, gain_two, grad_qkv, grad_out, grad_router, clipped, grad_first, grad_second = (
        pl.pallas_call(
            functools.partial(finish_kernel, sz),
            out_shape=(*smalls, shape(w_in.shape, F32), shape(w_out.shape, F32)),
            in_specs=[on_chip] * 10,
            out_specs=(anywhere,) * 10,
            scratch_shapes=[full(*both), dma((2, own)), dma((8,))],
            compiler_params=pltpu.CompilerParams(vmem_limit_bytes=48 * 2**20),
            name="finish",
        )(*[pltpu.with_memory_space_constraint(x, pltpu.VMEM) for x in packed])
    )
    return (
        output, grad_input, gain_one[0], gain_two[0], grad_qkv, grad_out.T, grad_router.T, grad_first, grad_second,
        clipped,
    )


def gelu_tanh(inputs):
    return (
        0.5
        * inputs
        * (1.0 + jnp.tanh(0.7978845608028654 * (inputs + 0.044715 * inputs * inputs * inputs)))
    )


def unit_and_factor(inputs):
    centered = inputs - jnp.mean(inputs, -1, keepdims=True)
    factor = lax.rsqrt(jnp.mean(centered * centered, -1, keepdims=True) + 1e-06)
    return (centered * factor, factor)


def general_norm_back(grad_norm, unit_rows, factor, gain):
    grad, gain_row = norm_back(grad_norm, unit_rows, factor, gain)
    return grad, gain_row[0]


def attn_forward(block_parts):
    queries, key_rows, value_rows = block_parts
    scores = jnp.einsum(
        "bhqd,bhkd->bhqk", queries, key_rows, preferred_element_type=jnp.float32
    ) * HEAD_DIM ** (-0.5)
    row_peak = jnp.max(scores, -1, keepdims=True)
    exponent = jnp.exp(scores - row_peak)
    summed = jnp.sum(exponent, -1, keepdims=True)
    soft_weights = (exponent / summed).astype(jnp.bfloat16)
    mixed = jnp.einsum(
        "bhqk,bhkd->bhqd", soft_weights, value_rows, preferred_element_type=jnp.float32
    ).astype(jnp.bfloat16)
    return (mixed, (row_peak + jnp.log(summed))[..., 0], jnp.max(row_peak, axis=(0, 2, 3)))


def attn_backward(block_parts):
    queries, key_rows, value_rows, grad_mixed, log_total = block_parts
    score_scale = HEAD_DIM ** (-0.5)
    scores = (
        jnp.einsum("bhqd,bhkd->bhqk", queries, key_rows, preferred_element_type=jnp.float32)
        * score_scale
    )
    soft_weights = jnp.exp(scores - log_total[..., None])
    grad_soft = jnp.einsum(
        "bhqd,bhkd->bhqk", grad_mixed, value_rows, preferred_element_type=jnp.float32
    )
    inner_sum = jnp.sum(soft_weights * grad_soft, -1, keepdims=True)
    grad_scores = (soft_weights * (grad_soft - inner_sum)).astype(jnp.bfloat16)
    grad_query = (
        jnp.einsum("bhqk,bhkd->bhqd", grad_scores, key_rows, preferred_element_type=jnp.float32)
        * score_scale
    ).astype(jnp.bfloat16)
    grad_key = (
        jnp.einsum("bhqk,bhqd->bhkd", grad_scores, queries, preferred_element_type=jnp.float32)
        * score_scale
    ).astype(jnp.bfloat16)
    grad_value = jnp.einsum(
        "bhqk,bhqd->bhkd",
        soft_weights.astype(jnp.bfloat16),
        grad_mixed,
        preferred_element_type=jnp.float32,
    ).astype(jnp.bfloat16)
    return (grad_query, grad_key, grad_value)


def general_body(
    inputs, cotangent, routes, gain_attn, gain_expert, tau, w_qkv, w_out_attn, w_router, w_in, w_out
):
    row_count, width = inputs.shape
    n_dp = lax.axis_size("dp")
    n_heads = lax.axis_size("heads")
    n_tensor = lax.axis_size("tensor")
    row_piece = w_qkv.shape[1]
    col_piece = w_qkv.shape[2]
    own_heads = col_piece // HEAD_DIM
    head_start = lax.axis_index("heads") * col_piece
    x_float = inputs.astype(jnp.float32)
    unit_one, factor_one = unit_and_factor(x_float)
    normed_one = (unit_one * gain_attn).astype(jnp.bfloat16)
    stack_qkv, stack_out = (
        lax.all_gather(w_qkv[None], ("dp", "heads", "tensor"), axis=0, tiled=True),
        lax.all_gather(w_out_attn[None], ("dp", "heads", "tensor"), axis=0, tiled=True),
    )
    full_qkv = (
        stack_qkv.reshape(n_dp, n_heads, n_tensor, 3, row_piece, col_piece)
        .transpose(3, 0, 2, 4, 1, 5)
        .reshape(3, width, width)
    )
    full_out = (
        stack_out.reshape(n_dp, n_heads, n_tensor, col_piece, row_piece)
        .transpose(1, 3, 0, 2, 4)
        .reshape(width, width)
    )
    proj_w = lax.dynamic_slice_in_dim(full_qkv, head_start, col_piece, 2)
    attn_w = lax.dynamic_slice_in_dim(full_out, head_start, col_piece, 0)
    normed_all = lax.all_gather(normed_one, "heads", axis=0, tiled=True)
    head_cols = attn_w.shape[0]
    local_heads = head_cols // HEAD_DIM
    joined_w = jnp.concatenate([proj_w[0], proj_w[1], proj_w[2]], 1)
    projected = jnp.dot(normed_all, joined_w, preferred_element_type=jnp.float32).astype(
        jnp.bfloat16
    )
    images = normed_all.shape[0] // SEQ
    per_block = 4 if images % 4 == 0 else 3 if images % 3 == 0 else 2 if images % 2 == 0 else 1
    block_shape = (images // per_block, per_block, SEQ, local_heads, HEAD_DIM)

    def to_blocks(row_matrix):
        return row_matrix.reshape(block_shape).transpose(0, 1, 3, 2, 4)

    def from_blocks(block_array):
        return block_array.transpose(0, 1, 3, 2, 4).reshape(-1, head_cols)

    queries = to_blocks(projected[:, :head_cols])
    key_rows = to_blocks(projected[:, head_cols : 2 * head_cols])
    value_rows = to_blocks(projected[:, 2 * head_cols :])
    mixed, log_total, head_peaks = lax.map(attn_forward, (queries, key_rows, value_rows))
    mixed_rows = from_blocks(mixed)
    block_peak = jnp.max(head_peaks, 0)
    attn_out = lax.psum_scatter(
        jnp.dot(mixed_rows, attn_w, preferred_element_type=jnp.float32),
        "heads",
        scatter_dimension=0,
        tiled=True,
    )
    peak_full = lax.dynamic_update_slice_in_dim(
        jnp.full((HEADS,), -1e30, jnp.float32), block_peak, lax.axis_index("heads") * local_heads, 0
    )
    hidden = x_float + attn_out
    peak_all = lax.pmax(peak_full, ("dp", "heads", "tensor"))
    peak_logit = lax.dynamic_slice_in_dim(
        peak_all, lax.axis_index("heads") * own_heads, own_heads, 0
    )
    unit_two, factor_two = unit_and_factor(hidden)
    normed_two = (unit_two * gain_expert).astype(jnp.bfloat16)
    group_rows, group_cot = (
        lax.all_gather(normed_two, "tensor", axis=0, tiled=True),
        lax.all_gather(cotangent, "tensor", axis=0, tiled=True),
    )
    first_w, second_w, router_w = (
        lax.all_gather(w_in, ("dp", "heads"), axis=0, tiled=True),
        lax.all_gather(w_out, ("dp", "heads"), axis=0, tiled=True),
        lax.all_gather(w_router, ("dp", "heads"), axis=0, tiled=True),
    )
    logits = jnp.dot(group_rows, router_w, preferred_element_type=jnp.float32)
    chosen = jnp.take_along_axis(logits, routes, 1)
    exponent = jnp.exp(chosen - jnp.max(chosen, -1, keepdims=True))
    gate_values = exponent / jnp.sum(exponent, -1, keepdims=True)
    group_count = routes.shape[0]
    experts = router_w.shape[1]
    capacity = (group_count * 5 // (16 * experts) + 1) * 8
    flat_ids = routes.reshape(-1)
    ordering = jnp.argsort(flat_ids, stable=True)
    sorted_ids = flat_ids[ordering]
    counts = jnp.sum(
        (flat_ids[:, None] == jnp.arange(experts, dtype=jnp.int32)[None, :]).astype(jnp.int32), 0
    )
    expert_ids = jnp.arange(experts, dtype=jnp.int32)
    starts = jnp.sum(jnp.where(expert_ids[None, :] < expert_ids[:, None], counts[None, :], 0), 1)
    slot_rank = jnp.arange(2 * group_count, dtype=jnp.int32) - starts[sorted_ids]
    slot_table = (
        jnp.full((experts * capacity,), 2 * group_count, jnp.int32)
        .at[sorted_ids * capacity + slot_rank]
        .set(ordering)
    )
    slot_token = slot_table // 2
    padded_rows = jnp.concatenate([group_rows, jnp.zeros((1, width), jnp.bfloat16)], 0)
    slot_in = padded_rows[slot_token].reshape(experts, capacity, width)
    slot_gate = jnp.concatenate([gate_values.reshape(-1), jnp.zeros((1,), jnp.float32)], 0)[
        slot_table
    ]
    pre_gelu = jnp.einsum("ecd,edf->ecf", slot_in, first_w, preferred_element_type=jnp.float32)
    activated = gelu_tanh(pre_gelu).astype(jnp.bfloat16)
    slot_out = jnp.einsum(
        "ecf,efd->ecd", activated, second_w, preferred_element_type=jnp.float32
    ).reshape(-1, width)
    partial_value = (
        jnp.zeros((group_count + 1, width), jnp.float32)
        .at[slot_token]
        .add(slot_gate[:, None] * slot_out)[:group_count]
    )
    expert_mix = lax.psum_scatter(
        partial_value.astype(jnp.bfloat16), "tensor", scatter_dimension=0, tiled=True
    ).astype(jnp.float32)
    output = (hidden + expert_mix).astype(jnp.bfloat16)
    padded_cot = jnp.concatenate([group_cot, jnp.zeros((1, width), jnp.bfloat16)], 0)
    slot_cot = padded_cot[slot_token].astype(jnp.float32)
    grad_slot_out = (
        (slot_gate[:, None] * slot_cot).astype(jnp.bfloat16).reshape(experts, capacity, width)
    )
    gate_part = (
        jnp.zeros((2 * group_count + 1,), jnp.float32)
        .at[slot_table]
        .add(jnp.sum(slot_cot * slot_out, -1))[: 2 * group_count]
        .reshape(group_count, 2)
    )
    grad_act = jnp.einsum(
        "ecd,efd->ecf", grad_slot_out, second_w, preferred_element_type=jnp.float32
    )
    grad_pre = jax.vjp(gelu_tanh, pre_gelu)[1](grad_act)[0].astype(jnp.bfloat16)
    grad_first = jnp.einsum("ecd,ecf->edf", slot_in, grad_pre, preferred_element_type=jnp.float32)
    grad_second = jnp.einsum(
        "ecf,ecd->efd", activated, grad_slot_out, preferred_element_type=jnp.float32
    )
    grad_slots = jnp.einsum(
        "ecf,edf->ecd", grad_pre, first_w, preferred_element_type=jnp.float32
    ).reshape(-1, width)
    grad_part = (
        jnp.zeros((group_count + 1, width), jnp.float32)
        .at[slot_token]
        .add(grad_slots)[:group_count]
    )
    grad_normed_two, grad_gates = (
        lax.psum_scatter(
            grad_part.astype(jnp.bfloat16), "tensor", scatter_dimension=0, tiled=True
        ).astype(jnp.float32),
        lax.psum_scatter(
            gate_part.astype(jnp.bfloat16), "tensor", scatter_dimension=0, tiled=True
        ).astype(jnp.float32),
    )
    shard_first, shard_second = (
        lax.psum_scatter(
            grad_first.astype(jnp.bfloat16), ("dp", "heads"), scatter_dimension=0, tiled=True
        ).astype(jnp.float32),
        lax.psum_scatter(
            grad_second.astype(jnp.bfloat16), ("dp", "heads"), scatter_dimension=0, tiled=True
        ).astype(jnp.float32),
    )
    offset = lax.axis_index("tensor") * row_count
    local_gates = lax.dynamic_slice_in_dim(gate_values, offset, row_count, 0)
    local_routes = lax.dynamic_slice_in_dim(routes, offset, row_count, 0)
    grad_chosen = local_gates * (grad_gates - jnp.sum(local_gates * grad_gates, -1, keepdims=True))
    columns = jnp.arange(experts, dtype=jnp.int32)[None, :]
    grad_logits = (
        jnp.where(local_routes[:, 0:1] == columns, grad_chosen[:, 0:1], 0.0)
        + jnp.where(local_routes[:, 1:2] == columns, grad_chosen[:, 1:2], 0.0)
    ).astype(jnp.bfloat16)
    grad_normed_two = grad_normed_two + jnp.einsum(
        "re,de->rd", grad_logits, router_w, preferred_element_type=jnp.float32
    )
    router_term = jnp.einsum(
        "rd,re->de", normed_two, grad_logits, preferred_element_type=jnp.float32
    )
    grad_hidden_norm, gain_two_term = general_norm_back(grad_normed_two, unit_two, factor_two, gain_expert)
    grad_hidden = cotangent.astype(jnp.float32) + grad_hidden_norm
    grad_attn = lax.all_gather(grad_hidden.astype(jnp.bfloat16), "heads", axis=0, tiled=True)
    grad_mixed = jnp.einsum(
        "rd,cd->rc", grad_attn, attn_w, preferred_element_type=jnp.float32
    ).astype(jnp.bfloat16)
    out_term = jnp.einsum("rc,rd->cd", mixed_rows, grad_attn, preferred_element_type=jnp.float32)
    grad_query, grad_key, grad_value = lax.map(
        attn_backward, (queries, key_rows, value_rows, to_blocks(grad_mixed), log_total)
    )
    grad_proj = jnp.concatenate(
        [from_blocks(grad_query), from_blocks(grad_key), from_blocks(grad_value)], 1
    )
    grad_normed_one = lax.psum_scatter(
        jnp.einsum("rc,dc->rd", grad_proj, joined_w, preferred_element_type=jnp.float32).astype(
            jnp.bfloat16
        ),
        "heads",
        scatter_dimension=0,
        tiled=True,
    ).astype(jnp.float32)
    proj_term = jnp.einsum("rd,rc->dc", normed_all, grad_proj, preferred_element_type=jnp.float32)
    proj_stack = jnp.stack(
        [
            proj_term[:, :head_cols],
            proj_term[:, head_cols : 2 * head_cols],
            proj_term[:, 2 * head_cols :],
        ],
        0,
    )
    whole_proj = lax.dynamic_update_slice_in_dim(
        jnp.zeros((3, width, width), jnp.float32), proj_stack, head_start, 2
    )
    whole_out = lax.dynamic_update_slice_in_dim(
        jnp.zeros((width, width), jnp.float32), out_term, head_start, 0
    )
    send_qkv = (
        whole_proj.reshape(3, n_dp, n_tensor, row_piece, n_heads, col_piece)
        .transpose(1, 4, 2, 0, 3, 5)
        .reshape(-1, 3, row_piece, col_piece)
    )
    send_out = (
        whole_out.reshape(n_heads, col_piece, n_dp, n_tensor, row_piece)
        .transpose(2, 0, 3, 1, 4)
        .reshape(-1, col_piece, row_piece)
    )
    shard_proj, shard_attn = (
        lax.psum_scatter(send_qkv, ("dp", "heads", "tensor"), scatter_dimension=0, tiled=True),
        lax.psum_scatter(send_out, ("dp", "heads", "tensor"), scatter_dimension=0, tiled=True),
    )
    grad_input_norm, gain_one_term = general_norm_back(grad_normed_one, unit_one, factor_one, gain_attn)
    grad_input = (grad_hidden + grad_input_norm).astype(jnp.bfloat16)
    gain_one_grad, gain_two_grad, router_all = lax.psum(
        (gain_one_term, gain_two_term, router_term), ("dp", "heads", "tensor")
    )
    router_grad = lax.dynamic_slice_in_dim(
        router_all, lax.axis_index(("dp", "heads")) * w_router.shape[0], w_router.shape[0], 0
    )
    local_tau = lax.dynamic_slice_in_dim(tau, lax.axis_index("heads") * own_heads, own_heads, 0)
    clip_factor = jnp.sqrt(local_tau / jnp.maximum(peak_logit, local_tau))
    clipped = (w_qkv[:2].astype(jnp.float32) * jnp.repeat(clip_factor, HEAD_DIM)).astype(
        jnp.bfloat16
    )
    return (
        output,
        grad_input,
        gain_one_grad,
        gain_two_grad,
        shard_proj[0],
        shard_attn[0],
        router_grad,
        shard_first,
        shard_second,
        clipped,
    )


def body(*args):
    inputs, _, routes, _, _, _, w_qkv, _, w_router, w_in, _ = args
    sz = Sizes(
        lax.axis_size("dp"), lax.axis_size("heads"), lax.axis_size("tensor"), inputs, routes, w_qkv, w_router, w_in
    )
    if sz.fits():
        return fast_body(sz, *args)
    return general_body(*args)


def solution(mesh):
    return jax.shard_map(
        body,
        mesh=mesh,
        in_specs=(
            P(("dp", "heads", "tensor"), None),
            P(("dp", "heads", "tensor"), None),
            P(("dp", "heads"), None),
            P(),
            P(),
            P(),
            P(None, ("dp", "tensor"), "heads"),
            P("heads", ("dp", "tensor")),
            P(("dp", "heads"), None),
            P(("dp", "heads"), None, "tensor"),
            P(("dp", "heads"), "tensor", None),
        ),
        out_specs=(
            P(("dp", "heads", "tensor"), None),
            P(("dp", "heads", "tensor"), None),
            P(),
            P(),
            P(None, ("dp", "tensor"), "heads"),
            P("heads", ("dp", "tensor")),
            P(("dp", "heads"), None),
            P(("dp", "heads"), None, "tensor"),
            P(("dp", "heads"), "tensor", None),
            P(None, ("dp", "tensor"), "heads"),
        ),
        check_vma=False,
    )
```
